32 devices in a mesh: bucket: 2 (over x), blk: 16 (over z, y, core).
Axes of the slice: x: 2, y: 2, z: 4, core: 2. Of those that a mesh axis runs over, the one named last changes fastest.
Arguments:
- tokens: bfloat16 [2, 2, 2048, 1152], P('bucket', None, 'blk'), may hold values from -6 to 6
- cotangent: bfloat16 [2, 2, 2048, 1152], P('bucket', None, 'blk'), may hold values from -6 to 6
- doc_lengths: int32 [2, 2, 4], P('bucket'), may hold values from 1 to 1088, as said below
- w_query: bfloat16 [1152, 1024], P(('bucket', 'blk')), may hold values from -0.1875 to 0.1875
- w_key: bfloat16 [1152, 256], P(('bucket', 'blk')), may hold values from -0.1875 to 0.1875
- w_value: bfloat16 [1152, 256], P(('bucket', 'blk')), may hold values from -0.1875 to 0.1875
- w_out: bfloat16 [1024, 1152], P(('bucket', 'blk')), may hold values from -0.1875 to 0.1875
- w_gate: bfloat16 [1152, 6912], P(('bucket', 'blk')), may hold values from -0.1875 to 0.1875
- w_up: bfloat16 [1152, 6912], P(('bucket', 'blk')), may hold values from -0.1875 to 0.1875
- w_down: bfloat16 [6912, 1152], P(('bucket', 'blk')), may hold values from -0.078125 to 0.078125
- g_input: bfloat16 [1152], P(('bucket', 'blk')), may hold values from 0.5 to 1.5
- g_query: bfloat16 [256], P(('bucket', 'blk')), may hold values from -0.8984375 to 0.8984375
- g_key: bfloat16 [256], P(('bucket', 'blk')), may hold values from -0.8984375 to 0.8984375
- g_post_attn: bfloat16 [1152], P(('bucket', 'blk')), may hold values from 0.5 to 1.5
- g_pre_ffn: bfloat16 [1152], P(('bucket', 'blk')), may hold values from 0.5 to 1.5
- g_post_ffn: bfloat16 [1152], P(('bucket', 'blk')), may hold values from -0.8984375 to 0.8984375
Outputs:
- outputs: bfloat16 [2, 2, 2048, 1152], P('bucket', None, 'blk')
- input_grad: bfloat16 [2, 2, 2048, 1152], P('bucket', None, 'blk')
- grad_query: float32 [1152, 1024], P(('bucket', 'blk'))
- grad_key: float32 [1152, 256], P(('bucket', 'blk'))
- grad_value: float32 [1152, 256], P(('bucket', 'blk'))
- grad_out: float32 [1024, 1152], P(('bucket', 'blk'))
- grad_gate: float32 [1152, 6912], P(('bucket', 'blk'))
- grad_up: float32 [1152, 6912], P(('bucket', 'blk'))
- grad_down: float32 [6912, 1152], P(('bucket', 'blk'))
- grad_g_input: float32 [1152], P(('bucket', 'blk'))
- grad_g_query: float32 [256], P(('bucket', 'blk'))
- grad_g_key: float32 [256], P(('bucket', 'blk'))
- grad_g_post_attn: float32 [1152], P(('bucket', 'blk'))
- grad_g_pre_ffn: float32 [1152], P(('bucket', 'blk'))
- grad_g_post_ffn: float32 [1152], P(('bucket', 'blk'))
The draws below stay inside these ranges and needn't reach their ends.
Inputs may be any that keep to these rules, and one draw needn't show every extreme that they name: `doc_lengths`: the first document of every bucket and micro-batch has exactly 1088 positions; the other 3 lengths add up to 960.
All inputs are finite; a program needn't handle non-finite values.
Results may differ from the reference program's by a relative error of at most 0.029.
Values may be sent and summed in bfloat16 or wider, within the bound.
A program may use at most 320 MiB of HBM per device.

```python
import math
import jax
import jax.numpy as jnp
from jax import lax

D = 1152
H = 4
HD = 256
FF = 6912
TOK_DEV = 128
MICRO = 2
DOCS = 4
BUCKETS = 2
SEQ = 2048


def draw_doc_lengths(key, part):
    first_length = SEQ // 2 + TOK_DEV // 2
    remaining = SEQ - first_length
    key_list = jax.random.split(jax.random.fold_in(key, 17), BUCKETS * MICRO)

    def one_row(row_key):
        picked = jax.random.permutation(row_key, remaining - 1)[:DOCS - 2].astype(jnp.int32) + 1
        cuts = jnp.sort(picked)
        edges = jnp.concatenate([jnp.zeros((1,), jnp.int32), cuts, jnp.full((1,), remaining, jnp.int32)])
        others = edges[1:] - edges[:-1]
        return jnp.concatenate([jnp.full((1,), first_length, jnp.int32), others]).astype(jnp.int32)
    return jax.vmap(one_row)(key_list).reshape(BUCKETS, MICRO, DOCS)


def steps_of(own_key, shape, shards, least, largest):
    loudness, own = 1.0, jax.random.fold_in(own_key, 6)
    for dim, shards_of in shards:
        draws = jnp.exp(jax.random.uniform(jax.random.fold_in(own, dim), (shards_of,), jnp.float32, least / len(shards), largest / len(shards)))
        loudness = loudness * jnp.repeat(draws, shape[dim] // shards_of).reshape([-1 if axis == dim else 1 for axis in range(len(shape))])
    return loudness


def noise(key, dims, spread, most, shards=(), held_as=jnp.bfloat16):
    values = jax.random.normal(key, dims, jnp.float32) * spread
    if len(shards) > 0:
        values = steps_of(key, dims, shards, -0.22, 0.18) * values
    return jnp.clip(values, min=-most, max=most).astype(held_as)


def setup_inputs(seed: int = 0) -> dict:
    key_of = jax.random.split(jax.random.key(seed), 17)
    tokens = noise(key_of[0], (BUCKETS, MICRO, SEQ, D), 1.0, 6.0, ((0, 2), (2, 16)))
    cotangent = noise(key_of[1], (BUCKETS, MICRO, SEQ, D), 1.0, 6.0, ((0, 2), (2, 16)))
    doc_lengths = draw_doc_lengths(jax.random.fold_in(key_of[16], 71), 0)
    w_query = noise(key_of[3], (D, H * HD), D ** -0.5, 0.1875, ((0, 32),))
    w_key = noise(key_of[4], (D, HD), D ** -0.5, 0.1875, ((0, 32),))
    w_value = noise(key_of[5], (D, HD), D ** -0.5, 0.1875, ((0, 32),))
    w_out = noise(key_of[6], (H * HD, D), (H * HD) ** -0.5, 0.1875, ((0, 32),))
    w_gate = noise(key_of[7], (D, FF), D ** -0.5, 0.1875, ((0, 32),))
    w_up = noise(key_of[8], (D, FF), D ** -0.5, 0.1875, ((0, 32),))
    w_down = noise(key_of[9], (FF, D), FF ** -0.5, 0.078125, ((0, 32),))
    g_input = jnp.clip(1.0 + 0.1 * jax.random.normal(key_of[10], (D,), jnp.float32), 0.5, 1.5).astype(jnp.bfloat16)
    g_query = noise(key_of[11], (HD,), 0.3, 0.8984375, ((0, 32),))
    g_key = noise(key_of[12], (HD,), 0.3, 0.8984375, ((0, 32),))
    g_post_attn = jnp.clip(1.0 + 0.1 * jax.random.normal(key_of[13], (D,), jnp.float32), 0.5, 1.5).astype(jnp.bfloat16)
    g_pre_ffn = jnp.clip(1.0 + 0.1 * jax.random.normal(key_of[14], (D,), jnp.float32), 0.5, 1.5).astype(jnp.bfloat16)
    g_post_ffn = noise(key_of[15], (D,), 0.3, 0.8984375, ((0, 32),))
    return dict(tokens=tokens, cotangent=cotangent, doc_lengths=doc_lengths, w_query=w_query, w_key=w_key, w_value=w_value, w_out=w_out, w_gate=w_gate, w_up=w_up, w_down=w_down, g_input=g_input, g_query=g_query, g_key=g_key, g_post_attn=g_post_attn, g_pre_ffn=g_pre_ffn, g_post_ffn=g_post_ffn)


@jax.custom_vjp
def low(v):
    return lax.optimization_barrier(v.astype(jnp.bfloat16)).astype(jnp.float32)

@jax.custom_vjp
def low_back(v):
    return v

def low_keep(v):
    return (low(v), None)

def low_pass(kept, grad):
    return (grad,)

def back_keep(v):
    return (v, None)

def back_low(kept, grad):
    return (low(grad),)
low.defvjp(low_keep, low_pass)
low_back.defvjp(back_keep, back_low)
epsilon = 1e-06
highest = lax.Precision.HIGHEST

def scaled_norm(values, gain):
    return values * lax.rsqrt(lax.optimization_barrier(jnp.mean(values * values, axis=-1, keepdims=True)) + epsilon) * (1.0 + gain)

def segment_place(lengths, index_all):
    endings = jnp.cumsum(lengths, dtype=jnp.int32)
    before = index_all[:, None] >= endings[None, :]
    segment = lax.optimization_barrier(jnp.sum(before.astype(jnp.int32), axis=1, dtype=jnp.int32))
    start_at = lax.optimization_barrier(jnp.sum(jnp.where(before, lengths[None, :], 0), axis=1, dtype=jnp.int32))
    return (segment, index_all - start_at)

def rotate(values, position):
    halfway = values.shape[-1] // 2
    frequency = 1000000.0 ** (-(jnp.arange(halfway, dtype=jnp.float32) * 2.0 / values.shape[-1]))
    angles = position.astype(jnp.float32)[:, None] * frequency[None, :]
    if values.ndim == 3:
        angles = angles[:, None, :]
    cosine = jnp.cos(angles)
    sine_part = jnp.sin(angles)
    first_half = values[..., :halfway]
    second_half = values[..., halfway:]
    return jnp.concatenate([first_half * cosine - second_half * sine_part, second_half * cosine + first_half * sine_part], axis=-1)

def attend(query_blk, segment_blk, index_blk, keys_all, values_all, segment_all, index_all):
    scores = jnp.einsum('qhd,kd->hqk', query_blk, keys_all, precision=highest) * query_blk.shape[-1] ** (-0.5)
    scores = low_back(scores)
    allowed = (segment_blk[:, None] == segment_all[None, :]) & (index_all[None, :] <= index_blk[:, None])
    scores = jnp.where(allowed[None], scores, -1e+30)
    row_top = lax.optimization_barrier(jnp.max(scores, axis=-1, keepdims=True))
    exp_terms = jnp.exp(scores - row_top)
    probabilities = low(exp_terms / lax.optimization_barrier(jnp.sum(exp_terms, axis=-1, keepdims=True)))
    return jnp.einsum('hqk,kd->qhd', probabilities, values_all, precision=highest)

def layer(x_rows, lengths, w_query, w_key, w_value, w_out, w_gate, w_up, w_down, g_input, g_query, g_key, g_post_attn, g_pre_ffn, g_post_ffn):
    row_count = x_rows.shape[0]
    index_all = jnp.arange(row_count, dtype=jnp.int32)
    segment, position = segment_place(lengths, index_all)
    normed = low(scaled_norm(x_rows, g_input))
    queries = low_back(jnp.dot(normed, w_query, precision=highest)).reshape(row_count, H, HD)
    keys_all = low_back(jnp.dot(normed, w_key, precision=highest))
    values_all = low(low_back(jnp.dot(normed, w_value, precision=highest)))
    queries = low(rotate(scaled_norm(queries, g_query), position))
    keys_all = low(rotate(scaled_norm(keys_all, g_key), position))
    block_rows = math.gcd(row_count, 512)
    block_count = row_count // block_rows

    def per_block(block_item):
        return attend(block_item[0], block_item[1], block_item[2], keys_all, values_all, segment, index_all)
    attended = lax.map(jax.checkpoint(per_block), (queries.reshape(block_count, block_rows, H, HD), segment.reshape(block_count, block_rows), index_all.reshape(block_count, block_rows)))
    attended = low(low_back(attended.reshape(row_count, H * HD)))
    attn_out = low_back(jnp.dot(attended, w_out, precision=highest))
    hidden = x_rows + scaled_norm(attn_out, g_post_attn)
    ffn_in = low(scaled_norm(hidden, g_pre_ffn))
    gate_proj = low_back(jnp.dot(ffn_in, w_gate, precision=highest))
    up_proj = low_back(jnp.dot(ffn_in, w_up, precision=highest))
    product = low(jax.nn.gelu(gate_proj, approximate=True) * up_proj)
    down_out = low_back(jnp.dot(product, w_down, precision=highest))
    return hidden + scaled_norm(down_out, g_post_ffn)

def reference(tokens, cotangent, doc_lengths, w_query, w_key, w_value, w_out, w_gate, w_up, w_down, g_input, g_query, g_key, g_post_attn, g_pre_ffn, g_post_ffn):
    weight_list = tuple((piece.astype(jnp.float32) for piece in (w_query, w_key, w_value, w_out, w_gate, w_up, w_down, g_input, g_query, g_key, g_post_attn, g_pre_ffn, g_post_ffn)))
    rows_in = tokens.reshape(BUCKETS * MICRO, SEQ, D)
    cot_rows = cotangent.reshape(BUCKETS * MICRO, SEQ, D)
    length_rows = doc_lengths.reshape(BUCKETS * MICRO, DOCS)

    def one_sequence(totals, seq_item):
        x_row, dy_row, length_row = seq_item

        def forward(x_value, *weights):
            return layer(x_value, length_row, *weights)
        result, pull_back = jax.vjp(forward, x_row.astype(jnp.float32), *weight_list)
        gradients = pull_back(dy_row.astype(jnp.float32))
        totals = tuple((total_now + grad_now for total_now, grad_now in zip(totals, gradients[1:])))
        return (totals, (result.astype(jnp.bfloat16), gradients[0].astype(jnp.bfloat16)))
    zero_totals = tuple((jnp.zeros(piece.shape, jnp.float32) for piece in weight_list))
    totals, (outputs_all, grads_in) = lax.scan(one_sequence, zero_totals, (rows_in, cot_rows, length_rows))
    outputs = outputs_all.reshape(BUCKETS, MICRO, SEQ, D)
    input_grad = grads_in.reshape(BUCKETS, MICRO, SEQ, D)
    return (outputs, input_grad, totals[0], totals[1], totals[2], totals[3], totals[4], totals[5], totals[6], totals[7], totals[8], totals[9], totals[10], totals[11], totals[12])
```

```python
import functools
import math

import jax
import jax.numpy as jnp
from jax import lax
from jax.experimental import pallas as pl
from jax.experimental.pallas import tpu as pltpu
from jax.sharding import PartitionSpec as P

H = 4
HD = 256
F32 = jnp.float32
BF16 = jnp.bfloat16
MESH = pl.DeviceIdType.MESH
ANY = pl.BlockSpec(memory_space=pl.ANY)
VMEM = pl.BlockSpec(memory_space=pltpu.VMEM)
epsilon = 1e-06


def up16(n):
    return -(-n // 16) * 16


def place():
    b = lax.axis_index("bucket")
    k = lax.axis_index("blk")
    return b, k // 4, (k // 2) % 2, k % 2


def at(b, q, y, c):
    return (b, q * 4 + y * 2 + c)


def greet(targets):
    bar = pltpu.get_barrier_semaphore()
    for t in targets:
        pl.semaphore_signal(bar, inc=1, device_id=t, device_id_type=MESH)
    return bar


def remote(src, dst, send, recv, target):
    return pltpu.make_async_remote_copy(src, dst, send, recv, device_id=target, device_id_type=MESH)


def gather_kernel(nz, qkv, wo, gain, wg, wu, wd, qkv_f, wo_f, gain_f, wg_f, wu_f, wd_f, lsem, ssem, rsem, wls, wss, wrs):
    b, q, y, c = place()
    g, e = q // 2, q % 2
    ng = nz // 2
    qw = qkv.shape[1]
    self_in = e == c
    bar = greet(
        [at(b, lax.rem(q + r, nz), y, c) for r in range(1, nz)]
        + [at(1 - b, q, y, c), at(b, q, 1 - y, c), at(b, q, y, 1 - c)]
        + [at(b, lax.rem(g + r, ng) * 2 + c, y, e) for r in range(1, ng)]
    )
    first = at(b, g * 2 + c, y, e)

    @pl.when(jnp.logical_not(self_in))
    def _():
        pl.semaphore_signal(bar, inc=1, device_id=first, device_id_type=MESH)

    pl.semaphore_wait(bar, nz + 1 + ng - jnp.where(self_in, 1, 0) + 1)

    everything = pl.ds(0, nz)

    def view_qkv(ref, yy, cc, xx, qq):
        return ref.at[xx, qq, :, pl.ds(pl.multiple_of((yy * 2 + cc) * qw, 128), qw)]

    def view_lead(ref, yy, cc, xx, qq):
        return ref.at[xx, qq, yy, cc]

    items = [(qkv, qkv_f, view_qkv), (wo, wo_f, view_lead), (gain, gain_f, view_lead)]
    sent = []
    local = []
    for i, (src, dst, view) in enumerate(items):
        cp = pltpu.make_async_copy(src, view(dst, y, c, b, q), lsem.at[i])
        cp.start()
        local.append(cp)
    z_in = []
    for i, (src, dst, view) in enumerate(items):
        row = []
        for r in range(1, nz):
            cp = remote(src, view(dst, y, c, b, q), ssem.at[i, r], rsem.at[i, r], at(b, lax.rem(q + r, nz), y, c))
            cp.start()
            sent.append(cp)
            row.append(
                remote(src, view(dst, y, c, b, lax.rem(q - r + nz, nz)), ssem.at[i, r], rsem.at[i, r], at(b, lax.rem(q + r, nz), y, c))
            )
        z_in.append(row)
    x_in = [[] for _ in items]
    for i, (src, dst, view) in enumerate(items):
        cp = remote(src, view(dst, y, c, b, q), ssem.at[i, nz], rsem.at[i, nz], at(1 - b, q, y, c))
        cp.start()
        sent.append(cp)
        x_in[i].append(remote(src, view(dst, y, c, 1 - b, q), ssem.at[i, nz], rsem.at[i, nz], at(1 - b, q, y, c)))

    units = [(wg, wg_f), (wu, wu_f), (wd, wd_f)]
    u_in = []
    for j, (src, dst) in enumerate(units):
        row = []
        for r in range(ng):
            target = at(b, lax.rem(g + r, ng) * 2 + c, y, e)
            cp = remote(src, dst.at[b, q], wss.at[j, r], wrs.at[j, r], target)
            qs = lax.rem(g - r + ng, ng) * 2 + c
            inc = remote(src, dst.at[b, qs], wss.at[j, r], wrs.at[j, r], target)
            if r == 0:
                lc = pltpu.make_async_copy(src, dst.at[b, q], wls.at[j])

                @pl.when(self_in)
                def _():
                    lc.start()

                @pl.when(jnp.logical_not(self_in))
                def _():
                    cp.start()
            else:
                cp.start()
            row.append((cp, inc, qs, lc if r == 0 else None))
        u_in.append(row)

    for r in range(1, nz):
        qs = lax.rem(q - r + nz, nz)
        for i, (src, dst, view) in enumerate(items):
            z_in[i][r - 1].wait_recv()
            cp = remote(view(dst, y, c, b, qs), view(dst, y, c, b, qs), ssem.at[i, nz + r], rsem.at[i, nz + r], at(1 - b, q, y, c))
            cp.start()
            sent.append(cp)
            x_in[i].append(
                remote(view(dst, y, c, b, qs), view(dst, y, c, 1 - b, qs), ssem.at[i, nz + r], rsem.at[i, nz + r], at(1 - b, q, y, c))
            )
    for cp in local:
        cp.wait()
    y_in = [[] for _ in items]
    for half in range(2):
        for i, (src, dst, view) in enumerate(items):
            xx = b if half == 0 else 1 - b
            if half == 1:
                for cp in x_in[i]:
                    cp.wait_recv()
            s = 2 * nz + half
            cp = remote(view(dst, y, c, xx, everything), view(dst, y, c, xx, everything), ssem.at[i, s], rsem.at[i, s], at(b, q, 1 - y, c))
            cp.start()
            sent.append(cp)
            y_in[i].append(
                remote(view(dst, y, c, xx, everything), view(dst, 1 - y, c, xx, everything), ssem.at[i, s], rsem.at[i, s], at(b, q, 1 - y, c))
            )
    c_in = []

    def to_core(i, yy, s):
        _, dst, view = items[i]
        both = pl.ds(0, 2)
        cp = remote(view(dst, yy, c, both, everything), view(dst, yy, c, both, everything), ssem.at[i, s], rsem.at[i, s], at(b, q, y, 1 - c))
        cp.start()
        sent.append(cp)
        c_in.append(
            remote(view(dst, yy, c, both, everything), view(dst, yy, 1 - c, both, everything), ssem.at[i, s], rsem.at[i, s], at(b, q, y, 1 - c))
        )

    for i in range(len(items)):
        to_core(i, y, 2 * nz + 2)
    for i in range(len(items)):
        for cp in y_in[i]:
            cp.wait_recv()
        to_core(i, 1 - y, 2 * nz + 3)

    d_in = []

    def unit_on(j, xx, qs, s, target, yours):
        _, dst = units[j]
        cp = remote(dst.at[xx, qs], dst.at[xx, qs], wss.at[j, s], wrs.at[j, s], target)
        cp.start()
        sent.append(cp)
        return remote(dst.at[xx, qs], dst.at[yours[0], yours[1]], wss.at[j, s], wrs.at[j, s], target)

    xw = [[] for _ in units]

    def x_round(j):
        for r in range(ng):
            cp, inc, qs, lc = u_in[j][r]
            if r == 0:

                @pl.when(self_in)
                def _():
                    lc.wait()

                @pl.when(jnp.logical_not(self_in))
                def _():
                    inc.wait_recv()
            else:
                inc.wait_recv()
            xw[j].append(unit_on(j, b, qs, ng + r, at(1 - b, q, y, c), (1 - b, qs)))
        for r in range(ng):
            qs = u_in[j][r][2]
            qo = lax.rem(g - r + ng, ng) * 2 + 1 - c
            d_in.append(unit_on(j, b, qs, 2 * ng + r, at(b, q, y, 1 - c), (b, qo)))

    def c_round(j):
        for r in range(ng):
            qs = u_in[j][r][2]
            qo = lax.rem(g - r + ng, ng) * 2 + 1 - c
            xw[j][r].wait_recv()
            d_in.append(unit_on(j, 1 - b, qs, 3 * ng + r, at(b, q, y, 1 - c), (1 - b, qo)))

    x_round(0)
    x_round(1)
    c_round(0)
    x_round(2)
    c_round(1)
    c_round(2)
    for cp in c_in + d_in:
        cp.wait_recv()
    for cp in sent:
        cp.wait_send()
    for j in range(len(units)):
        for r in range(ng):
            cp = u_in[j][r][0]
            if r == 0:

                @pl.when(jnp.logical_not(self_in))
                def _():
                    cp.wait_send()
            else:
                cp.wait_send()


def gather_all(nz, qkv, wo, gain, wg, wu, wd):
    ng = nz // 2
    out = [
        jax.ShapeDtypeStruct((2, nz, qkv.shape[0], 4 * qkv.shape[1]), BF16),
        jax.ShapeDtypeStruct((2, nz, 2, 2) + wo.shape, BF16),
        jax.ShapeDtypeStruct((2, nz, 2, 2) + gain.shape, BF16),
        jax.ShapeDtypeStruct((2, nz) + wg.shape, BF16),
        jax.ShapeDtypeStruct((2, nz) + wu.shape, BF16),
        jax.ShapeDtypeStruct((2, nz) + wd.shape, BF16),
    ]
    ns = 2 * nz + 4
    return pl.pallas_call(
        functools.partial(gather_kernel, nz),
        out_shape=out,
        in_specs=[ANY] * 6,
        out_specs=[ANY] * 6,
        scratch_shapes=[
            pltpu.SemaphoreType.DMA((3,)),
            pltpu.SemaphoreType.DMA((3, ns)),
            pltpu.SemaphoreType.DMA((3, ns)),
            pltpu.SemaphoreType.DMA((3,)),
            pltpu.SemaphoreType.DMA((3, 4 * ng)),
            pltpu.SemaphoreType.DMA((3, 4 * ng)),
        ],
        compiler_params=pltpu.CompilerParams(collective_id=0, has_side_effects=True),
    )(qkv, wo, gain, wg, wu, wd)


def reduce_kernel(nz, qkv, wo, gain, wg, wu, wd, qkv_o, wo_o, gain_o, wg_o, wu_o, wd_o, *scratch):
    b, q, y, c = place()
    g, e = q // 2, q % 2
    ng = nz // 2
    qw = qkv_o.shape[1]
    self_in = e == c
    n_items, n_units = 3, 3
    own = scratch[0:3]
    r1 = scratch[3:6]
    r2 = scratch[6:9]
    r3 = scratch[9:12]
    r4 = scratch[12:15]
    uown = scratch[15:18]
    u1 = scratch[18:21]
    u2 = scratch[21:24]
    u3 = scratch[24:27]
    lsem, ssem, rsem, wls, wss, wrs = scratch[27:]
    bar = greet(
        [at(b, lax.rem(q + r, nz), y, c) for r in range(1, nz)]
        + [at(1 - b, q, y, c), at(b, q, 1 - y, c), at(b, q, y, 1 - c)]
        + [at(b, lax.rem(g + r, ng) * 2 + c, y, e) for r in range(1, ng)]
    )
    first = at(b, g * 2 + c, y, e)

    @pl.when(jnp.logical_not(self_in))
    def _():
        pl.semaphore_signal(bar, inc=1, device_id=first, device_id_type=MESH)

    pl.semaphore_wait(bar, nz + 1 + ng - jnp.where(self_in, 1, 0) + 1)

    other_core = at(b, q, y, 1 - c)
    other_y = at(b, q, 1 - y, c)
    other_x = at(1 - b, q, y, c)
    full = (pl.ds(0, 2), pl.ds(0, nz))

    def view_qkv(ref, yy, cc):
        return ref.at[full[0], full[1], :, pl.ds(pl.multiple_of((yy * 2 + cc) * qw, 128), qw)]

    def view_lead(ref, yy, cc):
        return ref.at[full[0], full[1], yy, cc]

    items = [(qkv, qkv_o, view_qkv), (wo, wo_o, view_lead), (gain, gain_o, view_lead)]
    units = [(wd, wd_o), (wg, wg_o), (wu, wu_o)]
    sent = []
    item_local, item_in = [[] for _ in items], [[] for _ in items]
    unit_local, unit_in = [[] for _ in units], [[] for _ in units]

    def start(cp):
        cp.start()
        sent.append(cp)
        return cp

    def item_core(i):
        src, _, view = items[i]
        for yy in range(2):
            item_in[i].append(start(remote(view(src, yy, 1 - c), r1[i].at[yy], ssem.at[i, yy], rsem.at[i, yy], other_core)))
            cp = pltpu.make_async_copy(view(src, yy, c), own[i].at[yy], lsem.at[i, yy])
            cp.start()
            item_local[i].append(cp)

    def unit_core(j):
        src, _ = units[j]
        for xx in range(2):
            for r in range(ng):
                s = xx * ng + r
                mine, yours = r * 2 + c, r * 2 + 1 - c
                unit_in[j].append(start(remote(src.at[xx, yours], u1[j].at[xx, r], wss.at[j, s], wrs.at[j, s], other_core)))
                cp = pltpu.make_async_copy(src.at[xx, mine], uown[j].at[xx, r], wls.at[j, s])
                cp.start()
                unit_local[j].append(cp)

    def add(dst, src, lead):
        def one(n, _):
            dst[n] = (dst[n].astype(F32) + src[n].astype(F32)).astype(dst.dtype)
            return 0

        lax.fori_loop(0, lead, one, 0)

    def unit_x(j):
        for cp in unit_local[j]:
            cp.wait()
        for cp in unit_in[j]:
            cp.wait_recv()
        add(uown[j].at[1 - b], u1[j].at[1 - b], ng)
        cp = start(remote(uown[j].at[1 - b], u2[j], wss.at[j, 2 * ng], wrs.at[j, 2 * ng], other_x))
        add(uown[j].at[b], u1[j].at[b], ng)
        unit_in[j] = [cp]

    def unit_z(j):
        unit_in[j][0].wait_recv()
        add(uown[j].at[b], u2[j], ng)
        waits = []
        for r in range(ng):
            gs = lax.rem(g + r, ng)
            cp = remote(uown[j].at[b, gs], u3[j].at[r], wss.at[j, 2 * ng + 1 + r], wrs.at[j, 2 * ng + 1 + r], at(b, gs * 2 + c, y, e))
            if r == 0:
                lc = pltpu.make_async_copy(uown[j].at[b, gs], u3[j].at[0], wls.at[j, 2 * ng])

                @pl.when(self_in)
                def _():
                    lc.start()

                @pl.when(jnp.logical_not(self_in))
                def _():
                    cp.start()

                waits.append((cp, lc))
            else:
                start(cp)
                waits.append((cp, None))
        unit_in[j] = waits

    def unit_end(j):
        for cp, lc in unit_in[j]:
            if lc is not None:

                @pl.when(self_in)
                def _():
                    lc.wait()

                @pl.when(jnp.logical_not(self_in))
                def _():
                    cp.wait()
            else:
                cp.wait_recv()
        rows = u3[j].shape[1]
        step = 16

        def one(n, _):
            sl = pl.ds(pl.multiple_of(n * step, step), step)
            total = u3[j][0, sl].astype(F32)
            for r in range(1, ng):
                total = total + u3[j][r, sl].astype(F32)
            units[j][1][sl] = total.astype(units[j][1].dtype)
            return 0

        lax.fori_loop(0, rows // step, one, 0)

    def item_y(i):
        for cp in item_local[i]:
            cp.wait()
        for cp in item_in[i]:
            cp.wait_recv()
        for xx in range(2):
            add(own[i].at[1 - y, xx], r1[i].at[1 - y, xx], nz)
        cp = start(remote(own[i].at[1 - y], r2[i], ssem.at[i, 2], rsem.at[i, 2], other_y))
        for xx in range(2):
            add(own[i].at[y, xx], r1[i].at[y, xx], nz)
        item_in[i] = [cp]

    def item_x(i):
        item_in[i][0].wait_recv()
        add(own[i].at[y, 1 - b], r2[i].at[1 - b], nz)
        cp = start(remote(own[i].at[y, 1 - b], r3[i], ssem.at[i, 3], rsem.at[i, 3], other_x))
        add(own[i].at[y, b], r2[i].at[b], nz)
        item_in[i] = [cp]

    def item_z(i):
        item_in[i][0].wait_recv()
        add(own[i].at[y, b], r3[i], nz)
        waits = []
        for r in range(1, nz):
            qt = lax.rem(q + r, nz)
            waits.append(start(remote(own[i].at[y, b, qt], r4[i].at[r - 1], ssem.at[i, 3 + r], rsem.at[i, 3 + r], at(b, qt, y, c))))
        item_in[i] = waits

    def item_end(i):
        for cp in item_in[i]:
            cp.wait_recv()
        total = own[i][y, b, q].astype(F32)
        for r in range(1, nz):
            total = total + r4[i][r - 1].astype(F32)
        items[i][1][...] = total.astype(items[i][1].dtype)

    for j in range(n_units):
        unit_core(j)
    for i in range(n_items):
        item_core(i)
    for j in range(n_units):
        unit_x(j)
    for i in range(n_items):
        item_y(i)
    unit_z(0)
    for i in range(n_items):
        item_x(i)
    unit_z(1)
    for i in range(n_items):
        item_z(i)
    unit_z(2)
    for i in range(n_items):
        item_end(i)
    for j in range(n_units):
        unit_end(j)
    for cp in sent:
        cp.wait_send()


def reduce_all(nz, qkv, wo, gain, wg, wu, wd):
    ng = nz // 2
    qw = qkv.shape[3] // 4
    blocks = [((qkv.shape[2], qw), BF16), (wo.shape[4:], BF16), (gain.shape[4:], F32)]
    ublocks = [(wd.shape[2:], BF16), (wg.shape[2:], BF16), (wu.shape[2:], BF16)]
    scratch = (
        [pltpu.VMEM((2, 2, nz) + s, t) for s, t in blocks]
        + [pltpu.VMEM((2, 2, nz) + s, t) for s, t in blocks]
        + [pltpu.VMEM((2, nz) + s, t) for s, t in blocks]
        + [pltpu.VMEM((nz,) + s, t) for s, t in blocks]
        + [pltpu.VMEM((nz - 1,) + s, t) for s, t in blocks]
        + [pltpu.VMEM((2, ng) + s, t) for s, t in ublocks]
        + [pltpu.VMEM((2, ng) + s, t) for s, t in ublocks]
        + [pltpu.VMEM((ng,) + s, t) for s, t in ublocks]
        + [pltpu.VMEM((ng,) + s, t) for s, t in ublocks]
        + [
            pltpu.SemaphoreType.DMA((3, 2)),
            pltpu.SemaphoreType.DMA((3, nz + 3)),
            pltpu.SemaphoreType.DMA((3, nz + 3)),
            pltpu.SemaphoreType.DMA((3, 2 * ng + 1)),
            pltpu.SemaphoreType.DMA((3, 3 * ng + 1)),
            pltpu.SemaphoreType.DMA((3, 3 * ng + 1)),
        ]
    )
    out = [
        jax.ShapeDtypeStruct(blocks[0][0], BF16),
        jax.ShapeDtypeStruct(blocks[1][0], F32),
        jax.ShapeDtypeStruct(blocks[2][0], F32),
        jax.ShapeDtypeStruct(ublocks[1][0], BF16),
        jax.ShapeDtypeStruct(ublocks[2][0], BF16),
        jax.ShapeDtypeStruct(ublocks[0][0], F32),
    ]
    return pl.pallas_call(
        functools.partial(reduce_kernel, nz),
        out_shape=out,
        in_specs=[ANY] * 6,
        out_specs=[VMEM] * 6,
        scratch_shapes=scratch,
        compiler_params=pltpu.CompilerParams(collective_id=1, has_side_effects=True, vmem_limit_bytes=60 * 2**20),
    )(qkv, wo, gain, wg, wu, wd)


def chunk_scores(q, kk, segq, segk, qidx, j, scale):
    s = lax.dot_general(q, kk, (((1,), (1,)), ((), ())), preferred_element_type=F32) * scale
    kidx = j * 256 + lax.broadcasted_iota(jnp.int32, (1, 256), 1)
    return s, (segq == segk) & (kidx <= qidx)


def attn_fwd_kernel(nb, q_ref, kv_ref, segq_ref, segk_ref, o_ref, lse_ref, kvall, lsem, ssem, rsem):
    b, q, y, c = place()
    k = lax.axis_index("blk")
    nz = nb // 4
    hz = nz // 2
    half = q // hz
    ql = q - half * hz
    low = k < nb // 2
    is_mid = k == nb // 2
    mid = (b, nb // 2)
    bar = greet(
        [at(b, half * hz + lax.rem(ql + r, hz), y, c) for r in range(1, hz)] + [at(b, q, 1 - y, c), at(b, q, y, 1 - c)]
    )

    @pl.when(low)
    def _():
        pl.semaphore_signal(bar, inc=1, device_id=mid, device_id_type=MESH)

    @pl.when(is_mid)
    def _():
        for j in range(nb // 2):
            pl.semaphore_signal(bar, inc=1, device_id=(b, j), device_id_type=MESH)

    pl.semaphore_wait(bar, hz + 1 + jnp.where(low, 1, 0) + jnp.where(is_mid, nb // 2, 0))

    def view(qq, yy, cc):
        return kvall.at[qq, yy, cc]

    sent = []

    def start(cp):
        cp.start()
        sent.append(cp)
        return cp

    mine = pltpu.make_async_copy(kv_ref, view(q, y, c), lsem)
    mine.start()
    other_y = at(b, q, 1 - y, c)
    other_c = at(b, q, y, 1 - c)
    z_in = []
    for r in range(1, hz):
        target = at(b, half * hz + lax.rem(ql + r, hz), y, c)
        start(remote(kv_ref, view(q, y, c), ssem.at[r], rsem.at[r], target))
        src = half * hz + lax.rem(ql - r + hz, hz)
        z_in.append((remote(kv_ref, view(src, y, c), ssem.at[r], rsem.at[r], target), src))
    start(remote(kv_ref, view(q, y, c), ssem.at[hz], rsem.at[hz], other_y))
    y_in = [(remote(kv_ref, view(q, 1 - y, c), ssem.at[hz], rsem.at[hz], other_y), q)]
    ns = 2 * hz + hz * 2
    to_mid = remote(kv_ref, view(q, y, c), ssem.at[ns], rsem.at[ns + k % (nb // 2)], mid)

    @pl.when(low)
    def _():
        to_mid.start()

    mine.wait()
    c_in = []
    s = 2 * hz

    def to_core(qq, yy, s):
        start(remote(view(qq, yy, c), view(qq, yy, c), ssem.at[s], rsem.at[s], other_c))
        c_in.append(remote(view(qq, yy, c), view(qq, yy, 1 - c), ssem.at[s], rsem.at[s], other_c))

    to_core(q, y, s)
    s += 1
    for r, (cp, src) in enumerate(z_in):
        cp.wait_recv()
        n = hz + 1 + r
        start(remote(view(src, y, c), view(src, y, c), ssem.at[n], rsem.at[n], other_y))
        y_in.append((remote(view(src, y, c), view(src, 1 - y, c), ssem.at[n], rsem.at[n], other_y), src))
        to_core(src, y, s)
        s += 1
    for cp, src in y_in:
        cp.wait_recv()
        to_core(src, 1 - y, s)
        s += 1
    for cp in c_in:
        cp.wait_recv()

    @pl.when(is_mid)
    def _():
        for j in range(nb // 2):
            remote(kv_ref, view(j // 4, (j // 2) % 2, j % 2), ssem.at[ns], rsem.at[ns + j], mid).wait_recv()

    scale = HD ** (-0.5)
    lo = jnp.where(k <= nb // 2, 0, nb // 4)
    hi = k // 2 + 1
    rows = q_ref.shape[1]
    tok = rows // H
    qidx = k * tok + lax.broadcasted_iota(jnp.int32, (rows, 1), 0) % tok
    for m in range(q_ref.shape[0]):
        qm = q_ref[m]
        segq = segq_ref[m]

        def body(j, carry):
            mx, sm, acc = carry
            blk = kvall[j // 2, j % 2, :, m].reshape(256, 2 * HD)
            s, ok = chunk_scores(qm, blk[:, :HD], segq, segk_ref[m, j], qidx, j, scale)
            s = jnp.where(ok, s, -1e30)
            new = jnp.maximum(mx, jnp.max(s, axis=-1, keepdims=True))
            p = jnp.where(ok, jnp.exp(s - new), 0.0)
            alpha = jnp.exp(mx - new)
            sm = sm * alpha + jnp.sum(p, axis=-1, keepdims=True)
            acc = acc * alpha + jnp.dot(p.astype(BF16), blk[:, HD:], preferred_element_type=F32)
            return new, sm, acc

        mx, sm, acc = lax.fori_loop(
            lo, hi, body, (jnp.full((rows, 1), -1e30, F32), jnp.zeros((rows, 1), F32), jnp.zeros((rows, HD), F32))
        )
        o_ref[m] = acc / sm
        lse_ref[m] = mx + jnp.log(sm)
    for cp in sent:
        cp.wait_send()

    @pl.when(low)
    def _():
        to_mid.wait_send()


def attn_fwd(nb, q, kv, segq, segk):
    nz = nb // 4
    ns = 4 * (nz // 2)
    return pl.pallas_call(
        functools.partial(attn_fwd_kernel, nb),
        out_shape=[
            jax.ShapeDtypeStruct(q.shape, F32),
            jax.ShapeDtypeStruct(q.shape[:2] + (1,), F32),
            jax.ShapeDtypeStruct((nz, 2, 2) + kv.shape, BF16),
        ],
        in_specs=[VMEM] * 4,
        out_specs=[VMEM] * 3,
        scratch_shapes=[
            pltpu.SemaphoreType.DMA,
            pltpu.SemaphoreType.DMA((ns + 1,)),
            pltpu.SemaphoreType.DMA((ns + nb // 2,)),
        ],
        compiler_params=pltpu.CompilerParams(collective_id=2, has_side_effects=True, vmem_limit_bytes=60 * 2**20),
    )(q, kv, segq, segk)


def attn_bwd_kernel(
    nb, q_ref, kvall, do_ref, lse_ref, delta_ref, segq_ref, segk_ref, dq_ref, dkv_ref, part, r1, r2, r3, r4, ssem, rsem, msem, nsem
):
    b, q, y, c = place()
    k = lax.axis_index("blk")
    nz = nb // 4
    hz = nz // 2
    half = q // hz
    ql = q - half * hz
    low = k < nb // 2
    is_mid = k == nb // 2
    mid = (b, nb // 2)
    bar = greet(
        [at(b, half * hz + lax.rem(ql + r, hz), y, c) for r in range(1, hz)] + [at(b, q, 1 - y, c), at(b, q, y, 1 - c)]
    )

    @pl.when(low)
    def _():
        pl.semaphore_signal(bar, inc=1, device_id=mid, device_id_type=MESH)

    @pl.when(is_mid)
    def _():
        for j in range(nb // 2):
            pl.semaphore_signal(bar, inc=1, device_id=(b, j), device_id_type=MESH)

    pl.semaphore_wait(bar, hz + 1 + jnp.where(low, 1, 0) + jnp.where(is_mid, nb // 2, 0))
    other_y = at(b, q, 1 - y, c)
    other_c = at(b, q, y, 1 - c)
    sent = []

    def start(cp):
        cp.start()
        sent.append(cp)
        return cp

    def clear(n, _):
        part[half * hz + n // 4, (n // 2) % 2, n % 2] = jnp.zeros(part.shape[3:], BF16)
        return 0

    lax.fori_loop(0, 4 * hz, clear, 0)
    scale = HD ** (-0.5)
    lo = jnp.where(k <= nb // 2, 0, nb // 4)
    hi = k // 2 + 1
    rows = q_ref.shape[1]
    tok = rows // H
    qidx = k * tok + lax.broadcasted_iota(jnp.int32, (rows, 1), 0) % tok
    tn = (((0,), (0,)), ((), ()))
    nt = (((1,), (1,)), ((), ()))
    for m in range(q_ref.shape[0]):
        dq_ref[m] = jnp.zeros(dq_ref.shape[1:], F32)

        def body(j, _):
            qm, dom = q_ref[m], do_ref[m]
            blk = kvall[j // 2, j % 2, :, m].reshape(256, 2 * HD)
            s, ok = chunk_scores(qm, blk[:, :HD], segq_ref[m], segk_ref[m, j], qidx, j, scale)
            p = jnp.where(ok, jnp.exp(jnp.where(ok, s, -1e30) - lse_ref[m]), 0.0)
            dp = lax.dot_general(dom, blk[:, HD:], nt, preferred_element_type=F32)
            ds = (p * (dp - delta_ref[m])).astype(BF16)
            dq_ref[m] += jnp.dot(ds, blk[:, :HD], preferred_element_type=F32) * scale
            dk = lax.dot_general(ds, qm, tn, preferred_element_type=F32) * scale
            dv = lax.dot_general(p.astype(BF16), dom, tn, preferred_element_type=F32)
            part[j // 2, j % 2, :, m] = jnp.concatenate([dk, dv], axis=1).astype(BF16).reshape(2, tok, 2 * HD)
            return 0

        lax.fori_loop(lo, hi, body, 0)

    @pl.when(is_mid)
    def _():
        for j in range(nb // 2):
            remote(part.at[j // 4, (j // 2) % 2, j % 2], r4, msem.at[j], nsem, (b, j)).start()

    hs = pl.ds(half * hz, hz)
    cp = start(remote(part.at[hs, :, 1 - c], r1, ssem.at[0], rsem.at[0], other_c))
    cp.wait_recv()

    def add1(n, _):
        i = half * hz + n // 2
        part[i, n % 2, c] = (part[i, n % 2, c].astype(F32) + r1[n // 2, n % 2].astype(F32)).astype(BF16)
        return 0

    lax.fori_loop(0, 2 * hz, add1, 0)
    cp = start(remote(part.at[hs, 1 - y, c], r2, ssem.at[1], rsem.at[1], other_y))
    cp.wait_recv()

    def add2(n, _):
        i = half * hz + n
        part[i, y, c] = (part[i, y, c].astype(F32) + r2[n].astype(F32)).astype(BF16)
        return 0

    lax.fori_loop(0, hz, add2, 0)
    last = []
    for r in range(1, hz):
        qt = half * hz + lax.rem(ql + r, hz)
        last.append(start(remote(part.at[qt, y, c], r3.at[r - 1], ssem.at[1 + r], rsem.at[1 + r], at(b, qt, y, c))))
    total = part[q, y, c].astype(F32)
    for r, cp in enumerate(last):
        cp.wait_recv()
        total = total + r3[r].astype(F32)
    dkv_ref[...] = total

    @pl.when(low)
    def _():
        remote(part.at[0, 0, 0], r4, msem.at[0], nsem, mid).wait_recv()
        dkv_ref[...] += r4[...].astype(F32)

    for cp in sent:
        cp.wait_send()

    @pl.when(is_mid)
    def _():
        for j in range(nb // 2):
            remote(part.at[j // 4, (j // 2) % 2, j % 2], r4, msem.at[j], nsem, (b, j)).wait_send()


def attn_bwd(nb, q, kvall, do, lse, delta, segq, segk):
    nz = nb // 4
    hz = nz // 2
    blk = kvall.shape[3:]
    return pl.pallas_call(
        functools.partial(attn_bwd_kernel, nb),
        out_shape=[jax.ShapeDtypeStruct(q.shape, F32), jax.ShapeDtypeStruct(blk, F32)],
        in_specs=[VMEM] * 7,
        out_specs=[VMEM] * 2,
        scratch_shapes=[
            pltpu.VMEM(kvall.shape, BF16),
            pltpu.VMEM((hz, 2) + blk, BF16),
            pltpu.VMEM((hz,) + blk, BF16),
            pltpu.VMEM((hz - 1,) + blk, BF16),
            pltpu.VMEM(blk, BF16),
            pltpu.SemaphoreType.DMA((hz + 1,)),
            pltpu.SemaphoreType.DMA((hz + 1,)),
            pltpu.SemaphoreType.DMA((nb // 2,)),
            pltpu.SemaphoreType.DMA,
        ],
        compiler_params=pltpu.CompilerParams(collective_id=3, has_side_effects=True, vmem_limit_bytes=60 * 2**20),
    )(q, kvall, do, lse, delta, segq, segk)


def tiles(n, w):
    return [(i, min(w, n - i)) for i in range(0, n, w)]


def gelu_parts(z):
    k0 = math.sqrt(2.0 / math.pi)
    t = jnp.tanh(k0 * (z + 0.044715 * z * z * z))
    value = 0.5 * z * (1.0 + t)
    slope = 0.5 * (1.0 + t) + 0.5 * z * (1.0 - t * t) * (k0 * (1.0 + 3.0 * 0.044715 * z * z))
    return value, slope


def ffn_kernel(
    b_ref, h1_ref, dy_ref, gp_ref, wg, wu, wd, out_ref, db_ref, dgp_ref, gg_o, gu_o, gd_o,
    ball, ballt, gate, up, mm, fsend, frecv, dfall, dsend, drecv, sg, su, sd, ssem, rsem, osem,
):
    b, q, y, c = place()
    g = q // 2
    t = lax.rem(q, 2) * 2 + y
    micro, tok, width = b_ref.shape
    hidden = wd.shape[0]
    peers = []
    for p in range(1, 4):
        tt = lax.rem(t + p, 4)
        peers.append((p, tt, at(b, g * 2 + tt // 2, lax.rem(tt, 2), c)))
    bar = greet([p[2] for p in peers])
    pl.semaphore_wait(bar, 3)
    sent = []
    nt = (((1,), (1,)), ((), ()))

    def spread(phase, m, src, dst_of, recv_of):
        waits = []
        for p, tt, target in peers:
            cp = remote(src(tt), dst_of(p, tt), ssem.at[phase, m, p - 1], rsem.at[phase, m, p - 1], target)
            cp.start()
            sent.append(cp)
            ts = lax.rem(t + 4 - p, 4)
            waits.append(remote(src(tt), recv_of(p, ts), ssem.at[phase, m, p - 1], rsem.at[phase, m, p - 1], target))
        return waits

    a_in, f_in, df_in, db_in = [], [], [], []
    for m in range(micro):
        a_in.append(
            spread(0, m, lambda tt, m=m: b_ref.at[m], lambda p, tt, m=m: ball.at[m, t], lambda p, ts, m=m: ball.at[m, ts])
        )
        ball[m, t] = b_ref[m]

    def forward(m):
        for cp in a_in[m]:
            cp.wait_recv()

        def body(n, _):
            cols = pl.ds(pl.multiple_of(n * 256, 256), 256)
            x = ball[m].reshape(4 * tok, width)
            gv = jnp.dot(x, wg[:, cols], preferred_element_type=F32)
            uv = jnp.dot(x, wu[:, cols], preferred_element_type=F32)
            gate[m, :, cols] = gv.astype(BF16)
            up[m, :, cols] = uv.astype(BF16)
            mm[m, :, cols] = (gelu_parts(gv)[0] * uv).astype(BF16)
            return 0

        lax.fori_loop(0, hidden // 256, body, 0)
        for o, w in tiles(width, 256):
            f = jnp.dot(mm[m], wd[:, o : o + w], preferred_element_type=F32)
            fsend[m, :, :, o : o + w] = f.astype(BF16).reshape(4, tok, w)
        f_in.append(
            spread(1, m, lambda tt: fsend.at[m, tt], lambda p, tt: frecv.at[m, p - 1], lambda p, ts: frecv.at[m, p - 1])
        )

    def middle(m):
        for cp in f_in[m]:
            cp.wait_recv()
        f = fsend[m, t].astype(F32)
        for p in range(3):
            f = f + frecv[m, p].astype(F32)
        gp = 1.0 + gp_ref[...]
        r = lax.rsqrt(jnp.mean(f * f, axis=-1, keepdims=True) + epsilon)
        n = f * r
        dy = dy_ref[m].astype(F32)
        out_ref[m] = (h1_ref[m] + n * gp).astype(BF16)
        dg = dy * gp
        df = r * (dg - n * jnp.mean(dg * n, axis=-1, keepdims=True))
        part = jnp.sum(dy * n, axis=0, keepdims=True)
        if m == 0:
            dgp_ref[...] = part
        else:
            dgp_ref[...] += part
        dfall[m, t] = df.astype(BF16)
        df_in.append(
            spread(2, m, lambda tt: dfall.at[m, t], lambda p, tt: dfall.at[m, t], lambda p, ts: dfall.at[m, ts])
        )

    def backward(m):
        for cp in df_in[m]:
            cp.wait_recv()

        def body(n, _):
            cols = pl.ds(pl.multiple_of(n * 256, 256), 256)
            x = dfall[m].reshape(4 * tok, width)
            dm = lax.dot_general(x, wd[cols, :], nt, preferred_element_type=F32)
            value, slope = gelu_parts(gate[m, :, cols].astype(F32))
            uv = up[m, :, cols].astype(F32)
            gate[m, :, cols] = (dm * uv * slope).astype(BF16)
            up[m, :, cols] = (dm * value).astype(BF16)
            return 0

        lax.fori_loop(0, hidden // 256, body, 0)
        for o, w in tiles(width, 256):
            d = lax.dot_general(gate[m], wg[o : o + w, :], nt, preferred_element_type=F32)
            d = d + lax.dot_general(up[m], wu[o : o + w, :], nt, preferred_element_type=F32)
            dsend[m, :, :, o : o + w] = d.astype(BF16).reshape(4, tok, w)
        db_in.append(
            spread(3, m, lambda tt: dsend.at[m, tt], lambda p, tt: drecv.at[m, p - 1], lambda p, ts: drecv.at[m, p - 1])
        )

    for m in range(micro):
        forward(m)
    for m in range(micro):
        for i in range(4):
            ballt[:, (m * 4 + i) * tok : (m * 4 + i + 1) * tok] = ball[m, i].T
    for m in range(micro):
        middle(m)
    for m in range(micro):
        backward(m)

    def grads(n, _):
        cols = pl.ds(pl.multiple_of(n * 256, 256), 256)
        slot = lax.rem(n, 2)

        def out(m, o):
            cc = pl.ds(pl.multiple_of(m * 256, 256), 256)
            return [
                pltpu.make_async_copy(sg.at[o], gg_o.at[:, cc], osem.at[0, o]),
                pltpu.make_async_copy(su.at[o], gu_o.at[:, cc], osem.at[1, o]),
                pltpu.make_async_copy(sd.at[o], gd_o.at[cc, :], osem.at[2, o]),
            ]

        @pl.when(n >= 2)
        def _():
            for cp in out(n, slot):
                cp.wait()

        x = ballt[...]
        sg[slot] = jnp.dot(x, gate[:, :, cols].reshape(-1, 256), preferred_element_type=F32).astype(BF16)
        su[slot] = jnp.dot(x, up[:, :, cols].reshape(-1, 256), preferred_element_type=F32).astype(BF16)
        sd[slot] = jnp.dot(
            mm[:, :, cols].reshape(-1, 256).T, dfall[...].reshape(-1, width), preferred_element_type=F32
        ).astype(BF16)
        for cp in out(n, slot):
            cp.start()
        return 0

    steps = hidden // 256
    lax.fori_loop(0, steps, grads, 0)
    for n in range(max(steps - 2, 0), steps):
        o = n % 2
        pltpu.make_async_copy(sg.at[o], gg_o.at[:, n * 256 : n * 256 + 256], osem.at[0, o]).wait()
        pltpu.make_async_copy(su.at[o], gu_o.at[:, n * 256 : n * 256 + 256], osem.at[1, o]).wait()
        pltpu.make_async_copy(sd.at[o], gd_o.at[n * 256 : n * 256 + 256, :], osem.at[2, o]).wait()
    for m in range(micro):
        for cp in db_in[m]:
            cp.wait_recv()
        d = dsend[m, t].astype(F32)
        for p in range(3):
            d = d + drecv[m, p].astype(F32)
        db_ref[m] = d
    for cp in sent:
        cp.wait_send()


def ffn(b, h1, dy, gp, wg, wu, wd):
    micro, tok, width = b.shape
    hidden = wd.shape[0]
    wide = (micro, 4 * tok, hidden)
    return pl.pallas_call(
        ffn_kernel,
        out_shape=[
            jax.ShapeDtypeStruct(b.shape, BF16),
            jax.ShapeDtypeStruct(b.shape, F32),
            jax.ShapeDtypeStruct((1, width), F32),
            jax.ShapeDtypeStruct(wg.shape, BF16),
            jax.ShapeDtypeStruct(wu.shape, BF16),
            jax.ShapeDtypeStruct(wd.shape, BF16),
        ],
        in_specs=[VMEM] * 7,
        out_specs=[VMEM] * 3 + [ANY] * 3,
        scratch_shapes=[
            pltpu.VMEM((micro, 4, tok, width), BF16),
            pltpu.VMEM((width, micro * 4 * tok), BF16),
            pltpu.VMEM(wide, BF16),
            pltpu.VMEM(wide, BF16),
            pltpu.VMEM(wide, BF16),
            pltpu.VMEM((micro, 4, tok, width), BF16),
            pltpu.VMEM((micro, 3, tok, width), BF16),
            pltpu.VMEM((micro, 4, tok, width), BF16),
            pltpu.VMEM((micro, 4, tok, width), BF16),
            pltpu.VMEM((micro, 3, tok, width), BF16),
            pltpu.VMEM((2, width, 256), BF16),
            pltpu.VMEM((2, width, 256), BF16),
            pltpu.VMEM((2, 256, width), BF16),
            pltpu.SemaphoreType.DMA((4, micro, 3)),
            pltpu.SemaphoreType.DMA((4, micro, 3)),
            pltpu.SemaphoreType.DMA((3, 2)),
        ],
        compiler_params=pltpu.CompilerParams(collective_id=4, has_side_effects=True, vmem_limit_bytes=62 * 2**20),
    )(b, h1, dy, gp, wg, wu, wd)


def scaled_norm(values, gain):
    return values * lax.rsqrt(jnp.mean(values * values, axis=-1, keepdims=True) + epsilon) * (1.0 + gain)


def segments(lengths, index):
    docs = lengths.shape[1]
    ends = [sum(lengths[:, j] for j in range(i + 1)) for i in range(docs)]
    seg = jnp.zeros((lengths.shape[0], index.shape[0]), jnp.int32)
    first = jnp.zeros_like(seg)
    for i in range(docs):
        past = index[None, :] >= ends[i][:, None]
        seg = seg + past.astype(jnp.int32)
        first = first + jnp.where(past, lengths[:, i][:, None], 0)
    return seg, index[None, :] - first


def rotate(values, cosine, sine):
    half = values.shape[-1] // 2
    a, b = values[..., :half], values[..., half:]
    return jnp.concatenate([a * cosine - b * sine, b * cosine + a * sine], axis=-1)


def middle(attn_value, x_value, gain_attn, gain_pre):
    hidden = x_value + scaled_norm(attn_value, gain_attn)
    return (hidden, scaled_norm(hidden, gain_pre))


def shards(tokens, cotangent, doc_lengths, w_query, w_key, w_value, w_out, w_gate, w_up, w_down, *gains):
    nb = lax.axis_size("blk")
    nz = nb // 4
    me = lax.axis_index("blk")
    _, micro, tok, width = tokens.shape
    n_dev = 2 * nb
    nq = 2 * nz
    kr = w_gate.shape[0]
    qr, qp = 4 * kr, up16(4 * kr)
    dr = w_down.shape[0]
    dp = up16(dr)
    orow = w_out.shape[0]
    op = up16(orow)
    groups = [[4 * i + j for j in range(4)] for i in range(nz)]

    def fit(x, rows):
        return x if x.shape[0] == rows else jnp.pad(x, ((0, rows - x.shape[0]), (0, 0)))

    def slices(w):
        w = jnp.pad(w.reshape(kr, nq, 4, dr), ((0, 0), (0, 0), (0, 0), (0, dp - dr)))
        return w.transpose(2, 0, 1, 3).reshape(4, kr, nq * dp)

    fs = nq * dp
    w_qkv = jnp.concatenate([w_query, w_key, w_value], axis=1)
    qw = w_qkv.shape[1] // 4
    pack = jnp.concatenate([slices(w_gate), slices(w_up), w_qkv.reshape(kr, 4, qw).transpose(1, 0, 2)], axis=2)
    pack = lax.all_to_all(pack, "blk", split_axis=0, concat_axis=0, axis_index_groups=groups, tiled=True)
    pack = fit(pack.reshape(qr, 2 * fs + qw), qp)
    wide = [gain.shape[0] for gain in gains]
    flat = jnp.concatenate(gains)
    flat = jnp.pad(flat, (0, 16 * 128 - flat.shape[0])).reshape(16, 128)

    qkv_f, wo_f, gain_f, wg_f, wu_f, wd_f = gather_all(
        nz, pack[:, 2 * fs :], fit(w_out, op), flat, pack[:, :fs], pack[:, fs : 2 * fs], fit(w_down, dp)
    )
    wqkv = qkv_f[:, :, :qr].reshape(width, 4 * qw)
    wo = wo_f[:, :, :, :, :orow].reshape(n_dev * orow, width)
    wg = wg_f[:, :, :qr].reshape(width, fs)
    wu = wu_f[:, :, :qr].reshape(width, fs)
    wd = wd_f.reshape(fs, width)
    gain_rows = gain_f.reshape(n_dev, 16 * 128)
    full_gains, o = [], 0
    for w in wide:
        full_gains.append(gain_rows[:, o : o + w].reshape(n_dev * w).astype(F32))
        o += w
    gain_in, gain_query, gain_key, gain_attn, gain_pre, gain_post = full_gains

    lengths = doc_lengths[0]
    seg_all, pos_all = segments(lengths, jnp.arange(nb * tok, dtype=jnp.int32))
    seg_me, pos = segments(lengths, me * tok + jnp.arange(tok, dtype=jnp.int32))
    segq = jnp.tile(seg_me, (1, H))[:, :, None]
    segk = seg_all.reshape(micro, nb * tok // 256, 1, 256)
    freq = 1000000.0 ** (-(jnp.arange(HD // 2, dtype=F32) * 2.0 / HD))
    angle = pos.reshape(micro * tok).astype(F32)[:, None] * freq[None, :]
    cosine, sine = jnp.cos(angle), jnp.sin(angle)

    rows = micro * tok
    x = tokens[0].reshape(rows, width).astype(F32)
    dy = cotangent[0].reshape(rows, width)
    normed, pre_pull = jax.vjp(scaled_norm, x, gain_in)
    a = normed.astype(BF16)
    qkv = jnp.dot(a, wqkv, preferred_element_type=F32)
    n_q = H * HD
    q_raw = qkv[:, :n_q].reshape(rows, H, HD)
    k_raw = qkv[:, n_q : n_q + HD]
    v = qkv[:, n_q + HD :].astype(BF16)
    queries, query_pull = jax.vjp(
        lambda r, g: rotate(scaled_norm(r, g), cosine[:, None], sine[:, None]), q_raw, gain_query
    )
    keys, key_pull = jax.vjp(lambda r, g: rotate(scaled_norm(r, g), cosine, sine), k_raw, gain_key)

    def by_head(z):
        return z.reshape(micro, tok, H, HD).transpose(0, 2, 1, 3).reshape(micro, H * tok, HD)

    def by_row(z):
        return z.reshape(micro, H, tok, HD).transpose(0, 2, 1, 3).reshape(rows, H * HD)

    qh = by_head(queries.astype(BF16))
    kv = jnp.concatenate([keys.astype(BF16), v], axis=1).reshape(micro, tok, 2 * HD)
    oh, lse, kvall = attn_fwd(nb, qh, kv, segq, segk)
    o_b = by_row(oh.astype(BF16))
    attn = jnp.dot(o_b, wo, preferred_element_type=F32)
    (h1, ffn_in), mid_pull = jax.vjp(middle, attn, x, gain_attn, gain_pre)

    shape = (micro, tok, width)
    out, db, dg_post, gg, gu, gd = ffn(
        ffn_in.astype(BF16).reshape(shape), h1.reshape(shape), dy.reshape(shape), gain_post[None, :], wg, wu, wd
    )
    d_attn, d_x_mid, dg_attn, dg_pre = mid_pull((dy.astype(F32), db.reshape(rows, width)))
    d_attn = d_attn.astype(BF16)
    grad_out = lax.dot_general(o_b, d_attn, (((0,), (0,)), ((), ())), preferred_element_type=F32).astype(BF16)
    do = lax.dot_general(d_attn, wo, (((1,), (1,)), ((), ())), preferred_element_type=F32).astype(BF16)
    doh = by_head(do)
    delta = jnp.sum(doh.astype(F32) * oh, axis=-1, keepdims=True)
    dqh, dkv = attn_bwd(nb, qh, kvall, doh, lse, delta, segq, segk)
    dkv = dkv.reshape(rows, 2 * HD)
    dq_raw, dg_query = query_pull(by_row(dqh).reshape(rows, H, HD))
    dk_raw, dg_key = key_pull(dkv[:, :HD])
    d_qkv = jnp.concatenate([dq_raw.reshape(rows, n_q), dk_raw, dkv[:, HD:]], axis=1).astype(BF16)
    grad_qkv = lax.dot_general(a, d_qkv, (((0,), (0,)), ((), ())), preferred_element_type=F32).astype(BF16)
    da = lax.dot_general(d_qkv, wqkv, (((1,), (1,)), ((), ())), preferred_element_type=F32)
    d_x_pre, dg_in = pre_pull(da)
    d_x = (d_x_mid + d_x_pre).astype(BF16)

    def quads(z, r, p):
        z = z.reshape(2, nz, r, z.shape[-1])
        return z if r == p else jnp.pad(z, ((0, 0), (0, 0), (0, p - r), (0, 0)))

    go = grad_out.reshape(2, nz, 2, 2, orow, width)
    if op != orow:
        go = jnp.pad(go, ((0, 0),) * 4 + ((0, op - orow), (0, 0)))
    dgains = jnp.concatenate(
        [d.reshape(n_dev, w) for d, w in zip((dg_in, dg_query, dg_key, dg_attn, dg_pre, dg_post[0]), wide)], axis=1
    )
    used = dgains.shape[1]
    dgains = jnp.pad(dgains, ((0, 0), (0, 8 * 128 - used))).reshape(2, nz, 2, 2, 8, 128)
    s_qkv, s_wo, s_gain, s_wg, s_wu, s_wd = reduce_all(
        nz, quads(grad_qkv, qr, qp), go, dgains, quads(gg, qr, qp), quads(gu, qr, qp), gd.reshape(2, nz, dp, width)
    )
    back = jnp.concatenate([s_wg, s_wu, s_qkv], axis=1)[:qr].reshape(4, kr, 2 * fs + qw)
    back = lax.all_to_all(back, "blk", split_axis=0, concat_axis=0, axis_index_groups=groups, tiled=True)
    back = back.astype(F32)

    def rows_of(z):
        z = z.reshape(4, kr, nq, dp)[..., :dr]
        return z.transpose(1, 2, 0, 3).reshape(kr, nq * 4 * dr)

    s_qkv = back[:, :, 2 * fs :].transpose(1, 0, 2).reshape(kr, 4 * qw)
    flat = s_gain.reshape(-1)
    gain_grads, o = [], 0
    for w in wide:
        gain_grads.append(flat[o : o + w])
        o += w
    return (
        out[None],
        d_x.reshape(shape)[None],
        s_qkv[:, :n_q],
        s_qkv[:, n_q : n_q + HD],
        s_qkv[:, n_q + HD :],
        s_wo[:orow],
        rows_of(back[:, :, :fs]),
        rows_of(back[:, :, fs : 2 * fs]),
        s_wd[:dr],
        *gain_grads,
    )


def solution(mesh):
    sequence = P("bucket", None, "blk", None)
    split = ("bucket", "blk")
    return jax.shard_map(
        shards,
        mesh=mesh,
        in_specs=(sequence, sequence, P("bucket", None, None)) + (P(split, None),) * 7 + (P(split),) * 6,
        out_specs=(sequence, sequence) + (P(split, None),) * 7 + (P(split),) * 6,
        check_vma=False,
    )
```

```python
import functools
import math

import jax
import jax.numpy as jnp
from jax import lax
from jax.experimental import pallas as pl
from jax.experimental.pallas import tpu as pltpu
from jax.sharding import PartitionSpec as P

H = 4
HD = 256
F32 = jnp.float32
BF16 = jnp.bfloat16
MESH = pl.DeviceIdType.MESH
ANY = pl.BlockSpec(memory_space=pl.ANY)
VMEM = pl.BlockSpec(memory_space=pltpu.VMEM)
epsilon = 1e-06


def up16(n):
    return -(-n // 16) * 16


def place():
    b = lax.axis_index("bucket")
    k = lax.axis_index("blk")
    return b, k // 4, (k // 2) % 2, k % 2


def at(b, q, y, c):
    return (b, q * 4 + y * 2 + c)


def greet(targets):
    bar = pltpu.get_barrier_semaphore()
    for t in targets:
        pl.semaphore_signal(bar, inc=1, device_id=t, device_id_type=MESH)
    return bar


def remote(src, dst, send, recv, target):
    return pltpu.make_async_remote_copy(src, dst, send, recv, device_id=target, device_id_type=MESH)


def gather_kernel(nz, qkv, wo, gain, wg, wu, wd, qkv_f, wo_f, gain_f, wg_f, wu_f, wd_f, lsem, ssem, rsem, wls, wss, wrs):
    b, q, y, c = place()
    g, e = q // 2, q % 2
    ng = nz // 2
    qw = qkv.shape[1]
    self_in = e == c
    bar = greet(
        [at(b, lax.rem(q + r, nz), y, c) for r in range(1, nz)]
        + [at(1 - b, q, y, c), at(b, q, 1 - y, c), at(b, q, y, 1 - c)]
        + [at(b, lax.rem(g + r, ng) * 2 + c, y, e) for r in range(1, ng)]
    )
    first = at(b, g * 2 + c, y, e)

    @pl.when(jnp.logical_not(self_in))
    def _():
        pl.semaphore_signal(bar, inc=1, device_id=first, device_id_type=MESH)

    pl.semaphore_wait(bar, nz + 1 + ng - jnp.where(self_in, 1, 0) + 1)

    everything = pl.ds(0, nz)

    def view_qkv(ref, yy, cc, xx, qq):
        return ref.at[xx, qq, :, pl.ds(pl.multiple_of((yy * 2 + cc) * qw, 128), qw)]

    def view_lead(ref, yy, cc, xx, qq):
        return ref.at[xx, qq, yy, cc]

    items = [(qkv, qkv_f, view_qkv), (wo, wo_f, view_lead), (gain, gain_f, view_lead)]
    sent = []
    local = []
    for i, (src, dst, view) in enumerate(items):
        cp = pltpu.make_async_copy(src, view(dst, y, c, b, q), lsem.at[i])
        cp.start()
        local.append(cp)
    z_in = []
    for i, (src, dst, view) in enumerate(items):
        row = []
        for r in range(1, nz):
            cp = remote(src, view(dst, y, c, b, q), ssem.at[i, r], rsem.at[i, r], at(b, lax.rem(q + r, nz), y, c))
            cp.start()
            sent.append(cp)
            row.append(
                remote(src, view(dst, y, c, b, lax.rem(q - r + nz, nz)), ssem.at[i, r], rsem.at[i, r], at(b, lax.rem(q + r, nz), y, c))
            )
        z_in.append(row)
    x_in = [[] for _ in items]
    for i, (src, dst, view) in enumerate(items):
        cp = remote(src, view(dst, y, c, b, q), ssem.at[i, nz], rsem.at[i, nz], at(1 - b, q, y, c))
        cp.start()
        sent.append(cp)
        x_in[i].append(remote(src, view(dst, y, c, 1 - b, q), ssem.at[i, nz], rsem.at[i, nz], at(1 - b, q, y, c)))

    units = [(wg, wg_f), (wu, wu_f), (wd, wd_f)]
    u_in = []
    for j, (src, dst) in enumerate(units):
        row = []
        for r in range(ng):
            target = at(b, lax.rem(g + r, ng) * 2 + c, y, e)
            cp = remote(src, dst.at[b, q], wss.at[j, r], wrs.at[j, r], target)
            qs = lax.rem(g - r + ng, ng) * 2 + c
            inc = remote(src, dst.at[b, qs], wss.at[j, r], wrs.at[j, r], target)
            if r == 0:
                lc = pltpu.make_async_copy(src, dst.at[b, q], wls.at[j])

                @pl.when(self_in)
                def _():
                    lc.start()

                @pl.when(jnp.logical_not(self_in))
                def _():
                    cp.start()
            else:
                cp.start()
            row.append((cp, inc, qs, lc if r == 0 else None))
        u_in.append(row)

    for r in range(1, nz):
        qs = lax.rem(q - r + nz, nz)
        for i, (src, dst, view) in enumerate(items):
            z_in[i][r - 1].wait_recv()
            cp = remote(view(dst, y, c, b, qs), view(dst, y, c, b, qs), ssem.at[i, nz + r], rsem.at[i, nz + r], at(1 - b, q, y, c))
            cp.start()
            sent.append(cp)
            x_in[i].append(
                remote(view(dst, y, c, b, qs), view(dst, y, c, 1 - b, qs), ssem.at[i, nz + r], rsem.at[i, nz + r], at(1 - b, q, y, c))
            )
    for cp in local:
        cp.wait()
    y_in = [[] for _ in items]
    for half in range(2):
        for i, (src, dst, view) in enumerate(items):
            xx = b if half == 0 else 1 - b
            if half == 1:
                for cp in x_in[i]:
                    cp.wait_recv()
            s = 2 * nz + half
            cp = remote(view(dst, y, c, xx, everything), view(dst, y, c, xx, everything), ssem.at[i, s], rsem.at[i, s], at(b, q, 1 - y, c))
            cp.start()
            sent.append(cp)
            y_in[i].append(
                remote(view(dst, y, c, xx, everything), view(dst, 1 - y, c, xx, everything), ssem.at[i, s], rsem.at[i, s], at(b, q, 1 - y, c))
            )
    c_in = []

    def to_core(i, yy, s):
        _, dst, view = items[i]
        both = pl.ds(0, 2)
        cp = remote(view(dst, yy, c, both, everything), view(dst, yy, c, both, everything), ssem.at[i, s], rsem.at[i, s], at(b, q, y, 1 - c))
        cp.start()
        sent.append(cp)
        c_in.append(
            remote(view(dst, yy, c, both, everything), view(dst, yy, 1 - c, both, everything), ssem.at[i, s], rsem.at[i, s], at(b, q, y, 1 - c))
        )

    for i in range(len(items)):
        to_core(i, y, 2 * nz + 2)
    for i in range(len(items)):
        for cp in y_in[i]:
            cp.wait_recv()
        to_core(i, 1 - y, 2 * nz + 3)

    d_in = []

    def unit_on(j, xx, qs, s, target, yours):
        _, dst = units[j]
        cp = remote(dst.at[xx, qs], dst.at[xx, qs], wss.at[j, s], wrs.at[j, s], target)
        cp.start()
        sent.append(cp)
        return remote(dst.at[xx, qs], dst.at[yours[0], yours[1]], wss.at[j, s], wrs.at[j, s], target)

    xw = [[] for _ in units]

    def x_round(j):
        for r in range(ng):
            cp, inc, qs, lc = u_in[j][r]
            if r == 0:

                @pl.when(self_in)
                def _():
                    lc.wait()

                @pl.when(jnp.logical_not(self_in))
                def _():
                    inc.wait_recv()
            else:
                inc.wait_recv()
            xw[j].append(unit_on(j, b, qs, ng + r, at(1 - b, q, y, c), (1 - b, qs)))
        for r in range(ng):
            qs = u_in[j][r][2]
            qo = lax.rem(g - r + ng, ng) * 2 + 1 - c
            d_in.append(unit_on(j, b, qs, 2 * ng + r, at(b, q, y, 1 - c), (b, qo)))

    def c_round(j):
        for r in range(ng):
            qs = u_in[j][r][2]
            qo = lax.rem(g - r + ng, ng) * 2 + 1 - c
            xw[j][r].wait_recv()
            d_in.append(unit_on(j, 1 - b, qs, 3 * ng + r, at(b, q, y, 1 - c), (1 - b, qo)))

    x_round(0)
    x_round(1)
    c_round(0)
    x_round(2)
    c_round(1)
    c_round(2)
    for cp in c_in + d_in:
        cp.wait_recv()
    for cp in sent:
        cp.wait_send()
    for j in range(len(units)):
        for r in range(ng):
            cp = u_in[j][r][0]
            if r == 0:

                @pl.when(jnp.logical_not(self_in))
                def _():
                    cp.wait_send()
            else:
                cp.wait_send()


def gather_all(nz, qkv, wo, gain, wg, wu, wd):
    ng = nz // 2
    out = [
        jax.ShapeDtypeStruct((2, nz, qkv.shape[0], 4 * qkv.shape[1]), BF16),
        jax.ShapeDtypeStruct((2, nz, 2, 2) + wo.shape, BF16),
        jax.ShapeDtypeStruct((2, nz, 2, 2) + gain.shape, BF16),
        jax.ShapeDtypeStruct((2, nz) + wg.shape, BF16),
        jax.ShapeDtypeStruct((2, nz) + wu.shape, BF16),
        jax.ShapeDtypeStruct((2, nz) + wd.shape, BF16),
    ]
    ns = 2 * nz + 4
    return pl.pallas_call(
        functools.partial(gather_kernel, nz),
        out_shape=out,
        in_specs=[ANY] * 6,
        out_specs=[ANY] * 6,
        scratch_shapes=[
            pltpu.SemaphoreType.DMA((3,)),
            pltpu.SemaphoreType.DMA((3, ns)),
            pltpu.SemaphoreType.DMA((3, ns)),
            pltpu.SemaphoreType.DMA((3,)),
            pltpu.SemaphoreType.DMA((3, 4 * ng)),
            pltpu.SemaphoreType.DMA((3, 4 * ng)),
        ],
        compiler_params=pltpu.CompilerParams(collective_id=0, has_side_effects=True),
    )(qkv, wo, gain, wg, wu, wd)


def reduce_kernel(nz, qkv, wo, gain, wg, wu, wd, qkv_o, wo_o, gain_o, wg_o, wu_o, wd_o, *scratch):
    b, q, y, c = place()
    g, e = q // 2, q % 2
    ng = nz // 2
    qw = qkv_o.shape[1]
    self_in = e == c
    n_items, n_units = 3, 3
    own = scratch[0:3]
    r1 = scratch[3:6]
    r2 = scratch[6:9]
    r3 = scratch[9:12]
    r4 = scratch[12:15]
    uown = scratch[15:18]
    u1 = scratch[18:21]
    u2 = scratch[21:24]
    u3 = scratch[24:27]
    lsem, ssem, rsem, wls, wss, wrs = scratch[27:]
    bar = greet(
        [at(b, lax.rem(q + r, nz), y, c) for r in range(1, nz)]
        + [at(1 - b, q, y, c), at(b, q, 1 - y, c), at(b, q, y, 1 - c)]
        + [at(b, lax.rem(g + r, ng) * 2 + c, y, e) for r in range(1, ng)]
    )
    first = at(b, g * 2 + c, y, e)

    @pl.when(jnp.logical_not(self_in))
    def _():
        pl.semaphore_signal(bar, inc=1, device_id=first, device_id_type=MESH)

    pl.semaphore_wait(bar, nz + 1 + ng - jnp.where(self_in, 1, 0) + 1)

    other_core = at(b, q, y, 1 - c)
    other_y = at(b, q, 1 - y, c)
    other_x = at(1 - b, q, y, c)
    full = (pl.ds(0, 2), pl.ds(0, nz))

    def view_qkv(ref, yy, cc):
        return ref.at[full[0], full[1], :, pl.ds(pl.multiple_of((yy * 2 + cc) * qw, 128), qw)]

    def view_lead(ref, yy, cc):
        return ref.at[full[0], full[1], yy, cc]

    items = [(qkv, qkv_o, view_qkv), (wo, wo_o, view_lead), (gain, gain_o, view_lead)]
    units = [(wd, wd_o), (wg, wg_o), (wu, wu_o)]
    sent = []
    item_local, item_in = [[] for _ in items], [[] for _ in items]
    unit_local, unit_in = [[] for _ in units], [[] for _ in units]

    def start(cp):
        cp.start()
        sent.append(cp)
        return cp

    def item_core(i):
        src, _, view = items[i]
        for yy in range(2):
            item_in[i].append(start(remote(view(src, yy, 1 - c), r1[i].at[yy], ssem.at[i, yy], rsem.at[i, yy], other_core)))
            cp = pltpu.make_async_copy(view(src, yy, c), own[i].at[yy], lsem.at[i, yy])
            cp.start()
            item_local[i].append(cp)

    def unit_core(j):
        src, _ = units[j]
        for xx in range(2):
            for r in range(ng):
                s = xx * ng + r
                mine, yours = r * 2 + c, r * 2 + 1 - c
                unit_in[j].append(start(remote(src.at[xx, yours], u1[j].at[xx, r], wss.at[j, s], wrs.at[j, s], other_core)))
                cp = pltpu.make_async_copy(src.at[xx, mine], uown[j].at[xx, r], wls.at[j, s])
                cp.start()
                unit_local[j].append(cp)

    def add(dst, src, lead):
        def one(n, _):
            dst[n] = (dst[n].astype(F32) + src[n].astype(F32)).astype(dst.dtype)
            return 0

        lax.fori_loop(0, lead, one, 0)

    def unit_x(j):
        for cp in unit_local[j]:
            cp.wait()
        for cp in unit_in[j]:
            cp.wait_recv()
        add(uown[j].at[1 - b], u1[j].at[1 - b], ng)
        cp = start(remote(uown[j].at[1 - b], u2[j], wss.at[j, 2 * ng], wrs.at[j, 2 * ng], other_x))
        add(uown[j].at[b], u1[j].at[b], ng)
        unit_in[j] = [cp]

    def unit_z(j):
        unit_in[j][0].wait_recv()
        add(uown[j].at[b], u2[j], ng)
        waits = []
        for r in range(ng):
            gs = lax.rem(g + r, ng)
            cp = remote(uown[j].at[b, gs], u3[j].at[r], wss.at[j, 2 * ng + 1 + r], wrs.at[j, 2 * ng + 1 + r], at(b, gs * 2 + c, y, e))
            if r == 0:
                lc = pltpu.make_async_copy(uown[j].at[b, gs], u3[j].at[0], wls.at[j, 2 * ng])

                @pl.when(self_in)
                def _():
                    lc.start()

                @pl.when(jnp.logical_not(self_in))
                def _():
                    cp.start()

                waits.append((cp, lc))
            else:
                start(cp)
                waits.append((cp, None))
        unit_in[j] = waits

    def unit_end(j):
        for cp, lc in unit_in[j]:
            if lc is not None:

                @pl.when(self_in)
                def _():
                    lc.wait()

                @pl.when(jnp.logical_not(self_in))
                def _():
                    cp.wait()
            else:
                cp.wait_recv()
        rows = u3[j].shape[1]
        step = 16

        def one(n, _):
            sl = pl.ds(pl.multiple_of(n * step, step), step)
            total = u3[j][0, sl].astype(F32)
            for r in range(1, ng):
                total = total + u3[j][r, sl].astype(F32)
            units[j][1][sl] = total.astype(units[j][1].dtype)
            return 0

        lax.fori_loop(0, rows // step, one, 0)

    def item_y(i):
        for cp in item_local[i]:
            cp.wait()
        for cp in item_in[i]:
            cp.wait_recv()
        for xx in range(2):
            add(own[i].at[1 - y, xx], r1[i].at[1 - y, xx], nz)
        cp = start(remote(own[i].at[1 - y], r2[i], ssem.at[i, 2], rsem.at[i, 2], other_y))
        for xx in range(2):
            add(own[i].at[y, xx], r1[i].at[y, xx], nz)
        item_in[i] = [cp]

    def item_x(i):
        item_in[i][0].wait_recv()
        add(own[i].at[y, 1 - b], r2[i].at[1 - b], nz)
        cp = start(remote(own[i].at[y, 1 - b], r3[i], ssem.at[i, 3], rsem.at[i, 3], other_x))
        add(own[i].at[y, b], r2[i].at[b], nz)
        item_in[i] = [cp]

    def item_z(i):
        item_in[i][0].wait_recv()
        add(own[i].at[y, b], r3[i], nz)
        waits = []
        for r in range(1, nz):
            qt = lax.rem(q + r, nz)
            waits.append(start(remote(own[i].at[y, b, qt], r4[i].at[r - 1], ssem.at[i, 3 + r], rsem.at[i, 3 + r], at(b, qt, y, c))))
        item_in[i] = waits

    def item_end(i):
        for cp in item_in[i]:
            cp.wait_recv()
        total = own[i][y, b, q].astype(F32)
        for r in range(1, nz):
            total = total + r4[i][r - 1].astype(F32)
        items[i][1][...] = total.astype(items[i][1].dtype)

    for j in range(n_units):
        unit_core(j)
    for i in range(n_items):
        item_core(i)
    for j in range(n_units):
        unit_x(j)
    for i in range(n_items):
        item_y(i)
    unit_z(0)
    for i in range(n_items):
        item_x(i)
    unit_z(1)
    for i in range(n_items):
        item_z(i)
    unit_z(2)
    for i in range(n_items):
        item_end(i)
    for j in range(n_units):
        unit_end(j)
    for cp in sent:
        cp.wait_send()


def reduce_all(nz, qkv, wo, gain, wg, wu, wd):
    ng = nz // 2
    qw = qkv.shape[3] // 4
    blocks = [((qkv.shape[2], qw), BF16), (wo.shape[4:], BF16), (gain.shape[4:], F32)]
    ublocks = [(wd.shape[2:], BF16), (wg.shape[2:], BF16), (wu.shape[2:], BF16)]
    scratch = (
        [pltpu.VMEM((2, 2, nz) + s, t) for s, t in blocks]
        + [pltpu.VMEM((2, 2, nz) + s, t) for s, t in blocks]
        + [pltpu.VMEM((2, nz) + s, t) for s, t in blocks]
        + [pltpu.VMEM((nz,) + s, t) for s, t in blocks]
        + [pltpu.VMEM((nz - 1,) + s, t) for s, t in blocks]
        + [pltpu.VMEM((2, ng) + s, t) for s, t in ublocks]
        + [pltpu.VMEM((2, ng) + s, t) for s, t in ublocks]
        + [pltpu.VMEM((ng,) + s, t) for s, t in ublocks]
        + [pltpu.VMEM((ng,) + s, t) for s, t in ublocks]
        + [
            pltpu.SemaphoreType.DMA((3, 2)),
            pltpu.SemaphoreType.DMA((3, nz + 3)),
            pltpu.SemaphoreType.DMA((3, nz + 3)),
            pltpu.SemaphoreType.DMA((3, 2 * ng + 1)),
            pltpu.SemaphoreType.DMA((3, 3 * ng + 1)),
            pltpu.SemaphoreType.DMA((3, 3 * ng + 1)),
        ]
    )
    out = [
        jax.ShapeDtypeStruct(blocks[0][0], BF16),
        jax.ShapeDtypeStruct(blocks[1][0], F32),
        jax.ShapeDtypeStruct(blocks[2][0], F32),
        jax.ShapeDtypeStruct(ublocks[1][0], BF16),
        jax.ShapeDtypeStruct(ublocks[2][0], BF16),
        jax.ShapeDtypeStruct(ublocks[0][0], F32),
    ]
    return pl.pallas_call(
        functools.partial(reduce_kernel, nz),
        out_shape=out,
        in_specs=[ANY] * 6,
        out_specs=[VMEM] * 6,
        scratch_shapes=scratch,
        compiler_params=pltpu.CompilerParams(collective_id=1, has_side_effects=True, vmem_limit_bytes=60 * 2**20),
    )(qkv, wo, gain, wg, wu, wd)


def chunk_scores(q, kk, segq, segk, qidx, j, scale):
    s = lax.dot_general(q, kk, (((1,), (1,)), ((), ())), preferred_element_type=F32) * scale
    kidx = j * 256 + lax.broadcasted_iota(jnp.int32, (1, 256), 1)
    return s, (segq == segk) & (kidx <= qidx)


def attn_fwd_kernel(nb, q_ref, kv_ref, segq_ref, segk_ref, o_ref, lse_ref, kvall, lsem, ssem, rsem):
    b, q, y, c = place()
    k = lax.axis_index("blk")
    nz = nb // 4
    hz = nz // 2
    half = q // hz
    ql = q - half * hz
    low = k < nb // 2
    is_mid = k == nb // 2
    mid = (b, nb // 2)
    bar = greet(
        [at(b, half * hz + lax.rem(ql + r, hz), y, c) for r in range(1, hz)] + [at(b, q, 1 - y, c), at(b, q, y, 1 - c)]
    )

    @pl.when(low)
    def _():
        pl.semaphore_signal(bar, inc=1, device_id=mid, device_id_type=MESH)

    @pl.when(is_mid)
    def _():
        for j in range(nb // 2):
            pl.semaphore_signal(bar, inc=1, device_id=(b, j), device_id_type=MESH)

    pl.semaphore_wait(bar, hz + 1 + jnp.where(low, 1, 0) + jnp.where(is_mid, nb // 2, 0))

    def view(qq, yy, cc):
        return kvall.at[qq, yy, cc]

    sent = []

    def start(cp):
        cp.start()
        sent.append(cp)
        return cp

    mine = pltpu.make_async_copy(kv_ref, view(q, y, c), lsem)
    mine.start()
    other_y = at(b, q, 1 - y, c)
    other_c = at(b, q, y, 1 - c)
    z_in = []
    for r in range(1, hz):
        target = at(b, half * hz + lax.rem(ql + r, hz), y, c)
        start(remote(kv_ref, view(q, y, c), ssem.at[r], rsem.at[r], target))
        src = half * hz + lax.rem(ql - r + hz, hz)
        z_in.append((remote(kv_ref, view(src, y, c), ssem.at[r], rsem.at[r], target), src))
    start(remote(kv_ref, view(q, y, c), ssem.at[hz], rsem.at[hz], other_y))
    y_in = [(remote(kv_ref, view(q, 1 - y, c), ssem.at[hz], rsem.at[hz], other_y), q)]
    ns = 2 * hz + hz * 2
    to_mid = remote(kv_ref, view(q, y, c), ssem.at[ns], rsem.at[ns + k % (nb // 2)], mid)

    @pl.when(low)
    def _():
        to_mid.start()

    mine.wait()
    c_in = []
    s = 2 * hz

    def to_core(qq, yy, s):
        start(remote(view(qq, yy, c), view(qq, yy, c), ssem.at[s], rsem.at[s], other_c))
        c_in.append(remote(view(qq, yy, c), view(qq, yy, 1 - c), ssem.at[s], rsem.at[s], other_c))

    to_core(q, y, s)
    s += 1
    for r, (cp, src) in enumerate(z_in):
        cp.wait_recv()
        n = hz + 1 + r
        start(remote(view(src, y, c), view(src, y, c), ssem.at[n], rsem.at[n], other_y))
        y_in.append((remote(view(src, y, c), view(src, 1 - y, c), ssem.at[n], rsem.at[n], other_y), src))
        to_core(src, y, s)
        s += 1
    for cp, src in y_in:
        cp.wait_recv()
        to_core(src, 1 - y, s)
        s += 1
    for cp in c_in:
        cp.wait_recv()

    @pl.when(is_mid)
    def _():
        for j in range(nb // 2):
            remote(kv_ref, view(j // 4, (j // 2) % 2, j % 2), ssem.at[ns], rsem.at[ns + j], mid).wait_recv()

    scale = HD ** (-0.5)
    lo = jnp.where(k <= nb // 2, 0, nb // 4)
    hi = k // 2 + 1
    rows = q_ref.shape[1]
    tok = rows // H
    qidx = k * tok + lax.broadcasted_iota(jnp.int32, (rows, 1), 0) % tok
    for m in range(q_ref.shape[0]):
        qm = q_ref[m]
        segq = segq_ref[m]

        def body(j, carry):
            mx, sm, acc = carry
            blk = kvall[j // 2, j % 2, :, m].reshape(256, 2 * HD)
            s, ok = chunk_scores(qm, blk[:, :HD], segq, segk_ref[m, j], qidx, j, scale)
            s = jnp.where(ok, s, -1e30)
            new = jnp.maximum(mx, jnp.max(s, axis=-1, keepdims=True))
            p = jnp.where(ok, jnp.exp(s - new), 0.0)
            alpha = jnp.exp(mx - new)
            sm = sm * alpha + jnp.sum(p, axis=-1, keepdims=True)
            acc = acc * alpha + jnp.dot(p.astype(BF16), blk[:, HD:], preferred_element_type=F32)
            return new, sm, acc

        mx, sm, acc = lax.fori_loop(
            lo, hi, body, (jnp.full((rows, 1), -1e30, F32), jnp.zeros((rows, 1), F32), jnp.zeros((rows, HD), F32))
        )
        o_ref[m] = acc / sm
        lse_ref[m] = mx + jnp.log(sm)
    for cp in sent:
        cp.wait_send()

    @pl.when(low)
    def _():
        to_mid.wait_send()


def attn_fwd(nb, q, kv, segq, segk):
    nz = nb // 4
    ns = 4 * (nz // 2)
    return pl.pallas_call(
        functools.partial(attn_fwd_kernel, nb),
        out_shape=[
            jax.ShapeDtypeStruct(q.shape, F32),
            jax.ShapeDtypeStruct(q.shape[:2] + (1,), F32),
            jax.ShapeDtypeStruct((nz, 2, 2) + kv.shape, BF16),
        ],
        in_specs=[VMEM] * 4,
        out_specs=[VMEM] * 3,
        scratch_shapes=[
            pltpu.SemaphoreType.DMA,
            pltpu.SemaphoreType.DMA((ns + 1,)),
            pltpu.SemaphoreType.DMA((ns + nb // 2,)),
        ],
        compiler_params=pltpu.CompilerParams(collective_id=2, has_side_effects=True, vmem_limit_bytes=60 * 2**20),
    )(q, kv, segq, segk)


def attn_bwd_kernel(
    nb, q_ref, kvall, do_ref, lse_ref, delta_ref, segq_ref, segk_ref, dq_ref, dkv_ref, part, r1, r2, r3, r4, ssem, rsem, msem, nsem
):
    b, q, y, c = place()
    k = lax.axis_index("blk")
    nz = nb // 4
    hz = nz // 2
    half = q // hz
    ql = q - half * hz
    low = k < nb // 2
    is_mid = k == nb // 2
    mid = (b, nb // 2)
    bar = greet(
        [at(b, half * hz + lax.rem(ql + r, hz), y, c) for r in range(1, hz)] + [at(b, q, 1 - y, c), at(b, q, y, 1 - c)]
    )

    @pl.when(low)
    def _():
        pl.semaphore_signal(bar, inc=1, device_id=mid, device_id_type=MESH)

    @pl.when(is_mid)
    def _():
        for j in range(nb // 2):
            pl.semaphore_signal(bar, inc=1, device_id=(b, j), device_id_type=MESH)

    pl.semaphore_wait(bar, hz + 1 + jnp.where(low, 1, 0) + jnp.where(is_mid, nb // 2, 0))
    other_y = at(b, q, 1 - y, c)
    other_c = at(b, q, y, 1 - c)
    sent = []

    def start(cp):
        cp.start()
        sent.append(cp)
        return cp

    def clear(n, _):
        part[half * hz + n // 4, (n // 2) % 2, n % 2] = jnp.zeros(part.shape[3:], BF16)
        return 0

    lax.fori_loop(0, 4 * hz, clear, 0)
    scale = HD ** (-0.5)
    lo = jnp.where(k <= nb // 2, 0, nb // 4)
    hi = k // 2 + 1
    rows = q_ref.shape[1]
    tok = rows // H
    qidx = k * tok + lax.broadcasted_iota(jnp.int32, (rows, 1), 0) % tok
    tn = (((0,), (0,)), ((), ()))
    nt = (((1,), (1,)), ((), ()))
    for m in range(q_ref.shape[0]):
        dq_ref[m] = jnp.zeros(dq_ref.shape[1:], F32)

        def body(j, _):
            qm, dom = q_ref[m], do_ref[m]
            blk = kvall[j // 2, j % 2, :, m].reshape(256, 2 * HD)
            s, ok = chunk_scores(qm, blk[:, :HD], segq_ref[m], segk_ref[m, j], qidx, j, scale)
            p = jnp.where(ok, jnp.exp(jnp.where(ok, s, -1e30) - lse_ref[m]), 0.0)
            dp = lax.dot_general(dom, blk[:, HD:], nt, preferred_element_type=F32)
            ds = (p * (dp - delta_ref[m])).astype(BF16)
            dq_ref[m] += jnp.dot(ds, blk[:, :HD], preferred_element_type=F32) * scale
            dk = lax.dot_general(ds, qm, tn, preferred_element_type=F32) * scale
            dv = lax.dot_general(p.astype(BF16), dom, tn, preferred_element_type=F32)
            part[j // 2, j % 2, :, m] = jnp.concatenate([dk, dv], axis=1).astype(BF16).reshape(2, tok, 2 * HD)
            return 0

        lax.fori_loop(lo, hi, body, 0)

    @pl.when(is_mid)
    def _():
        for j in range(nb // 2):
            remote(part.at[j // 4, (j // 2) % 2, j % 2], r4, msem.at[j], nsem, (b, j)).start()

    hs = pl.ds(half * hz, hz)
    cp = start(remote(part.at[hs, :, 1 - c], r1, ssem.at[0], rsem.at[0], other_c))
    cp.wait_recv()

    def add1(n, _):
        i = half * hz + n // 2
        part[i, n % 2, c] = (part[i, n % 2, c].astype(F32) + r1[n // 2, n % 2].astype(F32)).astype(BF16)
        return 0

    lax.fori_loop(0, 2 * hz, add1, 0)
    cp = start(remote(part.at[hs, 1 - y, c], r2, ssem.at[1], rsem.at[1], other_y))
    cp.wait_recv()

    def add2(n, _):
        i = half * hz + n
        part[i, y, c] = (part[i, y, c].astype(F32) + r2[n].astype(F32)).astype(BF16)
        return 0

    lax.fori_loop(0, hz, add2, 0)
    last = []
    for r in range(1, hz):
        qt = half * hz + lax.rem(ql + r, hz)
        last.append(start(remote(part.at[qt, y, c], r3.at[r - 1], ssem.at[1 + r], rsem.at[1 + r], at(b, qt, y, c))))
    total = part[q, y, c].astype(F32)
    for r, cp in enumerate(last):
        cp.wait_recv()
        total = total + r3[r].astype(F32)
    dkv_ref[...] = total

    @pl.when(low)
    def _():
        remote(part.at[0, 0, 0], r4, msem.at[0], nsem, mid).wait_recv()
        dkv_ref[...] += r4[...].astype(F32)

    for cp in sent:
        cp.wait_send()

    @pl.when(is_mid)
    def _():
        for j in range(nb // 2):
            remote(part.at[j // 4, (j // 2) % 2, j % 2], r4, msem.at[j], nsem, (b, j)).wait_send()


def attn_bwd(nb, q, kvall, do, lse, delta, segq, segk):
    nz = nb // 4
    hz = nz // 2
    blk = kvall.shape[3:]
    return pl.pallas_call(
        functools.partial(attn_bwd_kernel, nb),
        out_shape=[jax.ShapeDtypeStruct(q.shape, F32), jax.ShapeDtypeStruct(blk, F32)],
        in_specs=[VMEM] * 7,
        out_specs=[VMEM] * 2,
        scratch_shapes=[
            pltpu.VMEM(kvall.shape, BF16),
            pltpu.VMEM((hz, 2) + blk, BF16),
            pltpu.VMEM((hz,) + blk, BF16),
            pltpu.VMEM((hz - 1,) + blk, BF16),
            pltpu.VMEM(blk, BF16),
            pltpu.SemaphoreType.DMA((hz + 1,)),
            pltpu.SemaphoreType.DMA((hz + 1,)),
            pltpu.SemaphoreType.DMA((nb // 2,)),
            pltpu.SemaphoreType.DMA,
        ],
        compiler_params=pltpu.CompilerParams(collective_id=3, has_side_effects=True, vmem_limit_bytes=60 * 2**20),
    )(q, kvall, do, lse, delta, segq, segk)


def tiles(n, w):
    return [(i, min(w, n - i)) for i in range(0, n, w)]


def gelu_parts(z):
    k0 = math.sqrt(2.0 / math.pi)
    t = jnp.tanh(k0 * (z + 0.044715 * z * z * z))
    value = 0.5 * z * (1.0 + t)
    slope = 0.5 * (1.0 + t) + 0.5 * z * (1.0 - t * t) * (k0 * (1.0 + 3.0 * 0.044715 * z * z))
    return value, slope


def ffn_kernel(
    b_ref, h1_ref, dy_ref, gp_ref, wg, wu, wd, out_ref, db_ref, dgp_ref, gg_o, gu_o, gd_o,
    ball, ballt, gate, up, mm, fsend, frecv, dfall, dsend, drecv, sg, su, sd, ssem, rsem, osem,
):
    b, q, y, c = place()
    g = q // 2
    t = lax.rem(q, 2) * 2 + y
    micro, tok, width = b_ref.shape
    hidden = wd.shape[0]
    peers = []
    for p in range(1, 4):
        tt = lax.rem(t + p, 4)
        peers.append((p, tt, at(b, g * 2 + tt // 2, lax.rem(tt, 2), c)))
    bar = greet([p[2] for p in peers])
    pl.semaphore_wait(bar, 3)
    sent = []
    nt = (((1,), (1,)), ((), ()))

    def spread(phase, m, src, dst_of, recv_of):
        waits = []
        for p, tt, target in peers:
            cp = remote(src(tt), dst_of(p, tt), ssem.at[phase, m, p - 1], rsem.at[phase, m, p - 1], target)
            cp.start()
            sent.append(cp)
            ts = lax.rem(t + 4 - p, 4)
            waits.append(remote(src(tt), recv_of(p, ts), ssem.at[phase, m, p - 1], rsem.at[phase, m, p - 1], target))
        return waits

    a_in, f_in, df_in, db_in = [], [], [], []
    for m in range(micro):
        a_in.append(
            spread(0, m, lambda tt, m=m: b_ref.at[m], lambda p, tt, m=m: ball.at[m, t], lambda p, ts, m=m: ball.at[m, ts])
        )
        ball[m, t] = b_ref[m]

    def forward(m):
        for cp in a_in[m]:
            cp.wait_recv()

        def body(n, _):
            cols = pl.ds(pl.multiple_of(n * 256, 256), 256)
            x = ball[m].reshape(4 * tok, width)
            gv = jnp.dot(x, wg[:, cols], preferred_element_type=F32)
            uv = jnp.dot(x, wu[:, cols], preferred_element_type=F32)
            gate[m, :, cols] = gv.astype(BF16)
            up[m, :, cols] = uv.astype(BF16)
            mm[m, :, cols] = (gelu_parts(gv)[0] * uv).astype(BF16)
            return 0

        lax.fori_loop(0, hidden // 256, body, 0)
        for o, w in tiles(width, 256):
            f = jnp.dot(mm[m], wd[:, o : o + w], preferred_element_type=F32)
            fsend[m, :, :, o : o + w] = f.astype(BF16).reshape(4, tok, w)
        f_in.append(
            spread(1, m, lambda tt: fsend.at[m, tt], lambda p, tt: frecv.at[m, p - 1], lambda p, ts: frecv.at[m, p - 1])
        )

    def middle(m):
        for cp in f_in[m]:
            cp.wait_recv()
        f = fsend[m, t].astype(F32)
        for p in range(3):
            f = f + frecv[m, p].astype(F32)
        gp = 1.0 + gp_ref[...]
        r = lax.rsqrt(jnp.mean(f * f, axis=-1, keepdims=True) + epsilon)
        n = f * r
        dy = dy_ref[m].astype(F32)
        out_ref[m] = (h1_ref[m] + n * gp).astype(BF16)
        dg = dy * gp
        df = r * (dg - n * jnp.mean(dg * n, axis=-1, keepdims=True))
        part = jnp.sum(dy * n, axis=0, keepdims=True)
        if m == 0:
            dgp_ref[...] = part
        else:
            dgp_ref[...] += part
        dfall[m, t] = df.astype(BF16)
        df_in.append(
            spread(2, m, lambda tt: dfall.at[m, t], lambda p, tt: dfall.at[m, t], lambda p, ts: dfall.at[m, ts])
        )

    def backward(m):
        for cp in df_in[m]:
            cp.wait_recv()

        def body(n, _):
            cols = pl.ds(pl.multiple_of(n * 256, 256), 256)
            x = dfall[m].reshape(4 * tok, width)
            dm = lax.dot_general(x, wd[cols, :], nt, preferred_element_type=F32)
            value, slope = gelu_parts(gate[m, :, cols].astype(F32))
            uv = up[m, :, cols].astype(F32)
            gate[m, :, cols] = (dm * uv * slope).astype(BF16)
            up[m, :, cols] = (dm * value).astype(BF16)
            return 0

        lax.fori_loop(0, hidden // 256, body, 0)
        for o, w in tiles(width, 256):
            d = lax.dot_general(gate[m], wg[o : o + w, :], nt, preferred_element_type=F32)
            d = d + lax.dot_general(up[m], wu[o : o + w, :], nt, preferred_element_type=F32)
            dsend[m, :, :, o : o + w] = d.astype(BF16).reshape(4, tok, w)
        db_in.append(
            spread(3, m, lambda tt: dsend.at[m, tt], lambda p, tt: drecv.at[m, p - 1], lambda p, ts: drecv.at[m, p - 1])
        )

    for m in range(micro):
        forward(m)
    for m in range(micro):
        for i in range(4):
            ballt[:, (m * 4 + i) * tok : (m * 4 + i + 1) * tok] = ball[m, i].T
    for m in range(micro):
        middle(m)
    for m in range(micro):
        backward(m)

    def grads(n, _):
        cols = pl.ds(pl.multiple_of(n * 256, 256), 256)
        slot = lax.rem(n, 2)

        def out(m, o):
            cc = pl.ds(pl.multiple_of(m * 256, 256), 256)
            return [
                pltpu.make_async_copy(sg.at[o], gg_o.at[:, cc], osem.at[0, o]),
                pltpu.make_async_copy(su.at[o], gu_o.at[:, cc], osem.at[1, o]),
                pltpu.make_async_copy(sd.at[o], gd_o.at[cc, :], osem.at[2, o]),
            ]

        @pl.when(n >= 2)
        def _():
            for cp in out(n, slot):
                cp.wait()

        x = ballt[...]
        sg[slot] = jnp.dot(x, gate[:, :, cols].reshape(-1, 256), preferred_element_type=F32).astype(BF16)
        su[slot] = jnp.dot(x, up[:, :, cols].reshape(-1, 256), preferred_element_type=F32).astype(BF16)
        sd[slot] = jnp.dot(
            mm[:, :, cols].reshape(-1, 256).T, dfall[...].reshape(-1, width), preferred_element_type=F32
        ).astype(BF16)
        for cp in out(n, slot):
            cp.start()
        return 0

    steps = hidden // 256
    lax.fori_loop(0, steps, grads, 0)
    for n in range(max(steps - 2, 0), steps):
        o = n % 2
        pltpu.make_async_copy(sg.at[o], gg_o.at[:, n * 256 : n * 256 + 256], osem.at[0, o]).wait()
        pltpu.make_async_copy(su.at[o], gu_o.at[:, n * 256 : n * 256 + 256], osem.at[1, o]).wait()
        pltpu.make_async_copy(sd.at[o], gd_o.at[n * 256 : n * 256 + 256, :], osem.at[2, o]).wait()
    for m in range(micro):
        for cp in db_in[m]:
            cp.wait_recv()
        d = dsend[m, t].astype(F32)
        for p in range(3):
            d = d + drecv[m, p].astype(F32)
        db_ref[m] = d
    for cp in sent:
        cp.wait_send()


def ffn(b, h1, dy, gp, wg, wu, wd):
    micro, tok, width = b.shape
    hidden = wd.shape[0]
    wide = (micro, 4 * tok, hidden)
    return pl.pallas_call(
        ffn_kernel,
        out_shape=[
            jax.ShapeDtypeStruct(b.shape, BF16),
            jax.ShapeDtypeStruct(b.shape, F32),
            jax.ShapeDtypeStruct((1, width), F32),
            jax.ShapeDtypeStruct(wg.shape, BF16),
            jax.ShapeDtypeStruct(wu.shape, BF16),
            jax.ShapeDtypeStruct(wd.shape, BF16),
        ],
        in_specs=[VMEM] * 7,
        out_specs=[VMEM] * 3 + [ANY] * 3,
        scratch_shapes=[
            pltpu.VMEM((micro, 4, tok, width), BF16),
            pltpu.VMEM((width, micro * 4 * tok), BF16),
            pltpu.VMEM(wide, BF16),
            pltpu.VMEM(wide, BF16),
            pltpu.VMEM(wide, BF16),
            pltpu.VMEM((micro, 4, tok, width), BF16),
            pltpu.VMEM((micro, 3, tok, width), BF16),
            pltpu.VMEM((micro, 4, tok, width), BF16),
            pltpu.VMEM((micro, 4, tok, width), BF16),
            pltpu.VMEM((micro, 3, tok, width), BF16),
            pltpu.VMEM((2, width, 256), BF16),
            pltpu.VMEM((2, width, 256), BF16),
            pltpu.VMEM((2, 256, width), BF16),
            pltpu.SemaphoreType.DMA((4, micro, 3)),
            pltpu.SemaphoreType.DMA((4, micro, 3)),
            pltpu.SemaphoreType.DMA((3, 2)),
        ],
        compiler_params=pltpu.CompilerParams(collective_id=4, has_side_effects=True, vmem_limit_bytes=62 * 2**20),
    )(b, h1, dy, gp, wg, wu, wd)


def halves(n):
    first = up16(n // 2)
    return [(0, first), (first, n - first)] if first < n else [(0, n)]


def norm_of(v):
    r = lax.rsqrt(jnp.mean(v * v, axis=-1, keepdims=True) + epsilon)
    return v * r, r


def norm_back(grad, n, r, scale):
    gs = grad * scale
    return r * (gs - n * jnp.mean(gs * n, axis=-1, keepdims=True)), jnp.sum(grad * n, axis=0, keepdims=True)


def spread_gains(block, width, n_dev):
    w = width // n_dev
    lane = lax.broadcasted_iota(jnp.int32, (128, width), 0)
    col = lax.broadcasted_iota(jnp.int32, (128, width), 1)
    pick = jnp.where(lax.rem(col, w) == lane, 1.0, 0.0).astype(BF16)
    wide = jnp.dot(block, pick, preferred_element_type=F32)
    row = lax.broadcasted_iota(jnp.int32, (n_dev * 16, width), 0) // 16
    mine = lax.broadcasted_iota(jnp.int32, (n_dev * 16, width), 1) // w
    return jnp.sum(jnp.where(row == mine, wide, 0.0).reshape(n_dev, 16, width), axis=0)


def collect_gains(rows, n_dev):
    width = rows.shape[1]
    w = width // n_dev
    row = lax.broadcasted_iota(jnp.int32, (n_dev, 8, width), 0)
    mine = lax.broadcasted_iota(jnp.int32, (n_dev, 8, width), 2) // w
    wide = jnp.where(row == mine, rows[None], 0.0).reshape(n_dev * 8, width)
    col = lax.broadcasted_iota(jnp.int32, (width, 128), 0)
    lane = lax.broadcasted_iota(jnp.int32, (width, 128), 1)
    pick = jnp.where(lax.rem(col, w) == lane, 1.0, 0.0)
    out = jnp.dot(wide, pick, preferred_element_type=F32, precision=lax.Precision.HIGHEST)
    return out.reshape(n_dev, 8, 128)


def front_barrier(nz, extra_mid):
    b, q, y, c = place()
    k = lax.axis_index("blk")
    nb = 4 * nz
    g, e = q // 2, q % 2
    ng = nz // 2
    bar = greet(
        [at(b, lax.rem(q + r, nz), y, c) for r in range(1, nz)]
        + [at(1 - b, q, y, c), at(b, q, 1 - y, c), at(b, q, y, 1 - c)]
        + [at(b, lax.rem(g + r, ng) * 2 + c, y, e) for r in range(1, ng)]
    )

    @pl.when(e != c)
    def _():
        pl.semaphore_signal(bar, inc=1, device_id=at(b, g * 2 + c, y, e), device_id_type=MESH)

    low = k < nb // 2
    is_mid = k == nb // 2

    @pl.when(low)
    def _():
        pl.semaphore_signal(bar, inc=1, device_id=(b, nb // 2), device_id_type=MESH)

    @pl.when(is_mid)
    def _():
        for j in range(nb // 2):
            pl.semaphore_signal(bar, inc=1, device_id=(b, j), device_id_type=MESH)

    pl.semaphore_wait(
        bar, nz + 1 + ng + 1 - jnp.where(e == c, 1, 0) + jnp.where(low, 1, 0) + jnp.where(is_mid, nb // 2, 0)
    )


def front_kernel(
    nz, x_ref, cos_ref, sin_ref, segq_ref, segk_ref, qkv_u, wo_u, gain_u, wg, wu, wd,
    b_o, h1_o, attn_h, raw_h, q_h, o_h, ob_h, lse_h, kv_h, wqkv_h, wo_h, gd_o, gh_o, wg_f, wu_f, wd_f,
    attn_s, raw_s, q_s, o_s, ob_s, lse_s, kvall, kv_own, wqkv, wo, gain_f,
    lsem, ssem, rsem, wls, wss, wrs, kls, kss, krs, osem,
):
    b, q, y, c = place()
    k = lax.axis_index("blk")
    nb = 4 * nz
    n_dev = 2 * nb
    g, e = q // 2, q % 2
    ng = nz // 2
    hz = nz // 2
    qw = qkv_u.shape[1]
    self_in = e == c
    front_barrier(nz, True)
    other_x, other_y, other_c = at(1 - b, q, y, c), at(b, q, 1 - y, c), at(b, q, y, 1 - c)
    everything, both = pl.ds(0, nz), pl.ds(0, 2)
    sent = []

    def start(cp):
        cp.start()
        sent.append(cp)
        return cp

    def view_qkv(ref, yy, cc, xx, qq):
        return ref.at[xx, qq, :, pl.ds(pl.multiple_of((yy * 2 + cc) * qw, 128), qw)]

    def view_lead(ref, yy, cc, xx, qq):
        return ref.at[xx, qq, yy, cc]

    items = [(qkv_u, wqkv, view_qkv), (gain_u, gain_f, view_lead), (wo_u, wo, view_lead)]
    local = [None] * 3
    z_in, x_in, y_in, c_in = ([[] for _ in items] for _ in range(4))

    def send_z(i):
        src, dst, view = items[i]
        local[i] = pltpu.make_async_copy(src, view(dst, y, c, b, q), lsem.at[i])
        local[i].start()
        for r in range(1, nz):
            t = at(b, lax.rem(q + r, nz), y, c)
            start(remote(src, view(dst, y, c, b, q), ssem.at[i, r], rsem.at[i, r], t))
            z_in[i].append(
                remote(src, view(dst, y, c, b, lax.rem(q - r + nz, nz)), ssem.at[i, r], rsem.at[i, r], t)
            )
        start(remote(src, view(dst, y, c, b, q), ssem.at[i, nz], rsem.at[i, nz], other_x))
        x_in[i].append(remote(src, view(dst, y, c, 1 - b, q), ssem.at[i, nz], rsem.at[i, nz], other_x))

    def send_x(i, r):
        _, dst, view = items[i]
        qs = lax.rem(q - r + nz, nz)
        z_in[i][r - 1].wait_recv()
        s = nz + r
        start(remote(view(dst, y, c, b, qs), view(dst, y, c, b, qs), ssem.at[i, s], rsem.at[i, s], other_x))
        x_in[i].append(
            remote(view(dst, y, c, b, qs), view(dst, y, c, 1 - b, qs), ssem.at[i, s], rsem.at[i, s], other_x)
        )

    def send_y(i, half):
        _, dst, view = items[i]
        xx = b if half == 0 else 1 - b
        if half == 0:
            local[i].wait()
        else:
            for cp in x_in[i]:
                cp.wait_recv()
        s = 2 * nz + half
        v = view(dst, y, c, xx, everything)
        start(remote(v, v, ssem.at[i, s], rsem.at[i, s], other_y))
        y_in[i].append(remote(v, view(dst, 1 - y, c, xx, everything), ssem.at[i, s], rsem.at[i, s], other_y))

    def send_c(i, half):
        _, dst, view = items[i]
        yy = y if half == 0 else 1 - y
        if half == 1:
            for cp in y_in[i]:
                cp.wait_recv()
        s = 2 * nz + 2 + half
        v = view(dst, yy, c, both, everything)
        start(remote(v, v, ssem.at[i, s], rsem.at[i, s], other_c))
        c_in[i].append(remote(v, view(dst, yy, 1 - c, both, everything), ssem.at[i, s], rsem.at[i, s], other_c))

    def done(i):
        for cp in c_in[i]:
            cp.wait_recv()

    pieces = [
        (src, dst, o, n) for src, dst in ((wg, wg_f), (wu, wu_f), (wd, wd_f)) for o, n in halves(src.shape[0])
    ]
    w_in, w_x, w_c, w_out = ([[] for _ in pieces] for _ in range(4))

    def w_send(j):
        src, dst, o, n = pieces[j]
        sl = pl.ds(o, n)
        for r in range(ng):
            t = at(b, lax.rem(g + r, ng) * 2 + c, y, e)
            qs = lax.rem(g - r + ng, ng) * 2 + c
            cp = remote(src.at[sl], dst.at[b, q, sl], wss.at[j, r], wrs.at[j, r], t)
            inc = remote(src.at[sl], dst.at[b, qs, sl], wss.at[j, r], wrs.at[j, r], t)
            if r == 0:
                lc = pltpu.make_async_copy(src.at[sl], dst.at[b, q, sl], wls.at[j])

                @pl.when(self_in)
                def _():
                    lc.start()

                @pl.when(jnp.logical_not(self_in))
                def _():
                    cp.start()

                w_in[j].append((inc, qs, lc))
                w_out[j].append(cp)
            else:
                start(cp)
                w_in[j].append((inc, qs, None))

    def w_on(j, xx, qs, s, target, yx, yq):
        _, dst, o, n = pieces[j]
        sl = pl.ds(o, n)
        start(remote(dst.at[xx, qs, sl], dst.at[xx, qs, sl], wss.at[j, s], wrs.at[j, s], target))
        return remote(dst.at[xx, qs, sl], dst.at[yx, yq, sl], wss.at[j, s], wrs.at[j, s], target)

    def w_across(j):
        for r, (inc, qs, lc) in enumerate(w_in[j]):
            if lc is not None:

                @pl.when(self_in)
                def _():
                    lc.wait()

                @pl.when(jnp.logical_not(self_in))
                def _():
                    inc.wait_recv()
            else:
                inc.wait_recv()
            w_x[j].append(w_on(j, b, qs, ng + r, other_x, 1 - b, qs))
        for r, (_, qs, _) in enumerate(w_in[j]):
            w_c[j].append(w_on(j, b, qs, 2 * ng + r, other_c, b, lax.rem(g - r + ng, ng) * 2 + 1 - c))

    def w_core(j):
        for r, (_, qs, _) in enumerate(w_in[j]):
            w_x[j][r].wait_recv()
            w_c[j].append(w_on(j, 1 - b, qs, 3 * ng + r, other_c, 1 - b, lax.rem(g - r + ng, ng) * 2 + 1 - c))

    last = len(pieces)
    steps = []
    for j in range(last):
        steps.append(lambda j=j: w_across(j))
        if j + 2 < last:
            steps.append(lambda j=j: w_send(j + 2))
        if j >= 1:
            steps.append(lambda j=j: w_core(j - 1))
    steps.append(lambda: w_core(last - 1))
    queue = iter(steps)

    def beside(n=1):
        for _ in range(n):
            step = next(queue, None)
            if step is not None:
                step()

    kept = []

    def keep(src, dst):
        cp = pltpu.make_async_copy(src, dst, osem.at[len(kept)])
        cp.start()
        kept.append(cp)

    send_z(0)
    send_z(1)
    w_send(0)
    w_send(1)
    micro, _, tok, _ = q_s.shape
    rows = micro * tok
    x = x_ref[...].astype(F32)
    n_x = norm_of(x)[0]
    for r in range(1, nz):
        send_x(0, r)
        send_x(1, r)
    send_y(0, 0)
    send_y(1, 0)
    send_z(2)
    beside(2)
    send_y(0, 1)
    send_y(1, 1)
    send_c(0, 0)
    send_c(1, 0)
    beside(2)
    for r in range(1, nz):
        send_x(2, r)
    send_c(0, 1)
    send_c(1, 1)
    send_y(2, 0)
    send_y(2, 1)
    send_c(2, 0)
    done(0)
    done(1)

    width = x_ref.shape[1]
    gains_d = spread_gains(gain_f[...].reshape(n_dev * 16, 128), width, n_dev)
    gains_h = spread_gains(gain_f[...].reshape(n_dev * 16, 128), HD, n_dev)
    gd_o[...] = gains_d
    gh_o[...] = gains_h
    a = (n_x * (1.0 + gains_d[0:1])).astype(BF16)
    cosine, sine = cos_ref[...], sin_ref[...]
    half = HD // 2
    for h in range(H + 2):
        w = wqkv[:, :, :, h * HD : (h + 1) * HD].reshape(width, HD)
        raw = jnp.dot(a, w, preferred_element_type=F32)
        if h == H + 1:
            kv_own[:, :, HD:] = raw.astype(BF16).reshape(micro, tok, HD)
            continue
        raw_s[:, h * HD : (h + 1) * HD] = raw
        z = norm_of(raw)[0] * (1.0 + (gains_h[1:2] if h < H else gains_h[2:3]))
        z1, z2 = z[:, :half], z[:, half:]
        z = jnp.concatenate([z1 * cosine - z2 * sine, z2 * cosine + z1 * sine], axis=1).astype(BF16)
        if h < H:
            q_s[:, h] = z.reshape(micro, tok, HD)
        else:
            kv_own[:, :, :HD] = z.reshape(micro, tok, HD)
    keep(wqkv, wqkv_h)
    keep(raw_s, raw_h)
    keep(q_s, q_h)

    side = q // hz
    ql = q - side * hz
    low = k < nb // 2
    is_mid = k == nb // 2
    mid = (b, nb // 2)

    def kview(qq, yy, cc):
        return kvall.at[qq, yy, cc]

    mine = pltpu.make_async_copy(kv_own, kview(q, y, c), kls)
    mine.start()
    kz_in, ky_in, kc_in = [], [], []
    for r in range(1, hz):
        t = at(b, side * hz + lax.rem(ql + r, hz), y, c)
        start(remote(kv_own, kview(q, y, c), kss.at[r], krs.at[r], t))
        src = side * hz + lax.rem(ql - r + hz, hz)
        kz_in.append((remote(kv_own, kview(src, y, c), kss.at[r], krs.at[r], t), src))
    start(remote(kv_own, kview(q, y, c), kss.at[hz], krs.at[hz], other_y))
    ky_in.append((remote(kv_own, kview(q, 1 - y, c), kss.at[hz], krs.at[hz], other_y), q))
    ns = 4 * hz
    to_mid = remote(kv_own, kview(q, y, c), kss.at[ns], krs.at[ns + lax.rem(k, nb // 2)], mid)

    @pl.when(low)
    def _():
        to_mid.start()

    slot = [2 * hz]

    def k_core(qq, yy):
        s = slot[0]
        slot[0] += 1
        start(remote(kview(qq, yy, c), kview(qq, yy, c), kss.at[s], krs.at[s], other_c))
        kc_in.append(remote(kview(qq, yy, c), kview(qq, yy, 1 - c), kss.at[s], krs.at[s], other_c))

    mine.wait()
    k_core(q, y)
    beside(1)
    for r, (cp, src) in enumerate(kz_in):
        cp.wait_recv()
        s = hz + 1 + r
        start(remote(kview(src, y, c), kview(src, y, c), kss.at[s], krs.at[s], other_y))
        ky_in.append((remote(kview(src, y, c), kview(src, 1 - y, c), kss.at[s], krs.at[s], other_y), src))
        k_core(src, y)
    beside(1)
    send_c(2, 1)
    for cp, src in ky_in:
        cp.wait_recv()
        k_core(src, 1 - y)
    beside(1)
    for cp in kc_in:
        cp.wait_recv()

    @pl.when(is_mid)
    def _():
        for j in range(nb // 2):
            remote(kv_own, kview(j // 4, (j // 2) % 2, j % 2), kss.at[ns], krs.at[ns + j], mid).wait_recv()

    scale = HD ** (-0.5)
    lo = jnp.where(k <= nb // 2, 0, nb // 4)
    hi = k // 2 + 1
    qrows = H * tok
    qidx = k * tok + lax.broadcasted_iota(jnp.int32, (qrows, 1), 0) % tok
    for m in range(micro):
        qm = q_s[m].reshape(qrows, HD)
        segq = segq_ref[m]

        def body(j, carry):
            mx, sm, acc = carry
            blk = kvall[j // 2, j % 2, :, m].reshape(256, 2 * HD)
            s, ok = chunk_scores(qm, blk[:, :HD], segq, segk_ref[m, j], qidx, j, scale)
            s = jnp.where(ok, s, -1e30)
            new = jnp.maximum(mx, jnp.max(s, axis=-1, keepdims=True))
            p = jnp.where(ok, jnp.exp(s - new), 0.0)
            alpha = jnp.exp(mx - new)
            sm = sm * alpha + jnp.sum(p, axis=-1, keepdims=True)
            acc = acc * alpha + jnp.dot(p.astype(BF16), blk[:, HD:], preferred_element_type=F32)
            return new, sm, acc

        mx, sm, acc = lax.fori_loop(
            lo, hi, body, (jnp.full((qrows, 1), -1e30, F32), jnp.zeros((qrows, 1), F32), jnp.zeros((qrows, HD), F32))
        )
        o = acc / sm
        o_s[m] = o
        lse_s[m] = mx + jnp.log(sm)
        for h in range(H):
            ob_s[m * tok : (m + 1) * tok, h * HD : (h + 1) * HD] = o[h * tok : (h + 1) * tok].astype(BF16)
        beside(1)
    keep(o_s, o_h)
    keep(lse_s, lse_h)
    keep(ob_s, ob_h)
    keep(kvall, kv_h)
    done(2)
    w = wo[...].reshape(H * HD, width)
    for o, n in tiles(width, 256):
        attn_s[:, o : o + n] = jnp.dot(ob_s[...], wo[:, :, :, :, :, o : o + n].reshape(H * HD, n), preferred_element_type=F32)
    keep(attn_s, attn_h)
    keep(wo, wo_h)
    h1 = x_ref[...].astype(F32) + norm_of(attn_s[...])[0] * (1.0 + gains_d[3:4])
    h1_o[...] = h1.reshape(micro, tok, width)
    b_o[...] = (norm_of(h1)[0] * (1.0 + gains_d[4:5])).astype(BF16).reshape(micro, tok, width)
    beside(len(steps))
    for j in range(last):
        for cp in w_c[j]:
            cp.wait_recv()
    for cp in sent:
        cp.wait_send()
    for j in range(last):

        @pl.when(jnp.logical_not(self_in))
        def _():
            w_out[j][0].wait_send()

    @pl.when(low)
    def _():
        to_mid.wait_send()

    for cp in kept:
        cp.wait()


def front(nz, x, cosine, sine, segq, segk, qkv, wo, gain, wg, wu, wd, micro):
    ng = nz // 2
    hz = nz // 2
    rows, width = x.shape
    tok = rows // micro
    nb = 4 * nz
    out = {
        "b": ((micro, tok, width), BF16),
        "h1": ((micro, tok, width), F32),
        "attn": ((rows, width), F32),
        "raw": ((rows, (H + 1) * HD), F32),
        "q": ((micro, H, tok, HD), BF16),
        "o": ((micro, H * tok, HD), F32),
        "ob": ((rows, H * HD), BF16),
        "lse": ((micro, H * tok, 1), F32),
        "kv": ((nz, 2, 2, micro, tok, 2 * HD), BF16),
        "wqkv": ((2, nz, qkv.shape[0], 4 * qkv.shape[1]), BF16),
        "wo": ((2, nz, 2, 2) + wo.shape, BF16),
        "gd": ((16, width), F32),
        "gh": ((16, HD), F32),
        "wg": ((2, nz) + wg.shape, BF16),
        "wu": ((2, nz) + wu.shape, BF16),
        "wd": ((2, nz) + wd.shape, BF16),
    }
    shapes = [jax.ShapeDtypeStruct(*v) for v in out.values()]
    scratch = [pltpu.VMEM(*out[n]) for n in ("attn", "raw", "q", "o", "ob", "lse", "kv")]
    ns = 2 * nz + 4
    n_pieces = sum(len(halves(u.shape[0])) for u in (wg, wu, wd))
    scratch += [pltpu.VMEM((micro, tok, 2 * HD), BF16), pltpu.VMEM(*out["wqkv"]), pltpu.VMEM(*out["wo"])]
    scratch += [pltpu.VMEM((2, nz, 2, 2) + gain.shape, BF16)]
    scratch += [
        pltpu.SemaphoreType.DMA((3,)),
        pltpu.SemaphoreType.DMA((3, ns)),
        pltpu.SemaphoreType.DMA((3, ns)),
        pltpu.SemaphoreType.DMA((n_pieces,)),
        pltpu.SemaphoreType.DMA((n_pieces, 4 * ng)),
        pltpu.SemaphoreType.DMA((n_pieces, 4 * ng)),
        pltpu.SemaphoreType.DMA,
        pltpu.SemaphoreType.DMA((4 * hz + 1,)),
        pltpu.SemaphoreType.DMA((4 * hz + nb // 2,)),
        pltpu.SemaphoreType.DMA((9,)),
    ]
    specs = [VMEM, VMEM] + [ANY] * 9 + [VMEM, VMEM] + [ANY] * 3
    got = pl.pallas_call(
        functools.partial(front_kernel, nz),
        out_shape=shapes,
        in_specs=[VMEM] * 5 + [ANY] * 6,
        out_specs=specs,
        scratch_shapes=scratch,
        compiler_params=pltpu.CompilerParams(collective_id=5, has_side_effects=True, vmem_limit_bytes=60 * 2**20),
    )(x, cosine, sine, segq, segk, qkv, wo, gain, wg, wu, wd)
    return dict(zip(out, got))


def back_kernel(
    nz, db_ref, h1_ref, dy_ref, x_ref, cos_ref, sin_ref, segq_ref, segk_ref, gd_ref, gh_ref, dgp_ref,
    attn_h, raw_h, q_h, o_h, ob_h, lse_h, kv_h, wqkv_h, wo_h, gg, gu, gdn,
    dx_o, qkv_o, wo_o, gain_o, wg_o, wu_o, wd_o,
    attn, raw, q_s, o_s, ob, lse, kvall, wqkv, wo,
    dh1, datt, do_s, delta, dq_s, dqkv, da, gqkv, gwo, ggain,
    k1, k2, k3, k4, i1, i2, i3, i4, j1, j2, j3, j4, h1s, h2s, h3s, h4s, *rest,
):
    (wown, w1, w2, w3) = (rest[0:3], rest[3:6], rest[6:9], rest[9:12])
    lsem, ssem, rsem, wls, wss, wrs, kss, krs, kms, kmr = rest[12:]
    b, q, y, c = place()
    k = lax.axis_index("blk")
    nb = 4 * nz
    n_dev = 2 * nb
    g, e = q // 2, q % 2
    ng = nz // 2
    hz = nz // 2
    qw = qkv_o.shape[1]
    self_in = e == c
    other_x, other_y, other_c = at(1 - b, q, y, c), at(b, q, 1 - y, c), at(b, q, y, 1 - c)
    both, everything = pl.ds(0, 2), pl.ds(0, nz)
    micro, _, tok, _ = q_s.shape
    rows, width = x_ref.shape
    nt = (((1,), (1,)), ((), ()))
    tn = (((0,), (0,)), ((), ()))
    loads = []
    for i, (src, dst) in enumerate(
        ((attn_h, attn), (wo_h, wo), (o_h, o_s), (q_h, q_s), (kv_h, kvall), (lse_h, lse), (ob_h, ob), (raw_h, raw), (wqkv_h, wqkv))
    ):
        cp = pltpu.make_async_copy(src, dst, lsem.at[i])
        cp.start()
        loads.append(cp)
    front_barrier(nz, True)
    sent = []

    def start(cp):
        cp.start()
        sent.append(cp)
        return cp

    def add(dst, src, n, step):
        def one(i, _):
            sl = pl.ds(pl.multiple_of(i * step, step), step)
            dst[sl] = dst[sl] + src[sl]
            return 0

        lax.fori_loop(0, n // step, one, 0)

    units = [(gdn, wd_o), (gg, wg_o), (gu, wu_o)]
    pieces = [(u, o, n) for u, (_, out) in enumerate(units) for o, n in halves(out.shape[0])]
    w_local, w_in = [None] * len(pieces), [None] * len(pieces)

    def w_core(j):
        u, o, n = pieces[j]
        src, sl = units[u][0], pl.ds(o, n)
        w_in[j] = start(remote(src.at[:, :, 1 - c, sl], w1[u].at[:, :, sl], wss.at[j, 0], wrs.at[j, 0], other_c))
        w_local[j] = pltpu.make_async_copy(src.at[:, :, c, sl], wown[u].at[:, :, sl], wls.at[j, 0])
        w_local[j].start()

    def w_x(j):
        u, o, n = pieces[j]
        sl = pl.ds(o, n)
        w_local[j].wait()
        w_in[j].wait_recv()
        for r in range(ng):
            add(wown[u].at[1 - b, r, sl], w1[u].at[1 - b, r, sl], n, 16)
        w_in[j] = start(remote(wown[u].at[1 - b, :, sl], w2[u].at[:, sl], wss.at[j, 1], wrs.at[j, 1], other_x))
        for r in range(ng):
            add(wown[u].at[b, r, sl], w1[u].at[b, r, sl], n, 16)

    def w_z(j):
        u, o, n = pieces[j]
        sl = pl.ds(o, n)
        w_in[j].wait_recv()
        for r in range(ng):
            add(wown[u].at[b, r, sl], w2[u].at[r, sl], n, 16)
        waits = []
        for r in range(ng):
            gs = lax.rem(g + r, ng)
            cp = remote(wown[u].at[b, gs, sl], w3[u].at[r, sl], wss.at[j, 2 + r], wrs.at[j, 2 + r], at(b, gs * 2 + c, y, e))
            lc = None
            if r == 0:
                lc = pltpu.make_async_copy(wown[u].at[b, gs, sl], w3[u].at[0, sl], wls.at[j, 1])

                @pl.when(self_in)
                def _():
                    lc.start()

                @pl.when(jnp.logical_not(self_in))
                def _():
                    cp.start()
            else:
                start(cp)
            waits.append((cp, lc))
        w_in[j] = waits

    def w_end(j):
        u, o, n = pieces[j]
        for cp, lc in w_in[j]:
            if lc is not None:

                @pl.when(self_in)
                def _():
                    lc.wait()

                @pl.when(jnp.logical_not(self_in))
                def _():
                    cp.wait()
            else:
                cp.wait_recv()
        out = units[u][1]

        def one(i, _):
            sl = pl.ds(pl.multiple_of(o + i * 16, 16), 16)
            total = w3[u][0, sl].astype(F32)
            for r in range(1, ng):
                total = total + w3[u][r, sl].astype(F32)
            out[sl] = total.astype(out.dtype)
            return 0

        lax.fori_loop(0, n // 16, one, 0)

    last = len(pieces)
    for j in range(last):
        w_core(j)
    steps = []
    for j in range(last + 4):
        if j < last:
            steps.append(lambda j=j: w_x(j))
        if 0 <= j - 2 < last:
            steps.append(lambda j=j: w_z(j - 2))
        if 0 <= j - 4 < last:
            steps.append(lambda j=j: w_end(j - 4))
    queue = iter(steps)

    def beside(n=1):
        for _ in range(n):
            step = next(queue, None)
            if step is not None:
                step()

    def view_qkv(ref, yy, cc):
        return ref.at[:, :, :, pl.ds(pl.multiple_of((yy * 2 + cc) * qw, 128), qw)]

    def view_lead(ref, yy, cc):
        return ref.at[:, :, yy, cc]

    items = [(gqkv, view_qkv, (i1, i2, i3, i4), qkv_o), (gwo, view_lead, (j1, j2, j3, j4), wo_o), (ggain, view_lead, (h1s, h2s, h3s, h4s), gain_o)]
    item_in = [[] for _ in items]

    def join(dst, src, lead):
        for idx in lead:
            dst[idx] = dst[idx] + src[idx]

    def grid2(v):
        return [(xx, qq) for xx in range(2) for qq in range(nz)]

    def item_core(i):
        src, view, (r1, _, _, _), _ = items[i]
        for yy in range(2):
            item_in[i].append(start(remote(view(src, yy, 1 - c), r1.at[yy], ssem.at[i, yy], rsem.at[i, yy], other_c)))

    def loop2(fn):
        def one(n, _):
            fn(lax.div(n, nz), lax.rem(n, nz))
            return 0

        lax.fori_loop(0, 2 * nz, one, 0)

    def item_y(i):
        src, view, (r1, r2, _, _), _ = items[i]
        for cp in item_in[i]:
            cp.wait_recv()
        for yy in (1 - y, y):
            v = view(src, yy, c)

            def fn(xx, qq):
                v[xx, qq] = v[xx, qq] + r1[yy, xx, qq]

            loop2(fn)
            if yy is not y:
                item_in[i] = [start(remote(v, r2, ssem.at[i, 2], rsem.at[i, 2], other_y))]

    def item_x(i):
        src, view, (_, r2, r3, _), _ = items[i]
        item_in[i][0].wait_recv()
        v = view(src, y, c)

        def fn(xx, qq):
            v[xx, qq] = v[xx, qq] + r2[xx, qq]

        loop2(fn)
        item_in[i] = [start(remote(v.at[1 - b], r3, ssem.at[i, 3], rsem.at[i, 3], other_x))]

    def item_z(i):
        src, view, (_, _, r3, r4), _ = items[i]
        item_in[i][0].wait_recv()
        v = view(src, y, c)
        for qq in range(nz):
            v[b, qq] = v[b, qq] + r3[qq]
        waits = []
        for r in range(1, nz):
            qt = lax.rem(q + r, nz)
            waits.append(start(remote(v.at[b, qt], r4.at[r - 1], ssem.at[i, 3 + r], rsem.at[i, 3 + r], at(b, qt, y, c))))
        item_in[i] = waits

    def item_end(i):
        src, view, (_, _, _, r4), out = items[i]
        for cp in item_in[i]:
            cp.wait_recv()
        v = view(src, y, c)
        total = v[b, q].astype(F32)
        for r in range(1, nz):
            total = total + r4[r - 1].astype(F32)
        out[...] = total.astype(out.dtype)

    gains = gd_ref[...]
    loads[0].wait()
    dy = dy_ref[...].astype(F32)
    n1, r1 = norm_of(h1_ref[...].reshape(rows, width))
    d, dg_pf = norm_back(db_ref[...].reshape(rows, width), n1, r1, 1.0 + gains[4:5])
    dh1[...] = dy + d
    n2, r2 = norm_of(attn[...])
    d, dg_pa = norm_back(dh1[...], n2, r2, 1.0 + gains[3:4])
    datt[...] = d.astype(BF16)
    loads[1].wait()
    loads[2].wait()
    for h in range(H):
        w = wo[...].reshape(H * HD, width)[h * HD : (h + 1) * HD]
        d = lax.dot_general(datt[...], w, nt, preferred_element_type=F32).astype(BF16)
        do_s[:, h] = d.reshape(micro, tok, HD)
        for m in range(micro):
            hs = slice(h * tok, (h + 1) * tok)
            delta[m, hs] = jnp.sum(d[m * tok : (m + 1) * tok].astype(F32) * o_s[m, hs], axis=-1, keepdims=True)
    beside(2)
    for i in (3, 4, 5):
        loads[i].wait()

    side = q // hz
    ql = q - side * hz
    low = k < nb // 2
    is_mid = k == nb // 2
    mid = (b, nb // 2)

    scale = HD ** (-0.5)
    lo = jnp.where(k <= nb // 2, 0, nb // 4)
    hi = k // 2 + 1
    part = kvall

    def clear(j, _):
        part[j // 2, j % 2] = jnp.zeros(part.shape[2:], BF16)
        return 0

    lax.fori_loop(hi, (side + 1) * 2 * hz, clear, 0)
    qrows = H * tok
    qidx = k * tok + lax.broadcasted_iota(jnp.int32, (qrows, 1), 0) % tok
    for m in range(micro):
        dq_s[m] = jnp.zeros(dq_s.shape[1:], F32)

        def body(j, _):
            qm, dom = q_s[m].reshape(qrows, HD), do_s[m].reshape(qrows, HD)
            blk = kvall[j // 2, j % 2, :, m].reshape(256, 2 * HD)
            s, ok = chunk_scores(qm, blk[:, :HD], segq_ref[m], segk_ref[m, j], qidx, j, scale)
            p = jnp.where(ok, jnp.exp(jnp.where(ok, s, -1e30) - lse[m]), 0.0)
            dp = lax.dot_general(dom, blk[:, HD:], nt, preferred_element_type=F32)
            ds = (p * (dp - delta[m])).astype(BF16)
            dq_s[m] += jnp.dot(ds, blk[:, :HD], preferred_element_type=F32) * scale
            dk = lax.dot_general(ds, qm, tn, preferred_element_type=F32) * scale
            dv = lax.dot_general(p.astype(BF16), dom, tn, preferred_element_type=F32)
            part[j // 2, j % 2, :, m] = jnp.concatenate([dk, dv], axis=1).astype(BF16).reshape(2, tok, 2 * HD)
            return 0

        lax.fori_loop(lo, hi, body, 0)
        beside(2)

    def of_mid(j):
        return remote(part.at[j // 4, (j // 2) % 2, j % 2], k4, kms.at[j], kmr, (b, j))

    @pl.when(is_mid)
    def _():
        for j in range(nb // 2):
            of_mid(j).start()

    hs = pl.ds(side * hz, hz)
    k_in = start(remote(part.at[hs, :, 1 - c], k1, kss.at[0], krs.at[0], other_c))
    loads[6].wait()
    obt = [ob[:, h * HD : (h + 1) * HD].T for h in range(H)]
    per = gwo.shape[0] * gwo.shape[1] * 4 // H
    for h in range(H):
        for o, n in tiles(width, 384):
            v = jnp.dot(obt[h], datt[:, o : o + n], preferred_element_type=F32).astype(BF16)
            n_lead = (2 * nz) // H
            xx, qq = (h * n_lead) // nz, (h * n_lead) % nz
            gwo[xx, qq : qq + n_lead, :, :, :, o : o + n] = v.reshape(n_lead, 2, 2, gwo.shape[4], n)
    item_core(1)
    k_in.wait_recv()

    def add1(n, _):
        i = side * hz + n // 2
        part[i, n % 2, c] = part[i, n % 2, c] + k1[n // 2, n % 2]
        return 0

    lax.fori_loop(0, 2 * hz, add1, 0)
    k_in = start(remote(part.at[hs, 1 - y, c], k2, kss.at[1], krs.at[1], other_y))
    loads[7].wait()
    cosine, sine = cos_ref[...], sin_ref[...]
    half = HD // 2
    gh = gh_ref[...]

    def unrotate(z):
        z1, z2 = z[:, :half], z[:, half:]
        return jnp.concatenate([z1 * cosine + z2 * sine, z2 * cosine - z1 * sine], axis=1)

    dg_q = jnp.zeros((1, HD), F32)
    for h in range(H):
        z = unrotate(dq_s[:, h * tok : (h + 1) * tok].reshape(rows, HD))
        n3, r3 = norm_of(raw[:, h * HD : (h + 1) * HD])
        d, dg = norm_back(z, n3, r3, 1.0 + gh[1:2])
        dqkv[:, h * HD : (h + 1) * HD] = d.astype(BF16)
        dg_q = dg_q + dg
    beside(2)
    k_in.wait_recv()

    def add2(n, _):
        i = side * hz + n
        part[i, y, c] = part[i, y, c] + k2[n]
        return 0

    lax.fori_loop(0, hz, add2, 0)
    k_last = []
    for r in range(1, hz):
        qt = side * hz + lax.rem(ql + r, hz)
        k_last.append(start(remote(part.at[qt, y, c], k3.at[r - 1], kss.at[1 + r], krs.at[1 + r], at(b, qt, y, c))))
    item_y(1)
    n_x, r_x = norm_of(x_ref[...].astype(F32))
    at_ = (n_x * (1.0 + gains[0:1])).astype(BF16).T

    def weight_grad(h):
        v = jnp.dot(at_, dqkv[:, h * HD : (h + 1) * HD], preferred_element_type=F32).astype(BF16)
        gqkv[:, :, :, h * HD : (h + 1) * HD] = v.reshape(gqkv.shape[:3] + (HD,))

    for h in range(H):
        weight_grad(h)
    beside(2)
    total = part[q, y, c].astype(F32)
    for r, cp in enumerate(k_last):
        cp.wait_recv()
        total = total + k3[r].astype(F32)

    @pl.when(low)
    def _():
        remote(part.at[0, 0, 0], k4, kms.at[0], kmr, mid).wait_recv()

    @pl.when(jnp.logical_not(low))
    def _():
        k4[...] = jnp.zeros(k4.shape, BF16)

    total = (total + k4[...].astype(F32)).reshape(rows, 2 * HD)
    n3, r3 = norm_of(raw[:, H * HD :])
    d, dg_k = norm_back(unrotate(total[:, :HD]), n3, r3, 1.0 + gh[2:3])
    dqkv[:, H * HD : (H + 1) * HD] = d.astype(BF16)
    dqkv[:, (H + 1) * HD :] = total[:, HD:].astype(BF16)
    weight_grad(H)
    weight_grad(H + 1)
    item_core(0)
    loads[8].wait()
    quads_at_once = max(1, 256 // wqkv.shape[2])
    for xx in range(2):
        for qq in range(0, nz, quads_at_once):
            n = min(quads_at_once, nz - qq)
            w = wqkv[xx, qq : qq + n].reshape(n * wqkv.shape[2], wqkv.shape[3])
            o = (xx * nz + qq) * wqkv.shape[2]
            da[o : o + n * wqkv.shape[2], :] = lax.dot_general(w, dqkv[...], nt, preferred_element_type=F32)
    d, dg_in = norm_back(da[...].T, n_x, r_x, 1.0 + gains[0:1])
    dx_o[...] = (dh1[...] + d).astype(BF16).reshape(dx_o.shape)
    none = jnp.zeros((1, width), F32)
    nohd = jnp.zeros((1, HD), F32)
    wide = jnp.concatenate([dg_in, none, none, dg_pa, dg_pf, dgp_ref[...], none, none], axis=0)
    slim = jnp.concatenate([nohd, dg_q, dg_k] + [nohd] * 5, axis=0)
    ggain[...] = (collect_gains(wide, n_dev) + collect_gains(slim, n_dev)).reshape(ggain.shape)
    item_core(2)
    item_x(1)
    item_y(0)
    item_y(2)
    beside(2)
    item_z(1)
    beside(2)
    item_x(0)
    item_x(2)
    beside(2)
    item_z(0)
    item_z(2)
    beside(2)
    item_end(1)
    beside(len(steps))
    item_end(0)
    item_end(2)
    for cp in sent:
        cp.wait_send()

    @pl.when(is_mid)
    def _():
        for j in range(nb // 2):
            of_mid(j).wait_send()


def back(nz, db, h1, dy, x, cosine, sine, segq, segk, dgp, f, gg, gu, gd):
    ng = nz // 2
    hz = nz // 2
    nb = 4 * nz
    micro, tok, width = db.shape
    rows = micro * tok
    qr = f["wqkv"].shape[2]
    qw = f["wqkv"].shape[3] // 4
    orow = f["wo"].shape[4]
    kv = f["kv"].shape

    def like(n):
        return pltpu.VMEM(f[n].shape, f[n].dtype)

    gsplit = [z.reshape(2, ng, 2, -1, z.shape[-1]) for z in (gd, gg, gu)]
    ublock = [z.shape[3:] for z in gsplit]
    iblock = [((qr, qw), BF16), ((orow, width), BF16), ((8, 128), F32)]
    scratch = [like(n) for n in ("attn", "raw", "q", "o", "ob", "lse", "kv", "wqkv", "wo")]
    scratch += [
        pltpu.VMEM((rows, width), F32),
        pltpu.VMEM((rows, width), BF16),
        pltpu.VMEM((micro, H, tok, HD), BF16),
        pltpu.VMEM((micro, H * tok, 1), F32),
        pltpu.VMEM((micro, H * tok, HD), F32),
        pltpu.VMEM((rows, (H + 2) * HD), BF16),
        pltpu.VMEM((width, rows), F32),
        pltpu.VMEM((2, nz, qr, 4 * qw), BF16),
        pltpu.VMEM((2, nz, 2, 2, orow, width), BF16),
        pltpu.VMEM((2, nz, 2, 2, 8, 128), F32),
        pltpu.VMEM((hz, 2) + kv[3:], BF16),
        pltpu.VMEM((hz,) + kv[3:], BF16),
        pltpu.VMEM((hz - 1,) + kv[3:], BF16),
        pltpu.VMEM(kv[3:], BF16),
    ]
    for s, t in iblock:
        scratch += [pltpu.VMEM(lead + s, t) for lead in ((2, 2, nz), (2, nz), (nz,), (nz - 1,))]
    for lead in ((2, ng), (2, ng), (ng,), (ng,)):
        scratch += [pltpu.VMEM(lead + s, BF16) for s in ublock]
    n_pieces = sum(len(halves(s[0])) for s in ublock)
    scratch += [
        pltpu.SemaphoreType.DMA((9,)),
        pltpu.SemaphoreType.DMA((3, nz + 3)),
        pltpu.SemaphoreType.DMA((3, nz + 3)),
        pltpu.SemaphoreType.DMA((n_pieces, 2)),
        pltpu.SemaphoreType.DMA((n_pieces, 2 + ng)),
        pltpu.SemaphoreType.DMA((n_pieces, 2 + ng)),
        pltpu.SemaphoreType.DMA((hz + 1,)),
        pltpu.SemaphoreType.DMA((hz + 1,)),
        pltpu.SemaphoreType.DMA((nb // 2,)),
        pltpu.SemaphoreType.DMA,
    ]
    out = [
        jax.ShapeDtypeStruct((micro, tok, width), BF16),
        jax.ShapeDtypeStruct((qr, qw), BF16),
        jax.ShapeDtypeStruct((orow, width), F32),
        jax.ShapeDtypeStruct((8, 128), F32),
        jax.ShapeDtypeStruct(ublock[1], BF16),
        jax.ShapeDtypeStruct(ublock[2], BF16),
        jax.ShapeDtypeStruct(ublock[0], F32),
    ]
    return pl.pallas_call(
        functools.partial(back_kernel, nz),
        out_shape=out,
        in_specs=[VMEM] * 11 + [ANY] * 12,
        out_specs=[VMEM] * 7,
        scratch_shapes=scratch,
        compiler_params=pltpu.CompilerParams(collective_id=6, has_side_effects=True, vmem_limit_bytes=63 * 2**20),
    )(
        db, h1, dy, x, cosine, sine, segq, segk, f["gd"], f["gh"], dgp,
        f["attn"], f["raw"], f["q"], f["o"], f["ob"], f["lse"], f["kv"], f["wqkv"], f["wo"], gsplit[1], gsplit[2], gsplit[0],
    )


def scaled_norm(values, gain):
    return values * lax.rsqrt(jnp.mean(values * values, axis=-1, keepdims=True) + epsilon) * (1.0 + gain)


def segments(lengths, index):
    docs = lengths.shape[1]
    ends = [sum(lengths[:, j] for j in range(i + 1)) for i in range(docs)]
    seg = jnp.zeros((lengths.shape[0], index.shape[0]), jnp.int32)
    first = jnp.zeros_like(seg)
    for i in range(docs):
        past = index[None, :] >= ends[i][:, None]
        seg = seg + past.astype(jnp.int32)
        first = first + jnp.where(past, lengths[:, i][:, None], 0)
    return seg, index[None, :] - first


def rotate(values, cosine, sine):
    half = values.shape[-1] // 2
    a, b = values[..., :half], values[..., half:]
    return jnp.concatenate([a * cosine - b * sine, b * cosine + a * sine], axis=-1)


def middle(attn_value, x_value, gain_attn, gain_pre):
    hidden = x_value + scaled_norm(attn_value, gain_attn)
    return (hidden, scaled_norm(hidden, gain_pre))


def shards(tokens, cotangent, doc_lengths, w_query, w_key, w_value, w_out, w_gate, w_up, w_down, *gains):
    nb = lax.axis_size("blk")
    nz = nb // 4
    me = lax.axis_index("blk")
    _, micro, tok, width = tokens.shape
    n_dev = 2 * nb
    nq = 2 * nz
    kr = w_gate.shape[0]
    qr, qp = 4 * kr, up16(4 * kr)
    dr = w_down.shape[0]
    dp = up16(dr)
    orow = w_out.shape[0]
    op = up16(orow)
    groups = [[4 * i + j for j in range(4)] for i in range(nz)]

    def fit(x, rows):
        return x if x.shape[0] == rows else jnp.pad(x, ((0, rows - x.shape[0]), (0, 0)))

    def slices(w):
        w = jnp.pad(w.reshape(kr, nq, 4, dr), ((0, 0), (0, 0), (0, 0), (0, dp - dr)))
        return w.transpose(2, 0, 1, 3).reshape(4, kr, nq * dp)

    fs = nq * dp
    w_qkv = jnp.concatenate([w_query, w_key, w_value], axis=1)
    qw = w_qkv.shape[1] // 4
    pack = jnp.concatenate([slices(w_gate), slices(w_up), w_qkv.reshape(kr, 4, qw).transpose(1, 0, 2)], axis=2)
    pack = lax.all_to_all(pack, "blk", split_axis=0, concat_axis=0, axis_index_groups=groups, tiled=True)
    pack = fit(pack.reshape(qr, 2 * fs + qw), qp)
    wide = [gain.shape[0] for gain in gains]
    def finish(out, d_x, s_qkv, s_wo, s_wg, s_wu, s_wd, gain_grads):
        both = jnp.concatenate([s_wg, s_wu, s_qkv], axis=1)[:qr].reshape(4, kr, 2 * fs + qw)
        both = lax.all_to_all(both, "blk", split_axis=0, concat_axis=0, axis_index_groups=groups, tiled=True)
        both = both.astype(F32)

        def rows_of(z):
            z = z.reshape(4, kr, nq, dp)[..., :dr]
            return z.transpose(1, 2, 0, 3).reshape(kr, nq * 4 * dr)

        s_qkv = both[:, :, 2 * fs :].transpose(1, 0, 2).reshape(kr, 4 * qw)
        n_q = H * HD
        return (
            out[None],
            d_x[None],
            s_qkv[:, :n_q],
            s_qkv[:, n_q : n_q + HD],
            s_qkv[:, n_q + HD :],
            s_wo[:orow],
            rows_of(both[:, :, :fs]),
            rows_of(both[:, :, fs : 2 * fs]),
            s_wd[:dr],
            *gain_grads,
        )

    lengths = doc_lengths[0]
    seg_all, pos_all = segments(lengths, jnp.arange(nb * tok, dtype=jnp.int32))
    seg_me, pos = segments(lengths, me * tok + jnp.arange(tok, dtype=jnp.int32))
    segq = jnp.tile(seg_me, (1, H))[:, :, None]
    segk = seg_all.reshape(micro, nb * tok // 256, 1, 256)
    freq = 1000000.0 ** (-(jnp.arange(HD // 2, dtype=F32) * 2.0 / HD))
    angle = pos.reshape(micro * tok).astype(F32)[:, None] * freq[None, :]
    cosine, sine = jnp.cos(angle), jnp.sin(angle)

    rows = micro * tok
    x = tokens[0].reshape(rows, width).astype(F32)
    dy = cotangent[0].reshape(rows, width)
    shape = (micro, tok, width)
    if qr == qp and orow == op and nz * dp <= 1024:
        flat = jnp.stack([jnp.pad(gain, (0, 128 - gain.shape[0])) for gain in gains] + [jnp.zeros((128,), BF16)] * 10)
        f = front(
            nz, tokens[0].reshape(rows, width), cosine, sine, segq, segk,
            pack[:, 2 * fs :], w_out, flat, pack[:, :fs], pack[:, fs : 2 * fs], fit(w_down, dp), micro,
        )
        wg, wu, wd = (f[n].reshape(-1, f[n].shape[-1]) for n in ("wg", "wu", "wd"))
        out, db, dg_post, gg, gu, gd = ffn(f["b"], f["h1"], dy.reshape(shape), f["gd"][5:6], wg, wu, wd)
        d_x, s_qkv, s_wo, s_gain, s_wg, s_wu, s_wd = back(
            nz, db, f["h1"], dy, tokens[0].reshape(rows, width), cosine, sine, segq, segk, dg_post, f, gg, gu, gd
        )
        gain_grads = [s_gain[i, :w] for i, w in enumerate(wide)]
        return finish(out, d_x, s_qkv, s_wo, s_wg, s_wu, s_wd, gain_grads)
    flat = jnp.concatenate(gains)
    flat = jnp.pad(flat, (0, 16 * 128 - flat.shape[0])).reshape(16, 128)

    qkv_f, wo_f, gain_f, wg_f, wu_f, wd_f = gather_all(
        nz, pack[:, 2 * fs :], fit(w_out, op), flat, pack[:, :fs], pack[:, fs : 2 * fs], fit(w_down, dp)
    )
    wqkv = qkv_f[:, :, :qr].reshape(width, 4 * qw)
    wo = wo_f[:, :, :, :, :orow].reshape(n_dev * orow, width)
    wg = wg_f[:, :, :qr].reshape(width, fs)
    wu = wu_f[:, :, :qr].reshape(width, fs)
    wd = wd_f.reshape(fs, width)
    gain_rows = gain_f.reshape(n_dev, 16 * 128)
    full_gains, o = [], 0
    for w in wide:
        full_gains.append(gain_rows[:, o : o + w].reshape(n_dev * w).astype(F32))
        o += w
    gain_in, gain_query, gain_key, gain_attn, gain_pre, gain_post = full_gains

    normed, pre_pull = jax.vjp(scaled_norm, x, gain_in)
    a = normed.astype(BF16)
    qkv = jnp.dot(a, wqkv, preferred_element_type=F32)
    n_q = H * HD
    q_raw = qkv[:, :n_q].reshape(rows, H, HD)
    k_raw = qkv[:, n_q : n_q + HD]
    v = qkv[:, n_q + HD :].astype(BF16)
    queries, query_pull = jax.vjp(
        lambda r, g: rotate(scaled_norm(r, g), cosine[:, None], sine[:, None]), q_raw, gain_query
    )
    keys, key_pull = jax.vjp(lambda r, g: rotate(scaled_norm(r, g), cosine, sine), k_raw, gain_key)

    def by_head(z):
        return z.reshape(micro, tok, H, HD).transpose(0, 2, 1, 3).reshape(micro, H * tok, HD)

    def by_row(z):
        return z.reshape(micro, H, tok, HD).transpose(0, 2, 1, 3).reshape(rows, H * HD)

    qh = by_head(queries.astype(BF16))
    kv = jnp.concatenate([keys.astype(BF16), v], axis=1).reshape(micro, tok, 2 * HD)
    oh, lse, kvall = attn_fwd(nb, qh, kv, segq, segk)
    o_b = by_row(oh.astype(BF16))
    attn = jnp.dot(o_b, wo, preferred_element_type=F32)
    (h1, ffn_in), mid_pull = jax.vjp(middle, attn, x, gain_attn, gain_pre)

    out, db, dg_post, gg, gu, gd = ffn(
        ffn_in.astype(BF16).reshape(shape), h1.reshape(shape), dy.reshape(shape), gain_post[None, :], wg, wu, wd
    )
    d_attn, d_x_mid, dg_attn, dg_pre = mid_pull((dy.astype(F32), db.reshape(rows, width)))
    d_attn = d_attn.astype(BF16)
    grad_out = lax.dot_general(o_b, d_attn, (((0,), (0,)), ((), ())), preferred_element_type=F32).astype(BF16)
    do = lax.dot_general(d_attn, wo, (((1,), (1,)), ((), ())), preferred_element_type=F32).astype(BF16)
    doh = by_head(do)
    delta = jnp.sum(doh.astype(F32) * oh, axis=-1, keepdims=True)
    dqh, dkv = attn_bwd(nb, qh, kvall, doh, lse, delta, segq, segk)
    dkv = dkv.reshape(rows, 2 * HD)
    dq_raw, dg_query = query_pull(by_row(dqh).reshape(rows, H, HD))
    dk_raw, dg_key = key_pull(dkv[:, :HD])
    d_qkv = jnp.concatenate([dq_raw.reshape(rows, n_q), dk_raw, dkv[:, HD:]], axis=1).astype(BF16)
    grad_qkv = lax.dot_general(a, d_qkv, (((0,), (0,)), ((), ())), preferred_element_type=F32).astype(BF16)
    da = lax.dot_general(d_qkv, wqkv, (((1,), (1,)), ((), ())), preferred_element_type=F32)
    d_x_pre, dg_in = pre_pull(da)
    d_x = (d_x_mid + d_x_pre).astype(BF16)

    def quads(z, r, p):
        z = z.reshape(2, nz, r, z.shape[-1])
        return z if r == p else jnp.pad(z, ((0, 0), (0, 0), (0, p - r), (0, 0)))

    go = grad_out.reshape(2, nz, 2, 2, orow, width)
    if op != orow:
        go = jnp.pad(go, ((0, 0),) * 4 + ((0, op - orow), (0, 0)))
    dgains = jnp.concatenate(
        [d.reshape(n_dev, w) for d, w in zip((dg_in, dg_query, dg_key, dg_attn, dg_pre, dg_post[0]), wide)], axis=1
    )
    used = dgains.shape[1]
    dgains = jnp.pad(dgains, ((0, 0), (0, 8 * 128 - used))).reshape(2, nz, 2, 2, 8, 128)
    s_qkv, s_wo, s_gain, s_wg, s_wu, s_wd = reduce_all(
        nz, quads(grad_qkv, qr, qp), go, dgains, quads(gg, qr, qp), quads(gu, qr, qp), gd.reshape(2, nz, dp, width)
    )
    flat = s_gain.reshape(-1)
    gain_grads, o = [], 0
    for w in wide:
        gain_grads.append(flat[o : o + w])
        o += w
    return finish(out, d_x.reshape(shape), s_qkv, s_wo, s_wg, s_wu, s_wd, gain_grads)


def solution(mesh):
    sequence = P("bucket", None, "blk", None)
    split = ("bucket", "blk")
    return jax.shard_map(
        shards,
        mesh=mesh,
        in_specs=(sequence, sequence, P("bucket", None, None)) + (P(split, None),) * 7 + (P(split),) * 6,
        out_specs=(sequence, sequence) + (P(split, None),) * 7 + (P(split),) * 6,
        check_vma=False,
    )
```

```python
import functools
import math

import jax
import jax.numpy as jnp
from jax import lax
from jax.experimental import pallas as pl
from jax.experimental.pallas import tpu as pltpu
from jax.sharding import PartitionSpec as P

H = 4
HD = 256
F32 = jnp.float32
BF16 = jnp.bfloat16
MESH = pl.DeviceIdType.MESH
ANY = pl.BlockSpec(memory_space=pl.ANY)
VMEM = pl.BlockSpec(memory_space=pltpu.VMEM)
epsilon = 1e-06


def up16(n):
    return -(-n // 16) * 16


def place():
    b = lax.axis_index("bucket")
    k = lax.axis_index("blk")
    return b, k // 4, (k // 2) % 2, k % 2


def at(b, q, y, c):
    return (b, q * 4 + y * 2 + c)


def greet(targets):
    bar = pltpu.get_barrier_semaphore()
    for t in targets:
        pl.semaphore_signal(bar, inc=1, device_id=t, device_id_type=MESH)
    return bar


def remote(src, dst, send, recv, target):
    return pltpu.make_async_remote_copy(src, dst, send, recv, device_id=target, device_id_type=MESH)


def gather_kernel(nz, qkv, wo, gain, wg, wu, wd, qkv_f, wo_f, gain_f, wg_f, wu_f, wd_f, lsem, ssem, rsem, wls, wss, wrs):
    b, q, y, c = place()
    g, e = q // 2, q % 2
    ng = nz // 2
    qw = qkv.shape[1]
    self_in = e == c
    bar = greet(
        [at(b, lax.rem(q + r, nz), y, c) for r in range(1, nz)]
        + [at(1 - b, q, y, c), at(b, q, 1 - y, c), at(b, q, y, 1 - c)]
        + [at(b, lax.rem(g + r, ng) * 2 + c, y, e) for r in range(1, ng)]
    )
    first = at(b, g * 2 + c, y, e)

    @pl.when(jnp.logical_not(self_in))
    def _():
        pl.semaphore_signal(bar, inc=1, device_id=first, device_id_type=MESH)

    pl.semaphore_wait(bar, nz + 1 + ng - jnp.where(self_in, 1, 0) + 1)

    everything = pl.ds(0, nz)

    def view_qkv(ref, yy, cc, xx, qq):
        return ref.at[xx, qq, :, pl.ds(pl.multiple_of((yy * 2 + cc) * qw, 128), qw)]

    def view_lead(ref, yy, cc, xx, qq):
        return ref.at[xx, qq, yy, cc]

    items = [(qkv, qkv_f, view_qkv), (wo, wo_f, view_lead), (gain, gain_f, view_lead)]
    sent = []
    local = []
    for i, (src, dst, view) in enumerate(items):
        cp = pltpu.make_async_copy(src, view(dst, y, c, b, q), lsem.at[i])
        cp.start()
        local.append(cp)
    z_in = []
    for i, (src, dst, view) in enumerate(items):
        row = []
        for r in range(1, nz):
            cp = remote(src, view(dst, y, c, b, q), ssem.at[i, r], rsem.at[i, r], at(b, lax.rem(q + r, nz), y, c))
            cp.start()
            sent.append(cp)
            row.append(
                remote(src, view(dst, y, c, b, lax.rem(q - r + nz, nz)), ssem.at[i, r], rsem.at[i, r], at(b, lax.rem(q + r, nz), y, c))
            )
        z_in.append(row)
    x_in = [[] for _ in items]
    for i, (src, dst, view) in enumerate(items):
        cp = remote(src, view(dst, y, c, b, q), ssem.at[i, nz], rsem.at[i, nz], at(1 - b, q, y, c))
        cp.start()
        sent.append(cp)
        x_in[i].append(remote(src, view(dst, y, c, 1 - b, q), ssem.at[i, nz], rsem.at[i, nz], at(1 - b, q, y, c)))

    units = [(wg, wg_f), (wu, wu_f), (wd, wd_f)]
    u_in = []
    for j, (src, dst) in enumerate(units):
        row = []
        for r in range(ng):
            target = at(b, lax.rem(g + r, ng) * 2 + c, y, e)
            cp = remote(src, dst.at[b, q], wss.at[j, r], wrs.at[j, r], target)
            qs = lax.rem(g - r + ng, ng) * 2 + c
            inc = remote(src, dst.at[b, qs], wss.at[j, r], wrs.at[j, r], target)
            if r == 0:
                lc = pltpu.make_async_copy(src, dst.at[b, q], wls.at[j])

                @pl.when(self_in)
                def _():
                    lc.start()

                @pl.when(jnp.logical_not(self_in))
                def _():
                    cp.start()
            else:
                cp.start()
            row.append((cp, inc, qs, lc if r == 0 else None))
        u_in.append(row)

    for r in range(1, nz):
        qs = lax.rem(q - r + nz, nz)
        for i, (src, dst, view) in enumerate(items):
            z_in[i][r - 1].wait_recv()
            cp = remote(view(dst, y, c, b, qs), view(dst, y, c, b, qs), ssem.at[i, nz + r], rsem.at[i, nz + r], at(1 - b, q, y, c))
            cp.start()
            sent.append(cp)
            x_in[i].append(
                remote(view(dst, y, c, b, qs), view(dst, y, c, 1 - b, qs), ssem.at[i, nz + r], rsem.at[i, nz + r], at(1 - b, q, y, c))
            )
    for cp in local:
        cp.wait()
    y_in = [[] for _ in items]
    for half in range(2):
        for i, (src, dst, view) in enumerate(items):
            xx = b if half == 0 else 1 - b
            if half == 1:
                for cp in x_in[i]:
                    cp.wait_recv()
            s = 2 * nz + half
            cp = remote(view(dst, y, c, xx, everything), view(dst, y, c, xx, everything), ssem.at[i, s], rsem.at[i, s], at(b, q, 1 - y, c))
            cp.start()
            sent.append(cp)
            y_in[i].append(
                remote(view(dst, y, c, xx, everything), view(dst, 1 - y, c, xx, everything), ssem.at[i, s], rsem.at[i, s], at(b, q, 1 - y, c))
            )
    c_in = []

    def to_core(i, yy, s):
        _, dst, view = items[i]
        both = pl.ds(0, 2)
        cp = remote(view(dst, yy, c, both, everything), view(dst, yy, c, both, everything), ssem.at[i, s], rsem.at[i, s], at(b, q, y, 1 - c))
        cp.start()
        sent.append(cp)
        c_in.append(
            remote(view(dst, yy, c, both, everything), view(dst, yy, 1 - c, both, everything), ssem.at[i, s], rsem.at[i, s], at(b, q, y, 1 - c))
        )

    for i in range(len(items)):
        to_core(i, y, 2 * nz + 2)
    for i in range(len(items)):
        for cp in y_in[i]:
            cp.wait_recv()
        to_core(i, 1 - y, 2 * nz + 3)

    d_in = []

    def unit_on(j, xx, qs, s, target, yours):
        _, dst = units[j]
        cp = remote(dst.at[xx, qs], dst.at[xx, qs], wss.at[j, s], wrs.at[j, s], target)
        cp.start()
        sent.append(cp)
        return remote(dst.at[xx, qs], dst.at[yours[0], yours[1]], wss.at[j, s], wrs.at[j, s], target)

    xw = [[] for _ in units]

    def x_round(j):
        for r in range(ng):
            cp, inc, qs, lc = u_in[j][r]
            if r == 0:

                @pl.when(self_in)
                def _():
                    lc.wait()

                @pl.when(jnp.logical_not(self_in))
                def _():
                    inc.wait_recv()
            else:
                inc.wait_recv()
            xw[j].append(unit_on(j, b, qs, ng + r, at(1 - b, q, y, c), (1 - b, qs)))
        for r in range(ng):
            qs = u_in[j][r][2]
            qo = lax.rem(g - r + ng, ng) * 2 + 1 - c
            d_in.append(unit_on(j, b, qs, 2 * ng + r, at(b, q, y, 1 - c), (b, qo)))

    def c_round(j):
        for r in range(ng):
            qs = u_in[j][r][2]
            qo = lax.rem(g - r + ng, ng) * 2 + 1 - c
            xw[j][r].wait_recv()
            d_in.append(unit_on(j, 1 - b, qs, 3 * ng + r, at(b, q, y, 1 - c), (1 - b, qo)))

    x_round(0)
    x_round(1)
    c_round(0)
    x_round(2)
    c_round(1)
    c_round(2)
    for cp in c_in + d_in:
        cp.wait_recv()
    for cp in sent:
        cp.wait_send()
    for j in range(len(units)):
        for r in range(ng):
            cp = u_in[j][r][0]
            if r == 0:

                @pl.when(jnp.logical_not(self_in))
                def _():
                    cp.wait_send()
            else:
                cp.wait_send()


def gather_all(nz, qkv, wo, gain, wg, wu, wd):
    ng = nz // 2
    out = [
        jax.ShapeDtypeStruct((2, nz, qkv.shape[0], 4 * qkv.shape[1]), BF16),
        jax.ShapeDtypeStruct((2, nz, 2, 2) + wo.shape, BF16),
        jax.ShapeDtypeStruct((2, nz, 2, 2) + gain.shape, BF16),
        jax.ShapeDtypeStruct((2, nz) + wg.shape, BF16),
        jax.ShapeDtypeStruct((2, nz) + wu.shape, BF16),
        jax.ShapeDtypeStruct((2, nz) + wd.shape, BF16),
    ]
    ns = 2 * nz + 4
    return pl.pallas_call(
        functools.partial(gather_kernel, nz),
        out_shape=out,
        in_specs=[ANY] * 6,
        out_specs=[ANY] * 6,
        scratch_shapes=[
            pltpu.SemaphoreType.DMA((3,)),
            pltpu.SemaphoreType.DMA((3, ns)),
            pltpu.SemaphoreType.DMA((3, ns)),
            pltpu.SemaphoreType.DMA((3,)),
            pltpu.SemaphoreType.DMA((3, 4 * ng)),
            pltpu.SemaphoreType.DMA((3, 4 * ng)),
        ],
        compiler_params=pltpu.CompilerParams(collective_id=0, has_side_effects=True),
    )(qkv, wo, gain, wg, wu, wd)


def reduce_kernel(nz, qkv, wo, gain, wg, wu, wd, qkv_o, wo_o, gain_o, wg_o, wu_o, wd_o, *scratch):
    b, q, y, c = place()
    g, e = q // 2, q % 2
    ng = nz // 2
    qw = qkv_o.shape[1]
    self_in = e == c
    n_items, n_units = 3, 3
    own = scratch[0:3]
    r1 = scratch[3:6]
    r2 = scratch[6:9]
    r3 = scratch[9:12]
    r4 = scratch[12:15]
    uown = scratch[15:18]
    u1 = scratch[18:21]
    u2 = scratch[21:24]
    u3 = scratch[24:27]
    lsem, ssem, rsem, wls, wss, wrs = scratch[27:]
    bar = greet(
        [at(b, lax.rem(q + r, nz), y, c) for r in range(1, nz)]
        + [at(1 - b, q, y, c), at(b, q, 1 - y, c), at(b, q, y, 1 - c)]
        + [at(b, lax.rem(g + r, ng) * 2 + c, y, e) for r in range(1, ng)]
    )
    first = at(b, g * 2 + c, y, e)

    @pl.when(jnp.logical_not(self_in))
    def _():
        pl.semaphore_signal(bar, inc=1, device_id=first, device_id_type=MESH)

    pl.semaphore_wait(bar, nz + 1 + ng - jnp.where(self_in, 1, 0) + 1)

    other_core = at(b, q, y, 1 - c)
    other_y = at(b, q, 1 - y, c)
    other_x = at(1 - b, q, y, c)
    full = (pl.ds(0, 2), pl.ds(0, nz))

    def view_qkv(ref, yy, cc):
        return ref.at[full[0], full[1], :, pl.ds(pl.multiple_of((yy * 2 + cc) * qw, 128), qw)]

    def view_lead(ref, yy, cc):
        return ref.at[full[0], full[1], yy, cc]

    items = [(qkv, qkv_o, view_qkv), (wo, wo_o, view_lead), (gain, gain_o, view_lead)]
    units = [(wd, wd_o), (wg, wg_o), (wu, wu_o)]
    sent = []
    item_local, item_in = [[] for _ in items], [[] for _ in items]
    unit_local, unit_in = [[] for _ in units], [[] for _ in units]

    def start(cp):
        cp.start()
        sent.append(cp)
        return cp

    def item_core(i):
        src, _, view = items[i]
        for yy in range(2):
            item_in[i].append(start(remote(view(src, yy, 1 - c), r1[i].at[yy], ssem.at[i, yy], rsem.at[i, yy], other_core)))
            cp = pltpu.make_async_copy(view(src, yy, c), own[i].at[yy], lsem.at[i, yy])
            cp.start()
            item_local[i].append(cp)

    def unit_core(j):
        src, _ = units[j]
        for xx in range(2):
            for r in range(ng):
                s = xx * ng + r
                mine, yours = r * 2 + c, r * 2 + 1 - c
                unit_in[j].append(start(remote(src.at[xx, yours], u1[j].at[xx, r], wss.at[j, s], wrs.at[j, s], other_core)))
                cp = pltpu.make_async_copy(src.at[xx, mine], uown[j].at[xx, r], wls.at[j, s])
                cp.start()
                unit_local[j].append(cp)

    def add(dst, src, lead):
        def one(n, _):
            dst[n] = (dst[n].astype(F32) + src[n].astype(F32)).astype(dst.dtype)
            return 0

        lax.fori_loop(0, lead, one, 0)

    def unit_x(j):
        for cp in unit_local[j]:
            cp.wait()
        for cp in unit_in[j]:
            cp.wait_recv()
        add(uown[j].at[1 - b], u1[j].at[1 - b], ng)
        cp = start(remote(uown[j].at[1 - b], u2[j], wss.at[j, 2 * ng], wrs.at[j, 2 * ng], other_x))
        add(uown[j].at[b], u1[j].at[b], ng)
        unit_in[j] = [cp]

    def unit_z(j):
        unit_in[j][0].wait_recv()
        add(uown[j].at[b], u2[j], ng)
        waits = []
        for r in range(ng):
            gs = lax.rem(g + r, ng)
            cp = remote(uown[j].at[b, gs], u3[j].at[r], wss.at[j, 2 * ng + 1 + r], wrs.at[j, 2 * ng + 1 + r], at(b, gs * 2 + c, y, e))
            if r == 0:
                lc = pltpu.make_async_copy(uown[j].at[b, gs], u3[j].at[0], wls.at[j, 2 * ng])

                @pl.when(self_in)
                def _():
                    lc.start()

                @pl.when(jnp.logical_not(self_in))
                def _():
                    cp.start()

                waits.append((cp, lc))
            else:
                start(cp)
                waits.append((cp, None))
        unit_in[j] = waits

    def unit_end(j):
        for cp, lc in unit_in[j]:
            if lc is not None:

                @pl.when(self_in)
                def _():
                    lc.wait()

                @pl.when(jnp.logical_not(self_in))
                def _():
                    cp.wait()
            else:
                cp.wait_recv()
        rows = u3[j].shape[1]
        step = 16

        def one(n, _):
            sl = pl.ds(pl.multiple_of(n * step, step), step)
            total = u3[j][0, sl].astype(F32)
            for r in range(1, ng):
                total = total + u3[j][r, sl].astype(F32)
            units[j][1][sl] = total.astype(units[j][1].dtype)
            return 0

        lax.fori_loop(0, rows // step, one, 0)

    def item_y(i):
        for cp in item_local[i]:
            cp.wait()
        for cp in item_in[i]:
            cp.wait_recv()
        for xx in range(2):
            add(own[i].at[1 - y, xx], r1[i].at[1 - y, xx], nz)
        cp = start(remote(own[i].at[1 - y], r2[i], ssem.at[i, 2], rsem.at[i, 2], other_y))
        for xx in range(2):
            add(own[i].at[y, xx], r1[i].at[y, xx], nz)
        item_in[i] = [cp]

    def item_x(i):
        item_in[i][0].wait_recv()
        add(own[i].at[y, 1 - b], r2[i].at[1 - b], nz)
        cp = start(remote(own[i].at[y, 1 - b], r3[i], ssem.at[i, 3], rsem.at[i, 3], other_x))
        add(own[i].at[y, b], r2[i].at[b], nz)
        item_in[i] = [cp]

    def item_z(i):
        item_in[i][0].wait_recv()
        add(own[i].at[y, b], r3[i], nz)
        waits = []
        for r in range(1, nz):
            qt = lax.rem(q + r, nz)
            waits.append(start(remote(own[i].at[y, b, qt], r4[i].at[r - 1], ssem.at[i, 3 + r], rsem.at[i, 3 + r], at(b, qt, y, c))))
        item_in[i] = waits

    def item_end(i):
        for cp in item_in[i]:
            cp.wait_recv()
        total = own[i][y, b, q].astype(F32)
        for r in range(1, nz):
            total = total + r4[i][r - 1].astype(F32)
        items[i][1][...] = total.astype(items[i][1].dtype)

    for j in range(n_units):
        unit_core(j)
    for i in range(n_items):
        item_core(i)
    for j in range(n_units):
        unit_x(j)
    for i in range(n_items):
        item_y(i)
    unit_z(0)
    for i in range(n_items):
        item_x(i)
    unit_z(1)
    for i in range(n_items):
        item_z(i)
    unit_z(2)
    for i in range(n_items):
        item_end(i)
    for j in range(n_units):
        unit_end(j)
    for cp in sent:
        cp.wait_send()


def reduce_all(nz, qkv, wo, gain, wg, wu, wd):
    ng = nz // 2
    qw = qkv.shape[3] // 4
    blocks = [((qkv.shape[2], qw), BF16), (wo.shape[4:], BF16), (gain.shape[4:], F32)]
    ublocks = [(wd.shape[2:], BF16), (wg.shape[2:], BF16), (wu.shape[2:], BF16)]
    scratch = (
        [pltpu.VMEM((2, 2, nz) + s, t) for s, t in blocks]
        + [pltpu.VMEM((2, 2, nz) + s, t) for s, t in blocks]
        + [pltpu.VMEM((2, nz) + s, t) for s, t in blocks]
        + [pltpu.VMEM((nz,) + s, t) for s, t in blocks]
        + [pltpu.VMEM((nz - 1,) + s, t) for s, t in blocks]
        + [pltpu.VMEM((2, ng) + s, t) for s, t in ublocks]
        + [pltpu.VMEM((2, ng) + s, t) for s, t in ublocks]
        + [pltpu.VMEM((ng,) + s, t) for s, t in ublocks]
        + [pltpu.VMEM((ng,) + s, t) for s, t in ublocks]
        + [
            pltpu.SemaphoreType.DMA((3, 2)),
            pltpu.SemaphoreType.DMA((3, nz + 3)),
            pltpu.SemaphoreType.DMA((3, nz + 3)),
            pltpu.SemaphoreType.DMA((3, 2 * ng + 1)),
            pltpu.SemaphoreType.DMA((3, 3 * ng + 1)),
            pltpu.SemaphoreType.DMA((3, 3 * ng + 1)),
        ]
    )
    out = [
        jax.ShapeDtypeStruct(blocks[0][0], BF16),
        jax.ShapeDtypeStruct(blocks[1][0], F32),
        jax.ShapeDtypeStruct(blocks[2][0], F32),
        jax.ShapeDtypeStruct(ublocks[1][0], BF16),
        jax.ShapeDtypeStruct(ublocks[2][0], BF16),
        jax.ShapeDtypeStruct(ublocks[0][0], F32),
    ]
    return pl.pallas_call(
        functools.partial(reduce_kernel, nz),
        out_shape=out,
        in_specs=[ANY] * 6,
        out_specs=[VMEM] * 6,
        scratch_shapes=scratch,
        compiler_params=pltpu.CompilerParams(collective_id=1, has_side_effects=True, vmem_limit_bytes=60 * 2**20),
    )(qkv, wo, gain, wg, wu, wd)


def chunk_scores(q, kk, segq, segk, qidx, j, scale):
    s = lax.dot_general(q, kk, (((1,), (1,)), ((), ())), preferred_element_type=F32) * scale
    kidx = j * 256 + lax.broadcasted_iota(jnp.int32, (1, 256), 1)
    return s, (segq == segk) & (kidx <= qidx)


def attn_fwd_kernel(nb, q_ref, kv_ref, segq_ref, segk_ref, o_ref, lse_ref, kvall, lsem, ssem, rsem):
    b, q, y, c = place()
    k = lax.axis_index("blk")
    nz = nb // 4
    hz = nz // 2
    half = q // hz
    ql = q - half * hz
    low = k < nb // 2
    is_mid = k == nb // 2
    mid = (b, nb // 2)
    bar = greet(
        [at(b, half * hz + lax.rem(ql + r, hz), y, c) for r in range(1, hz)] + [at(b, q, 1 - y, c), at(b, q, y, 1 - c)]
    )

    @pl.when(low)
    def _():
        pl.semaphore_signal(bar, inc=1, device_id=mid, device_id_type=MESH)

    @pl.when(is_mid)
    def _():
        for j in range(nb // 2):
            pl.semaphore_signal(bar, inc=1, device_id=(b, j), device_id_type=MESH)

    pl.semaphore_wait(bar, hz + 1 + jnp.where(low, 1, 0) + jnp.where(is_mid, nb // 2, 0))

    def view(qq, yy, cc):
        return kvall.at[qq, yy, cc]

    sent = []

    def start(cp):
        cp.start()
        sent.append(cp)
        return cp

    mine = pltpu.make_async_copy(kv_ref, view(q, y, c), lsem)
    mine.start()
    other_y = at(b, q, 1 - y, c)
    other_c = at(b, q, y, 1 - c)
    z_in = []
    for r in range(1, hz):
        target = at(b, half * hz + lax.rem(ql + r, hz), y, c)
        start(remote(kv_ref, view(q, y, c), ssem.at[r], rsem.at[r], target))
        src = half * hz + lax.rem(ql - r + hz, hz)
        z_in.append((remote(kv_ref, view(src, y, c), ssem.at[r], rsem.at[r], target), src))
    start(remote(kv_ref, view(q, y, c), ssem.at[hz], rsem.at[hz], other_y))
    y_in = [(remote(kv_ref, view(q, 1 - y, c), ssem.at[hz], rsem.at[hz], other_y), q)]
    ns = 2 * hz + hz * 2
    to_mid = remote(kv_ref, view(q, y, c), ssem.at[ns], rsem.at[ns + k % (nb // 2)], mid)

    @pl.when(low)
    def _():
        to_mid.start()

    mine.wait()
    c_in = []
    s = 2 * hz

    def to_core(qq, yy, s):
        start(remote(view(qq, yy, c), view(qq, yy, c), ssem.at[s], rsem.at[s], other_c))
        c_in.append(remote(view(qq, yy, c), view(qq, yy, 1 - c), ssem.at[s], rsem.at[s], other_c))

    to_core(q, y, s)
    s += 1
    for r, (cp, src) in enumerate(z_in):
        cp.wait_recv()
        n = hz + 1 + r
        start(remote(view(src, y, c), view(src, y, c), ssem.at[n], rsem.at[n], other_y))
        y_in.append((remote(view(src, y, c), view(src, 1 - y, c), ssem.at[n], rsem.at[n], other_y), src))
        to_core(src, y, s)
        s += 1
    for cp, src in y_in:
        cp.wait_recv()
        to_core(src, 1 - y, s)
        s += 1
    for cp in c_in:
        cp.wait_recv()

    @pl.when(is_mid)
    def _():
        for j in range(nb // 2):
            remote(kv_ref, view(j // 4, (j // 2) % 2, j % 2), ssem.at[ns], rsem.at[ns + j], mid).wait_recv()

    scale = HD ** (-0.5)
    lo = jnp.where(k <= nb // 2, 0, nb // 4)
    hi = k // 2 + 1
    rows = q_ref.shape[1]
    tok = rows // H
    qidx = k * tok + lax.broadcasted_iota(jnp.int32, (rows, 1), 0) % tok
    for m in range(q_ref.shape[0]):
        qm = q_ref[m]
        segq = segq_ref[m]

        def body(j, carry):
            mx, sm, acc = carry
            blk = kvall[j // 2, j % 2, :, m].reshape(256, 2 * HD)
            s, ok = chunk_scores(qm, blk[:, :HD], segq, segk_ref[m, j], qidx, j, scale)
            s = jnp.where(ok, s, -1e30)
            new = jnp.maximum(mx, jnp.max(s, axis=-1, keepdims=True))
            p = jnp.where(ok, jnp.exp(s - new), 0.0)
            alpha = jnp.exp(mx - new)
            sm = sm * alpha + jnp.sum(p, axis=-1, keepdims=True)
            acc = acc * alpha + jnp.dot(p.astype(BF16), blk[:, HD:], preferred_element_type=F32)
            return new, sm, acc

        mx, sm, acc = lax.fori_loop(
            lo, hi, body, (jnp.full((rows, 1), -1e30, F32), jnp.zeros((rows, 1), F32), jnp.zeros((rows, HD), F32))
        )
        o_ref[m] = acc / sm
        lse_ref[m] = mx + jnp.log(sm)
    for cp in sent:
        cp.wait_send()

    @pl.when(low)
    def _():
        to_mid.wait_send()


def attn_fwd(nb, q, kv, segq, segk):
    nz = nb // 4
    ns = 4 * (nz // 2)
    return pl.pallas_call(
        functools.partial(attn_fwd_kernel, nb),
        out_shape=[
            jax.ShapeDtypeStruct(q.shape, F32),
            jax.ShapeDtypeStruct(q.shape[:2] + (1,), F32),
            jax.ShapeDtypeStruct((nz, 2, 2) + kv.shape, BF16),
        ],
        in_specs=[VMEM] * 4,
        out_specs=[VMEM] * 3,
        scratch_shapes=[
            pltpu.SemaphoreType.DMA,
            pltpu.SemaphoreType.DMA((ns + 1,)),
            pltpu.SemaphoreType.DMA((ns + nb // 2,)),
        ],
        compiler_params=pltpu.CompilerParams(collective_id=2, has_side_effects=True, vmem_limit_bytes=60 * 2**20),
    )(q, kv, segq, segk)


def attn_bwd_kernel(
    nb, q_ref, kvall, do_ref, lse_ref, delta_ref, segq_ref, segk_ref, dq_ref, dkv_ref, part, r1, r2, r3, r4, ssem, rsem, msem, nsem
):
    b, q, y, c = place()
    k = lax.axis_index("blk")
    nz = nb // 4
    hz = nz // 2
    half = q // hz
    ql = q - half * hz
    low = k < nb // 2
    is_mid = k == nb // 2
    mid = (b, nb // 2)
    bar = greet(
        [at(b, half * hz + lax.rem(ql + r, hz), y, c) for r in range(1, hz)] + [at(b, q, 1 - y, c), at(b, q, y, 1 - c)]
    )

    @pl.when(low)
    def _():
        pl.semaphore_signal(bar, inc=1, device_id=mid, device_id_type=MESH)

    @pl.when(is_mid)
    def _():
        for j in range(nb // 2):
            pl.semaphore_signal(bar, inc=1, device_id=(b, j), device_id_type=MESH)

    pl.semaphore_wait(bar, hz + 1 + jnp.where(low, 1, 0) + jnp.where(is_mid, nb // 2, 0))
    other_y = at(b, q, 1 - y, c)
    other_c = at(b, q, y, 1 - c)
    sent = []

    def start(cp):
        cp.start()
        sent.append(cp)
        return cp

    def clear(n, _):
        part[half * hz + n // 4, (n // 2) % 2, n % 2] = jnp.zeros(part.shape[3:], BF16)
        return 0

    lax.fori_loop(0, 4 * hz, clear, 0)
    scale = HD ** (-0.5)
    lo = jnp.where(k <= nb // 2, 0, nb // 4)
    hi = k // 2 + 1
    rows = q_ref.shape[1]
    tok = rows // H
    qidx = k * tok + lax.broadcasted_iota(jnp.int32, (rows, 1), 0) % tok
    tn = (((0,), (0,)), ((), ()))
    nt = (((1,), (1,)), ((), ()))
    for m in range(q_ref.shape[0]):
        dq_ref[m] = jnp.zeros(dq_ref.shape[1:], F32)

        def body(j, _):
            qm, dom = q_ref[m], do_ref[m]
            blk = kvall[j // 2, j % 2, :, m].reshape(256, 2 * HD)
            s, ok = chunk_scores(qm, blk[:, :HD], segq_ref[m], segk_ref[m, j], qidx, j, scale)
            p = jnp.where(ok, jnp.exp(jnp.where(ok, s, -1e30) - lse_ref[m]), 0.0)
            dp = lax.dot_general(dom, blk[:, HD:], nt, preferred_element_type=F32)
            ds = (p * (dp - delta_ref[m])).astype(BF16)
            dq_ref[m] += jnp.dot(ds, blk[:, :HD], preferred_element_type=F32) * scale
            dk = lax.dot_general(ds, qm, tn, preferred_element_type=F32) * scale
            dv = lax.dot_general(p.astype(BF16), dom, tn, preferred_element_type=F32)
            part[j // 2, j % 2, :, m] = jnp.concatenate([dk, dv], axis=1).astype(BF16).reshape(2, tok, 2 * HD)
            return 0

        lax.fori_loop(lo, hi, body, 0)

    @pl.when(is_mid)
    def _():
        for j in range(nb // 2):
            remote(part.at[j // 4, (j // 2) % 2, j % 2], r4, msem.at[j], nsem, (b, j)).start()

    hs = pl.ds(half * hz, hz)
    cp = start(remote(part.at[hs, :, 1 - c], r1, ssem.at[0], rsem.at[0], other_c))
    cp.wait_recv()

    def add1(n, _):
        i = half * hz + n // 2
        part[i, n % 2, c] = (part[i, n % 2, c].astype(F32) + r1[n // 2, n % 2].astype(F32)).astype(BF16)
        return 0

    lax.fori_loop(0, 2 * hz, add1, 0)
    cp = start(remote(part.at[hs, 1 - y, c], r2, ssem.at[1], rsem.at[1], other_y))
    cp.wait_recv()

    def add2(n, _):
        i = half * hz + n
        part[i, y, c] = (part[i, y, c].astype(F32) + r2[n].astype(F32)).astype(BF16)
        return 0

    lax.fori_loop(0, hz, add2, 0)
    last = []
    for r in range(1, hz):
        qt = half * hz + lax.rem(ql + r, hz)
        last.append(start(remote(part.at[qt, y, c], r3.at[r - 1], ssem.at[1 + r], rsem.at[1 + r], at(b, qt, y, c))))
    total = part[q, y, c].astype(F32)
    for r, cp in enumerate(last):
        cp.wait_recv()
        total = total + r3[r].astype(F32)
    dkv_ref[...] = total

    @pl.when(low)
    def _():
        remote(part.at[0, 0, 0], r4, msem.at[0], nsem, mid).wait_recv()
        dkv_ref[...] += r4[...].astype(F32)

    for cp in sent:
        cp.wait_send()

    @pl.when(is_mid)
    def _():
        for j in range(nb // 2):
            remote(part.at[j // 4, (j // 2) % 2, j % 2], r4, msem.at[j], nsem, (b, j)).wait_send()


def attn_bwd(nb, q, kvall, do, lse, delta, segq, segk):
    nz = nb // 4
    hz = nz // 2
    blk = kvall.shape[3:]
    return pl.pallas_call(
        functools.partial(attn_bwd_kernel, nb),
        out_shape=[jax.ShapeDtypeStruct(q.shape, F32), jax.ShapeDtypeStruct(blk, F32)],
        in_specs=[VMEM] * 7,
        out_specs=[VMEM] * 2,
        scratch_shapes=[
            pltpu.VMEM(kvall.shape, BF16),
            pltpu.VMEM((hz, 2) + blk, BF16),
            pltpu.VMEM((hz,) + blk, BF16),
            pltpu.VMEM((hz - 1,) + blk, BF16),
            pltpu.VMEM(blk, BF16),
            pltpu.SemaphoreType.DMA((hz + 1,)),
            pltpu.SemaphoreType.DMA((hz + 1,)),
            pltpu.SemaphoreType.DMA((nb // 2,)),
            pltpu.SemaphoreType.DMA,
        ],
        compiler_params=pltpu.CompilerParams(collective_id=3, has_side_effects=True, vmem_limit_bytes=60 * 2**20),
    )(q, kvall, do, lse, delta, segq, segk)


def tiles(n, w):
    return [(i, min(w, n - i)) for i in range(0, n, w)]


def gelu_parts(z):
    k0 = math.sqrt(2.0 / math.pi)
    t = jnp.tanh(k0 * (z + 0.044715 * z * z * z))
    value = 0.5 * z * (1.0 + t)
    slope = 0.5 * (1.0 + t) + 0.5 * z * (1.0 - t * t) * (k0 * (1.0 + 3.0 * 0.044715 * z * z))
    return value, slope


def ffn_kernel(
    b_ref, h1_ref, dy_ref, gp_ref, wg, wu, wd, out_ref, db_ref, dgp_ref, gg_o, gu_o, gd_o,
    ball, ballt, gate, up, mm, fsend, frecv, dfall, dsend, drecv, sg, su, sd, ssem, rsem, osem,
):
    b, q, y, c = place()
    g = q // 2
    t = lax.rem(q, 2) * 2 + y
    micro, tok, width = b_ref.shape
    hidden = wd.shape[0]
    peers = []
    for p in range(1, 4):
        tt = lax.rem(t + p, 4)
        peers.append((p, tt, at(b, g * 2 + tt // 2, lax.rem(tt, 2), c)))
    bar = greet([p[2] for p in peers])
    pl.semaphore_wait(bar, 3)
    sent = []
    nt = (((1,), (1,)), ((), ()))

    def spread(phase, m, src, dst_of, recv_of):
        waits = []
        for p, tt, target in peers:
            cp = remote(src(tt), dst_of(p, tt), ssem.at[phase, m, p - 1], rsem.at[phase, m, p - 1], target)
            cp.start()
            sent.append(cp)
            ts = lax.rem(t + 4 - p, 4)
            waits.append(remote(src(tt), recv_of(p, ts), ssem.at[phase, m, p - 1], rsem.at[phase, m, p - 1], target))
        return waits

    a_in, f_in, df_in, db_in = [], [], [], []
    for m in range(micro):
        a_in.append(
            spread(0, m, lambda tt, m=m: b_ref.at[m], lambda p, tt, m=m: ball.at[m, t], lambda p, ts, m=m: ball.at[m, ts])
        )
        ball[m, t] = b_ref[m]

    def forward(m):
        for cp in a_in[m]:
            cp.wait_recv()

        def body(n, _):
            cols = pl.ds(pl.multiple_of(n * 256, 256), 256)
            x = ball[m].reshape(4 * tok, width)
            gv = jnp.dot(x, wg[:, cols], preferred_element_type=F32)
            uv = jnp.dot(x, wu[:, cols], preferred_element_type=F32)
            gate[m, :, cols] = gv.astype(BF16)
            up[m, :, cols] = uv.astype(BF16)
            mm[m, :, cols] = (gelu_parts(gv)[0] * uv).astype(BF16)
            return 0

        lax.fori_loop(0, hidden // 256, body, 0)
        for o, w in tiles(width, 256):
            f = jnp.dot(mm[m], wd[:, o : o + w], preferred_element_type=F32)
            fsend[m, :, :, o : o + w] = f.astype(BF16).reshape(4, tok, w)
        f_in.append(
            spread(1, m, lambda tt: fsend.at[m, tt], lambda p, tt: frecv.at[m, p - 1], lambda p, ts: frecv.at[m, p - 1])
        )

    def middle(m):
        for cp in f_in[m]:
            cp.wait_recv()
        f = fsend[m, t].astype(F32)
        for p in range(3):
            f = f + frecv[m, p].astype(F32)
        gp = 1.0 + gp_ref[...]
        r = lax.rsqrt(jnp.mean(f * f, axis=-1, keepdims=True) + epsilon)
        n = f * r
        dy = dy_ref[m].astype(F32)
        out_ref[m] = (h1_ref[m] + n * gp).astype(BF16)
        dg = dy * gp
        df = r * (dg - n * jnp.mean(dg * n, axis=-1, keepdims=True))
        part = jnp.sum(dy * n, axis=0, keepdims=True)
        if m == 0:
            dgp_ref[...] = part
        else:
            dgp_ref[...] += part
        dfall[m, t] = df.astype(BF16)
        df_in.append(
            spread(2, m, lambda tt: dfall.at[m, t], lambda p, tt: dfall.at[m, t], lambda p, ts: dfall.at[m, ts])
        )

    def backward(m):
        for cp in df_in[m]:
            cp.wait_recv()

        def body(n, _):
            cols = pl.ds(pl.multiple_of(n * 256, 256), 256)
            x = dfall[m].reshape(4 * tok, width)
            dm = lax.dot_general(x, wd[cols, :], nt, preferred_element_type=F32)
            value, slope = gelu_parts(gate[m, :, cols].astype(F32))
            uv = up[m, :, cols].astype(F32)
            gate[m, :, cols] = (dm * uv * slope).astype(BF16)
            up[m, :, cols] = (dm * value).astype(BF16)
            return 0

        lax.fori_loop(0, hidden // 256, body, 0)
        for o, w in tiles(width, 256):
            d = lax.dot_general(gate[m], wg[o : o + w, :], nt, preferred_element_type=F32)
            d = d + lax.dot_general(up[m], wu[o : o + w, :], nt, preferred_element_type=F32)
            dsend[m, :, :, o : o + w] = d.astype(BF16).reshape(4, tok, w)
        db_in.append(
            spread(3, m, lambda tt: dsend.at[m, tt], lambda p, tt: drecv.at[m, p - 1], lambda p, ts: drecv.at[m, p - 1])
        )

    for m in range(micro):
        forward(m)
    for m in range(micro):
        for i in range(4):
            ballt[:, (m * 4 + i) * tok : (m * 4 + i + 1) * tok] = ball[m, i].T
    for m in range(micro):
        middle(m)
    for m in range(micro):
        backward(m)

    def grads(n, _):
        cols = pl.ds(pl.multiple_of(n * 256, 256), 256)
        slot = lax.rem(n, 2)

        def out(m, o):
            cc = pl.ds(pl.multiple_of(m * 256, 256), 256)
            return [
                pltpu.make_async_copy(sg.at[o], gg_o.at[:, cc], osem.at[0, o]),
                pltpu.make_async_copy(su.at[o], gu_o.at[:, cc], osem.at[1, o]),
                pltpu.make_async_copy(sd.at[o], gd_o.at[cc, :], osem.at[2, o]),
            ]

        @pl.when(n >= 2)
        def _():
            for cp in out(n, slot):
                cp.wait()

        x = ballt[...]
        sg[slot] = jnp.dot(x, gate[:, :, cols].reshape(-1, 256), preferred_element_type=F32).astype(BF16)
        su[slot] = jnp.dot(x, up[:, :, cols].reshape(-1, 256), preferred_element_type=F32).astype(BF16)
        sd[slot] = jnp.dot(
            mm[:, :, cols].reshape(-1, 256).T, dfall[...].reshape(-1, width), preferred_element_type=F32
        ).astype(BF16)
        for cp in out(n, slot):
            cp.start()
        return 0

    steps = hidden // 256
    lax.fori_loop(0, steps, grads, 0)
    for n in range(max(steps - 2, 0), steps):
        o = n % 2
        pltpu.make_async_copy(sg.at[o], gg_o.at[:, n * 256 : n * 256 + 256], osem.at[0, o]).wait()
        pltpu.make_async_copy(su.at[o], gu_o.at[:, n * 256 : n * 256 + 256], osem.at[1, o]).wait()
        pltpu.make_async_copy(sd.at[o], gd_o.at[n * 256 : n * 256 + 256, :], osem.at[2, o]).wait()
    for m in range(micro):
        for cp in db_in[m]:
            cp.wait_recv()
        d = dsend[m, t].astype(F32)
        for p in range(3):
            d = d + drecv[m, p].astype(F32)
        db_ref[m] = d
    for cp in sent:
        cp.wait_send()


def ffn(b, h1, dy, gp, wg, wu, wd):
    micro, tok, width = b.shape
    hidden = wd.shape[0]
    wide = (micro, 4 * tok, hidden)
    return pl.pallas_call(
        ffn_kernel,
        out_shape=[
            jax.ShapeDtypeStruct(b.shape, BF16),
            jax.ShapeDtypeStruct(b.shape, F32),
            jax.ShapeDtypeStruct((1, width), F32),
            jax.ShapeDtypeStruct(wg.shape, BF16),
            jax.ShapeDtypeStruct(wu.shape, BF16),
            jax.ShapeDtypeStruct(wd.shape, BF16),
        ],
        in_specs=[VMEM] * 7,
        out_specs=[VMEM] * 3 + [ANY] * 3,
        scratch_shapes=[
            pltpu.VMEM((micro, 4, tok, width), BF16),
            pltpu.VMEM((width, micro * 4 * tok), BF16),
            pltpu.VMEM(wide, BF16),
            pltpu.VMEM(wide, BF16),
            pltpu.VMEM(wide, BF16),
            pltpu.VMEM((micro, 4, tok, width), BF16),
            pltpu.VMEM((micro, 3, tok, width), BF16),
            pltpu.VMEM((micro, 4, tok, width), BF16),
            pltpu.VMEM((micro, 4, tok, width), BF16),
            pltpu.VMEM((micro, 3, tok, width), BF16),
            pltpu.VMEM((2, width, 256), BF16),
            pltpu.VMEM((2, width, 256), BF16),
            pltpu.VMEM((2, 256, width), BF16),
            pltpu.SemaphoreType.DMA((4, micro, 3)),
            pltpu.SemaphoreType.DMA((4, micro, 3)),
            pltpu.SemaphoreType.DMA((3, 2)),
        ],
        compiler_params=pltpu.CompilerParams(collective_id=4, has_side_effects=True, vmem_limit_bytes=62 * 2**20),
    )(b, h1, dy, gp, wg, wu, wd)


def halves(n):
    first = up16(n // 2)
    return [(0, first), (first, n - first)] if first < n else [(0, n)]


def norm_of(v):
    r = lax.rsqrt(jnp.mean(v * v, axis=-1, keepdims=True) + epsilon)
    return v * r, r


def norm_back(grad, n, r, scale):
    gs = grad * scale
    return r * (gs - n * jnp.mean(gs * n, axis=-1, keepdims=True)), jnp.sum(grad * n, axis=0, keepdims=True)


def spread_gains(block, width, n_dev):
    w = width // n_dev
    lane = lax.broadcasted_iota(jnp.int32, (128, width), 0)
    col = lax.broadcasted_iota(jnp.int32, (128, width), 1)
    pick = jnp.where(lax.rem(col, w) == lane, 1.0, 0.0).astype(BF16)
    wide = jnp.dot(block, pick, preferred_element_type=F32)
    row = lax.broadcasted_iota(jnp.int32, (n_dev * 16, width), 0) // 16
    mine = lax.broadcasted_iota(jnp.int32, (n_dev * 16, width), 1) // w
    return jnp.sum(jnp.where(row == mine, wide, 0.0).reshape(n_dev, 16, width), axis=0)


def collect_gains(rows, n_dev):
    width = rows.shape[1]
    w = width // n_dev
    row = lax.broadcasted_iota(jnp.int32, (n_dev, 8, width), 0)
    mine = lax.broadcasted_iota(jnp.int32, (n_dev, 8, width), 2) // w
    wide = jnp.where(row == mine, rows[None], 0.0).reshape(n_dev * 8, width)
    col = lax.broadcasted_iota(jnp.int32, (width, 128), 0)
    lane = lax.broadcasted_iota(jnp.int32, (width, 128), 1)
    pick = jnp.where(lax.rem(col, w) == lane, 1.0, 0.0)
    out = jnp.dot(wide, pick, preferred_element_type=F32, precision=lax.Precision.HIGHEST)
    return out.reshape(n_dev, 8, 128)


def pack_rows(kr, kp):
    row = lax.broadcasted_iota(jnp.int32, (4 * kr, 4 * kp), 0)
    col = lax.broadcasted_iota(jnp.int32, (4 * kr, 4 * kp), 1)
    return jnp.where(lax.div(row, kr) * kp + lax.rem(row, kr) == col, 1.0, 0.0).astype(BF16)


def kv_columns(which, qw):
    return 2 * which * qw + HD, (2 * which + 1) * qw + HD


def half_mask(n, tok):
    row = lax.rem(lax.broadcasted_iota(jnp.int32, (n, tok), 0), tok)
    return lax.broadcasted_iota(jnp.int32, (n, tok), 1) <= row


def segment_of(len_ref, m, index):
    end = jnp.int32(0)
    seg = jnp.zeros(index.shape, jnp.int32)
    for i in range(len_ref.shape[1]):
        end = end + len_ref[m, i]
        seg = seg + jnp.where(index >= end, 1, 0)
    return seg


def front_barrier(nz):
    b, q, y, c = place()
    k = lax.axis_index("blk")
    nb = 4 * nz
    g, e = q // 2, q % 2
    ng = nz // 2
    bar = greet(
        [at(b, lax.rem(q + r, nz), y, c) for r in range(1, nz)]
        + [at(1 - b, q, y, c), at(b, q, 1 - y, c), at(b, q, y, 1 - c), at(b, q, 1 - y, 1 - c)]
        + [at(b, g * 2 + 1 - e, 1 - y, c)]
        + [at(b, lax.rem(g + r, ng) * 2 + c, y, e) for r in range(1, ng)]
    )

    @pl.when(e != c)
    def _():
        pl.semaphore_signal(bar, inc=1, device_id=at(b, g * 2 + c, y, e), device_id_type=MESH)

    is_first, is_mid = k == 0, k == nb // 2

    @pl.when(is_first)
    def _():
        pl.semaphore_signal(bar, inc=1, device_id=(b, nb // 2), device_id_type=MESH)

    @pl.when(is_mid)
    def _():
        pl.semaphore_signal(bar, inc=1, device_id=(b, 0), device_id_type=MESH)

    pl.semaphore_wait(
        bar, nz + 3 + ng + 1 - jnp.where(e == c, 1, 0) + jnp.where(is_first, 1, 0) + jnp.where(is_mid, 1, 0)
    )


def front_kernel(
    nz, x_ref, cos_ref, sin_ref, len_ref, qkv_x, wo_u, gain_u, wg_x, wu_x, wd_x,
    ball, h1_o, attn_h, raw_h, q_h, o_h, ob_h, lse_h, kv_h, wqkv_h, wo_h, xq_h, xkv_h, xo_h, xlse_h, gd_o, gh_o, wg_f, wu_f, wd_f,
    attn_s, raw_s, q_s, o_s, ob_s, lse_s, kvall, kv_own, wqkv, wo, gain_f, qkv_u, wg, wu, wd, qkv_r, wg_r, wu_r, b_s,
    xq, xkv, xo_s, xlse_s, xob, xin, xss, xrs,
    lsem, ssem, rsem, wls, wss, wrs, kls, kss, krs, osem, qss, qrs, tss, trs,
):
    b, q, y, c = place()
    k = lax.axis_index("blk")
    nb = 4 * nz
    n_dev = 2 * nb
    g, e = q // 2, q % 2
    ng = nz // 2
    hz = nz // 2
    qw = qkv_u.shape[1]
    self_in = e == c
    front_barrier(nz)
    other_x, other_y, other_c = at(1 - b, q, y, c), at(b, q, 1 - y, c), at(b, q, y, 1 - c)
    everything, both = pl.ds(0, nz), pl.ds(0, 2)
    kr = qkv_u.shape[0] // 4
    sent = []

    def start(cp):
        cp.start()
        sent.append(cp)
        return cp

    quad = [(y, 1 - c), (1 - y, c), (1 - y, 1 - c)]
    trades = [(qkv_x, qkv_r, qkv_u), (wg_x, wg_r, wg), (wu_x, wu_r, wu)]
    t_in = [[] for _ in trades]

    def trade(i):
        src, dst, _ = trades[i]
        for p, (yy, cc) in enumerate(quad):
            t = at(b, q, yy, cc)
            start(remote(src.at[yy * 2 + cc], dst.at[y * 2 + c], qss.at[i, p], qrs.at[i, p], t))
            t_in[i].append(remote(src.at[yy * 2 + cc], dst.at[yy * 2 + cc], qss.at[i, p], qrs.at[i, p], t))
        t_in[i].append(pltpu.make_async_copy(src.at[y * 2 + c], dst.at[y * 2 + c], qrs.at[i, 3]))
        t_in[i][3].start()

    def traded(i):
        _, src, dst = trades[i]
        for p in range(3):
            t_in[i][p].wait_recv()
        t_in[i][3].wait()
        pick = pack_rows(kr, src.shape[1])
        for o, n in tiles(src.shape[2], 256):
            v = jnp.dot(pick, src[:, :, o : o + n].reshape(4 * src.shape[1], n), preferred_element_type=F32)
            dst[:, o : o + n] = v.astype(BF16)

    def view_q(ref, yy, cc, xx, qq):
        return ref.at[xx, qq, :, pl.ds(pl.multiple_of((yy * 2 + cc) * qw, 128), HD)]

    def view_kv(ref, yy, cc, xx, qq):
        return ref.at[xx, qq, :, pl.ds(pl.multiple_of((yy * 2 + cc) * qw + HD, 128), qw - HD)]

    def view_lead(ref, yy, cc, xx, qq):
        return ref.at[xx, qq, yy, cc]

    GAIN, KV, Q, WO = range(4)
    items = [
        (gain_u, gain_f, view_lead, True),
        (qkv_u.at[:, HD:], wqkv, view_kv, True),
        (qkv_u.at[:, :HD], wqkv, view_q, False),
        (wo_u, wo, view_lead, False),
    ]
    local = [None] * 4
    z_in, a_in, b_in, c_in = ([[] for _ in items] for _ in range(4))

    def hop(i, v, w, s, t):
        start(remote(v, v, ssem.at[i, s], rsem.at[i, s], t))
        return remote(v, w, ssem.at[i, s], rsem.at[i, s], t)

    def second(i):
        return (other_x, 1 - b, y) if items[i][3] else (other_y, b, 1 - y)

    def send_z(i):
        src, dst, view, _ = items[i]
        local[i] = pltpu.make_async_copy(src, view(dst, y, c, b, q), lsem.at[i])
        local[i].start()
        for r in range(1, nz):
            t = at(b, lax.rem(q + r, nz), y, c)
            start(remote(src, view(dst, y, c, b, q), ssem.at[i, r], rsem.at[i, r], t))
            z_in[i].append(
                remote(src, view(dst, y, c, b, lax.rem(q - r + nz, nz)), ssem.at[i, r], rsem.at[i, r], t)
            )
        t, xx, yy = second(i)
        start(remote(src, view(dst, y, c, b, q), ssem.at[i, nz], rsem.at[i, nz], t))
        a_in[i].append(remote(src, view(dst, yy, c, xx, q), ssem.at[i, nz], rsem.at[i, nz], t))

    def send_a(i):
        _, dst, view, _ = items[i]
        t, xx, yy = second(i)
        for r in range(1, nz):
            qs = lax.rem(q - r + nz, nz)
            z_in[i][r - 1].wait_recv()
            a_in[i].append(hop(i, view(dst, y, c, b, qs), view(dst, yy, c, xx, qs), nz + r, t))

    def send_b(i, half):
        _, dst, view, x_first = items[i]
        if half == 0:
            local[i].wait()
            xx, yy = b, y
        else:
            for cp in a_in[i]:
                cp.wait_recv()
            _, xx, yy = second(i)
        t, xi, yi = (other_y, xx, 1 - yy) if x_first else (other_x, 1 - xx, yy)
        b_in[i].append(
            (hop(i, view(dst, yy, c, xx, everything), view(dst, yi, c, xi, everything), 2 * nz + half, t), xi, yi)
        )
        to_core(i, xx, yy, 2 * nz + 2 + half)

    def to_core(i, xx, yy, s):
        _, dst, view, _ = items[i]
        c_in[i].append(hop(i, view(dst, yy, c, xx, everything), view(dst, yy, 1 - c, xx, everything), s, other_c))

    def send_c(i):
        for half, (cp, xx, yy) in enumerate(b_in[i]):
            cp.wait_recv()
            to_core(i, xx, yy, 2 * nz + 4 + half)

    def done(i):
        for cp in c_in[i]:
            cp.wait_recv()

    pieces = [
        (src, dst, o, n) for src, dst in ((wd, wd_f), (wg, wg_f), (wu, wu_f)) for o, n in halves(src.shape[0])
    ]
    w_in, w_x, w_c, w_out = ([[] for _ in pieces] for _ in range(4))

    def w_send(j):
        src, dst, o, n = pieces[j]
        sl = pl.ds(o, n)
        for r in range(ng):
            t = at(b, lax.rem(g + r, ng) * 2 + c, y, e)
            qs = lax.rem(g - r + ng, ng) * 2 + c
            cp = remote(src.at[sl], dst.at[b, q, sl], wss.at[j, r], wrs.at[j, r], t)
            inc = remote(src.at[sl], dst.at[b, qs, sl], wss.at[j, r], wrs.at[j, r], t)
            if r == 0:
                lc = pltpu.make_async_copy(src.at[sl], dst.at[b, q, sl], wls.at[j])

                @pl.when(self_in)
                def _():
                    lc.start()

                @pl.when(jnp.logical_not(self_in))
                def _():
                    cp.start()

                w_in[j].append((inc, qs, lc))
                w_out[j].append(cp)
            else:
                start(cp)
                w_in[j].append((inc, qs, None))

    def w_on(j, xx, qs, s, target, yx, yq):
        _, dst, o, n = pieces[j]
        sl = pl.ds(o, n)
        start(remote(dst.at[xx, qs, sl], dst.at[xx, qs, sl], wss.at[j, s], wrs.at[j, s], target))
        return remote(dst.at[xx, qs, sl], dst.at[yx, yq, sl], wss.at[j, s], wrs.at[j, s], target)

    def w_across(j):
        for r, (inc, qs, lc) in enumerate(w_in[j]):
            if lc is not None:

                @pl.when(self_in)
                def _():
                    lc.wait()

                @pl.when(jnp.logical_not(self_in))
                def _():
                    inc.wait_recv()
            else:
                inc.wait_recv()
            w_x[j].append(w_on(j, b, qs, ng + r, other_x, 1 - b, qs))
        for r, (_, qs, _) in enumerate(w_in[j]):
            w_c[j].append(w_on(j, b, qs, 2 * ng + r, other_c, b, lax.rem(g - r + ng, ng) * 2 + 1 - c))

    def w_core(j):
        for r, (_, qs, _) in enumerate(w_in[j]):
            w_x[j][r].wait_recv()
            w_c[j].append(w_on(j, 1 - b, qs, 3 * ng + r, other_c, 1 - b, lax.rem(g - r + ng, ng) * 2 + 1 - c))

    last = len(pieces)

    kept = []

    def keep(src, dst):
        cp = pltpu.make_async_copy(src, dst, osem.at[len(kept)])
        cp.start()
        kept.append(cp)

    trade(0)
    send_z(GAIN)
    dr = wd_x.shape[0]
    if wd.shape[0] == dr:
        wd[...] = wd_x[...]
    else:
        whole = dr // 16 * 16
        wd[:whole] = wd_x[:whole]
        rest = jnp.zeros((wd.shape[0] - dr, wd.shape[1]), BF16)
        wd[whole:] = jnp.concatenate([wd_x[whole:], rest], axis=0)
    w_send(0)
    traded(0)
    send_z(KV)
    send_z(Q)
    trade(1)
    micro, _, tok, _ = q_s.shape
    rows = micro * tok
    x = x_ref[...].astype(F32)
    n_x = norm_of(x)[0]
    send_a(GAIN)
    send_a(KV)
    send_b(GAIN, 0)
    send_b(KV, 0)
    traded(1)
    w_send(1)
    send_b(GAIN, 1)
    send_b(KV, 1)
    send_a(Q)
    send_b(Q, 0)
    trade(2)
    w_across(0)
    w_send(2)
    send_z(WO)
    send_c(GAIN)
    send_c(KV)
    done(GAIN)
    done(KV)
    width = x_ref.shape[1]
    gains_d = spread_gains(gain_f[...].reshape(n_dev * 16, 128), width, n_dev)
    gains_h = spread_gains(gain_f[...].reshape(n_dev * 16, 128), HD, n_dev)
    gd_o[...] = gains_d
    gh_o[...] = gains_h
    a = (n_x * (1.0 + gains_d[0:1])).astype(BF16)
    cosine, sine = cos_ref[...], sin_ref[...]
    half = HD // 2

    def project(h):
        if h < H:
            w = wqkv[:, :, :, h * qw : h * qw + HD]
        else:
            o1, o2 = kv_columns(h - H, qw)
            w = jnp.concatenate([wqkv[:, :, :, o1 : o1 + half], wqkv[:, :, :, o2 : o2 + half]], axis=3)
        raw = jnp.dot(a, w.reshape(width, HD), preferred_element_type=F32)
        if h == H + 1:
            kv_own[:, :, HD:] = raw.astype(BF16).reshape(micro, tok, HD)
            return
        raw_s[:, h * HD : (h + 1) * HD] = raw
        z = norm_of(raw)[0] * (1.0 + (gains_h[1:2] if h < H else gains_h[2:3]))
        z1, z2 = z[:, :half], z[:, half:]
        z = jnp.concatenate([z1 * cosine - z2 * sine, z2 * cosine + z1 * sine], axis=1).astype(BF16)
        if h < H:
            q_s[:, h] = z.reshape(micro, tok, HD)
        else:
            kv_own[:, :, :HD] = z.reshape(micro, tok, HD)

    project(H)
    project(H + 1)
    ht = tok // 2
    is_first, is_mid = k == 0, k == nb // 2
    first, mid = (b, 0), (b, nb // 2)
    x_kv = remote(kv_own.at[:, :ht], xkv, xss.at[0], xrs.at[0], first)
    x_q = remote(q_s.at[:, :, :ht], xq, xss.at[1], xrs.at[1], first)
    x_o = remote(xob, xin, xss.at[2], xrs.at[2], mid)

    @pl.when(is_mid)
    def _():
        x_kv.start()

    side = q // hz
    ql = q - side * hz

    def kview(qq, yy, cc):
        return kvall.at[qq - side * hz, yy, cc]

    mine = pltpu.make_async_copy(kv_own, kview(q, y, c), kls)
    mine.start()
    kz_in, ky_in, kc_in = [], [], []
    for r in range(1, hz):
        t = at(b, side * hz + lax.rem(ql + r, hz), y, c)
        start(remote(kv_own, kview(q, y, c), kss.at[r], krs.at[r], t))
        src = side * hz + lax.rem(ql - r + hz, hz)
        kz_in.append((remote(kv_own, kview(src, y, c), kss.at[r], krs.at[r], t), src))
    start(remote(kv_own, kview(q, y, c), kss.at[hz], krs.at[hz], other_y))
    ky_in.append((remote(kv_own, kview(q, 1 - y, c), kss.at[hz], krs.at[hz], other_y), q))
    slot = [2 * hz]

    def k_core(qq, yy):
        s = slot[0]
        slot[0] += 1
        start(remote(kview(qq, yy, c), kview(qq, yy, c), kss.at[s], krs.at[s], other_c))
        kc_in.append(remote(kview(qq, yy, c), kview(qq, yy, 1 - c), kss.at[s], krs.at[s], other_c))

    mine.wait()
    k_core(q, y)
    traded(2)
    send_b(Q, 1)
    w_across(1)
    w_send(3)
    w_core(0)
    send_a(WO)
    send_b(WO, 0)
    for r, (cp, src) in enumerate(kz_in):
        cp.wait_recv()
        s = hz + 1 + r
        start(remote(kview(src, y, c), kview(src, y, c), kss.at[s], krs.at[s], other_y))
        ky_in.append((remote(kview(src, y, c), kview(src, 1 - y, c), kss.at[s], krs.at[s], other_y), src))
        k_core(src, y)
    send_c(Q)
    w_across(2)
    w_send(4)
    w_core(1)
    done(Q)
    for h in range(H):
        project(h)

    @pl.when(is_mid)
    def _():
        x_q.start()

    keep(wqkv, wqkv_h)
    keep(raw_s, raw_h)
    keep(q_s, q_h)
    send_b(WO, 1)
    for cp, src in ky_in:
        cp.wait_recv()
        k_core(src, 1 - y)
    w_across(3)
    w_send(5)
    w_core(2)
    for cp in kc_in:
        cp.wait_recv()

    scale = HD ** (-0.5)
    lo = side * (nb // 4)
    hi = k // 2 + 1
    qrows = H * tok
    qidx = k * tok + lax.rem(lax.broadcasted_iota(jnp.int32, (qrows, 1), 0), tok)

    def online(carry, s, ok, values):
        mx, sm, acc = carry
        if ok is not None:
            s = jnp.where(ok, s, -1e30)
        new = jnp.maximum(mx, jnp.max(s, axis=-1, keepdims=True))
        p = jnp.exp(s - new)
        if ok is not None:
            p = jnp.where(ok, p, 0.0)
        alpha = jnp.exp(mx - new)
        sm = sm * alpha + jnp.sum(p, axis=-1, keepdims=True)
        return new, sm, acc * alpha + jnp.dot(p.astype(BF16), values, preferred_element_type=F32)

    def empty(n):
        return jnp.full((n, 1), -1e30, F32), jnp.zeros((n, 1), F32), jnp.zeros((n, HD), F32)

    @pl.when(is_first)
    def _():
        x_kv.wait_recv()
        x_q.wait_recv()
        for m in range(micro):
            qm = xq[m].reshape(H * ht, HD)

            def body(j, carry):
                blk = kvall[j // 2, j % 2, :, m].reshape(256, 2 * HD)
                s = lax.dot_general(qm, blk[:, :HD], (((1,), (1,)), ((), ())), preferred_element_type=F32) * scale
                return online(carry, s, None, blk[:, HD:])

            carry = lax.fori_loop(0, nb // 4, body, empty(H * ht))
            blk = xkv[m]
            s = lax.dot_general(qm, blk[:, :HD], (((1,), (1,)), ((), ())), preferred_element_type=F32) * scale
            mx, sm, acc = online(carry, s, half_mask(H * ht, ht), blk[:, HD:])
            xo_s[m] = acc / sm
            xlse_s[m] = mx + jnp.log(sm)
            xob[m] = xo_s[m].astype(BF16).reshape(H, ht, HD)
        x_o.start()

    team = e * 2 + y
    t_in_b = []
    for m in range(micro):
        qm = q_s[m].reshape(qrows, HD)
        segq = segment_of(len_ref, m, qidx)

        def body(j, carry):
            blk = kvall[j // 2 - side * hz, j % 2, :, m].reshape(256, 2 * HD)
            kidx = j * 256 + lax.broadcasted_iota(jnp.int32, (1, 256), 1)
            s, ok = chunk_scores(qm, blk[:, :HD], segq, segment_of(len_ref, m, kidx), qidx, j, scale)
            return online(carry, s, ok, blk[:, HD:])

        mx, sm, acc = lax.fori_loop(lo, hi, body, empty(qrows))
        o = acc / sm
        o_s[m] = o
        lse_s[m] = mx + jnp.log(sm)
        rs = slice(m * tok, (m + 1) * tok)
        for h in range(H):
            ob_s[rs, h * HD : (h + 1) * HD] = o[h * tok : (h + 1) * tok].astype(BF16)
        if m == 0:
            w_across(4)
            w_core(3)
            send_c(WO)
            done(WO)

            @pl.when(is_mid)
            def _():
                x_o.wait_recv()

        @pl.when(is_mid)
        def _():
            for h in range(H):
                ob_s[m * tok : m * tok + ht, h * HD : (h + 1) * HD] = xin[m, h]

        for o, n in tiles(width, 256):
            w = wo[:, :, :, :, :, o : o + n].reshape(H * HD, n)
            attn_s[rs, o : o + n] = jnp.dot(ob_s[rs], w, preferred_element_type=F32)
        h1 = x_ref[rs].astype(F32) + norm_of(attn_s[rs])[0] * (1.0 + gains_d[3:4])
        h1_o[m] = h1
        b_s[m] = (norm_of(h1)[0] * (1.0 + gains_d[4:5])).astype(BF16)
        for p in range(1, 4):
            tt, ts = lax.rem(team + p, 4), lax.rem(team + 4 - p, 4)
            t = at(b, g * 2 + tt // 2, lax.rem(tt, 2), c)
            start(remote(b_s.at[m], ball.at[m, team], tss.at[m, p - 1], trs.at[m, p - 1], t))
            t_in_b.append(remote(b_s.at[m], ball.at[m, ts], tss.at[m, p - 1], trs.at[m, p - 1], t))
        ball[m, team] = b_s[m]
    for src, dst in ((xq, xq_h), (xkv, xkv_h), (xo_s, xo_h), (xlse_s, xlse_h)):
        keep(src, dst)
    keep(o_s, o_h)
    keep(lse_s, lse_h)
    keep(ob_s, ob_h)
    keep(kvall, kv_h)
    keep(attn_s, attn_h)
    keep(wo, wo_h)
    w_core(4)
    w_across(5)
    w_core(5)
    for cp in t_in_b:
        cp.wait_recv()
    for j in range(last):
        for cp in w_c[j]:
            cp.wait_recv()
    for cp in sent:
        cp.wait_send()
    for j in range(last):

        @pl.when(jnp.logical_not(self_in))
        def _():
            w_out[j][0].wait_send()

    @pl.when(is_mid)
    def _():
        x_kv.wait_send()
        x_q.wait_send()

    @pl.when(is_first)
    def _():
        x_o.wait_send()

    for cp in kept:
        cp.wait()


def front(nz, x, cosine, sine, lengths, qkv, wo, gain, wg, wu, wd, kr, dp, micro):
    ng = nz // 2
    hz = nz // 2
    rows, width = x.shape
    tok = rows // micro
    nb = 4 * nz
    out = {
        "ball": ((micro, 4, tok, width), BF16),
        "h1": ((micro, tok, width), F32),
        "attn": ((rows, width), F32),
        "raw": ((rows, (H + 1) * HD), F32),
        "q": ((micro, H, tok, HD), BF16),
        "o": ((micro, H * tok, HD), F32),
        "ob": ((rows, H * HD), BF16),
        "lse": ((micro, H * tok, 1), F32),
        "kv": ((hz, 2, 2, micro, tok, 2 * HD), BF16),
        "wqkv": ((2, nz, 4 * kr, 4 * qkv.shape[2]), BF16),
        "wo": ((2, nz, 2, 2) + wo.shape, BF16),
        "xq": ((micro, H, tok // 2, HD), BF16),
        "xkv": ((micro, tok // 2, 2 * HD), BF16),
        "xo": ((micro, H * tok // 2, HD), F32),
        "xlse": ((micro, H * tok // 2, 1), F32),
        "gd": ((16, width), F32),
        "gh": ((16, HD), F32),
        "wg": ((2, nz, 4 * kr, wg.shape[2]), BF16),
        "wu": ((2, nz, 4 * kr, wg.shape[2]), BF16),
        "wd": ((2, nz, dp, width), BF16),
    }
    shapes = [jax.ShapeDtypeStruct(*v) for v in out.values()]
    scratch = [pltpu.VMEM(*out[n]) for n in ("attn", "raw", "q", "o", "ob", "lse", "kv")]
    ns = 2 * nz + 6
    n_pieces = 2 * len(halves(4 * kr)) + len(halves(dp))
    scratch += [pltpu.VMEM((micro, tok, 2 * HD), BF16), pltpu.VMEM(*out["wqkv"]), pltpu.VMEM(*out["wo"])]
    scratch += [pltpu.VMEM((2, nz, 2, 2) + gain.shape, BF16)]
    scratch += [pltpu.VMEM((4 * kr, z.shape[2]), BF16) for z in (qkv, wg, wu)] + [pltpu.VMEM((dp, width), BF16)]
    scratch += [pltpu.VMEM(z.shape, BF16) for z in (qkv, wg, wu)] + [pltpu.VMEM((micro, tok, width), BF16)]
    scratch += [pltpu.VMEM(*out[n]) for n in ("xq", "xkv", "xo", "xlse", "xq", "xq")]
    scratch += [pltpu.SemaphoreType.DMA((3,)), pltpu.SemaphoreType.DMA((3,))]
    scratch += [
        pltpu.SemaphoreType.DMA((4,)),
        pltpu.SemaphoreType.DMA((4, ns)),
        pltpu.SemaphoreType.DMA((4, ns)),
        pltpu.SemaphoreType.DMA((n_pieces,)),
        pltpu.SemaphoreType.DMA((n_pieces, 4 * ng)),
        pltpu.SemaphoreType.DMA((n_pieces, 4 * ng)),
        pltpu.SemaphoreType.DMA,
        pltpu.SemaphoreType.DMA((4 * hz,)),
        pltpu.SemaphoreType.DMA((4 * hz,)),
        pltpu.SemaphoreType.DMA((13,)),
        pltpu.SemaphoreType.DMA((3, 3)),
        pltpu.SemaphoreType.DMA((3, 4)),
        pltpu.SemaphoreType.DMA((micro, 3)),
        pltpu.SemaphoreType.DMA((micro, 3)),
    ]
    specs = [VMEM, VMEM] + [ANY] * 13 + [VMEM, VMEM] + [ANY] * 3
    got = pl.pallas_call(
        functools.partial(front_kernel, nz),
        out_shape=shapes,
        in_specs=[VMEM] * 3 + [pl.BlockSpec(memory_space=pltpu.SMEM)] + [ANY] * 5 + [VMEM],
        out_specs=specs,
        scratch_shapes=scratch,
        compiler_params=pltpu.CompilerParams(collective_id=5, has_side_effects=True, vmem_limit_bytes=60 * 2**20),
    )(x, cosine, sine, lengths, qkv, wo, gain, wg, wu, wd)
    return dict(zip(out, got))


def mlp_kernel(
    ball, h1_ref, dy_ref, gd_ref, wg, wu, wd, out_ref, db_ref, dgp_ref, gg_o, gu_o, gd_o,
    ballt, gate, up, mm, fsend, frecv, dfall, dsend, drecv, sg, su, sd, ssem, rsem, osem,
):
    b, q, y, c = place()
    g = q // 2
    t = lax.rem(q, 2) * 2 + y
    micro, tok, width = h1_ref.shape
    hidden = wd.shape[0]
    peers = []
    for p in range(1, 4):
        tt = lax.rem(t + p, 4)
        peers.append((p, tt, at(b, g * 2 + tt // 2, lax.rem(tt, 2), c)))
    bar = greet([p[2] for p in peers])
    pl.semaphore_wait(bar, 3)
    sent = []
    nt = (((1,), (1,)), ((), ()))

    def spread(phase, m, src, dst_of, recv_of):
        waits = []
        for p, tt, target in peers:
            cp = remote(src(tt), dst_of(p, tt), ssem.at[phase, m, p - 1], rsem.at[phase, m, p - 1], target)
            cp.start()
            sent.append(cp)
            ts = lax.rem(t + 4 - p, 4)
            waits.append(remote(src(tt), recv_of(p, ts), ssem.at[phase, m, p - 1], rsem.at[phase, m, p - 1], target))
        return waits

    f_in, df_in, db_in = [], [], []

    def forward(m):
        def body(n, _):
            cols = pl.ds(pl.multiple_of(n * 256, 256), 256)
            x = ball[m].reshape(4 * tok, width)
            gv = jnp.dot(x, wg[:, cols], preferred_element_type=F32)
            uv = jnp.dot(x, wu[:, cols], preferred_element_type=F32)
            gate[m, :, cols] = gv.astype(BF16)
            up[m, :, cols] = uv.astype(BF16)
            mm[m, :, cols] = (gelu_parts(gv)[0] * uv).astype(BF16)
            return 0

        lax.fori_loop(0, hidden // 256, body, 0)
        for o, w in tiles(width, 256):
            f = jnp.dot(mm[m], wd[:, o : o + w], preferred_element_type=F32)
            fsend[m, :, :, o : o + w] = f.astype(BF16).reshape(4, tok, w)
        f_in.append(
            spread(1, m, lambda tt: fsend.at[m, tt], lambda p, tt: frecv.at[m, p - 1], lambda p, ts: frecv.at[m, p - 1])
        )

    def middle(m):
        for cp in f_in[m]:
            cp.wait_recv()
        f = fsend[m, t].astype(F32)
        for p in range(3):
            f = f + frecv[m, p].astype(F32)
        gp = 1.0 + gd_ref[5:6]
        r = lax.rsqrt(jnp.mean(f * f, axis=-1, keepdims=True) + epsilon)
        n = f * r
        dy = dy_ref[m].astype(F32)
        out_ref[m] = (h1_ref[m] + n * gp).astype(BF16)
        dg = dy * gp
        df = r * (dg - n * jnp.mean(dg * n, axis=-1, keepdims=True))
        part = jnp.sum(dy * n, axis=0, keepdims=True)
        if m == 0:
            dgp_ref[...] = part
        else:
            dgp_ref[...] += part
        dfall[m, t] = df.astype(BF16)
        df_in.append(
            spread(2, m, lambda tt: dfall.at[m, t], lambda p, tt: dfall.at[m, t], lambda p, ts: dfall.at[m, ts])
        )

    def backward(m):
        for cp in df_in[m]:
            cp.wait_recv()

        def body(n, _):
            cols = pl.ds(pl.multiple_of(n * 256, 256), 256)
            x = dfall[m].reshape(4 * tok, width)
            dm = lax.dot_general(x, wd[cols, :], nt, preferred_element_type=F32)
            value, slope = gelu_parts(gate[m, :, cols].astype(F32))
            uv = up[m, :, cols].astype(F32)
            gate[m, :, cols] = (dm * uv * slope).astype(BF16)
            up[m, :, cols] = (dm * value).astype(BF16)
            return 0

        lax.fori_loop(0, hidden // 256, body, 0)
        for o, w in tiles(width, 256):
            d = lax.dot_general(gate[m], wg[o : o + w, :], nt, preferred_element_type=F32)
            d = d + lax.dot_general(up[m], wu[o : o + w, :], nt, preferred_element_type=F32)
            dsend[m, :, :, o : o + w] = d.astype(BF16).reshape(4, tok, w)
        db_in.append(
            spread(3, m, lambda tt: dsend.at[m, tt], lambda p, tt: drecv.at[m, p - 1], lambda p, ts: drecv.at[m, p - 1])
        )

    for m in range(micro):
        forward(m)
    for m in range(micro):
        for i in range(4):
            ballt[:, (m * 4 + i) * tok : (m * 4 + i + 1) * tok] = ball[m, i].T
    for m in range(micro):
        middle(m)
    for m in range(micro):
        backward(m)

    def grads(n, _):
        cols = pl.ds(pl.multiple_of(n * 256, 256), 256)
        slot = lax.rem(n, 2)

        def out(m, o):
            cc = pl.ds(pl.multiple_of(m * 256, 256), 256)
            return [
                pltpu.make_async_copy(sg.at[o], gg_o.at[:, cc], osem.at[0, o]),
                pltpu.make_async_copy(su.at[o], gu_o.at[:, cc], osem.at[1, o]),
                pltpu.make_async_copy(sd.at[o], gd_o.at[cc, :], osem.at[2, o]),
            ]

        @pl.when(n >= 2)
        def _():
            for cp in out(n, slot):
                cp.wait()

        x = ballt[...]
        sg[slot] = jnp.dot(x, gate[:, :, cols].reshape(-1, 256), preferred_element_type=F32).astype(BF16)
        su[slot] = jnp.dot(x, up[:, :, cols].reshape(-1, 256), preferred_element_type=F32).astype(BF16)
        sd[slot] = jnp.dot(
            mm[:, :, cols].reshape(-1, 256).T, dfall[...].reshape(-1, width), preferred_element_type=F32
        ).astype(BF16)
        for cp in out(n, slot):
            cp.start()
        return 0

    steps = hidden // 256
    lax.fori_loop(0, steps, grads, 0)
    for n in range(max(steps - 2, 0), steps):
        o = n % 2
        pltpu.make_async_copy(sg.at[o], gg_o.at[:, n * 256 : n * 256 + 256], osem.at[0, o]).wait()
        pltpu.make_async_copy(su.at[o], gu_o.at[:, n * 256 : n * 256 + 256], osem.at[1, o]).wait()
        pltpu.make_async_copy(sd.at[o], gd_o.at[n * 256 : n * 256 + 256, :], osem.at[2, o]).wait()
    for m in range(micro):
        for cp in db_in[m]:
            cp.wait_recv()
        d = dsend[m, t].astype(F32)
        for p in range(3):
            d = d + drecv[m, p].astype(F32)
        db_ref[m] = d
    for cp in sent:
        cp.wait_send()


def mlp(ball, h1, dy, gp, wg, wu, wd):
    micro, tok, width = h1.shape
    hidden = wd.shape[0]
    wide = (micro, 4 * tok, hidden)
    return pl.pallas_call(
        mlp_kernel,
        out_shape=[
            jax.ShapeDtypeStruct(h1.shape, BF16),
            jax.ShapeDtypeStruct(h1.shape, F32),
            jax.ShapeDtypeStruct((1, width), F32),
            jax.ShapeDtypeStruct(wg.shape, BF16),
            jax.ShapeDtypeStruct(wu.shape, BF16),
            jax.ShapeDtypeStruct(wd.shape, BF16),
        ],
        in_specs=[VMEM] * 7,
        out_specs=[VMEM] * 3 + [ANY] * 3,
        scratch_shapes=[
            pltpu.VMEM((width, micro * 4 * tok), BF16),
            pltpu.VMEM(wide, BF16),
            pltpu.VMEM(wide, BF16),
            pltpu.VMEM(wide, BF16),
            pltpu.VMEM((micro, 4, tok, width), BF16),
            pltpu.VMEM((micro, 3, tok, width), BF16),
            pltpu.VMEM((micro, 4, tok, width), BF16),
            pltpu.VMEM((micro, 4, tok, width), BF16),
            pltpu.VMEM((micro, 3, tok, width), BF16),
            pltpu.VMEM((2, width, 256), BF16),
            pltpu.VMEM((2, width, 256), BF16),
            pltpu.VMEM((2, 256, width), BF16),
            pltpu.SemaphoreType.DMA((4, micro, 3)),
            pltpu.SemaphoreType.DMA((4, micro, 3)),
            pltpu.SemaphoreType.DMA((3, 2)),
        ],
        compiler_params=pltpu.CompilerParams(collective_id=7, has_side_effects=True, vmem_limit_bytes=62 * 2**20),
    )(ball, h1, dy, gp, wg, wu, wd)


def back_kernel(
    nz, db_ref, h1_ref, dy_ref, x_ref, cos_ref, sin_ref, len_ref, gd_ref, gh_ref, dgp_ref,
    attn_h, raw_h, q_h, o_h, ob_h, lse_h, kv_h, wqkv_h, wo_h, xq_h, xkv_h, xo_h, xlse_h, gg, gu, gdn,
    dx_o, q_o, kv_o, wo_o, gain_o, wg_o, wu_o, wd_o,
    attn, raw, q_s, o_s, ob, lse, kvall, wqkv, wo, xq, xkv, xo, xlse,
    xdo, xdq, xdkv, xpart, qin, kvin, dkv_s, dh1, datt, do_s, delta, dqkv, da, gqkv, gwo, ggain,
    k1, k2, k3, *rest,
):
    hops = [rest[4 * i : 4 * i + 4] for i in range(4)]
    rest = rest[16:]
    wown, w1, w2, w3 = (rest[3 * i : 3 * i + 3] for i in range(4))
    qsum, kvsum, q_t, kv_t, wg_t, wu_t = rest[12:18]
    lsem, ssem, rsem, wls, wss, wrs, kss, krs, xss, xrs, qss, qrs = rest[18:]
    b, q, y, c = place()
    k = lax.axis_index("blk")
    nb = 4 * nz
    n_dev = 2 * nb
    g, e = q // 2, q % 2
    ng = nz // 2
    hz = nz // 2
    qw = gqkv.shape[3] // 4
    kr = gqkv.shape[2] // 4
    self_in = e == c
    other_x, other_y, other_c = at(1 - b, q, y, c), at(b, q, 1 - y, c), at(b, q, y, 1 - c)
    both, everything = pl.ds(0, 2), pl.ds(0, nz)
    micro, _, tok, _ = q_s.shape
    rows, width = x_ref.shape
    nt = (((1,), (1,)), ((), ()))
    tn = (((0,), (0,)), ((), ()))
    loads = []
    for i, (src, dst) in enumerate(
        ((attn_h, attn), (wo_h, wo), (o_h, o_s), (q_h, q_s), (kv_h, kvall), (lse_h, lse), (ob_h, ob), (raw_h, raw), (wqkv_h, wqkv),
         (xq_h, xq), (xkv_h, xkv), (xo_h, xo), (xlse_h, xlse))
    ):
        cp = pltpu.make_async_copy(src, dst, lsem.at[i])
        cp.start()
        loads.append(cp)
    front_barrier(nz)
    sent = []

    def start(cp):
        cp.start()
        sent.append(cp)
        return cp

    def add(dst, src, n, step):
        def one(i, _):
            sl = pl.ds(pl.multiple_of(i * step, step), step)
            dst[sl] = dst[sl] + src[sl]
            return 0

        lax.fori_loop(0, n // step, one, 0)

    quad = [(y, 1 - c), (1 - y, c), (1 - y, 1 - c)]
    t_in = []

    def trade(src, dst, s, cols):
        for p, (yy, cc) in enumerate(quad):
            there = remote(src.at[yy * 2 + cc, :, cols], dst.at[y * 2 + c, :, cols], qss.at[s, p], qrs.at[s, p], at(b, q, yy, cc))
            here = remote(src.at[yy * 2 + cc, :, cols], dst.at[yy * 2 + cc, :, cols], qss.at[s, p], qrs.at[s, p], at(b, q, yy, cc))
            start(there)
            t_in.append(here)
        dst[y * 2 + c, :, cols] = src[y * 2 + c, :, cols]

    def unpack_rows(total, kp):
        v = lax.dot_general(pack_rows(kr, kp), total, tn, preferred_element_type=F32)
        return v.astype(BF16).reshape(4, kp, total.shape[1])

    units = [(gg, wg_o, wg_t), (gu, wu_o, wu_t), (gdn, wd_o, None)]
    fs = gg.shape[4]
    near = fs // 256 * 128
    pieces = [(u, (0, gg.shape[3]), cols) for u in range(2) for cols in ((0, near), (near, fs - near))]
    pieces += [(2, r, (0, width)) for r in halves(gdn.shape[3])]
    w_local, w_in = [None] * len(pieces), [None] * len(pieces)

    def part_of(j):
        u, (ro, rn), (co, cn) = pieces[j]
        return u, pl.ds(ro, rn), pl.ds(co, cn), rn

    def w_core(j):
        u, sl, cl, _ = part_of(j)
        src = units[u][0]
        w_in[j] = start(remote(src.at[:, :, 1 - c, sl, cl], w1[u].at[:, :, sl, cl], wss.at[j, 0], wrs.at[j, 0], other_c))
        w_local[j] = pltpu.make_async_copy(src.at[:, :, c, sl, cl], wown[u].at[:, :, sl, cl], wls.at[j, 0])
        w_local[j].start()

    def w_x(j):
        u, sl, cl, n = part_of(j)
        w_local[j].wait()
        w_in[j].wait_recv()
        for r in range(ng):
            add(wown[u].at[1 - b, r, sl, cl], w1[u].at[1 - b, r, sl, cl], n, 16)
        w_in[j] = start(remote(wown[u].at[1 - b, :, sl, cl], w2[u].at[:, sl, cl], wss.at[j, 1], wrs.at[j, 1], other_x))
        for r in range(ng):
            add(wown[u].at[b, r, sl, cl], w1[u].at[b, r, sl, cl], n, 16)

    def w_z(j):
        u, sl, cl, n = part_of(j)
        w_in[j].wait_recv()
        for r in range(ng):
            add(wown[u].at[b, r, sl, cl], w2[u].at[r, sl, cl], n, 16)
        waits = []
        for r in range(ng):
            gs = lax.rem(g + r, ng)
            src, dst = wown[u].at[b, gs, sl, cl], w3[u].at[r, sl, cl]
            cp = remote(src, dst, wss.at[j, 2 + r], wrs.at[j, 2 + r], at(b, gs * 2 + c, y, e))
            lc = None
            if r == 0:
                lc = pltpu.make_async_copy(src, dst, wls.at[j, 1])

                @pl.when(self_in)
                def _():
                    lc.start()

                @pl.when(jnp.logical_not(self_in))
                def _():
                    cp.start()
            else:
                start(cp)
            waits.append((cp, lc))
        w_in[j] = waits

    def w_end(j):
        u, (ro, rn), (co, cn) = pieces[j]
        for cp, lc in w_in[j]:
            if lc is not None:

                @pl.when(self_in)
                def _():
                    lc.wait()

                @pl.when(jnp.logical_not(self_in))
                def _():
                    cp.wait()
            else:
                cp.wait_recv()
        _, out, send = units[u]
        if send is None:

            def one(i, _):
                sl = pl.ds(pl.multiple_of(ro + i * 16, 16), 16)
                total = w3[u][0, sl].astype(F32)
                for r in range(1, ng):
                    total = total + w3[u][r, sl].astype(F32)
                out[sl] = total
                return 0

            lax.fori_loop(0, rn // 16, one, 0)
        else:

            def one(i, _):
                cols = pl.ds(pl.multiple_of(co + i * 128, 128), 128)
                total = w3[u][0, :, cols].astype(F32)
                for r in range(1, ng):
                    total = total + w3[u][r, :, cols].astype(F32)
                send[:, :, cols] = unpack_rows(total.astype(BF16), send.shape[1])
                return 0

            lax.fori_loop(0, cn // 128, one, 0)
            trade(send, out, j, pl.ds(co, cn))

    for j in range(len(pieces)):
        w_core(j)

    def view_q(ref, yy, cc):
        return ref.at[:, :, :, pl.ds(pl.multiple_of((yy * 2 + cc) * qw, 128), HD)]

    def view_kv(ref, yy, cc):
        return ref.at[:, :, :, pl.ds(pl.multiple_of((yy * 2 + cc) * qw + HD, 128), qw - HD)]

    def view_lead(ref, yy, cc):
        return ref.at[:, :, yy, cc]

    items = [
        (gqkv, view_q, hops[0], qsum),
        (gwo, view_lead, hops[1], wo_o),
        (ggain, view_lead, hops[2], gain_o),
        (gqkv, view_kv, hops[3], kvsum),
    ]
    item_in = [[] for _ in items]

    def join(dst, src, lead):
        for idx in lead:
            dst[idx] = dst[idx] + src[idx]

    def grid2(v):
        return [(xx, qq) for xx in range(2) for qq in range(nz)]

    def item_core(i):
        src, view, (r1, _, _, _), _ = items[i]
        for yy in range(2):
            item_in[i].append(start(remote(view(src, yy, 1 - c), r1.at[yy], ssem.at[i, yy], rsem.at[i, yy], other_c)))

    def loop2(fn):
        def one(n, _):
            fn(lax.div(n, nz), lax.rem(n, nz))
            return 0

        lax.fori_loop(0, 2 * nz, one, 0)

    def item_y(i):
        src, view, (r1, r2, _, _), _ = items[i]
        for cp in item_in[i]:
            cp.wait_recv()
        for yy in (1 - y, y):
            v = view(src, yy, c)

            def fn(xx, qq):
                v[xx, qq] = v[xx, qq] + r1[yy, xx, qq]

            loop2(fn)
            if yy is not y:
                item_in[i] = [start(remote(v, r2, ssem.at[i, 2], rsem.at[i, 2], other_y))]

    def item_x(i):
        src, view, (_, r2, r3, _), _ = items[i]
        item_in[i][0].wait_recv()
        v = view(src, y, c)

        def fn(xx, qq):
            v[xx, qq] = v[xx, qq] + r2[xx, qq]

        loop2(fn)
        item_in[i] = [start(remote(v.at[1 - b], r3, ssem.at[i, 3], rsem.at[i, 3], other_x))]

    def item_z(i):
        src, view, (_, _, r3, r4), _ = items[i]
        item_in[i][0].wait_recv()
        v = view(src, y, c)
        for qq in range(nz):
            v[b, qq] = v[b, qq] + r3[qq]
        waits = []
        for r in range(1, nz):
            qt = lax.rem(q + r, nz)
            waits.append(start(remote(v.at[b, qt], r4.at[r - 1], ssem.at[i, 3 + r], rsem.at[i, 3 + r], at(b, qt, y, c))))
        item_in[i] = waits

    def item_end(i):
        src, view, (_, _, _, r4), out = items[i]
        for cp in item_in[i]:
            cp.wait_recv()
        v = view(src, y, c)
        total = v[b, q].astype(F32)
        for r in range(1, nz):
            total = total + r4[r - 1].astype(F32)
        if i in (0, 3):
            send, dst = (q_t, q_o) if i == 0 else (kv_t, kv_o)
            send[...] = unpack_rows(total.astype(BF16), send.shape[1])
            trade(send, dst, len(pieces) + i // 3, pl.ds(0, send.shape[2]))
        else:
            out[...] = total

    gains = gd_ref[...]
    loads[0].wait()
    dy = dy_ref[...].astype(F32)
    n1, r1 = norm_of(h1_ref[...].reshape(rows, width))
    d, dg_pf = norm_back(db_ref[...].reshape(rows, width), n1, r1, 1.0 + gains[4:5])
    dh1[...] = dy + d
    n2, r2 = norm_of(attn[...])
    d, dg_pa = norm_back(dh1[...], n2, r2, 1.0 + gains[3:4])
    datt[...] = d.astype(BF16)
    w_x(0)
    loads[1].wait()
    loads[2].wait()
    for h in range(H):
        w = wo[...].reshape(H * HD, width)[h * HD : (h + 1) * HD]
        d = lax.dot_general(datt[...], w, nt, preferred_element_type=F32).astype(BF16)
        do_s[:, h] = d.reshape(micro, tok, HD)
        for m in range(micro):
            hs = slice(h * tok, (h + 1) * tok)
            delta[m, hs] = jnp.sum(d[m * tok : (m + 1) * tok].astype(F32) * o_s[m, hs], axis=-1, keepdims=True)
    ht = tok // 2
    is_first, is_mid = k == 0, k == nb // 2
    first, mid = (b, 0), (b, nb // 2)
    x_do = remote(do_s.at[:, :, :ht], xdo, xss.at[0], xrs.at[0], first)
    x_dq = remote(xdq, qin, xss.at[1], xrs.at[1], mid)
    x_dkv = remote(xdkv, kvin, xss.at[2], xrs.at[2], mid)

    @pl.when(is_mid)
    def _():
        x_do.start()

    w_x(1)
    for i in (3, 4, 5, 9, 10, 11, 12):
        loads[i].wait()

    @pl.when(is_mid)
    def _():
        x_do.wait_send()
        do_s[:, :, :ht] = jnp.zeros((micro, H, ht, HD), BF16)
        for m in range(micro):
            for h in range(H):
                delta[m, h * tok : h * tok + ht] = jnp.zeros((ht, 1), F32)


    side = q // hz
    ql = q - side * hz
    scale = HD ** (-0.5)
    lo = side * (nb // 4)
    hi = k // 2 + 1
    part = kvall

    def clear(j, _):
        part[j // 2 - side * hz, j % 2] = jnp.zeros(part.shape[2:], BF16)
        return 0

    @pl.when(jnp.logical_not(is_first))
    def _():
        lax.fori_loop(hi, (side + 1) * 2 * hz, clear, 0)

    def grads_of(qm, dom, blk, p, dl):
        dp = lax.dot_general(dom, blk[:, HD:], nt, preferred_element_type=F32)
        ds = (p * (dp - dl)).astype(BF16)
        dq = jnp.dot(ds, blk[:, :HD], preferred_element_type=F32) * scale
        dk = lax.dot_general(ds, qm, tn, preferred_element_type=F32) * scale
        dv = lax.dot_general(p.astype(BF16), dom, tn, preferred_element_type=F32)
        return dq, jnp.concatenate([dk, dv], axis=1)

    @pl.when(is_first)
    def _():
        x_do.wait_recv()
        for m in range(micro):
            qm, dom = xq[m].reshape(H * ht, HD), xdo[m].reshape(H * ht, HD)
            dl = jnp.sum(dom.astype(F32) * xo[m], axis=-1, keepdims=True)

            def one(blk, ok):
                s = lax.dot_general(qm, blk[:, :HD], nt, preferred_element_type=F32) * scale
                p = jnp.exp(s - xlse[m]) if ok is None else jnp.where(ok, jnp.exp(jnp.where(ok, s, -1e30) - xlse[m]), 0.0)
                return grads_of(qm, dom, blk, p, dl)

            dq, g0 = one(kvall[0, 0, :, m].reshape(256, 2 * HD), None)
            xpart[m] = g0.astype(BF16)

            def body(j, dq):
                d, g = one(kvall[j // 2, j % 2, :, m].reshape(256, 2 * HD), None)
                part[j // 2, j % 2, :, m] = g.astype(BF16).reshape(2, tok, 2 * HD)
                return dq + d

            dq = lax.fori_loop(1, nb // 4, body, dq)
            d, g = one(xkv[m], half_mask(H * ht, ht))
            xdq[m] = (dq + d).astype(BF16).reshape(H, ht, HD)
            xdkv[m] = g.astype(BF16)
        x_dq.start()
        x_dkv.start()

    qrows = H * tok
    qidx = k * tok + lax.rem(lax.broadcasted_iota(jnp.int32, (qrows, 1), 0), tok)
    dq_s = o_s
    for m in range(micro):
        dq_s[m] = jnp.zeros(dq_s.shape[1:], F32)
        segq = segment_of(len_ref, m, qidx)

        def body(j, _):
            qm, dom = q_s[m].reshape(qrows, HD), do_s[m].reshape(qrows, HD)
            blk = kvall[j // 2 - side * hz, j % 2, :, m].reshape(256, 2 * HD)
            kidx = j * 256 + lax.broadcasted_iota(jnp.int32, (1, 256), 1)
            s, ok = chunk_scores(qm, blk[:, :HD], segq, segment_of(len_ref, m, kidx), qidx, j, scale)
            p = jnp.where(ok, jnp.exp(jnp.where(ok, s, -1e30) - lse[m]), 0.0)
            dq, g = grads_of(qm, dom, blk, p, delta[m])
            dq_s[m] += dq
            part[j // 2 - side * hz, j % 2, :, m] = g.astype(BF16).reshape(2, tok, 2 * HD)
            return 0

        lax.fori_loop(lo, hi, body, 0)

        @pl.when(is_first)
        def _():
            g = part[0, 0, :, m].reshape(256, 2 * HD).astype(F32) + xpart[m].astype(F32)
            part[0, 0, :, m] = g.astype(BF16).reshape(2, tok, 2 * HD)

        w_z(m)
        w_x(m + 2)

    k_in = start(remote(part.at[:, :, 1 - c], k1, kss.at[0], krs.at[0], other_c))
    loads[6].wait()
    obt = [ob[:, h * HD : (h + 1) * HD].T for h in range(H)]
    per = gwo.shape[0] * gwo.shape[1] * 4 // H
    for h in range(H):
        for o, n in tiles(width, 384):
            v = jnp.dot(obt[h], datt[:, o : o + n], preferred_element_type=F32).astype(BF16)
            n_lead = (2 * nz) // H
            xx, qq = (h * n_lead) // nz, (h * n_lead) % nz
            gwo[xx, qq : qq + n_lead, :, :, :, o : o + n] = v.reshape(n_lead, 2, 2, gwo.shape[4], n)
    item_core(1)
    k_in.wait_recv()

    def add1(n, _):
        part[n // 2, n % 2, c] = part[n // 2, n % 2, c] + k1[n // 2, n % 2]
        return 0

    lax.fori_loop(0, 2 * hz, add1, 0)
    k_in = start(remote(part.at[:, 1 - y, c], k2, kss.at[1], krs.at[1], other_y))
    loads[7].wait()
    cosine, sine = cos_ref[...], sin_ref[...]
    half = HD // 2
    gh = gh_ref[...]

    def unrotate(z):
        z1, z2 = z[:, :half], z[:, half:]
        return jnp.concatenate([z1 * cosine + z2 * sine, z2 * cosine - z1 * sine], axis=1)

    @pl.when(is_mid)
    def _():
        x_dq.wait_recv()
        for h in range(H):
            dq_s[:, h * tok : h * tok + ht] = qin[:, h].astype(F32)

    dg_q = jnp.zeros((1, HD), F32)
    for h in range(H):
        z = unrotate(dq_s[:, h * tok : (h + 1) * tok].reshape(rows, HD))
        n3, r3 = norm_of(raw[:, h * HD : (h + 1) * HD])
        d, dg = norm_back(z, n3, r3, 1.0 + gh[1:2])
        dqkv[:, h * qw : h * qw + HD] = d.astype(BF16)
        dg_q = dg_q + dg
    w_z(2)
    w_x(4)
    k_in.wait_recv()

    def add2(n, _):
        part[n, y, c] = part[n, y, c] + k2[n]
        return 0

    lax.fori_loop(0, hz, add2, 0)
    k_last = []
    for r in range(1, hz):
        qt = lax.rem(ql + r, hz)
        t = at(b, side * hz + qt, y, c)
        k_last.append(start(remote(part.at[qt, y, c], k3.at[r - 1], kss.at[1 + r], krs.at[1 + r], t)))
    item_y(1)
    n_x, r_x = norm_of(x_ref[...].astype(F32))
    at_ = (n_x * (1.0 + gains[0:1])).astype(BF16).T

    def weight_grad(o, n):
        v = jnp.dot(at_, dqkv[:, o : o + n], preferred_element_type=F32).astype(BF16)
        gqkv[:, :, :, o : o + n] = v.reshape(gqkv.shape[:3] + (n,))

    for h in range(H):
        weight_grad(h * qw, HD)
    item_core(0)
    w_z(3)
    w_x(5)
    w_end(0)
    total = part[ql, y, c].astype(F32)
    for r, cp in enumerate(k_last):
        cp.wait_recv()
        total = total + k3[r].astype(F32)

    dkv_s[...] = total

    @pl.when(is_mid)
    def _():
        x_dkv.wait_recv()
        dkv_s[:, :ht] += kvin[...].astype(F32)

    total = dkv_s[...].reshape(rows, 2 * HD)
    n3, r3 = norm_of(raw[:, H * HD :])
    d, dg_k = norm_back(unrotate(total[:, :HD]), n3, r3, 1.0 + gh[2:3])
    for i, z in enumerate((d, total[:, HD:])):
        for o, v in zip(kv_columns(i, qw), (z[:, :half], z[:, half:])):
            dqkv[:, o : o + half] = v.astype(BF16)
            weight_grad(o, half)
    item_core(3)
    loads[8].wait()
    quads_at_once = max(1, 256 // wqkv.shape[2])
    for xx in range(2):
        for qq in range(0, nz, quads_at_once):
            n = min(quads_at_once, nz - qq)
            w = wqkv[xx, qq : qq + n].reshape(n * wqkv.shape[2], wqkv.shape[3])
            o = (xx * nz + qq) * wqkv.shape[2]
            da[o : o + n * wqkv.shape[2], :] = lax.dot_general(w, dqkv[...], nt, preferred_element_type=F32)
    d, dg_in = norm_back(da[...].T, n_x, r_x, 1.0 + gains[0:1])
    dx_o[...] = (dh1[...] + d).astype(BF16).reshape(dx_o.shape)
    none = jnp.zeros((1, width), F32)
    nohd = jnp.zeros((1, HD), F32)
    wide = jnp.concatenate([dg_in, none, none, dg_pa, dg_pf, dgp_ref[...], none, none], axis=0)
    slim = jnp.concatenate([nohd, dg_q, dg_k] + [nohd] * 5, axis=0)
    ggain[...] = (collect_gains(wide, n_dev) + collect_gains(slim, n_dev)).reshape(ggain.shape)
    item_core(2)
    item_x(1)
    item_y(0)
    item_y(3)
    item_y(2)
    w_end(1)
    w_z(4)
    item_z(1)
    w_end(2)
    w_z(5)
    item_x(0)
    item_x(3)
    item_x(2)
    w_end(3)
    item_z(0)
    item_z(3)
    item_z(2)
    item_end(1)
    w_end(4)
    w_end(5)
    item_end(0)
    item_end(3)
    item_end(2)
    for cp in t_in:
        cp.wait_recv()
    for cp in sent:
        cp.wait_send()

    @pl.when(is_first)
    def _():
        x_dq.wait_send()
        x_dkv.wait_send()


def back(nz, db, h1, dy, x, cosine, sine, lengths, dgp, f, gg, gu, gd, kp):
    ng = nz // 2
    hz = nz // 2
    nb = 4 * nz
    micro, tok, width = db.shape
    rows = micro * tok
    qr = f["wqkv"].shape[2]
    qw = f["wqkv"].shape[3] // 4
    orow = f["wo"].shape[4]
    kv = f["kv"].shape

    def like(n):
        return pltpu.VMEM(f[n].shape, f[n].dtype)

    gsplit = [z.reshape(2, ng, 2, -1, z.shape[-1]) for z in (gg, gu, gd)]
    ublock = [gsplit[i].shape[3:] for i in (2, 0, 1)]
    iblock = [((qr, HD), BF16), ((orow, width), BF16), ((8, 128), F32), ((qr, qw - HD), BF16)]
    scratch = [like(n) for n in ("attn", "raw", "q", "o", "ob", "lse", "kv", "wqkv", "wo", "xq", "xkv", "xo", "xlse")]
    scratch += [like("xq"), like("xq"), like("xkv"), pltpu.VMEM((micro, 256, 2 * HD), BF16), like("xq"), like("xkv")]
    scratch += [pltpu.VMEM(kv[3:], F32)]
    scratch += [
        pltpu.VMEM((rows, width), F32),
        pltpu.VMEM((rows, width), BF16),
        pltpu.VMEM((micro, H, tok, HD), BF16),
        pltpu.VMEM((micro, H * tok, 1), F32),
        pltpu.VMEM((rows, (H + 2) * HD), BF16),
        pltpu.VMEM((width, rows), F32),
        pltpu.VMEM((2, nz, qr, 4 * qw), BF16),
        pltpu.VMEM((2, nz, 2, 2, orow, width), BF16),
        pltpu.VMEM((2, nz, 2, 2, 8, 128), F32),
        pltpu.VMEM((hz, 2) + kv[3:], BF16),
        pltpu.VMEM((hz,) + kv[3:], BF16),
        pltpu.VMEM((hz - 1,) + kv[3:], BF16),
    ]
    for s, t in iblock:
        scratch += [pltpu.VMEM(lead + s, t) for lead in ((2, 2, nz), (2, nz), (nz,), (nz - 1,))]
    for lead in ((2, ng), (2, ng), (ng,), (ng,)):
        scratch += [pltpu.VMEM(lead + ublock[i], BF16) for i in (1, 2, 0)]
    fs = ublock[1][1]
    scratch += [pltpu.VMEM((8, 128), BF16)] * 2
    scratch += [pltpu.VMEM((4, kp, n), BF16) for n in (HD, qw - HD, fs, fs)]
    n_pieces = 4 + len(halves(ublock[0][0]))
    scratch += [
        pltpu.SemaphoreType.DMA((13,)),
        pltpu.SemaphoreType.DMA((4, nz + 3)),
        pltpu.SemaphoreType.DMA((4, nz + 3)),
        pltpu.SemaphoreType.DMA((n_pieces, 2)),
        pltpu.SemaphoreType.DMA((n_pieces, 2 + ng)),
        pltpu.SemaphoreType.DMA((n_pieces, 2 + ng)),
        pltpu.SemaphoreType.DMA((hz + 1,)),
        pltpu.SemaphoreType.DMA((hz + 1,)),
        pltpu.SemaphoreType.DMA((3,)),
        pltpu.SemaphoreType.DMA((3,)),
        pltpu.SemaphoreType.DMA((n_pieces + 2, 3)),
        pltpu.SemaphoreType.DMA((n_pieces + 2, 3)),
    ]
    out = [
        jax.ShapeDtypeStruct((micro, tok, width), BF16),
        jax.ShapeDtypeStruct((4, kp, HD), BF16),
        jax.ShapeDtypeStruct((4, kp, qw - HD), BF16),
        jax.ShapeDtypeStruct((orow, width), F32),
        jax.ShapeDtypeStruct((8, 128), F32),
        jax.ShapeDtypeStruct((4, kp, fs), BF16),
        jax.ShapeDtypeStruct((4, kp, fs), BF16),
        jax.ShapeDtypeStruct(ublock[0], F32),
    ]
    return pl.pallas_call(
        functools.partial(back_kernel, nz),
        out_shape=out,
        in_specs=[VMEM] * 6 + [pl.BlockSpec(memory_space=pltpu.SMEM)] + [VMEM] * 3 + [ANY] * 16,
        out_specs=[VMEM] * 8,
        scratch_shapes=scratch,
        compiler_params=pltpu.CompilerParams(collective_id=6, has_side_effects=True, vmem_limit_bytes=63 * 2**20),
    )(
        db, h1, dy, x, cosine, sine, lengths, f["gd"], f["gh"], dgp,
        f["attn"], f["raw"], f["q"], f["o"], f["ob"], f["lse"], f["kv"], f["wqkv"], f["wo"],
        f["xq"], f["xkv"], f["xo"], f["xlse"], *gsplit,
    )


def scaled_norm(values, gain):
    return values * lax.rsqrt(jnp.mean(values * values, axis=-1, keepdims=True) + epsilon) * (1.0 + gain)


def segments(lengths, index):
    docs = lengths.shape[1]
    ends = [sum(lengths[:, j] for j in range(i + 1)) for i in range(docs)]
    seg = jnp.zeros((lengths.shape[0], index.shape[0]), jnp.int32)
    first = jnp.zeros_like(seg)
    for i in range(docs):
        past = index[None, :] >= ends[i][:, None]
        seg = seg + past.astype(jnp.int32)
        first = first + jnp.where(past, lengths[:, i][:, None], 0)
    return seg, index[None, :] - first


def rotate(values, cosine, sine):
    half = values.shape[-1] // 2
    a, b = values[..., :half], values[..., half:]
    return jnp.concatenate([a * cosine - b * sine, b * cosine + a * sine], axis=-1)


def middle(attn_value, x_value, gain_attn, gain_pre):
    hidden = x_value + scaled_norm(attn_value, gain_attn)
    return (hidden, scaled_norm(hidden, gain_pre))


def layer_apart(tokens, cotangent, doc_lengths, w_query, w_key, w_value, w_out, w_gate, w_up, w_down, *gains):
    nb = lax.axis_size("blk")
    nz = nb // 4
    me = lax.axis_index("blk")
    _, micro, tok, width = tokens.shape
    n_dev = 2 * nb
    nq = 2 * nz
    kr = w_gate.shape[0]
    qr, qp = 4 * kr, up16(4 * kr)
    dr = w_down.shape[0]
    dp = up16(dr)
    orow = w_out.shape[0]
    op = up16(orow)
    groups = [[4 * i + j for j in range(4)] for i in range(nz)]

    def fit(x, rows):
        return x if x.shape[0] == rows else jnp.pad(x, ((0, rows - x.shape[0]), (0, 0)))

    def slices(w):
        w = jnp.pad(w.reshape(kr, nq, 4, dr), ((0, 0), (0, 0), (0, 0), (0, dp - dr)))
        return w.transpose(2, 0, 1, 3).reshape(4, kr, nq * dp)

    fs = nq * dp
    w_qkv = jnp.concatenate([w_query, w_key, w_value], axis=1)
    qw = w_qkv.shape[1] // 4
    pack = jnp.concatenate([slices(w_gate), slices(w_up), w_qkv.reshape(kr, 4, qw).transpose(1, 0, 2)], axis=2)
    pack = lax.all_to_all(pack, "blk", split_axis=0, concat_axis=0, axis_index_groups=groups, tiled=True)
    pack = fit(pack.reshape(qr, 2 * fs + qw), qp)
    wide = [gain.shape[0] for gain in gains]
    flat = jnp.concatenate(gains)
    flat = jnp.pad(flat, (0, 16 * 128 - flat.shape[0])).reshape(16, 128)

    qkv_f, wo_f, gain_f, wg_f, wu_f, wd_f = gather_all(
        nz, pack[:, 2 * fs :], fit(w_out, op), flat, pack[:, :fs], pack[:, fs : 2 * fs], fit(w_down, dp)
    )
    wqkv = qkv_f[:, :, :qr].reshape(width, 4 * qw)
    wo = wo_f[:, :, :, :, :orow].reshape(n_dev * orow, width)
    wg = wg_f[:, :, :qr].reshape(width, fs)
    wu = wu_f[:, :, :qr].reshape(width, fs)
    wd = wd_f.reshape(fs, width)
    gain_rows = gain_f.reshape(n_dev, 16 * 128)
    full_gains, o = [], 0
    for w in wide:
        full_gains.append(gain_rows[:, o : o + w].reshape(n_dev * w).astype(F32))
        o += w
    gain_in, gain_query, gain_key, gain_attn, gain_pre, gain_post = full_gains

    lengths = doc_lengths[0]
    seg_all, pos_all = segments(lengths, jnp.arange(nb * tok, dtype=jnp.int32))
    seg_me, pos = segments(lengths, me * tok + jnp.arange(tok, dtype=jnp.int32))
    segq = jnp.tile(seg_me, (1, H))[:, :, None]
    segk = seg_all.reshape(micro, nb * tok // 256, 1, 256)
    freq = 1000000.0 ** (-(jnp.arange(HD // 2, dtype=F32) * 2.0 / HD))
    angle = pos.reshape(micro * tok).astype(F32)[:, None] * freq[None, :]
    cosine, sine = jnp.cos(angle), jnp.sin(angle)

    rows = micro * tok
    x = tokens[0].reshape(rows, width).astype(F32)
    dy = cotangent[0].reshape(rows, width)
    normed, pre_pull = jax.vjp(scaled_norm, x, gain_in)
    a = normed.astype(BF16)
    qkv = jnp.dot(a, wqkv, preferred_element_type=F32)
    n_q = H * HD
    q_raw = qkv[:, :n_q].reshape(rows, H, HD)
    k_raw = qkv[:, n_q : n_q + HD]
    v = qkv[:, n_q + HD :].astype(BF16)
    queries, query_pull = jax.vjp(
        lambda r, g: rotate(scaled_norm(r, g), cosine[:, None], sine[:, None]), q_raw, gain_query
    )
    keys, key_pull = jax.vjp(lambda r, g: rotate(scaled_norm(r, g), cosine, sine), k_raw, gain_key)

    def by_head(z):
        return z.reshape(micro, tok, H, HD).transpose(0, 2, 1, 3).reshape(micro, H * tok, HD)

    def by_row(z):
        return z.reshape(micro, H, tok, HD).transpose(0, 2, 1, 3).reshape(rows, H * HD)

    qh = by_head(queries.astype(BF16))
    kv = jnp.concatenate([keys.astype(BF16), v], axis=1).reshape(micro, tok, 2 * HD)
    oh, lse, kvall = attn_fwd(nb, qh, kv, segq, segk)
    o_b = by_row(oh.astype(BF16))
    attn = jnp.dot(o_b, wo, preferred_element_type=F32)
    (h1, ffn_in), mid_pull = jax.vjp(middle, attn, x, gain_attn, gain_pre)

    shape = (micro, tok, width)
    out, db, dg_post, gg, gu, gd = ffn(
        ffn_in.astype(BF16).reshape(shape), h1.reshape(shape), dy.reshape(shape), gain_post[None, :], wg, wu, wd
    )
    d_attn, d_x_mid, dg_attn, dg_pre = mid_pull((dy.astype(F32), db.reshape(rows, width)))
    d_attn = d_attn.astype(BF16)
    grad_out = lax.dot_general(o_b, d_attn, (((0,), (0,)), ((), ())), preferred_element_type=F32).astype(BF16)
    do = lax.dot_general(d_attn, wo, (((1,), (1,)), ((), ())), preferred_element_type=F32).astype(BF16)
    doh = by_head(do)
    delta = jnp.sum(doh.astype(F32) * oh, axis=-1, keepdims=True)
    dqh, dkv = attn_bwd(nb, qh, kvall, doh, lse, delta, segq, segk)
    dkv = dkv.reshape(rows, 2 * HD)
    dq_raw, dg_query = query_pull(by_row(dqh).reshape(rows, H, HD))
    dk_raw, dg_key = key_pull(dkv[:, :HD])
    d_qkv = jnp.concatenate([dq_raw.reshape(rows, n_q), dk_raw, dkv[:, HD:]], axis=1).astype(BF16)
    grad_qkv = lax.dot_general(a, d_qkv, (((0,), (0,)), ((), ())), preferred_element_type=F32).astype(BF16)
    da = lax.dot_general(d_qkv, wqkv, (((1,), (1,)), ((), ())), preferred_element_type=F32)
    d_x_pre, dg_in = pre_pull(da)
    d_x = (d_x_mid + d_x_pre).astype(BF16)

    def quads(z, r, p):
        z = z.reshape(2, nz, r, z.shape[-1])
        return z if r == p else jnp.pad(z, ((0, 0), (0, 0), (0, p - r), (0, 0)))

    go = grad_out.reshape(2, nz, 2, 2, orow, width)
    if op != orow:
        go = jnp.pad(go, ((0, 0),) * 4 + ((0, op - orow), (0, 0)))
    dgains = jnp.concatenate(
        [d.reshape(n_dev, w) for d, w in zip((dg_in, dg_query, dg_key, dg_attn, dg_pre, dg_post[0]), wide)], axis=1
    )
    used = dgains.shape[1]
    dgains = jnp.pad(dgains, ((0, 0), (0, 8 * 128 - used))).reshape(2, nz, 2, 2, 8, 128)
    s_qkv, s_wo, s_gain, s_wg, s_wu, s_wd = reduce_all(
        nz, quads(grad_qkv, qr, qp), go, dgains, quads(gg, qr, qp), quads(gu, qr, qp), gd.reshape(2, nz, dp, width)
    )
    back = jnp.concatenate([s_wg, s_wu, s_qkv], axis=1)[:qr].reshape(4, kr, 2 * fs + qw)
    back = lax.all_to_all(back, "blk", split_axis=0, concat_axis=0, axis_index_groups=groups, tiled=True)
    back = back.astype(F32)

    def rows_of(z):
        z = z.reshape(4, kr, nq, dp)[..., :dr]
        return z.transpose(1, 2, 0, 3).reshape(kr, nq * 4 * dr)

    s_qkv = back[:, :, 2 * fs :].transpose(1, 0, 2).reshape(kr, 4 * qw)
    flat = s_gain.reshape(-1)
    gain_grads, o = [], 0
    for w in wide:
        gain_grads.append(flat[o : o + w])
        o += w
    return (
        out[None],
        d_x.reshape(shape)[None],
        s_qkv[:, :n_q],
        s_qkv[:, n_q : n_q + HD],
        s_qkv[:, n_q + HD :],
        s_wo[:orow],
        rows_of(back[:, :, :fs]),
        rows_of(back[:, :, fs : 2 * fs]),
        s_wd[:dr],
        *gain_grads,
    )


def layer_fused(tokens, cotangent, doc_lengths, w_query, w_key, w_value, w_out, w_gate, w_up, w_down, *gains):
    nb = lax.axis_size("blk")
    nz = nb // 4
    me = lax.axis_index("blk")
    _, micro, tok, width = tokens.shape
    rows = micro * tok
    nq = 2 * nz
    kr, dr = w_gate.shape[0], w_down.shape[0]
    kp, dp = up16(kr), up16(dr)
    fs = nq * dp
    shape = (micro, tok, width)

    def slices(w):
        w = jnp.pad(w.reshape(kr, nq, 4, dr), ((0, kp - kr), (0, 0), (0, 0), (0, dp - dr)))
        return w.transpose(2, 0, 1, 3).reshape(4, kp, fs)

    w_kv = jnp.concatenate([w_key, w_value], axis=1)
    w_qkv = jnp.concatenate([w_query.reshape(kr, 4, -1), w_kv.reshape(kr, 4, -1)], axis=2)
    w_qkv = jnp.pad(w_qkv, ((0, kp - kr), (0, 0), (0, 0))).transpose(1, 0, 2)
    flat = jnp.stack([jnp.pad(gain, (0, 128 - gain.shape[0])) for gain in gains] + [jnp.zeros((128,), BF16)] * 10)
    lengths = doc_lengths[0]
    _, pos = segments(lengths, me * tok + jnp.arange(tok, dtype=jnp.int32))
    freq = 1000000.0 ** (-(jnp.arange(HD // 2, dtype=F32) * 2.0 / HD))
    angle = pos.reshape(rows).astype(F32)[:, None] * freq[None, :]
    cosine, sine = jnp.cos(angle), jnp.sin(angle)
    x = tokens[0].reshape(rows, width)
    dy = cotangent[0]
    f = front(nz, x, cosine, sine, lengths, w_qkv, w_out, flat, slices(w_gate), slices(w_up), w_down, kr, dp, micro)
    wg, wu, wd = (f[n].reshape(-1, f[n].shape[-1]) for n in ("wg", "wu", "wd"))
    out, db, dg_post, gg, gu, gd = mlp(f["ball"], f["h1"], dy, f["gd"], wg, wu, wd)
    d_x, s_q, s_kv, s_wo, s_gain, s_wg, s_wu, s_wd = back(
        nz, db, f["h1"], dy.reshape(rows, width), x, cosine, sine, lengths, dg_post, f, gg, gu, gd, kp
    )

    def rows_of(z):
        z = z[:, :kr].reshape(4, kr, nq, dp)[..., :dr].astype(F32)
        return z.transpose(1, 2, 0, 3).reshape(kr, nq * 4 * dr)

    def columns(z):
        return z[:, :kr].astype(F32).transpose(1, 0, 2).reshape(kr, -1)

    s_kv = columns(s_kv)
    return (
        out[None],
        d_x[None],
        columns(s_q),
        s_kv[:, :HD],
        s_kv[:, HD:],
        s_wo,
        rows_of(s_wg),
        rows_of(s_wu),
        s_wd[:dr],
        *(s_gain[i, : gain.shape[0]] for i, gain in enumerate(gains)),
    )


def shards(tokens, cotangent, doc_lengths, *params):
    nb = lax.axis_size("blk")
    w_out, w_gate = params[3], params[4]
    fits = nb * tokens.shape[2] <= 2048 and (4 * w_gate.shape[0]) % 16 == 0 and w_out.shape[0] % 16 == 0
    layer = layer_fused if fits else layer_apart
    return layer(tokens, cotangent, doc_lengths, *params)


def solution(mesh):
    sequence = P("bucket", None, "blk", None)
    split = ("bucket", "blk")
    return jax.shard_map(
        shards,
        mesh=mesh,
        in_specs=(sequence, sequence, P("bucket", None, None)) + (P(split, None),) * 7 + (P(split),) * 6,
        out_specs=(sequence, sequence) + (P(split, None),) * 7 + (P(split),) * 6,
        check_vma=False,
    )
```

```python
import functools
import math

import jax
import jax.numpy as jnp
from jax import lax
from jax.experimental import pallas as pl
from jax.experimental.pallas import tpu as pltpu
from jax.sharding import PartitionSpec as P

H = 4
HD = 256
F32 = jnp.float32
BF16 = jnp.bfloat16
MESH = pl.DeviceIdType.MESH
ANY = pl.BlockSpec(memory_space=pl.ANY)
VMEM = pl.BlockSpec(memory_space=pltpu.VMEM)
epsilon = 1e-06


def up16(n):
    return -(-n // 16) * 16


def place():
    b = lax.axis_index("bucket")
    k = lax.axis_index("blk")
    return b, k // 4, (k // 2) % 2, k % 2


def at(b, q, y, c):
    return (b, q * 4 + y * 2 + c)


def greet(targets):
    bar = pltpu.get_barrier_semaphore()
    for t in targets:
        pl.semaphore_signal(bar, inc=1, device_id=t, device_id_type=MESH)
    return bar


def remote(src, dst, send, recv, target):
    return pltpu.make_async_remote_copy(src, dst, send, recv, device_id=target, device_id_type=MESH)


def gather_kernel(nz, qkv, wo, gain, wg, wu, wd, qkv_f, wo_f, gain_f, wg_f, wu_f, wd_f, lsem, ssem, rsem, wls, wss, wrs):
    b, q, y, c = place()
    g, e = q // 2, q % 2
    ng = nz // 2
    qw = qkv.shape[1]
    self_in = e == c
    bar = greet(
        [at(b, lax.rem(q + r, nz), y, c) for r in range(1, nz)]
        + [at(1 - b, q, y, c), at(b, q, 1 - y, c), at(b, q, y, 1 - c)]
        + [at(b, lax.rem(g + r, ng) * 2 + c, y, e) for r in range(1, ng)]
    )
    first = at(b, g * 2 + c, y, e)

    @pl.when(jnp.logical_not(self_in))
    def _():
        pl.semaphore_signal(bar, inc=1, device_id=first, device_id_type=MESH)

    pl.semaphore_wait(bar, nz + 1 + ng - jnp.where(self_in, 1, 0) + 1)

    everything = pl.ds(0, nz)

    def view_qkv(ref, yy, cc, xx, qq):
        return ref.at[xx, qq, :, pl.ds(pl.multiple_of((yy * 2 + cc) * qw, 128), qw)]

    def view_lead(ref, yy, cc, xx, qq):
        return ref.at[xx, qq, yy, cc]

    items = [(qkv, qkv_f, view_qkv), (wo, wo_f, view_lead), (gain, gain_f, view_lead)]
    sent = []
    local = []
    for i, (src, dst, view) in enumerate(items):
        cp = pltpu.make_async_copy(src, view(dst, y, c, b, q), lsem.at[i])
        cp.start()
        local.append(cp)
    z_in = []
    for i, (src, dst, view) in enumerate(items):
        row = []
        for r in range(1, nz):
            cp = remote(src, view(dst, y, c, b, q), ssem.at[i, r], rsem.at[i, r], at(b, lax.rem(q + r, nz), y, c))
            cp.start()
            sent.append(cp)
            row.append(
                remote(src, view(dst, y, c, b, lax.rem(q - r + nz, nz)), ssem.at[i, r], rsem.at[i, r], at(b, lax.rem(q + r, nz), y, c))
            )
        z_in.append(row)
    x_in = [[] for _ in items]
    for i, (src, dst, view) in enumerate(items):
        cp = remote(src, view(dst, y, c, b, q), ssem.at[i, nz], rsem.at[i, nz], at(1 - b, q, y, c))
        cp.start()
        sent.append(cp)
        x_in[i].append(remote(src, view(dst, y, c, 1 - b, q), ssem.at[i, nz], rsem.at[i, nz], at(1 - b, q, y, c)))

    units = [(wg, wg_f), (wu, wu_f), (wd, wd_f)]
    u_in = []
    for j, (src, dst) in enumerate(units):
        row = []
        for r in range(ng):
            target = at(b, lax.rem(g + r, ng) * 2 + c, y, e)
            cp = remote(src, dst.at[b, q], wss.at[j, r], wrs.at[j, r], target)
            qs = lax.rem(g - r + ng, ng) * 2 + c
            inc = remote(src, dst.at[b, qs], wss.at[j, r], wrs.at[j, r], target)
            if r == 0:
                lc = pltpu.make_async_copy(src, dst.at[b, q], wls.at[j])

                @pl.when(self_in)
                def _():
                    lc.start()

                @pl.when(jnp.logical_not(self_in))
                def _():
                    cp.start()
            else:
                cp.start()
            row.append((cp, inc, qs, lc if r == 0 else None))
        u_in.append(row)

    for r in range(1, nz):
        qs = lax.rem(q - r + nz, nz)
        for i, (src, dst, view) in enumerate(items):
            z_in[i][r - 1].wait_recv()
            cp = remote(view(dst, y, c, b, qs), view(dst, y, c, b, qs), ssem.at[i, nz + r], rsem.at[i, nz + r], at(1 - b, q, y, c))
            cp.start()
            sent.append(cp)
            x_in[i].append(
                remote(view(dst, y, c, b, qs), view(dst, y, c, 1 - b, qs), ssem.at[i, nz + r], rsem.at[i, nz + r], at(1 - b, q, y, c))
            )
    for cp in local:
        cp.wait()
    y_in = [[] for _ in items]
    for half in range(2):
        for i, (src, dst, view) in enumerate(items):
            xx = b if half == 0 else 1 - b
            if half == 1:
                for cp in x_in[i]:
                    cp.wait_recv()
            s = 2 * nz + half
            cp = remote(view(dst, y, c, xx, everything), view(dst, y, c, xx, everything), ssem.at[i, s], rsem.at[i, s], at(b, q, 1 - y, c))
            cp.start()
            sent.append(cp)
            y_in[i].append(
                remote(view(dst, y, c, xx, everything), view(dst, 1 - y, c, xx, everything), ssem.at[i, s], rsem.at[i, s], at(b, q, 1 - y, c))
            )
    c_in = []

    def to_core(i, yy, s):
        _, dst, view = items[i]
        both = pl.ds(0, 2)
        cp = remote(view(dst, yy, c, both, everything), view(dst, yy, c, both, everything), ssem.at[i, s], rsem.at[i, s], at(b, q, y, 1 - c))
        cp.start()
        sent.append(cp)
        c_in.append(
            remote(view(dst, yy, c, both, everything), view(dst, yy, 1 - c, both, everything), ssem.at[i, s], rsem.at[i, s], at(b, q, y, 1 - c))
        )

    for i in range(len(items)):
        to_core(i, y, 2 * nz + 2)
    for i in range(len(items)):
        for cp in y_in[i]:
            cp.wait_recv()
        to_core(i, 1 - y, 2 * nz + 3)

    d_in = []

    def unit_on(j, xx, qs, s, target, yours):
        _, dst = units[j]
        cp = remote(dst.at[xx, qs], dst.at[xx, qs], wss.at[j, s], wrs.at[j, s], target)
        cp.start()
        sent.append(cp)
        return remote(dst.at[xx, qs], dst.at[yours[0], yours[1]], wss.at[j, s], wrs.at[j, s], target)

    xw = [[] for _ in units]

    def x_round(j):
        for r in range(ng):
            cp, inc, qs, lc = u_in[j][r]
            if r == 0:

                @pl.when(self_in)
                def _():
                    lc.wait()

                @pl.when(jnp.logical_not(self_in))
                def _():
                    inc.wait_recv()
            else:
                inc.wait_recv()
            xw[j].append(unit_on(j, b, qs, ng + r, at(1 - b, q, y, c), (1 - b, qs)))
        for r in range(ng):
            qs = u_in[j][r][2]
            qo = lax.rem(g - r + ng, ng) * 2 + 1 - c
            d_in.append(unit_on(j, b, qs, 2 * ng + r, at(b, q, y, 1 - c), (b, qo)))

    def c_round(j):
        for r in range(ng):
            qs = u_in[j][r][2]
            qo = lax.rem(g - r + ng, ng) * 2 + 1 - c
            xw[j][r].wait_recv()
            d_in.append(unit_on(j, 1 - b, qs, 3 * ng + r, at(b, q, y, 1 - c), (1 - b, qo)))

    x_round(0)
    x_round(1)
    c_round(0)
    x_round(2)
    c_round(1)
    c_round(2)
    for cp in c_in + d_in:
        cp.wait_recv()
    for cp in sent:
        cp.wait_send()
    for j in range(len(units)):
        for r in range(ng):
            cp = u_in[j][r][0]
            if r == 0:

                @pl.when(jnp.logical_not(self_in))
                def _():
                    cp.wait_send()
            else:
                cp.wait_send()


def gather_all(nz, qkv, wo, gain, wg, wu, wd):
    ng = nz // 2
    out = [
        jax.ShapeDtypeStruct((2, nz, qkv.shape[0], 4 * qkv.shape[1]), BF16),
        jax.ShapeDtypeStruct((2, nz, 2, 2) + wo.shape, BF16),
        jax.ShapeDtypeStruct((2, nz, 2, 2) + gain.shape, BF16),
        jax.ShapeDtypeStruct((2, nz) + wg.shape, BF16),
        jax.ShapeDtypeStruct((2, nz) + wu.shape, BF16),
        jax.ShapeDtypeStruct((2, nz) + wd.shape, BF16),
    ]
    ns = 2 * nz + 4
    return pl.pallas_call(
        functools.partial(gather_kernel, nz),
        out_shape=out,
        in_specs=[ANY] * 6,
        out_specs=[ANY] * 6,
        scratch_shapes=[
            pltpu.SemaphoreType.DMA((3,)),
            pltpu.SemaphoreType.DMA((3, ns)),
            pltpu.SemaphoreType.DMA((3, ns)),
            pltpu.SemaphoreType.DMA((3,)),
            pltpu.SemaphoreType.DMA((3, 4 * ng)),
            pltpu.SemaphoreType.DMA((3, 4 * ng)),
        ],
        compiler_params=pltpu.CompilerParams(collective_id=0, has_side_effects=True),
    )(qkv, wo, gain, wg, wu, wd)


def reduce_kernel(nz, qkv, wo, gain, wg, wu, wd, qkv_o, wo_o, gain_o, wg_o, wu_o, wd_o, *scratch):
    b, q, y, c = place()
    g, e = q // 2, q % 2
    ng = nz // 2
    qw = qkv_o.shape[1]
    self_in = e == c
    n_items, n_units = 3, 3
    own = scratch[0:3]
    r1 = scratch[3:6]
    r2 = scratch[6:9]
    r3 = scratch[9:12]
    r4 = scratch[12:15]
    uown = scratch[15:18]
    u1 = scratch[18:21]
    u2 = scratch[21:24]
    u3 = scratch[24:27]
    lsem, ssem, rsem, wls, wss, wrs = scratch[27:]
    bar = greet(
        [at(b, lax.rem(q + r, nz), y, c) for r in range(1, nz)]
        + [at(1 - b, q, y, c), at(b, q, 1 - y, c), at(b, q, y, 1 - c)]
        + [at(b, lax.rem(g + r, ng) * 2 + c, y, e) for r in range(1, ng)]
    )
    first = at(b, g * 2 + c, y, e)

    @pl.when(jnp.logical_not(self_in))
    def _():
        pl.semaphore_signal(bar, inc=1, device_id=first, device_id_type=MESH)

    pl.semaphore_wait(bar, nz + 1 + ng - jnp.where(self_in, 1, 0) + 1)

    other_core = at(b, q, y, 1 - c)
    other_y = at(b, q, 1 - y, c)
    other_x = at(1 - b, q, y, c)
    full = (pl.ds(0, 2), pl.ds(0, nz))

    def view_qkv(ref, yy, cc):
        return ref.at[full[0], full[1], :, pl.ds(pl.multiple_of((yy * 2 + cc) * qw, 128), qw)]

    def view_lead(ref, yy, cc):
        return ref.at[full[0], full[1], yy, cc]

    items = [(qkv, qkv_o, view_qkv), (wo, wo_o, view_lead), (gain, gain_o, view_lead)]
    units = [(wd, wd_o), (wg, wg_o), (wu, wu_o)]
    sent = []
    item_local, item_in = [[] for _ in items], [[] for _ in items]
    unit_local, unit_in = [[] for _ in units], [[] for _ in units]

    def start(cp):
        cp.start()
        sent.append(cp)
        return cp

    def item_core(i):
        src, _, view = items[i]
        for yy in range(2):
            item_in[i].append(start(remote(view(src, yy, 1 - c), r1[i].at[yy], ssem.at[i, yy], rsem.at[i, yy], other_core)))
            cp = pltpu.make_async_copy(view(src, yy, c), own[i].at[yy], lsem.at[i, yy])
            cp.start()
            item_local[i].append(cp)

    def unit_core(j):
        src, _ = units[j]
        for xx in range(2):
            for r in range(ng):
                s = xx * ng + r
                mine, yours = r * 2 + c, r * 2 + 1 - c
                unit_in[j].append(start(remote(src.at[xx, yours], u1[j].at[xx, r], wss.at[j, s], wrs.at[j, s], other_core)))
                cp = pltpu.make_async_copy(src.at[xx, mine], uown[j].at[xx, r], wls.at[j, s])
                cp.start()
                unit_local[j].append(cp)

    def add(dst, src, lead):
        def one(n, _):
            dst[n] = (dst[n].astype(F32) + src[n].astype(F32)).astype(dst.dtype)
            return 0

        lax.fori_loop(0, lead, one, 0)

    def unit_x(j):
        for cp in unit_local[j]:
            cp.wait()
        for cp in unit_in[j]:
            cp.wait_recv()
        add(uown[j].at[1 - b], u1[j].at[1 - b], ng)
        cp = start(remote(uown[j].at[1 - b], u2[j], wss.at[j, 2 * ng], wrs.at[j, 2 * ng], other_x))
        add(uown[j].at[b], u1[j].at[b], ng)
        unit_in[j] = [cp]

    def unit_z(j):
        unit_in[j][0].wait_recv()
        add(uown[j].at[b], u2[j], ng)
        waits = []
        for r in range(ng):
            gs = lax.rem(g + r, ng)
            cp = remote(uown[j].at[b, gs], u3[j].at[r], wss.at[j, 2 * ng + 1 + r], wrs.at[j, 2 * ng + 1 + r], at(b, gs * 2 + c, y, e))
            if r == 0:
                lc = pltpu.make_async_copy(uown[j].at[b, gs], u3[j].at[0], wls.at[j, 2 * ng])

                @pl.when(self_in)
                def _():
                    lc.start()

                @pl.when(jnp.logical_not(self_in))
                def _():
                    cp.start()

                waits.append((cp, lc))
            else:
                start(cp)
                waits.append((cp, None))
        unit_in[j] = waits

    def unit_end(j):
        for cp, lc in unit_in[j]:
            if lc is not None:

                @pl.when(self_in)
                def _():
                    lc.wait()

                @pl.when(jnp.logical_not(self_in))
                def _():
                    cp.wait()
            else:
                cp.wait_recv()
        rows = u3[j].shape[1]
        step = 16

        def one(n, _):
            sl = pl.ds(pl.multiple_of(n * step, step), step)
            total = u3[j][0, sl].astype(F32)
            for r in range(1, ng):
                total = total + u3[j][r, sl].astype(F32)
            units[j][1][sl] = total.astype(units[j][1].dtype)
            return 0

        lax.fori_loop(0, rows // step, one, 0)

    def item_y(i):
        for cp in item_local[i]:
            cp.wait()
        for cp in item_in[i]:
            cp.wait_recv()
        for xx in range(2):
            add(own[i].at[1 - y, xx], r1[i].at[1 - y, xx], nz)
        cp = start(remote(own[i].at[1 - y], r2[i], ssem.at[i, 2], rsem.at[i, 2], other_y))
        for xx in range(2):
            add(own[i].at[y, xx], r1[i].at[y, xx], nz)
        item_in[i] = [cp]

    def item_x(i):
        item_in[i][0].wait_recv()
        add(own[i].at[y, 1 - b], r2[i].at[1 - b], nz)
        cp = start(remote(own[i].at[y, 1 - b], r3[i], ssem.at[i, 3], rsem.at[i, 3], other_x))
        add(own[i].at[y, b], r2[i].at[b], nz)
        item_in[i] = [cp]

    def item_z(i):
        item_in[i][0].wait_recv()
        add(own[i].at[y, b], r3[i], nz)
        waits = []
        for r in range(1, nz):
            qt = lax.rem(q + r, nz)
            waits.append(start(remote(own[i].at[y, b, qt], r4[i].at[r - 1], ssem.at[i, 3 + r], rsem.at[i, 3 + r], at(b, qt, y, c))))
        item_in[i] = waits

    def item_end(i):
        for cp in item_in[i]:
            cp.wait_recv()
        total = own[i][y, b, q].astype(F32)
        for r in range(1, nz):
            total = total + r4[i][r - 1].astype(F32)
        items[i][1][...] = total.astype(items[i][1].dtype)

    for j in range(n_units):
        unit_core(j)
    for i in range(n_items):
        item_core(i)
    for j in range(n_units):
        unit_x(j)
    for i in range(n_items):
        item_y(i)
    unit_z(0)
    for i in range(n_items):
        item_x(i)
    unit_z(1)
    for i in range(n_items):
        item_z(i)
    unit_z(2)
    for i in range(n_items):
        item_end(i)
    for j in range(n_units):
        unit_end(j)
    for cp in sent:
        cp.wait_send()


def reduce_all(nz, qkv, wo, gain, wg, wu, wd):
    ng = nz // 2
    qw = qkv.shape[3] // 4
    blocks = [((qkv.shape[2], qw), BF16), (wo.shape[4:], BF16), (gain.shape[4:], F32)]
    ublocks = [(wd.shape[2:], BF16), (wg.shape[2:], BF16), (wu.shape[2:], BF16)]
    scratch = (
        [pltpu.VMEM((2, 2, nz) + s, t) for s, t in blocks]
        + [pltpu.VMEM((2, 2, nz) + s, t) for s, t in blocks]
        + [pltpu.VMEM((2, nz) + s, t) for s, t in blocks]
        + [pltpu.VMEM((nz,) + s, t) for s, t in blocks]
        + [pltpu.VMEM((nz - 1,) + s, t) for s, t in blocks]
        + [pltpu.VMEM((2, ng) + s, t) for s, t in ublocks]
        + [pltpu.VMEM((2, ng) + s, t) for s, t in ublocks]
        + [pltpu.VMEM((ng,) + s, t) for s, t in ublocks]
        + [pltpu.VMEM((ng,) + s, t) for s, t in ublocks]
        + [
            pltpu.SemaphoreType.DMA((3, 2)),
            pltpu.SemaphoreType.DMA((3, nz + 3)),
            pltpu.SemaphoreType.DMA((3, nz + 3)),
            pltpu.SemaphoreType.DMA((3, 2 * ng + 1)),
            pltpu.SemaphoreType.DMA((3, 3 * ng + 1)),
            pltpu.SemaphoreType.DMA((3, 3 * ng + 1)),
        ]
    )
    out = [
        jax.ShapeDtypeStruct(blocks[0][0], BF16),
        jax.ShapeDtypeStruct(blocks[1][0], F32),
        jax.ShapeDtypeStruct(blocks[2][0], F32),
        jax.ShapeDtypeStruct(ublocks[1][0], BF16),
        jax.ShapeDtypeStruct(ublocks[2][0], BF16),
        jax.ShapeDtypeStruct(ublocks[0][0], F32),
    ]
    return pl.pallas_call(
        functools.partial(reduce_kernel, nz),
        out_shape=out,
        in_specs=[ANY] * 6,
        out_specs=[VMEM] * 6,
        scratch_shapes=scratch,
        compiler_params=pltpu.CompilerParams(collective_id=1, has_side_effects=True, vmem_limit_bytes=60 * 2**20),
    )(qkv, wo, gain, wg, wu, wd)


def chunk_scores(q, kk, segq, segk, qidx, j, scale):
    s = lax.dot_general(q, kk, (((1,), (1,)), ((), ())), preferred_element_type=F32) * scale
    kidx = j * 256 + lax.broadcasted_iota(jnp.int32, (1, 256), 1)
    return s, (segq == segk) & (kidx <= qidx)


def attn_fwd_kernel(nb, q_ref, kv_ref, segq_ref, segk_ref, o_ref, lse_ref, kvall, lsem, ssem, rsem):
    b, q, y, c = place()
    k = lax.axis_index("blk")
    nz = nb // 4
    hz = nz // 2
    half = q // hz
    ql = q - half * hz
    low = k < nb // 2
    is_mid = k == nb // 2
    mid = (b, nb // 2)
    bar = greet(
        [at(b, half * hz + lax.rem(ql + r, hz), y, c) for r in range(1, hz)] + [at(b, q, 1 - y, c), at(b, q, y, 1 - c)]
    )

    @pl.when(low)
    def _():
        pl.semaphore_signal(bar, inc=1, device_id=mid, device_id_type=MESH)

    @pl.when(is_mid)
    def _():
        for j in range(nb // 2):
            pl.semaphore_signal(bar, inc=1, device_id=(b, j), device_id_type=MESH)

    pl.semaphore_wait(bar, hz + 1 + jnp.where(low, 1, 0) + jnp.where(is_mid, nb // 2, 0))

    def view(qq, yy, cc):
        return kvall.at[qq, yy, cc]

    sent = []

    def start(cp):
        cp.start()
        sent.append(cp)
        return cp

    mine = pltpu.make_async_copy(kv_ref, view(q, y, c), lsem)
    mine.start()
    other_y = at(b, q, 1 - y, c)
    other_c = at(b, q, y, 1 - c)
    z_in = []
    for r in range(1, hz):
        target = at(b, half * hz + lax.rem(ql + r, hz), y, c)
        start(remote(kv_ref, view(q, y, c), ssem.at[r], rsem.at[r], target))
        src = half * hz + lax.rem(ql - r + hz, hz)
        z_in.append((remote(kv_ref, view(src, y, c), ssem.at[r], rsem.at[r], target), src))
    start(remote(kv_ref, view(q, y, c), ssem.at[hz], rsem.at[hz], other_y))
    y_in = [(remote(kv_ref, view(q, 1 - y, c), ssem.at[hz], rsem.at[hz], other_y), q)]
    ns = 2 * hz + hz * 2
    to_mid = remote(kv_ref, view(q, y, c), ssem.at[ns], rsem.at[ns + k % (nb // 2)], mid)

    @pl.when(low)
    def _():
        to_mid.start()

    mine.wait()
    c_in = []
    s = 2 * hz

    def to_core(qq, yy, s):
        start(remote(view(qq, yy, c), view(qq, yy, c), ssem.at[s], rsem.at[s], other_c))
        c_in.append(remote(view(qq, yy, c), view(qq, yy, 1 - c), ssem.at[s], rsem.at[s], other_c))

    to_core(q, y, s)
    s += 1
    for r, (cp, src) in enumerate(z_in):
        cp.wait_recv()
        n = hz + 1 + r
        start(remote(view(src, y, c), view(src, y, c), ssem.at[n], rsem.at[n], other_y))
        y_in.append((remote(view(src, y, c), view(src, 1 - y, c), ssem.at[n], rsem.at[n], other_y), src))
        to_core(src, y, s)
        s += 1
    for cp, src in y_in:
        cp.wait_recv()
        to_core(src, 1 - y, s)
        s += 1
    for cp in c_in:
        cp.wait_recv()

    @pl.when(is_mid)
    def _():
        for j in range(nb // 2):
            remote(kv_ref, view(j // 4, (j // 2) % 2, j % 2), ssem.at[ns], rsem.at[ns + j], mid).wait_recv()

    scale = HD ** (-0.5)
    lo = jnp.where(k <= nb // 2, 0, nb // 4)
    hi = k // 2 + 1
    rows = q_ref.shape[1]
    tok = rows // H
    qidx = k * tok + lax.broadcasted_iota(jnp.int32, (rows, 1), 0) % tok
    for m in range(q_ref.shape[0]):
        qm = q_ref[m]
        segq = segq_ref[m]

        def body(j, carry):
            mx, sm, acc = carry
            blk = kvall[j // 2, j % 2, :, m].reshape(256, 2 * HD)
            s, ok = chunk_scores(qm, blk[:, :HD], segq, segk_ref[m, j], qidx, j, scale)
            s = jnp.where(ok, s, -1e30)
            new = jnp.maximum(mx, jnp.max(s, axis=-1, keepdims=True))
            p = jnp.where(ok, jnp.exp(s - new), 0.0)
            alpha = jnp.exp(mx - new)
            sm = sm * alpha + jnp.sum(p, axis=-1, keepdims=True)
            acc = acc * alpha + jnp.dot(p.astype(BF16), blk[:, HD:], preferred_element_type=F32)
            return new, sm, acc

        mx, sm, acc = lax.fori_loop(
            lo, hi, body, (jnp.full((rows, 1), -1e30, F32), jnp.zeros((rows, 1), F32), jnp.zeros((rows, HD), F32))
        )
        o_ref[m] = acc / sm
        lse_ref[m] = mx + jnp.log(sm)
    for cp in sent:
        cp.wait_send()

    @pl.when(low)
    def _():
        to_mid.wait_send()


def attn_fwd(nb, q, kv, segq, segk):
    nz = nb // 4
    ns = 4 * (nz // 2)
    return pl.pallas_call(
        functools.partial(attn_fwd_kernel, nb),
        out_shape=[
            jax.ShapeDtypeStruct(q.shape, F32),
            jax.ShapeDtypeStruct(q.shape[:2] + (1,), F32),
            jax.ShapeDtypeStruct((nz, 2, 2) + kv.shape, BF16),
        ],
        in_specs=[VMEM] * 4,
        out_specs=[VMEM] * 3,
        scratch_shapes=[
            pltpu.SemaphoreType.DMA,
            pltpu.SemaphoreType.DMA((ns + 1,)),
            pltpu.SemaphoreType.DMA((ns + nb // 2,)),
        ],
        compiler_params=pltpu.CompilerParams(collective_id=2, has_side_effects=True, vmem_limit_bytes=60 * 2**20),
    )(q, kv, segq, segk)


def attn_bwd_kernel(
    nb, q_ref, kvall, do_ref, lse_ref, delta_ref, segq_ref, segk_ref, dq_ref, dkv_ref, part, r1, r2, r3, r4, ssem, rsem, msem, nsem
):
    b, q, y, c = place()
    k = lax.axis_index("blk")
    nz = nb // 4
    hz = nz // 2
    half = q // hz
    ql = q - half * hz
    low = k < nb // 2
    is_mid = k == nb // 2
    mid = (b, nb // 2)
    bar = greet(
        [at(b, half * hz + lax.rem(ql + r, hz), y, c) for r in range(1, hz)] + [at(b, q, 1 - y, c), at(b, q, y, 1 - c)]
    )

    @pl.when(low)
    def _():
        pl.semaphore_signal(bar, inc=1, device_id=mid, device_id_type=MESH)

    @pl.when(is_mid)
    def _():
        for j in range(nb // 2):
            pl.semaphore_signal(bar, inc=1, device_id=(b, j), device_id_type=MESH)

    pl.semaphore_wait(bar, hz + 1 + jnp.where(low, 1, 0) + jnp.where(is_mid, nb // 2, 0))
    other_y = at(b, q, 1 - y, c)
    other_c = at(b, q, y, 1 - c)
    sent = []

    def start(cp):
        cp.start()
        sent.append(cp)
        return cp

    def clear(n, _):
        part[half * hz + n // 4, (n // 2) % 2, n % 2] = jnp.zeros(part.shape[3:], BF16)
        return 0

    lax.fori_loop(0, 4 * hz, clear, 0)
    scale = HD ** (-0.5)
    lo = jnp.where(k <= nb // 2, 0, nb // 4)
    hi = k // 2 + 1
    rows = q_ref.shape[1]
    tok = rows // H
    qidx = k * tok + lax.broadcasted_iota(jnp.int32, (rows, 1), 0) % tok
    tn = (((0,), (0,)), ((), ()))
    nt = (((1,), (1,)), ((), ()))
    for m in range(q_ref.shape[0]):
        dq_ref[m] = jnp.zeros(dq_ref.shape[1:], F32)

        def body(j, _):
            qm, dom = q_ref[m], do_ref[m]
            blk = kvall[j // 2, j % 2, :, m].reshape(256, 2 * HD)
            s, ok = chunk_scores(qm, blk[:, :HD], segq_ref[m], segk_ref[m, j], qidx, j, scale)
            p = jnp.where(ok, jnp.exp(jnp.where(ok, s, -1e30) - lse_ref[m]), 0.0)
            dp = lax.dot_general(dom, blk[:, HD:], nt, preferred_element_type=F32)
            ds = (p * (dp - delta_ref[m])).astype(BF16)
            dq_ref[m] += jnp.dot(ds, blk[:, :HD], preferred_element_type=F32) * scale
            dk = lax.dot_general(ds, qm, tn, preferred_element_type=F32) * scale
            dv = lax.dot_general(p.astype(BF16), dom, tn, preferred_element_type=F32)
            part[j // 2, j % 2, :, m] = jnp.concatenate([dk, dv], axis=1).astype(BF16).reshape(2, tok, 2 * HD)
            return 0

        lax.fori_loop(lo, hi, body, 0)

    @pl.when(is_mid)
    def _():
        for j in range(nb // 2):
            remote(part.at[j // 4, (j // 2) % 2, j % 2], r4, msem.at[j], nsem, (b, j)).start()

    hs = pl.ds(half * hz, hz)
    cp = start(remote(part.at[hs, :, 1 - c], r1, ssem.at[0], rsem.at[0], other_c))
    cp.wait_recv()

    def add1(n, _):
        i = half * hz + n // 2
        part[i, n % 2, c] = (part[i, n % 2, c].astype(F32) + r1[n // 2, n % 2].astype(F32)).astype(BF16)
        return 0

    lax.fori_loop(0, 2 * hz, add1, 0)
    cp = start(remote(part.at[hs, 1 - y, c], r2, ssem.at[1], rsem.at[1], other_y))
    cp.wait_recv()

    def add2(n, _):
        i = half * hz + n
        part[i, y, c] = (part[i, y, c].astype(F32) + r2[n].astype(F32)).astype(BF16)
        return 0

    lax.fori_loop(0, hz, add2, 0)
    last = []
    for r in range(1, hz):
        qt = half * hz + lax.rem(ql + r, hz)
        last.append(start(remote(part.at[qt, y, c], r3.at[r - 1], ssem.at[1 + r], rsem.at[1 + r], at(b, qt, y, c))))
    total = part[q, y, c].astype(F32)
    for r, cp in enumerate(last):
        cp.wait_recv()
        total = total + r3[r].astype(F32)
    dkv_ref[...] = total

    @pl.when(low)
    def _():
        remote(part.at[0, 0, 0], r4, msem.at[0], nsem, mid).wait_recv()
        dkv_ref[...] += r4[...].astype(F32)

    for cp in sent:
        cp.wait_send()

    @pl.when(is_mid)
    def _():
        for j in range(nb // 2):
            remote(part.at[j // 4, (j // 2) % 2, j % 2], r4, msem.at[j], nsem, (b, j)).wait_send()


def attn_bwd(nb, q, kvall, do, lse, delta, segq, segk):
    nz = nb // 4
    hz = nz // 2
    blk = kvall.shape[3:]
    return pl.pallas_call(
        functools.partial(attn_bwd_kernel, nb),
        out_shape=[jax.ShapeDtypeStruct(q.shape, F32), jax.ShapeDtypeStruct(blk, F32)],
        in_specs=[VMEM] * 7,
        out_specs=[VMEM] * 2,
        scratch_shapes=[
            pltpu.VMEM(kvall.shape, BF16),
            pltpu.VMEM((hz, 2) + blk, BF16),
            pltpu.VMEM((hz,) + blk, BF16),
            pltpu.VMEM((hz - 1,) + blk, BF16),
            pltpu.VMEM(blk, BF16),
            pltpu.SemaphoreType.DMA((hz + 1,)),
            pltpu.SemaphoreType.DMA((hz + 1,)),
            pltpu.SemaphoreType.DMA((nb // 2,)),
            pltpu.SemaphoreType.DMA,
        ],
        compiler_params=pltpu.CompilerParams(collective_id=3, has_side_effects=True, vmem_limit_bytes=60 * 2**20),
    )(q, kvall, do, lse, delta, segq, segk)


def tiles(n, w):
    return [(i, min(w, n - i)) for i in range(0, n, w)]


def gelu_parts(z):
    k0 = math.sqrt(2.0 / math.pi)
    z2 = z * z
    h = 0.5 + 0.5 * jnp.tanh(z * (k0 + (k0 * 0.044715) * z2))
    value = z * h
    slope = h + 2.0 * value * (1.0 - h) * (k0 + (3.0 * k0 * 0.044715) * z2)
    return value, slope


def ffn_kernel(
    b_ref, h1_ref, dy_ref, gp_ref, wg, wu, wd, out_ref, db_ref, dgp_ref, gg_o, gu_o, gd_o,
    ball, ballt, gate, up, mm, fsend, frecv, dfall, dsend, drecv, sg, su, sd, ssem, rsem, osem,
):
    b, q, y, c = place()
    g = q // 2
    t = lax.rem(q, 2) * 2 + y
    micro, tok, width = b_ref.shape
    hidden = wd.shape[0]
    peers = []
    for p in range(1, 4):
        tt = lax.rem(t + p, 4)
        peers.append((p, tt, at(b, g * 2 + tt // 2, lax.rem(tt, 2), c)))
    bar = greet([p[2] for p in peers])
    pl.semaphore_wait(bar, 3)
    sent = []
    nt = (((1,), (1,)), ((), ()))

    def spread(phase, m, src, dst_of, recv_of):
        waits = []
        for p, tt, target in peers:
            cp = remote(src(tt), dst_of(p, tt), ssem.at[phase, m, p - 1], rsem.at[phase, m, p - 1], target)
            cp.start()
            sent.append(cp)
            ts = lax.rem(t + 4 - p, 4)
            waits.append(remote(src(tt), recv_of(p, ts), ssem.at[phase, m, p - 1], rsem.at[phase, m, p - 1], target))
        return waits

    a_in, f_in, df_in, db_in = [], [], [], []
    for m in range(micro):
        a_in.append(
            spread(0, m, lambda tt, m=m: b_ref.at[m], lambda p, tt, m=m: ball.at[m, t], lambda p, ts, m=m: ball.at[m, ts])
        )
        ball[m, t] = b_ref[m]

    def forward(m):
        for cp in a_in[m]:
            cp.wait_recv()

        def body(n, _):
            cols = pl.ds(pl.multiple_of(n * 256, 256), 256)
            x = ball[m].reshape(4 * tok, width)
            gv = jnp.dot(x, wg[:, cols], preferred_element_type=F32)
            uv = jnp.dot(x, wu[:, cols], preferred_element_type=F32)
            gate[m, :, cols] = gv.astype(BF16)
            up[m, :, cols] = uv.astype(BF16)
            mm[m, :, cols] = (gelu_parts(gv)[0] * uv).astype(BF16)
            return 0

        lax.fori_loop(0, hidden // 256, body, 0)
        for o, w in tiles(width, 256):
            f = jnp.dot(mm[m], wd[:, o : o + w], preferred_element_type=F32)
            fsend[m, :, :, o : o + w] = f.astype(BF16).reshape(4, tok, w)
        f_in.append(
            spread(1, m, lambda tt: fsend.at[m, tt], lambda p, tt: frecv.at[m, p - 1], lambda p, ts: frecv.at[m, p - 1])
        )

    def middle(m):
        for cp in f_in[m]:
            cp.wait_recv()
        f = fsend[m, t].astype(F32)
        for p in range(3):
            f = f + frecv[m, p].astype(F32)
        gp = 1.0 + gp_ref[...]
        r = lax.rsqrt(jnp.mean(f * f, axis=-1, keepdims=True) + epsilon)
        n = f * r
        dy = dy_ref[m].astype(F32)
        out_ref[m] = (h1_ref[m] + n * gp).astype(BF16)
        dg = dy * gp
        df = r * (dg - n * jnp.mean(dg * n, axis=-1, keepdims=True))
        part = jnp.sum(dy * n, axis=0, keepdims=True)
        if m == 0:
            dgp_ref[...] = part
        else:
            dgp_ref[...] += part
        dfall[m, t] = df.astype(BF16)
        df_in.append(
            spread(2, m, lambda tt: dfall.at[m, t], lambda p, tt: dfall.at[m, t], lambda p, ts: dfall.at[m, ts])
        )

    def backward(m):
        for cp in df_in[m]:
            cp.wait_recv()

        def body(n, _):
            cols = pl.ds(pl.multiple_of(n * 256, 256), 256)
            x = dfall[m].reshape(4 * tok, width)
            dm = lax.dot_general(x, wd[cols, :], nt, preferred_element_type=F32)
            value, slope = gelu_parts(gate[m, :, cols].astype(F32))
            uv = up[m, :, cols].astype(F32)
            gate[m, :, cols] = (dm * uv * slope).astype(BF16)
            up[m, :, cols] = (dm * value).astype(BF16)
            return 0

        lax.fori_loop(0, hidden // 256, body, 0)
        for o, w in tiles(width, 256):
            d = lax.dot_general(gate[m], wg[o : o + w, :], nt, preferred_element_type=F32)
            d = d + lax.dot_general(up[m], wu[o : o + w, :], nt, preferred_element_type=F32)
            dsend[m, :, :, o : o + w] = d.astype(BF16).reshape(4, tok, w)
        db_in.append(
            spread(3, m, lambda tt: dsend.at[m, tt], lambda p, tt: drecv.at[m, p - 1], lambda p, ts: drecv.at[m, p - 1])
        )

    for m in range(micro):
        forward(m)
    for m in range(micro):
        for i in range(4):
            ballt[:, (m * 4 + i) * tok : (m * 4 + i + 1) * tok] = ball[m, i].T
    for m in range(micro):
        middle(m)
    for m in range(micro):
        backward(m)

    def grads(n, _):
        cols = pl.ds(pl.multiple_of(n * 256, 256), 256)
        slot = lax.rem(n, 2)

        def out(m, o):
            cc = pl.ds(pl.multiple_of(m * 256, 256), 256)
            return [
                pltpu.make_async_copy(sg.at[o], gg_o.at[:, cc], osem.at[0, o]),
                pltpu.make_async_copy(su.at[o], gu_o.at[:, cc], osem.at[1, o]),
                pltpu.make_async_copy(sd.at[o], gd_o.at[cc, :], osem.at[2, o]),
            ]

        @pl.when(n >= 2)
        def _():
            for cp in out(n, slot):
                cp.wait()

        x = ballt[...]
        sg[slot] = jnp.dot(x, gate[:, :, cols].reshape(-1, 256), preferred_element_type=F32).astype(BF16)
        su[slot] = jnp.dot(x, up[:, :, cols].reshape(-1, 256), preferred_element_type=F32).astype(BF16)
        sd[slot] = jnp.dot(
            mm[:, :, cols].reshape(-1, 256).T, dfall[...].reshape(-1, width), preferred_element_type=F32
        ).astype(BF16)
        for cp in out(n, slot):
            cp.start()
        return 0

    steps = hidden // 256
    lax.fori_loop(0, steps, grads, 0)
    for n in range(max(steps - 2, 0), steps):
        o = n % 2
        pltpu.make_async_copy(sg.at[o], gg_o.at[:, n * 256 : n * 256 + 256], osem.at[0, o]).wait()
        pltpu.make_async_copy(su.at[o], gu_o.at[:, n * 256 : n * 256 + 256], osem.at[1, o]).wait()
        pltpu.make_async_copy(sd.at[o], gd_o.at[n * 256 : n * 256 + 256, :], osem.at[2, o]).wait()
    for m in range(micro):
        for cp in db_in[m]:
            cp.wait_recv()
        d = dsend[m, t].astype(F32)
        for p in range(3):
            d = d + drecv[m, p].astype(F32)
        db_ref[m] = d
    for cp in sent:
        cp.wait_send()


def ffn(b, h1, dy, gp, wg, wu, wd):
    micro, tok, width = b.shape
    hidden = wd.shape[0]
    wide = (micro, 4 * tok, hidden)
    return pl.pallas_call(
        ffn_kernel,
        out_shape=[
            jax.ShapeDtypeStruct(b.shape, BF16),
            jax.ShapeDtypeStruct(b.shape, F32),
            jax.ShapeDtypeStruct((1, width), F32),
            jax.ShapeDtypeStruct(wg.shape, BF16),
            jax.ShapeDtypeStruct(wu.shape, BF16),
            jax.ShapeDtypeStruct(wd.shape, BF16),
        ],
        in_specs=[VMEM] * 7,
        out_specs=[VMEM] * 3 + [ANY] * 3,
        scratch_shapes=[
            pltpu.VMEM((micro, 4, tok, width), BF16),
            pltpu.VMEM((width, micro * 4 * tok), BF16),
            pltpu.VMEM(wide, BF16),
            pltpu.VMEM(wide, BF16),
            pltpu.VMEM(wide, BF16),
            pltpu.VMEM((micro, 4, tok, width), BF16),
            pltpu.VMEM((micro, 3, tok, width), BF16),
            pltpu.VMEM((micro, 4, tok, width), BF16),
            pltpu.VMEM((micro, 4, tok, width), BF16),
            pltpu.VMEM((micro, 3, tok, width), BF16),
            pltpu.VMEM((2, width, 256), BF16),
            pltpu.VMEM((2, width, 256), BF16),
            pltpu.VMEM((2, 256, width), BF16),
            pltpu.SemaphoreType.DMA((4, micro, 3)),
            pltpu.SemaphoreType.DMA((4, micro, 3)),
            pltpu.SemaphoreType.DMA((3, 2)),
        ],
        compiler_params=pltpu.CompilerParams(collective_id=4, has_side_effects=True, vmem_limit_bytes=62 * 2**20),
    )(b, h1, dy, gp, wg, wu, wd)


class Team:
    def __init__(self, place_of, c, ssem, rsem, sent):
        b, g, e, y = place_of
        self.t, self.ty, self.tz, self.td = e * 2 + y, e * 2 + 1 - y, (1 - e) * 2 + y, (1 - e) * 2 + 1 - y
        self.dev_y, self.dev_z = at(b, g * 2 + e, 1 - y, c), at(b, g * 2 + 1 - e, y, c)
        self.ssem, self.rsem, self.sent = ssem, rsem, sent

    def hop(self, src, dst, here, s, target):
        cp = remote(src, dst, self.ssem.at[s], self.rsem.at[s], target)
        cp.start()
        self.sent.append(cp)
        return remote(src, here, self.ssem.at[s], self.rsem.at[s], target)


class Gather(Team):
    def begin(self, slots):
        h = slots.shape[1] // 2
        self.a, self.b = pl.ds(0, h), pl.ds(h, h)
        self.slots = slots
        own = slots.at[self.t]
        y, z = slots.at[self.ty], slots.at[self.tz]
        self.ya = self.hop(own.at[self.a], own.at[self.a], y.at[self.a], 0, self.dev_y)
        self.zb = self.hop(own.at[self.b], own.at[self.b], z.at[self.b], 1, self.dev_z)
        self.yb = self.hop(own.at[self.b], own.at[self.b], y.at[self.b], 2, self.dev_y)
        self.za = self.hop(own.at[self.a], own.at[self.a], z.at[self.a], 3, self.dev_z)

    def forward(self):
        y, z, d = (self.slots.at[i] for i in (self.ty, self.tz, self.td))
        self.ya.wait_recv()
        self.da = self.hop(y.at[self.a], y.at[self.a], d.at[self.a], 4, self.dev_z)
        self.zb.wait_recv()
        self.db = self.hop(z.at[self.b], z.at[self.b], d.at[self.b], 5, self.dev_y)

    def end(self):
        for cp in (self.yb, self.za, self.da, self.db):
            cp.wait_recv()


class Sum(Team):
    def begin(self, parts, got, mid):
        h = parts.shape[1] // 2
        self.a, self.b = pl.ds(0, h), pl.ds(h, h)
        self.parts, self.got, self.mid = parts, got, mid
        y, z, d = (parts.at[i] for i in (self.ty, self.tz, self.td))
        self.ma = self.hop(d.at[self.a], mid.at[0], mid.at[0], 0, self.dev_y)
        self.mb = self.hop(d.at[self.b], mid.at[1], mid.at[1], 1, self.dev_z)
        self.ya = self.hop(y.at[self.a], got.at[0, self.a], got.at[0, self.a], 2, self.dev_y)
        self.zb = self.hop(z.at[self.b], got.at[1, self.b], got.at[1, self.b], 3, self.dev_z)

    def forward(self):
        z, y = self.parts.at[self.tz], self.parts.at[self.ty]
        self.ma.wait_recv()
        z[self.a] = z[self.a] + self.mid[0]
        self.za = self.hop(z.at[self.a], self.got.at[1, self.a], self.got.at[1, self.a], 4, self.dev_z)
        self.mb.wait_recv()
        y[self.b] = y[self.b] + self.mid[1]
        self.yb = self.hop(y.at[self.b], self.got.at[0, self.b], self.got.at[0, self.b], 5, self.dev_y)

    def end(self):
        for cp in (self.ya, self.zb, self.za, self.yb):
            cp.wait_recv()
        own, got = self.parts.at[self.t], self.got
        return own[...].astype(F32) + got[0].astype(F32) + got[1].astype(F32)


def mlp_kernel(
    ball_h, h1_ref, dy_ref, gd_ref, wg_h, wu_h, wd_h, out_ref, db_ref, dgp_ref, gg_o, gu_o, gd_o,
    wg, wu, wd, ball, ballt, gate, up, mm, fsend, frecv, fmid, dfall, dsend, drecv, dmid, sg, su, sd, ssem, rsem, osem, wsem, bsem,
):
    b, q, y, c = place()
    g, e = q // 2, q % 2
    t = e * 2 + y
    micro, tok, width = h1_ref.shape
    hidden = wd.shape[0]

    def load(n):
        cols = pl.ds(pl.multiple_of(n * 256, 256), 256)
        return [
            pltpu.make_async_copy(wg_h.at[:, cols], wg.at[:, cols], wsem.at[0, n]),
            pltpu.make_async_copy(wu_h.at[:, cols], wu.at[:, cols], wsem.at[1, n]),
        ]

    cut = ball_h.shape[2] // tok
    loads = [
        pltpu.make_async_copy(ball_h.at[m // cut, :, pl.ds(m % cut * tok, tok)], ball.at[m], bsem.at[m]) for m in range(micro)
    ]
    loads.append(pltpu.make_async_copy(wd_h, wd, bsem.at[micro]))
    loads[0].start()
    for n in range(hidden // 256):
        for cp in load(n):
            cp.start()
    for cp in loads[1:]:
        cp.start()
    bar = greet([at(b, q, 1 - y, c), at(b, g * 2 + 1 - e, y, c)])
    pl.semaphore_wait(bar, 2)
    sent = []
    nt = (((1,), (1,)), ((), ()))

    def team(kind, phase, m):
        return kind((b, g, e, y), c, ssem.at[phase, m], rsem.at[phase, m], sent)

    f_sum = [team(Sum, 0, m) for m in range(micro)]
    df_all = [team(Gather, 1, m) for m in range(micro)]
    db_sum = [team(Sum, 2, m) for m in range(micro)]

    def rise(m):
        loads[m].wait()

        def body(n, _):
            if m == 0:
                for cp in load(n):
                    cp.wait()
            cols = pl.ds(pl.multiple_of(n * 256, 256), 256)
            x = ball[m].reshape(4 * tok, width)
            gv = jnp.dot(x, wg[:, cols], preferred_element_type=F32)
            uv = jnp.dot(x, wu[:, cols], preferred_element_type=F32)
            value, slope = gelu_parts(gv)
            gate[m, :, cols] = (uv * slope).astype(BF16)
            up[m, :, cols] = value.astype(BF16)
            mm[m, :, cols] = (value * uv).astype(BF16)
            return 0

        lax.fori_loop(0, hidden // 256, body, 0)

    def fall(m):
        if m == 0:
            loads[micro].wait()
        for o, w in tiles(width, 256):
            f = jnp.dot(mm[m], wd[:, o : o + w], preferred_element_type=F32)
            fsend[m, :, :, o : o + w] = f.astype(BF16).reshape(4, tok, w)
        f_sum[m].begin(fsend.at[m], frecv.at[m], fmid.at[m])

    def middle(m):
        f = f_sum[m].end()
        gp = 1.0 + gd_ref[5:6]
        r = lax.rsqrt(jnp.mean(f * f, axis=-1, keepdims=True) + epsilon)
        n = f * r
        dy = dy_ref[m].astype(F32)
        out_ref[m] = (h1_ref[m] + n * gp).astype(BF16)
        dg = dy * gp
        df = r * (dg - n * jnp.mean(dg * n, axis=-1, keepdims=True))
        part = jnp.sum(dy * n, axis=0, keepdims=True)
        if m == 0:
            dgp_ref[...] = part
        else:
            dgp_ref[...] += part
        dfall[m, t] = df.astype(BF16)
        df_all[m].begin(dfall.at[m])

    def back_rise(m):
        df_all[m].end()

        def body(n, _):
            cols = pl.ds(pl.multiple_of(n * 256, 256), 256)
            x = dfall[m].reshape(4 * tok, width)
            dm = lax.dot_general(x, wd[cols, :], nt, preferred_element_type=F32)
            gate[m, :, cols] = (dm * gate[m, :, cols].astype(F32)).astype(BF16)
            up[m, :, cols] = (dm * up[m, :, cols].astype(F32)).astype(BF16)
            return 0

        lax.fori_loop(0, hidden // 256, body, 0)

    def back_fall(m):
        for o, w in tiles(width, 256):
            d = lax.dot_general(gate[m], wg[o : o + w, :], nt, preferred_element_type=F32)
            d = d + lax.dot_general(up[m], wu[o : o + w, :], nt, preferred_element_type=F32)
            dsend[m, :, :, o : o + w] = d.astype(BF16).reshape(4, tok, w)
        db_sum[m].begin(dsend.at[m], drecv.at[m], dmid.at[m])

    for m in range(micro):
        rise(m)
        if m >= 1:
            f_sum[m - 1].forward()
        if m >= 2:
            middle(m - 2)
        if m >= 3:
            df_all[m - 3].forward()
        fall(m)
    for m in range(micro):
        for i in range(4):
            o = (m * 4 + i) * tok
            ballt[:, o : o + tok] = ball[m, i].T
    middle(micro - 2)
    if micro >= 3:
        df_all[micro - 3].forward()
    for m in range(micro):
        back_rise(m)
        if m == 0:
            f_sum[micro - 1].forward()
            df_all[micro - 2].forward()
        else:
            db_sum[m - 1].forward()
        if m == 1:
            df_all[micro - 1].forward()
        back_fall(m)
        if m == 0:
            middle(micro - 1)

    def grads(n, _):
        cols = pl.ds(pl.multiple_of(n * 256, 256), 256)
        slot = lax.rem(n, 2)

        def out(m, o):
            cc = pl.ds(pl.multiple_of(m * 256, 256), 256)
            return [
                pltpu.make_async_copy(sg.at[o], gg_o.at[:, cc], osem.at[0, o]),
                pltpu.make_async_copy(su.at[o], gu_o.at[:, cc], osem.at[1, o]),
                pltpu.make_async_copy(sd.at[o], gd_o.at[cc, :], osem.at[2, o]),
            ]

        @pl.when(n >= 2)
        def _():
            for cp in out(n, slot):
                cp.wait()

        x = ballt[...]
        sg[slot] = jnp.dot(x, gate[:, :, cols].reshape(-1, 256), preferred_element_type=F32).astype(BF16)
        su[slot] = jnp.dot(x, up[:, :, cols].reshape(-1, 256), preferred_element_type=F32).astype(BF16)
        sd[slot] = jnp.dot(
            mm[:, :, cols].reshape(-1, 256).T, dfall[...].reshape(-1, width), preferred_element_type=F32
        ).astype(BF16)
        for cp in out(n, slot):
            cp.start()
        return 0

    steps = hidden // 256
    lax.fori_loop(0, min(2, steps), grads, 0)
    db_sum[micro - 1].forward()
    lax.fori_loop(min(2, steps), steps, grads, 0)
    for n in range(max(steps - 2, 0), steps):
        o = n % 2
        pltpu.make_async_copy(sg.at[o], gg_o.at[:, n * 256 : n * 256 + 256], osem.at[0, o]).wait()
        pltpu.make_async_copy(su.at[o], gu_o.at[:, n * 256 : n * 256 + 256], osem.at[1, o]).wait()
        pltpu.make_async_copy(sd.at[o], gd_o.at[n * 256 : n * 256 + 256, :], osem.at[2, o]).wait()
    for m in range(micro):
        db_ref[m] = db_sum[m].end()
    for cp in sent:
        cp.wait_send()


def mlp(ball, h1, dy, gp, wg, wu, wd):
    micro, tok, width = h1.shape
    hidden = wd.shape[0]
    wide = (micro, 4 * tok, hidden)
    return pl.pallas_call(
        mlp_kernel,
        out_shape=[
            jax.ShapeDtypeStruct(h1.shape, BF16),
            jax.ShapeDtypeStruct(h1.shape, F32),
            jax.ShapeDtypeStruct((1, width), F32),
            jax.ShapeDtypeStruct(wg.shape, BF16),
            jax.ShapeDtypeStruct(wu.shape, BF16),
            jax.ShapeDtypeStruct(wd.shape, BF16),
        ],
        in_specs=[ANY] + [VMEM] * 3 + [ANY] * 3,
        out_specs=[VMEM] * 3 + [ANY] * 3,
        scratch_shapes=[
            pltpu.VMEM(wg.shape, BF16),
            pltpu.VMEM(wu.shape, BF16),
            pltpu.VMEM(wd.shape, BF16),
            pltpu.VMEM((micro, 4, tok, width), BF16),
            pltpu.VMEM((width, micro * 4 * tok), BF16),
            pltpu.VMEM(wide, BF16),
            pltpu.VMEM(wide, BF16),
            pltpu.VMEM(wide, BF16),
            pltpu.VMEM((micro, 4, tok, width), BF16),
            pltpu.VMEM((micro, 2, tok, width), BF16),
            pltpu.VMEM((micro, 2, tok // 2, width), BF16),
            pltpu.VMEM((micro, 4, tok, width), BF16),
            pltpu.VMEM((micro, 4, tok, width), BF16),
            pltpu.VMEM((micro, 2, tok, width), BF16),
            pltpu.VMEM((micro, 2, tok // 2, width), BF16),
            pltpu.VMEM((2, width, 256), BF16),
            pltpu.VMEM((2, width, 256), BF16),
            pltpu.VMEM((2, 256, width), BF16),
            pltpu.SemaphoreType.DMA((3, micro, 6)),
            pltpu.SemaphoreType.DMA((3, micro, 6)),
            pltpu.SemaphoreType.DMA((3, 2)),
            pltpu.SemaphoreType.DMA((2, hidden // 256)),
            pltpu.SemaphoreType.DMA((micro + 1,)),
        ],
        compiler_params=pltpu.CompilerParams(collective_id=7, has_side_effects=True, vmem_limit_bytes=62 * 2**20),
    )(ball, h1, dy, gp, wg, wu, wd)


def halves(n):
    first = up16(n // 2)
    return [(0, first), (first, n - first)] if first < n else [(0, n)]


def norm_of(v):
    r = lax.rsqrt(jnp.mean(v * v, axis=-1, keepdims=True) + epsilon)
    return v * r, r


def norm_back(grad, n, r, scale):
    gs = grad * scale
    return r * (gs - n * jnp.mean(gs * n, axis=-1, keepdims=True)), jnp.sum(grad * n, axis=0, keepdims=True)


def spread_gains(block, width, n_dev):
    w = width // n_dev
    lane = lax.broadcasted_iota(jnp.int32, (128, width), 0)
    col = lax.broadcasted_iota(jnp.int32, (128, width), 1)
    pick = jnp.where(lax.rem(col, w) == lane, 1.0, 0.0).astype(BF16)
    wide = jnp.dot(block, pick, preferred_element_type=F32)
    row = lax.broadcasted_iota(jnp.int32, (n_dev * 16, width), 0) // 16
    mine = lax.broadcasted_iota(jnp.int32, (n_dev * 16, width), 1) // w
    return jnp.sum(jnp.where(row == mine, wide, 0.0).reshape(n_dev, 16, width), axis=0)


def collect_gains(rows, n_dev):
    width = rows.shape[1]
    w = width // n_dev
    row = lax.broadcasted_iota(jnp.int32, (n_dev, 8, width), 0)
    mine = lax.broadcasted_iota(jnp.int32, (n_dev, 8, width), 2) // w
    wide = jnp.where(row == mine, rows[None], 0.0).reshape(n_dev * 8, width)
    col = lax.broadcasted_iota(jnp.int32, (width, 128), 0)
    lane = lax.broadcasted_iota(jnp.int32, (width, 128), 1)
    pick = jnp.where(lax.rem(col, w) == lane, 1.0, 0.0)
    out = jnp.dot(wide, pick, preferred_element_type=F32, precision=lax.Precision.HIGHEST)
    return out.reshape(n_dev, 8, 128)


def pack_rows(kr, kp):
    row = lax.broadcasted_iota(jnp.int32, (4 * kr, 4 * kp), 0)
    col = lax.broadcasted_iota(jnp.int32, (4 * kr, 4 * kp), 1)
    return jnp.where(lax.div(row, kr) * kp + lax.rem(row, kr) == col, 1.0, 0.0).astype(BF16)


def kv_columns(which, qw):
    return 2 * which * qw + HD, (2 * which + 1) * qw + HD


def half_mask(n, tok):
    row = lax.rem(lax.broadcasted_iota(jnp.int32, (n, tok), 0), tok)
    return lax.broadcasted_iota(jnp.int32, (n, tok), 1) <= row


def segment_of(len_ref, m, index):
    end = jnp.int32(0)
    seg = jnp.zeros(index.shape, jnp.int32)
    for i in range(len_ref.shape[1]):
        end = end + len_ref[m, i]
        seg = seg + jnp.where(index >= end, 1, 0)
    return seg


def front_barrier(nz):
    b, q, y, c = place()
    k = lax.axis_index("blk")
    nb = 4 * nz
    g, e = q // 2, q % 2
    ng = nz // 2
    bar = greet(
        [at(b, lax.rem(q + r, nz), y, c) for r in range(1, nz)]
        + [at(1 - b, q, y, c), at(b, q, 1 - y, c), at(b, q, y, 1 - c), at(b, q, 1 - y, 1 - c)]
        + [at(b, lax.rem(g + r, ng) * 2 + c, y, e) for r in range(1, ng)]
    )

    @pl.when(e != c)
    def _():
        pl.semaphore_signal(bar, inc=1, device_id=at(b, g * 2 + c, y, e), device_id_type=MESH)

    is_first, is_mid = k == 0, k == nb // 2

    @pl.when(is_first)
    def _():
        pl.semaphore_signal(bar, inc=1, device_id=(b, nb // 2), device_id_type=MESH)

    @pl.when(is_mid)
    def _():
        pl.semaphore_signal(bar, inc=1, device_id=(b, 0), device_id_type=MESH)

    pl.semaphore_wait(
        bar, nz + 2 + ng + 1 - jnp.where(e == c, 1, 0) + jnp.where(is_first, 1, 0) + jnp.where(is_mid, 1, 0)
    )


def front_kernel(
    nz, x_ref, cos_ref, sin_ref, len_ref, wq_ref, wk_ref, wv_ref, wo_u, gain_u, wg_ref, wu_ref, wd_x,
    ball, h1_o, attn_h, raw_h, q_h, o_h, ob_h, lse_h, kv_h, wqkv_h, wo_h, xq_h, xkv_h, xo_h, xlse_h, gd_o, gh_o, wg_f, wu_f, wd_f,
    attn_s, raw_s, q_s, o_s, ob_s, lse_s, kvall, kv_own, wqkv, wo, gain_f, qkv_u, wg, wu, wd, qkv_x, wg_x, wu_x, qkv_r, wg_r, wu_r,
    xq, xkv, xo_s, xlse_s, xob, xin, xss, xrs,
    lsem, ssem, rsem, wls, wss, wrs, kls, kss, krs, osem, qss, qrs, tss, trs,
):
    b, q, y, c = place()
    k = lax.axis_index("blk")
    nb = 4 * nz
    n_dev = 2 * nb
    g, e = q // 2, q % 2
    ng = nz // 2
    hz = nz // 2
    qw = qkv_u.shape[1]
    self_in = e == c
    front_barrier(nz)
    other_x, other_y, other_c = at(1 - b, q, y, c), at(b, q, 1 - y, c), at(b, q, y, 1 - c)
    everything, both = pl.ds(0, nz), pl.ds(0, 2)
    kr = qkv_u.shape[0] // 4
    dr, dp = wd_x.shape[0], wd.shape[0]

    def split_rows(ref, out):
        out[...] = jnp.zeros(out.shape, BF16)
        for n in range(2 * nz):
            for j in range(4):
                o = (4 * n + j) * dr
                out[j, :kr, n * dp : n * dp + dr] = ref[:, o : o + dr]

    sent = []

    def start(cp):
        cp.start()
        sent.append(cp)
        return cp

    quad = [(y, 1 - c), (1 - y, c), (1 - y, 1 - c)]
    trades = [(qkv_x, qkv_r, qkv_u), (wg_x, wg_r, wg), (wu_x, wu_r, wu)]
    t_in = [[] for _ in trades]

    def trade(i):
        src, dst, _ = trades[i]
        for p, (yy, cc) in enumerate(quad):
            t = at(b, q, yy, cc)
            start(remote(src.at[yy * 2 + cc], dst.at[y * 2 + c], qss.at[i, p], qrs.at[i, p], t))
            t_in[i].append(remote(src.at[yy * 2 + cc], dst.at[yy * 2 + cc], qss.at[i, p], qrs.at[i, p], t))
        t_in[i].append(pltpu.make_async_copy(src.at[y * 2 + c], dst.at[y * 2 + c], qrs.at[i, 3]))
        t_in[i][3].start()

    def traded(i):
        _, src, dst = trades[i]
        for p in range(3):
            t_in[i][p].wait_recv()
        t_in[i][3].wait()
        pick = pack_rows(kr, src.shape[1])
        for o, n in tiles(src.shape[2], 256):
            v = jnp.dot(pick, src[:, :, o : o + n].reshape(4 * src.shape[1], n), preferred_element_type=F32)
            dst[:, o : o + n] = v.astype(BF16)

    def view_q(ref, yy, cc, xx, qq):
        return ref.at[xx, qq, :, pl.ds(pl.multiple_of((yy * 2 + cc) * qw, 128), HD)]

    def view_kv(ref, yy, cc, xx, qq):
        return ref.at[xx, qq, :, pl.ds(pl.multiple_of((yy * 2 + cc) * qw + HD, 128), qw - HD)]

    def view_lead(ref, yy, cc, xx, qq):
        return ref.at[xx, qq, yy, cc]

    GAIN, KV, Q, WO = range(4)
    items = [
        (gain_u, gain_f, view_lead, True),
        (qkv_u.at[:, HD:], wqkv, view_kv, True),
        (qkv_u.at[:, :HD], wqkv, view_q, True),
        (wo_u, wo, view_lead, True),
    ]
    local = [None] * 4
    z_in, a_in, b_in, c_in = ([[] for _ in items] for _ in range(4))

    def hop(i, v, w, s, t):
        start(remote(v, v, ssem.at[i, s], rsem.at[i, s], t))
        return remote(v, w, ssem.at[i, s], rsem.at[i, s], t)

    def second(i):
        return (other_x, 1 - b, y) if items[i][3] else (other_y, b, 1 - y)

    def send_z(i):
        src, dst, view, _ = items[i]
        local[i] = pltpu.make_async_copy(src, view(dst, y, c, b, q), lsem.at[i])
        local[i].start()
        for r in range(1, nz):
            t = at(b, lax.rem(q + r, nz), y, c)
            start(remote(src, view(dst, y, c, b, q), ssem.at[i, r], rsem.at[i, r], t))
            z_in[i].append(
                remote(src, view(dst, y, c, b, lax.rem(q - r + nz, nz)), ssem.at[i, r], rsem.at[i, r], t)
            )
        t, xx, yy = second(i)
        start(remote(src, view(dst, y, c, b, q), ssem.at[i, nz], rsem.at[i, nz], t))
        a_in[i].append(remote(src, view(dst, yy, c, xx, q), ssem.at[i, nz], rsem.at[i, nz], t))

    def send_a(i):
        _, dst, view, _ = items[i]
        t, xx, yy = second(i)
        for r in range(1, nz):
            qs = lax.rem(q - r + nz, nz)
            z_in[i][r - 1].wait_recv()
            a_in[i].append(hop(i, view(dst, y, c, b, qs), view(dst, yy, c, xx, qs), nz + r, t))

    def send_b(i, half):
        _, dst, view, x_first = items[i]
        if half == 0:
            local[i].wait()
            xx, yy = b, y
        else:
            for cp in a_in[i]:
                cp.wait_recv()
            _, xx, yy = second(i)
        t, xi, yi = (other_y, xx, 1 - yy) if x_first else (other_x, 1 - xx, yy)
        b_in[i].append(
            (hop(i, view(dst, yy, c, xx, everything), view(dst, yi, c, xi, everything), 2 * nz + half, t), xi, yi)
        )
        to_core(i, xx, yy, 2 * nz + 2 + half)

    def to_core(i, xx, yy, s):
        _, dst, view, _ = items[i]
        c_in[i].append(hop(i, view(dst, yy, c, xx, everything), view(dst, yy, 1 - c, xx, everything), s, other_c))

    def send_c(i):
        for half, (cp, xx, yy) in enumerate(b_in[i]):
            cp.wait_recv()
            to_core(i, xx, yy, 2 * nz + 4 + half)

    def done(i):
        for cp in c_in[i]:
            cp.wait_recv()

    pieces = [
        (src, dst, o, n) for src, dst in ((wd, wd_f), (wg, wg_f), (wu, wu_f)) for o, n in halves(src.shape[0])
    ]
    w_in, w_x, w_c, w_out = ([[] for _ in pieces] for _ in range(4))

    def w_send(j):
        src, dst, o, n = pieces[j]
        sl = pl.ds(o, n)
        for r in range(ng):
            t = at(b, lax.rem(g + r, ng) * 2 + c, y, e)
            qs = lax.rem(g - r + ng, ng) * 2 + c
            cp = remote(src.at[sl], dst.at[b, q, sl], wss.at[j, r], wrs.at[j, r], t)
            inc = remote(src.at[sl], dst.at[b, qs, sl], wss.at[j, r], wrs.at[j, r], t)
            if r == 0:
                lc = pltpu.make_async_copy(src.at[sl], dst.at[b, q, sl], wls.at[j])

                @pl.when(self_in)
                def _():
                    lc.start()

                @pl.when(jnp.logical_not(self_in))
                def _():
                    cp.start()

                w_in[j].append((inc, qs, lc))
                w_out[j].append(cp)
            else:
                start(cp)
                w_in[j].append((inc, qs, None))

    def w_on(j, xx, qs, s, target, yx, yq):
        _, dst, o, n = pieces[j]
        sl = pl.ds(o, n)
        start(remote(dst.at[xx, qs, sl], dst.at[xx, qs, sl], wss.at[j, s], wrs.at[j, s], target))
        return remote(dst.at[xx, qs, sl], dst.at[yx, yq, sl], wss.at[j, s], wrs.at[j, s], target)

    def w_across(j):
        for r, (inc, qs, lc) in enumerate(w_in[j]):
            if lc is not None:

                @pl.when(self_in)
                def _():
                    lc.wait()

                @pl.when(jnp.logical_not(self_in))
                def _():
                    inc.wait_recv()
            else:
                inc.wait_recv()
            w_x[j].append(w_on(j, b, qs, ng + r, other_x, 1 - b, qs))
        for r, (_, qs, _) in enumerate(w_in[j]):
            w_c[j].append(w_on(j, b, qs, 2 * ng + r, other_c, b, lax.rem(g - r + ng, ng) * 2 + 1 - c))

    def w_core(j):
        for r, (_, qs, _) in enumerate(w_in[j]):
            w_x[j][r].wait_recv()
            w_c[j].append(w_on(j, 1 - b, qs, 3 * ng + r, other_c, 1 - b, lax.rem(g - r + ng, ng) * 2 + 1 - c))

    last = len(pieces)

    kept = []

    def keep(src, dst):
        cp = pltpu.make_async_copy(src, dst, osem.at[len(kept)])
        cp.start()
        kept.append(cp)

    qkv_x[...] = jnp.zeros(qkv_x.shape, BF16)
    per = qw - HD
    for j in range(4):
        qkv_x[j, :kr, :HD] = wq_ref[:, j * HD : (j + 1) * HD]
        o = j * per % HD
        qkv_x[j, :kr, HD:] = (wk_ref if j * per < HD else wv_ref)[:, o : o + per]
    trade(0)
    send_z(GAIN)
    if wd.shape[0] == dr:
        wd[...] = wd_x[...]
    else:
        whole = dr // 16 * 16
        wd[:whole] = wd_x[:whole]
        rest = jnp.zeros((wd.shape[0] - dr, wd.shape[1]), BF16)
        wd[whole:] = jnp.concatenate([wd_x[whole:], rest], axis=0)
    w_send(0)
    traded(0)
    send_z(KV)
    send_z(Q)
    split_rows(wg_ref, wg_x)
    trade(1)
    split_rows(wu_ref, wu_x)
    micro, _, tok, _ = q_s.shape
    rows = micro * tok
    x = x_ref[...].astype(F32)
    n_x = norm_of(x)[0]
    send_a(GAIN)
    send_a(KV)
    send_b(GAIN, 0)
    send_b(KV, 0)
    traded(1)
    w_send(1)
    send_b(GAIN, 1)
    send_b(KV, 1)
    send_a(Q)
    send_b(Q, 0)
    trade(2)
    w_across(0)
    w_send(2)
    send_z(WO)
    send_c(GAIN)
    send_c(KV)
    done(GAIN)
    done(KV)
    width = x_ref.shape[1]
    gains_d = spread_gains(gain_f[...].reshape(n_dev * 16, 128), width, n_dev)
    gains_h = spread_gains(gain_f[...].reshape(n_dev * 16, 128), HD, n_dev)
    gd_o[...] = gains_d
    gh_o[...] = gains_h
    a = (n_x * (1.0 + gains_d[0:1])).astype(BF16)
    cosine, sine = cos_ref[...], sin_ref[...]
    half = HD // 2

    def project(h):
        if h < H:
            w = wqkv[:, :, :, h * qw : h * qw + HD]
        else:
            o1, o2 = kv_columns(h - H, qw)
            w = jnp.concatenate([wqkv[:, :, :, o1 : o1 + half], wqkv[:, :, :, o2 : o2 + half]], axis=3)
        raw = jnp.dot(a, w.reshape(width, HD), preferred_element_type=F32)
        if h == H + 1:
            kv_own[:, :, HD:] = raw.astype(BF16).reshape(micro, tok, HD)
            return
        raw_s[:, h * HD : (h + 1) * HD] = raw
        z = norm_of(raw)[0] * (1.0 + (gains_h[1:2] if h < H else gains_h[2:3]))
        z1, z2 = z[:, :half], z[:, half:]
        z = jnp.concatenate([z1 * cosine - z2 * sine, z2 * cosine + z1 * sine], axis=1).astype(BF16)
        if h < H:
            q_s[:, h] = z.reshape(micro, tok, HD)
        else:
            kv_own[:, :, :HD] = z.reshape(micro, tok, HD)

    project(H)
    project(H + 1)
    ht = tok // 2
    is_first, is_mid = k == 0, k == nb // 2
    first, mid = (b, 0), (b, nb // 2)
    x_kv = remote(kv_own.at[:, :ht], xkv, xss.at[0], xrs.at[0], first)
    x_q = remote(q_s.at[:, :, :ht], xq, xss.at[1], xrs.at[1], first)
    x_o = remote(xob, xin, xss.at[2], xrs.at[2], mid)

    @pl.when(is_mid)
    def _():
        x_kv.start()

    side = q // hz
    ql = q - side * hz

    def kview(qq, yy, cc):
        return kvall.at[qq - side * hz, yy, cc]

    mine = pltpu.make_async_copy(kv_own, kview(q, y, c), kls)
    mine.start()
    kz_in, ky_in, kc_in = [], [], []
    for r in range(1, hz):
        t = at(b, side * hz + lax.rem(ql + r, hz), y, c)
        start(remote(kv_own, kview(q, y, c), kss.at[r], krs.at[r], t))
        src = side * hz + lax.rem(ql - r + hz, hz)
        kz_in.append((remote(kv_own, kview(src, y, c), kss.at[r], krs.at[r], t), src))
    start(remote(kv_own, kview(q, y, c), kss.at[hz], krs.at[hz], other_y))
    ky_in.append((remote(kv_own, kview(q, 1 - y, c), kss.at[hz], krs.at[hz], other_y), q))
    slot = [2 * hz]

    def k_core(qq, yy):
        s = slot[0]
        slot[0] += 1
        start(remote(kview(qq, yy, c), kview(qq, yy, c), kss.at[s], krs.at[s], other_c))
        kc_in.append(remote(kview(qq, yy, c), kview(qq, yy, 1 - c), kss.at[s], krs.at[s], other_c))

    mine.wait()
    k_core(q, y)
    traded(2)
    send_b(Q, 1)
    w_across(1)
    w_send(3)
    w_core(0)
    send_a(WO)
    send_b(WO, 0)
    for r, (cp, src) in enumerate(kz_in):
        cp.wait_recv()
        s = hz + 1 + r
        start(remote(kview(src, y, c), kview(src, y, c), kss.at[s], krs.at[s], other_y))
        ky_in.append((remote(kview(src, y, c), kview(src, 1 - y, c), kss.at[s], krs.at[s], other_y), src))
        k_core(src, y)
    send_c(Q)
    w_across(2)
    w_send(4)
    w_core(1)
    done(Q)
    for h in range(H):
        project(h)

    @pl.when(is_mid)
    def _():
        x_q.start()

    keep(wqkv, wqkv_h)
    keep(raw_s, raw_h)
    keep(q_s, q_h)
    send_b(WO, 1)
    for cp, src in ky_in:
        cp.wait_recv()
        k_core(src, 1 - y)
    w_across(3)
    w_send(5)
    w_core(2)
    for cp in kc_in:
        cp.wait_recv()

    scale = HD ** (-0.5)
    lo = side * (nb // 4)
    hi = k // 2 + 1
    qrows = H * tok
    qidx = k * tok + lax.rem(lax.broadcasted_iota(jnp.int32, (qrows, 1), 0), tok)

    def online(carry, s, ok, values):
        mx, sm, acc = carry
        if ok is not None:
            s = jnp.where(ok, s, -1e30)
        new = jnp.maximum(mx, jnp.max(s, axis=-1, keepdims=True))
        p = jnp.exp(s - new)
        if ok is not None:
            p = jnp.where(ok, p, 0.0)
        alpha = jnp.exp(mx - new)
        sm = sm * alpha + jnp.sum(p, axis=-1, keepdims=True)
        return new, sm, acc * alpha + jnp.dot(p.astype(BF16), values, preferred_element_type=F32)

    def empty(n):
        return jnp.full((n, 1), -1e30, F32), jnp.zeros((n, 1), F32), jnp.zeros((n, HD), F32)

    @pl.when(is_first)
    def _():
        x_kv.wait_recv()
        x_q.wait_recv()
        for m in range(micro):
            qm = xq[m].reshape(H * ht, HD)

            def body(j, carry):
                blk = kvall[j // 2, j % 2, :, m].reshape(256, 2 * HD)
                s = lax.dot_general(qm, blk[:, :HD], (((1,), (1,)), ((), ())), preferred_element_type=F32) * scale
                return online(carry, s, None, blk[:, HD:])

            carry = lax.fori_loop(0, nb // 4, body, empty(H * ht))
            blk = xkv[m]
            s = lax.dot_general(qm, blk[:, :HD], (((1,), (1,)), ((), ())), preferred_element_type=F32) * scale
            mx, sm, acc = online(carry, s, half_mask(H * ht, ht), blk[:, HD:])
            xo_s[m] = acc / sm
            xlse_s[m] = mx + jnp.log(sm)
            xob[m] = xo_s[m].astype(BF16).reshape(H, ht, HD)
        x_o.start()

    b_all = [Gather((b, g, e, y), c, tss.at[m], trs.at[m], sent) for m in range(micro)]
    for m in range(micro):
        qm = q_s[m].reshape(qrows, HD)
        segq = segment_of(len_ref, m, qidx)

        def body(j, carry):
            blk = kvall[j // 2 - side * hz, j % 2, :, m].reshape(256, 2 * HD)
            kidx = j * 256 + lax.broadcasted_iota(jnp.int32, (1, 256), 1)
            s, ok = chunk_scores(qm, blk[:, :HD], segq, segment_of(len_ref, m, kidx), qidx, j, scale)
            return online(carry, s, ok, blk[:, HD:])

        mx, sm, acc = lax.fori_loop(lo, hi, body, empty(qrows))
        o = acc / sm
        o_s[m] = o
        lse_s[m] = mx + jnp.log(sm)
        rs = slice(m * tok, (m + 1) * tok)
        for h in range(H):
            ob_s[rs, h * HD : (h + 1) * HD] = o[h * tok : (h + 1) * tok].astype(BF16)
        if m == 0:
            w_across(4)
            w_core(3)
            send_c(WO)
            done(WO)

            @pl.when(is_mid)
            def _():
                x_o.wait_recv()

        @pl.when(is_mid)
        def _():
            for h in range(H):
                ob_s[m * tok : m * tok + ht, h * HD : (h + 1) * HD] = xin[m, h]

        for o, n in tiles(width, 256):
            w = wo[:, :, :, :, :, o : o + n].reshape(H * HD, n)
            attn_s[rs, o : o + n] = jnp.dot(ob_s[rs], w, preferred_element_type=F32)
        h1 = x_ref[rs].astype(F32) + norm_of(attn_s[rs])[0] * (1.0 + gains_d[3:4])
        h1_o[m] = h1
        ball[m, e * 2 + y] = (norm_of(h1)[0] * (1.0 + gains_d[4:5])).astype(BF16)
        b_all[m].begin(ball.at[m])
        if m > 0:
            b_all[m - 1].forward()
    for src, dst in ((xq, xq_h), (xkv, xkv_h), (xo_s, xo_h), (xlse_s, xlse_h)):
        keep(src, dst)
    keep(o_s, o_h)
    keep(lse_s, lse_h)
    keep(ob_s, ob_h)
    keep(kvall, kv_h)
    keep(attn_s, attn_h)
    keep(wo, wo_h)
    w_core(4)
    b_all[micro - 1].forward()
    w_across(5)
    w_core(5)
    for m in range(micro):
        b_all[m].end()
    for j in range(last):
        for cp in w_c[j]:
            cp.wait_recv()
    for cp in sent:
        cp.wait_send()
    for j in range(last):

        @pl.when(jnp.logical_not(self_in))
        def _():
            w_out[j][0].wait_send()

    @pl.when(is_mid)
    def _():
        x_kv.wait_send()
        x_q.wait_send()

    @pl.when(is_first)
    def _():
        x_o.wait_send()

    for cp in kept:
        cp.wait()


def front(nz, x, cosine, sine, lengths, wq, wk, wv, wo, gain, wg, wu, wd, dp, micro):
    kr, kp = wg.shape[0], up16(wg.shape[0])
    fs = 2 * nz * dp
    qw = (wq.shape[1] + wk.shape[1] + wv.shape[1]) // 4
    ng = nz // 2
    hz = nz // 2
    rows, width = x.shape
    tok = rows // micro
    nb = 4 * nz
    out = {
        "ball": ((micro, 4, tok, width), BF16),
        "h1": ((micro, tok, width), F32),
        "attn": ((rows, width), F32),
        "raw": ((rows, (H + 1) * HD), F32),
        "q": ((micro, H, tok, HD), BF16),
        "o": ((micro, H * tok, HD), F32),
        "ob": ((rows, H * HD), BF16),
        "lse": ((micro, H * tok, 1), F32),
        "kv": ((hz, 2, 2, micro, tok, 2 * HD), BF16),
        "wqkv": ((2, nz, 4 * kr, 4 * qw), BF16),
        "wo": ((2, nz, 2, 2) + wo.shape, BF16),
        "xq": ((micro, H, tok // 2, HD), BF16),
        "xkv": ((micro, tok // 2, 2 * HD), BF16),
        "xo": ((micro, H * tok // 2, HD), F32),
        "xlse": ((micro, H * tok // 2, 1), F32),
        "gd": ((16, width), F32),
        "gh": ((16, HD), F32),
        "wg": ((2, nz, 4 * kr, fs), BF16),
        "wu": ((2, nz, 4 * kr, fs), BF16),
        "wd": ((2, nz, dp, width), BF16),
    }
    shapes = [jax.ShapeDtypeStruct(*v) for v in out.values()]
    scratch = [pltpu.VMEM(*out[n]) for n in ("attn", "raw", "q", "o", "ob", "lse", "kv")]
    ns = 2 * nz + 6
    n_pieces = 2 * len(halves(4 * kr)) + len(halves(dp))
    scratch += [pltpu.VMEM((micro, tok, 2 * HD), BF16), pltpu.VMEM(*out["wqkv"]), pltpu.VMEM(*out["wo"])]
    scratch += [pltpu.VMEM((2, nz, 2, 2) + gain.shape, BF16)]
    scratch += [pltpu.VMEM((4 * kr, n), BF16) for n in (qw, fs, fs)] + [pltpu.VMEM((dp, width), BF16)]
    scratch += [pltpu.VMEM((4, kp, n), BF16) for n in (qw, fs, fs) * 2]
    scratch += [pltpu.VMEM(*out[n]) for n in ("xq", "xkv", "xo", "xlse", "xq", "xq")]
    scratch += [pltpu.SemaphoreType.DMA((3,)), pltpu.SemaphoreType.DMA((3,))]
    scratch += [
        pltpu.SemaphoreType.DMA((4,)),
        pltpu.SemaphoreType.DMA((4, ns)),
        pltpu.SemaphoreType.DMA((4, ns)),
        pltpu.SemaphoreType.DMA((n_pieces,)),
        pltpu.SemaphoreType.DMA((n_pieces, 4 * ng)),
        pltpu.SemaphoreType.DMA((n_pieces, 4 * ng)),
        pltpu.SemaphoreType.DMA,
        pltpu.SemaphoreType.DMA((4 * hz,)),
        pltpu.SemaphoreType.DMA((4 * hz,)),
        pltpu.SemaphoreType.DMA((13,)),
        pltpu.SemaphoreType.DMA((3, 3)),
        pltpu.SemaphoreType.DMA((3, 4)),
        pltpu.SemaphoreType.DMA((micro, 6)),
        pltpu.SemaphoreType.DMA((micro, 6)),
    ]
    specs = [VMEM, VMEM] + [ANY] * 13 + [VMEM, VMEM] + [ANY] * 3
    got = pl.pallas_call(
        functools.partial(front_kernel, nz),
        out_shape=shapes,
        in_specs=[VMEM] * 3 + [pl.BlockSpec(memory_space=pltpu.SMEM)] + [VMEM] * 3 + [ANY] * 2 + [VMEM] * 3,
        out_specs=specs,
        scratch_shapes=scratch,
        compiler_params=pltpu.CompilerParams(collective_id=5, has_side_effects=True, vmem_limit_bytes=60 * 2**20),
    )(x, cosine, sine, lengths, wq, wk, wv, wo, gain, wg, wu, wd)
    return dict(zip(out, got))


def back_kernel(
    nz, db_ref, h1_ref, dy_ref, x_ref, cos_ref, sin_ref, len_ref, gd_ref, gh_ref, dgp_ref,
    attn_h, raw_h, q_h, o_h, ob_h, lse_h, kv_h, wqkv_h, wo_h, xq_h, xkv_h, xo_h, xlse_h, gg, gu, gdn,
    dx_o, q_o, k_o, v_o, wo_o, gain_o, wg_o, wu_o, wd_o,
    attn, raw, q_s, o_s, ob, lse, kvall, wqkv, wo, xq, xkv, xo, xlse,
    xdo, xdq, xdkv, xpart, qin, kvin, dh1, datt, do_s, delta, dqkv, da, gqkv, gwo, ggain,
    k1, k2, k3, *rest,
):
    hops = [rest[4 * i : 4 * i + 4] for i in range(4)]
    rest = rest[16:]
    wown, w1, w2, w3 = (rest[3 * i : 3 * i + 3] for i in range(4))
    q_r, kv_r, q_t, kv_t, wg_t, wu_t = rest[12:18]
    lsem, ssem, rsem, wls, wss, wrs, kss, krs, xss, xrs, qss, qrs = rest[18:]
    b, q, y, c = place()
    k = lax.axis_index("blk")
    nb = 4 * nz
    n_dev = 2 * nb
    g, e = q // 2, q % 2
    ng = nz // 2
    hz = nz // 2
    qw = gqkv.shape[3] // 4
    kr = gqkv.shape[2] // 4
    self_in = e == c
    other_x, other_y, other_c = at(1 - b, q, y, c), at(b, q, 1 - y, c), at(b, q, y, 1 - c)
    both, everything = pl.ds(0, 2), pl.ds(0, nz)
    micro, _, tok, _ = q_s.shape
    rows, width = x_ref.shape
    nt = (((1,), (1,)), ((), ()))
    tn = (((0,), (0,)), ((), ()))
    loads = []
    for i, (src, dst) in enumerate(
        ((attn_h, attn), (wo_h, wo), (o_h, o_s), (q_h, q_s), (kv_h, kvall), (lse_h, lse), (ob_h, ob), (raw_h, raw), (wqkv_h, wqkv),
         (xq_h, xq), (xkv_h, xkv), (xo_h, xo), (xlse_h, xlse))
    ):
        cp = pltpu.make_async_copy(src, dst, lsem.at[i])
        cp.start()
        loads.append(cp)
    front_barrier(nz)
    sent = []

    def start(cp):
        cp.start()
        sent.append(cp)
        return cp

    def add(dst, src, n, step):
        def one(i, _):
            sl = pl.ds(pl.multiple_of(i * step, step), step)
            dst[sl] = dst[sl] + src[sl]
            return 0

        lax.fori_loop(0, n // step, one, 0)

    quad = [(y, 1 - c), (1 - y, c), (1 - y, 1 - c)]
    t_in = []

    def trade(src, dst, s, cols):
        for p, (yy, cc) in enumerate(quad):
            there = remote(src.at[yy * 2 + cc, :, cols], dst.at[y * 2 + c, :, cols], qss.at[s, p], qrs.at[s, p], at(b, q, yy, cc))
            here = remote(src.at[yy * 2 + cc, :, cols], dst.at[yy * 2 + cc, :, cols], qss.at[s, p], qrs.at[s, p], at(b, q, yy, cc))
            start(there)
            t_in.append(here)
        dst[y * 2 + c, :, cols] = src[y * 2 + c, :, cols]

    def unpack_rows(total, kp):
        v = lax.dot_general(pack_rows(kr, kp), total, tn, preferred_element_type=F32)
        return v.astype(BF16).reshape(4, kp, total.shape[1])

    units = [(gg, wg_o, wg_t), (gu, wu_o, wu_t), (gdn, wd_o, None)]
    fs = gg.shape[4]
    near = fs // 256 * 128
    pieces = [(u, (0, gg.shape[3]), cols) for u in range(2) for cols in ((0, near), (near, fs - near))]
    pieces += [(2, r, (0, width)) for r in halves(gdn.shape[3])]
    dr = wd_o.shape[0]
    w_local, w_in = [None] * len(pieces), [None] * len(pieces)

    def part_of(j):
        u, (ro, rn), (co, cn) = pieces[j]
        return u, pl.ds(ro, rn), pl.ds(co, cn), rn

    def w_core(j):
        u, sl, cl, _ = part_of(j)
        src = units[u][0]
        w_in[j] = start(remote(src.at[:, :, 1 - c, sl, cl], w1[u].at[:, :, sl, cl], wss.at[j, 0], wrs.at[j, 0], other_c))
        w_local[j] = pltpu.make_async_copy(src.at[:, :, c, sl, cl], wown[u].at[:, :, sl, cl], wls.at[j, 0])
        w_local[j].start()

    def w_x(j):
        u, sl, cl, n = part_of(j)
        w_local[j].wait()
        w_in[j].wait_recv()
        for r in range(ng):
            add(wown[u].at[1 - b, r, sl, cl], w1[u].at[1 - b, r, sl, cl], n, 16)
        w_in[j] = start(remote(wown[u].at[1 - b, :, sl, cl], w2[u].at[:, sl, cl], wss.at[j, 1], wrs.at[j, 1], other_x))
        for r in range(ng):
            add(wown[u].at[b, r, sl, cl], w1[u].at[b, r, sl, cl], n, 16)

    def w_z(j):
        u, sl, cl, n = part_of(j)
        w_in[j].wait_recv()
        for r in range(ng):
            add(wown[u].at[b, r, sl, cl], w2[u].at[r, sl, cl], n, 16)
        waits = []
        for r in range(ng):
            gs = lax.rem(g + r, ng)
            src, dst = wown[u].at[b, gs, sl, cl], w3[u].at[r, sl, cl]
            cp = remote(src, dst, wss.at[j, 2 + r], wrs.at[j, 2 + r], at(b, gs * 2 + c, y, e))
            lc = None
            if r == 0:
                lc = pltpu.make_async_copy(src, dst, wls.at[j, 1])

                @pl.when(self_in)
                def _():
                    lc.start()

                @pl.when(jnp.logical_not(self_in))
                def _():
                    cp.start()
            else:
                start(cp)
            waits.append((cp, lc))
        w_in[j] = waits

    def w_end(j):
        u, (ro, rn), (co, cn) = pieces[j]
        for cp, lc in w_in[j]:
            if lc is not None:

                @pl.when(self_in)
                def _():
                    lc.wait()

                @pl.when(jnp.logical_not(self_in))
                def _():
                    cp.wait()
            else:
                cp.wait_recv()
        _, out, send = units[u]
        if send is None:

            def total_of(sl):
                total = w3[u][0, sl].astype(F32)
                for r in range(1, ng):
                    total = total + w3[u][r, sl].astype(F32)
                return total

            def one(i, _):
                sl = pl.ds(pl.multiple_of(ro + i * 16, 16), 16)
                out[sl] = total_of(sl)
                return 0

            end = min(ro + rn, dr)
            full = (end - ro) // 16
            lax.fori_loop(0, full, one, 0)
            if ro + full * 16 < end:
                out[ro + full * 16 : end] = total_of(pl.ds(ro + full * 16, 16))[: end - ro - full * 16]
        else:

            def one(i, _):
                cols = pl.ds(pl.multiple_of(co + i * 128, 128), 128)
                total = w3[u][0, :, cols].astype(F32)
                for r in range(1, ng):
                    total = total + w3[u][r, :, cols].astype(F32)
                send[:, :, cols] = unpack_rows(total.astype(BF16), send.shape[1])
                return 0

            lax.fori_loop(0, cn // 128, one, 0)
            trade(send, out, j, pl.ds(co, cn))

    w_core(0)
    w_core(1)

    def view_q(ref, yy, cc):
        return ref.at[:, :, :, pl.ds(pl.multiple_of((yy * 2 + cc) * qw, 128), HD)]

    def view_kv(ref, yy, cc):
        return ref.at[:, :, :, pl.ds(pl.multiple_of((yy * 2 + cc) * qw + HD, 128), qw - HD)]

    def view_lead(ref, yy, cc):
        return ref.at[:, :, yy, cc]

    items = [
        (gqkv, view_q, hops[0], None),
        (gwo, view_lead, hops[1], wo_o),
        (ggain, view_lead, hops[2], gain_o),
        (gqkv, view_kv, hops[3], None),
    ]
    item_in = [[] for _ in items]

    def join(dst, src, lead):
        for idx in lead:
            dst[idx] = dst[idx] + src[idx]

    def grid2(v):
        return [(xx, qq) for xx in range(2) for qq in range(nz)]

    def item_core(i):
        src, view, (r1, _, _, _), _ = items[i]
        for yy in range(2):
            item_in[i].append(start(remote(view(src, yy, 1 - c), r1.at[yy], ssem.at[i, yy], rsem.at[i, yy], other_c)))

    def loop2(fn):
        def one(n, _):
            fn(lax.div(n, nz), lax.rem(n, nz))
            return 0

        lax.fori_loop(0, 2 * nz, one, 0)

    def item_y(i):
        src, view, (r1, r2, _, _), _ = items[i]
        for cp in item_in[i]:
            cp.wait_recv()
        for yy in (1 - y, y):
            v = view(src, yy, c)

            def fn(xx, qq):
                v[xx, qq] = v[xx, qq] + r1[yy, xx, qq]

            loop2(fn)
            if yy is not y:
                item_in[i] = [start(remote(v, r2, ssem.at[i, 2], rsem.at[i, 2], other_y))]

    def item_x(i):
        src, view, (_, r2, r3, _), _ = items[i]
        item_in[i][0].wait_recv()
        v = view(src, y, c)

        def fn(xx, qq):
            v[xx, qq] = v[xx, qq] + r2[xx, qq]

        loop2(fn)
        item_in[i] = [start(remote(v.at[1 - b], r3, ssem.at[i, 3], rsem.at[i, 3], other_x))]

    def item_z(i):
        src, view, (_, _, r3, r4), _ = items[i]
        item_in[i][0].wait_recv()
        v = view(src, y, c)
        for qq in range(nz):
            v[b, qq] = v[b, qq] + r3[qq]
        waits = []
        for r in range(1, nz):
            qt = lax.rem(q + r, nz)
            waits.append(start(remote(v.at[b, qt], r4.at[r - 1], ssem.at[i, 3 + r], rsem.at[i, 3 + r], at(b, qt, y, c))))
        item_in[i] = waits

    def item_end(i):
        src, view, (_, _, _, r4), out = items[i]
        for cp in item_in[i]:
            cp.wait_recv()
        v = view(src, y, c)
        total = v[b, q].astype(F32)
        for r in range(1, nz):
            total = total + r4[r - 1].astype(F32)
        if i in (0, 3):
            send, dst = (q_t, q_r) if i == 0 else (kv_t, kv_r)
            send[...] = unpack_rows(total.astype(BF16), send.shape[1])
            trade(send, dst, len(pieces) + i // 3, pl.ds(0, send.shape[2]))
        else:
            out[...] = total

    gains = gd_ref[...]
    loads[0].wait()
    dy = dy_ref[...].astype(F32)
    n1, r1 = norm_of(h1_ref[...].reshape(rows, width))
    d, dg_pf = norm_back(db_ref[...].reshape(rows, width), n1, r1, 1.0 + gains[4:5])
    dh1[...] = dy + d
    n2, r2 = norm_of(attn[...])
    d, dg_pa = norm_back(dh1[...], n2, r2, 1.0 + gains[3:4])
    datt[...] = d.astype(BF16)
    w_x(0)
    w_core(2)
    w_core(3)
    loads[1].wait()
    loads[2].wait()
    for h in range(H):
        w = wo[...].reshape(H * HD, width)[h * HD : (h + 1) * HD]
        d = lax.dot_general(datt[...], w, nt, preferred_element_type=F32).astype(BF16)
        do_s[:, h] = d.reshape(micro, tok, HD)
        for m in range(micro):
            hs = slice(h * tok, (h + 1) * tok)
            delta[m, hs] = jnp.sum(d[m * tok : (m + 1) * tok].astype(F32) * o_s[m, hs], axis=-1, keepdims=True)
    ht = tok // 2
    is_first, is_mid = k == 0, k == nb // 2
    first, mid = (b, 0), (b, nb // 2)
    x_do = remote(do_s.at[:, :, :ht], xdo, xss.at[0], xrs.at[0], first)
    x_dq = remote(xdq, qin, xss.at[1], xrs.at[1], mid)
    x_dkv = remote(xdkv, kvin, xss.at[2], xrs.at[2], mid)

    @pl.when(is_mid)
    def _():
        x_do.start()

    w_x(1)
    w_core(4)
    w_core(5)
    for i in (3, 4, 5, 9, 10, 11, 12):
        loads[i].wait()

    @pl.when(is_mid)
    def _():
        x_do.wait_send()
        do_s[:, :, :ht] = jnp.zeros((micro, H, ht, HD), BF16)
        for m in range(micro):
            for h in range(H):
                delta[m, h * tok : h * tok + ht] = jnp.zeros((ht, 1), F32)


    side = q // hz
    ql = q - side * hz
    scale = HD ** (-0.5)
    lo = side * (nb // 4)
    hi = k // 2 + 1
    part = kvall

    def clear(j, _):
        part[j // 2 - side * hz, j % 2] = jnp.zeros(part.shape[2:], BF16)
        return 0

    @pl.when(jnp.logical_not(is_first))
    def _():
        lax.fori_loop(hi, (side + 1) * 2 * hz, clear, 0)

    def grads_of(qm, dom, blk, p, dl):
        dp = lax.dot_general(dom, blk[:, HD:], nt, preferred_element_type=F32)
        ds = (p * (dp - dl)).astype(BF16)
        dq = jnp.dot(ds, blk[:, :HD], preferred_element_type=F32) * scale
        dk = lax.dot_general(ds, qm, tn, preferred_element_type=F32) * scale
        dv = lax.dot_general(p.astype(BF16), dom, tn, preferred_element_type=F32)
        return dq, jnp.concatenate([dk, dv], axis=1)

    @pl.when(is_first)
    def _():
        x_do.wait_recv()
        for m in range(micro):
            qm, dom = xq[m].reshape(H * ht, HD), xdo[m].reshape(H * ht, HD)
            dl = jnp.sum(dom.astype(F32) * xo[m], axis=-1, keepdims=True)

            def one(blk, ok):
                s = lax.dot_general(qm, blk[:, :HD], nt, preferred_element_type=F32) * scale
                p = jnp.exp(s - xlse[m]) if ok is None else jnp.where(ok, jnp.exp(jnp.where(ok, s, -1e30) - xlse[m]), 0.0)
                return grads_of(qm, dom, blk, p, dl)

            dq, g0 = one(kvall[0, 0, :, m].reshape(256, 2 * HD), None)
            xpart[m] = g0.astype(BF16)

            def body(j, dq):
                d, g = one(kvall[j // 2, j % 2, :, m].reshape(256, 2 * HD), None)
                part[j // 2, j % 2, :, m] = g.astype(BF16).reshape(2, tok, 2 * HD)
                return dq + d

            dq = lax.fori_loop(1, nb // 4, body, dq)
            d, g = one(xkv[m], half_mask(H * ht, ht))
            xdq[m] = (dq + d).astype(BF16).reshape(H, ht, HD)
            xdkv[m] = g.astype(BF16)
        x_dq.start()
        x_dkv.start()

    qrows = H * tok
    qidx = k * tok + lax.rem(lax.broadcasted_iota(jnp.int32, (qrows, 1), 0), tok)
    dq_s = o_s
    for m in range(micro):
        dq_s[m] = jnp.zeros(dq_s.shape[1:], F32)
        segq = segment_of(len_ref, m, qidx)

        def body(j, _):
            qm, dom = q_s[m].reshape(qrows, HD), do_s[m].reshape(qrows, HD)
            blk = kvall[j // 2 - side * hz, j % 2, :, m].reshape(256, 2 * HD)
            kidx = j * 256 + lax.broadcasted_iota(jnp.int32, (1, 256), 1)
            s, ok = chunk_scores(qm, blk[:, :HD], segq, segment_of(len_ref, m, kidx), qidx, j, scale)
            p = jnp.where(ok, jnp.exp(jnp.where(ok, s, -1e30) - lse[m]), 0.0)
            dq, g = grads_of(qm, dom, blk, p, delta[m])
            dq_s[m] += dq
            part[j // 2 - side * hz, j % 2, :, m] = g.astype(BF16).reshape(2, tok, 2 * HD)
            return 0

        lax.fori_loop(lo, hi, body, 0)

        @pl.when(is_first)
        def _():
            g = part[0, 0, :, m].reshape(256, 2 * HD).astype(F32) + xpart[m].astype(F32)
            part[0, 0, :, m] = g.astype(BF16).reshape(2, tok, 2 * HD)

        w_z(m)
        w_x(m + 2)

    k_in = start(remote(part.at[:, :, 1 - c], k1, kss.at[0], krs.at[0], other_c))
    loads[6].wait()
    obt = [ob[:, h * HD : (h + 1) * HD].T for h in range(H)]
    per = gwo.shape[0] * gwo.shape[1] * 4 // H
    for h in range(H):
        for o, n in tiles(width, 384):
            v = jnp.dot(obt[h], datt[:, o : o + n], preferred_element_type=F32).astype(BF16)
            n_lead = (2 * nz) // H
            xx, qq = (h * n_lead) // nz, (h * n_lead) % nz
            gwo[xx, qq : qq + n_lead, :, :, :, o : o + n] = v.reshape(n_lead, 2, 2, gwo.shape[4], n)
    item_core(1)
    k_in.wait_recv()

    def add1(n, _):
        part[n // 2, n % 2, c] = part[n // 2, n % 2, c] + k1[n // 2, n % 2]
        return 0

    lax.fori_loop(0, 2 * hz, add1, 0)
    k_in = start(remote(part.at[:, 1 - y, c], k2, kss.at[1], krs.at[1], other_y))
    loads[7].wait()
    cosine, sine = cos_ref[...], sin_ref[...]
    half = HD // 2
    gh = gh_ref[...]

    def unrotate(z):
        z1, z2 = z[:, :half], z[:, half:]
        return jnp.concatenate([z1 * cosine + z2 * sine, z2 * cosine - z1 * sine], axis=1)

    @pl.when(is_mid)
    def _():
        x_dq.wait_recv()
        for h in range(H):
            dq_s[:, h * tok : h * tok + ht] = qin[:, h].astype(F32)

    dg_q = jnp.zeros((1, HD), F32)
    for h in range(H):
        z = unrotate(dq_s[:, h * tok : (h + 1) * tok].reshape(rows, HD))
        n3, r3 = norm_of(raw[:, h * HD : (h + 1) * HD])
        d, dg = norm_back(z, n3, r3, 1.0 + gh[1:2])
        dqkv[:, h * qw : h * qw + HD] = d.astype(BF16)
        dg_q = dg_q + dg
    w_z(2)
    w_x(4)
    k_in.wait_recv()

    def add2(n, _):
        part[n, y, c] = part[n, y, c] + k2[n]
        return 0

    lax.fori_loop(0, hz, add2, 0)
    k_last = []
    for r in range(1, hz):
        qt = lax.rem(ql + r, hz)
        t = at(b, side * hz + qt, y, c)
        k_last.append(start(remote(part.at[qt, y, c], k3.at[r - 1], kss.at[1 + r], krs.at[1 + r], t)))
    item_y(1)
    n_x, r_x = norm_of(x_ref[...].astype(F32))
    at_ = (n_x * (1.0 + gains[0:1])).astype(BF16).T

    def weight_grad(o, n):
        v = jnp.dot(at_, dqkv[:, o : o + n], preferred_element_type=F32).astype(BF16)
        gqkv[:, :, :, o : o + n] = v.reshape(gqkv.shape[:3] + (n,))

    for h in range(H):
        weight_grad(h * qw, HD)
    item_core(0)
    w_z(3)
    w_x(5)
    w_end(0)
    total = part[ql, y, c].astype(F32)
    for r, cp in enumerate(k_last):
        cp.wait_recv()
        total = total + k3[r].astype(F32)

    dq_s[:, :tok] = total[:, :, :HD]
    dq_s[:, tok : 2 * tok] = total[:, :, HD:]

    @pl.when(is_mid)
    def _():
        x_dkv.wait_recv()
        dq_s[:, :ht] += kvin[:, :, :HD].astype(F32)
        dq_s[:, tok : tok + ht] += kvin[:, :, HD:].astype(F32)

    d_key, d_value = dq_s[:, :tok].reshape(rows, HD), dq_s[:, tok : 2 * tok].reshape(rows, HD)
    n3, r3 = norm_of(raw[:, H * HD :])
    d, dg_k = norm_back(unrotate(d_key), n3, r3, 1.0 + gh[2:3])
    for i, z in enumerate((d, d_value)):
        for o, v in zip(kv_columns(i, qw), (z[:, :half], z[:, half:])):
            dqkv[:, o : o + half] = v.astype(BF16)
            weight_grad(o, half)
    item_core(3)
    loads[8].wait()
    quads_at_once = max(1, 256 // wqkv.shape[2])
    for xx in range(2):
        for qq in range(0, nz, quads_at_once):
            n = min(quads_at_once, nz - qq)
            w = wqkv[xx, qq : qq + n].reshape(n * wqkv.shape[2], wqkv.shape[3])
            o = (xx * nz + qq) * wqkv.shape[2]
            da[o : o + n * wqkv.shape[2], :] = lax.dot_general(w, dqkv[...], nt, preferred_element_type=F32)
    d, dg_in = norm_back(da[...].T, n_x, r_x, 1.0 + gains[0:1])
    dx_o[...] = (dh1[...] + d).astype(BF16).reshape(dx_o.shape)
    none = jnp.zeros((1, width), F32)
    nohd = jnp.zeros((1, HD), F32)
    wide = jnp.concatenate([dg_in, none, none, dg_pa, dg_pf, dgp_ref[...], none, none], axis=0)
    slim = jnp.concatenate([nohd, dg_q, dg_k] + [nohd] * 5, axis=0)
    ggain[...] = (collect_gains(wide, n_dev) + collect_gains(slim, n_dev)).reshape(ggain.shape)
    item_core(2)
    item_x(1)
    item_y(0)
    item_y(3)
    item_y(2)
    w_end(1)
    w_z(4)
    item_z(1)
    w_end(2)
    w_z(5)
    item_x(0)
    item_x(3)
    item_x(2)
    w_end(3)
    item_z(0)
    item_z(3)
    item_z(2)
    item_end(1)
    w_end(4)
    w_end(5)
    item_end(0)
    item_end(3)
    item_end(2)
    for cp in t_in:
        cp.wait_recv()
    for j in range(4):
        q_o[:, j * HD : (j + 1) * HD] = q_r[j, :kr].astype(F32)
        half_o = k_o if j < 2 else v_o
        half_o[:, j % 2 * half : (j % 2 + 1) * half] = kv_r[j, :kr].astype(F32)
    for cp in sent:
        cp.wait_send()

    @pl.when(is_first)
    def _():
        x_dq.wait_send()
        x_dkv.wait_send()


def back(nz, db, h1, dy, x, cosine, sine, lengths, dgp, f, gg, gu, gd, kp, dr):
    ng = nz // 2
    hz = nz // 2
    nb = 4 * nz
    micro, tok, width = db.shape
    rows = micro * tok
    qr = f["wqkv"].shape[2]
    qw = f["wqkv"].shape[3] // 4
    orow = f["wo"].shape[4]
    kv = f["kv"].shape

    def like(n):
        return pltpu.VMEM(f[n].shape, f[n].dtype)

    gsplit = [z.reshape(2, ng, 2, -1, z.shape[-1]) for z in (gg, gu, gd)]
    ublock = [gsplit[i].shape[3:] for i in (2, 0, 1)]
    iblock = [((qr, HD), BF16), ((orow, width), BF16), ((8, 128), F32), ((qr, qw - HD), BF16)]
    scratch = [like(n) for n in ("attn", "raw", "q", "o", "ob", "lse", "kv", "wqkv", "wo", "xq", "xkv", "xo", "xlse")]
    scratch += [like("xq"), like("xq"), like("xkv"), pltpu.VMEM((micro, 256, 2 * HD), BF16), like("xq"), like("xkv")]
    scratch += [
        pltpu.VMEM((rows, width), F32),
        pltpu.VMEM((rows, width), BF16),
        pltpu.VMEM((micro, H, tok, HD), BF16),
        pltpu.VMEM((micro, H * tok, 1), F32),
        pltpu.VMEM((rows, (H + 2) * HD), BF16),
        pltpu.VMEM((width, rows), F32),
        pltpu.VMEM((2, nz, qr, 4 * qw), BF16),
        pltpu.VMEM((2, nz, 2, 2, orow, width), BF16),
        pltpu.VMEM((2, nz, 2, 2, 8, 128), F32),
        pltpu.VMEM((hz, 2) + kv[3:], BF16),
        pltpu.VMEM((hz,) + kv[3:], BF16),
        pltpu.VMEM((hz - 1,) + kv[3:], BF16),
    ]
    for s, t in iblock:
        scratch += [pltpu.VMEM(lead + s, t) for lead in ((2, 2, nz), (2, nz), (nz,), (nz - 1,))]
    for lead in ((2, ng), (2, ng), (ng,), (ng,)):
        scratch += [pltpu.VMEM(lead + ublock[i], BF16) for i in (1, 2, 0)]
    fs = ublock[1][1]
    scratch += [pltpu.VMEM((4, kp, n), BF16) for n in (HD, qw - HD)]
    scratch += [pltpu.VMEM((4, kp, n), BF16) for n in (HD, qw - HD, fs, fs)]
    n_pieces = 4 + len(halves(ublock[0][0]))
    scratch += [
        pltpu.SemaphoreType.DMA((13,)),
        pltpu.SemaphoreType.DMA((4, nz + 3)),
        pltpu.SemaphoreType.DMA((4, nz + 3)),
        pltpu.SemaphoreType.DMA((n_pieces, 2)),
        pltpu.SemaphoreType.DMA((n_pieces, 2 + ng)),
        pltpu.SemaphoreType.DMA((n_pieces, 2 + ng)),
        pltpu.SemaphoreType.DMA((hz + 1,)),
        pltpu.SemaphoreType.DMA((hz + 1,)),
        pltpu.SemaphoreType.DMA((3,)),
        pltpu.SemaphoreType.DMA((3,)),
        pltpu.SemaphoreType.DMA((n_pieces + 2, 3)),
        pltpu.SemaphoreType.DMA((n_pieces + 2, 3)),
    ]
    out = [
        jax.ShapeDtypeStruct((micro, tok, width), BF16),
        jax.ShapeDtypeStruct((qr // 4, H * HD), F32),
        jax.ShapeDtypeStruct((qr // 4, HD), F32),
        jax.ShapeDtypeStruct((qr // 4, HD), F32),
        jax.ShapeDtypeStruct((orow, width), F32),
        jax.ShapeDtypeStruct((8, 128), F32),
        jax.ShapeDtypeStruct((4, kp, fs), BF16),
        jax.ShapeDtypeStruct((4, kp, fs), BF16),
        jax.ShapeDtypeStruct((dr, width), F32),
    ]
    return pl.pallas_call(
        functools.partial(back_kernel, nz),
        out_shape=out,
        in_specs=[VMEM] * 6 + [pl.BlockSpec(memory_space=pltpu.SMEM)] + [VMEM] * 3 + [ANY] * 16,
        out_specs=[VMEM] * 9,
        scratch_shapes=scratch,
        compiler_params=pltpu.CompilerParams(collective_id=6, has_side_effects=True, vmem_limit_bytes=63 * 2**20),
    )(
        db, h1, dy, x, cosine, sine, lengths, f["gd"], f["gh"], dgp,
        f["attn"], f["raw"], f["q"], f["o"], f["ob"], f["lse"], f["kv"], f["wqkv"], f["wo"],
        f["xq"], f["xkv"], f["xo"], f["xlse"], *gsplit,
    )


def scaled_norm(values, gain):
    return values * lax.rsqrt(jnp.mean(values * values, axis=-1, keepdims=True) + epsilon) * (1.0 + gain)


def segments(lengths, index):
    docs = lengths.shape[1]
    ends = [sum(lengths[:, j] for j in range(i + 1)) for i in range(docs)]
    seg = jnp.zeros((lengths.shape[0], index.shape[0]), jnp.int32)
    first = jnp.zeros_like(seg)
    for i in range(docs):
        past = index[None, :] >= ends[i][:, None]
        seg = seg + past.astype(jnp.int32)
        first = first + jnp.where(past, lengths[:, i][:, None], 0)
    return seg, index[None, :] - first


def rotate(values, cosine, sine):
    half = values.shape[-1] // 2
    a, b = values[..., :half], values[..., half:]
    return jnp.concatenate([a * cosine - b * sine, b * cosine + a * sine], axis=-1)


def middle(attn_value, x_value, gain_attn, gain_pre):
    hidden = x_value + scaled_norm(attn_value, gain_attn)
    return (hidden, scaled_norm(hidden, gain_pre))


def layer_apart(tokens, cotangent, doc_lengths, w_query, w_key, w_value, w_out, w_gate, w_up, w_down, *gains):
    nb = lax.axis_size("blk")
    nz = nb // 4
    me = lax.axis_index("blk")
    _, micro, tok, width = tokens.shape
    n_dev = 2 * nb
    nq = 2 * nz
    kr = w_gate.shape[0]
    qr, qp = 4 * kr, up16(4 * kr)
    dr = w_down.shape[0]
    dp = up16(dr)
    orow = w_out.shape[0]
    op = up16(orow)
    groups = [[4 * i + j for j in range(4)] for i in range(nz)]

    def fit(x, rows):
        return x if x.shape[0] == rows else jnp.pad(x, ((0, rows - x.shape[0]), (0, 0)))

    def slices(w):
        w = jnp.pad(w.reshape(kr, nq, 4, dr), ((0, 0), (0, 0), (0, 0), (0, dp - dr)))
        return w.transpose(2, 0, 1, 3).reshape(4, kr, nq * dp)

    fs = nq * dp
    w_qkv = jnp.concatenate([w_query, w_key, w_value], axis=1)
    qw = w_qkv.shape[1] // 4
    pack = jnp.concatenate([slices(w_gate), slices(w_up), w_qkv.reshape(kr, 4, qw).transpose(1, 0, 2)], axis=2)
    pack = lax.all_to_all(pack, "blk", split_axis=0, concat_axis=0, axis_index_groups=groups, tiled=True)
    pack = fit(pack.reshape(qr, 2 * fs + qw), qp)
    wide = [gain.shape[0] for gain in gains]
    flat = jnp.concatenate(gains)
    flat = jnp.pad(flat, (0, 16 * 128 - flat.shape[0])).reshape(16, 128)

    qkv_f, wo_f, gain_f, wg_f, wu_f, wd_f = gather_all(
        nz, pack[:, 2 * fs :], fit(w_out, op), flat, pack[:, :fs], pack[:, fs : 2 * fs], fit(w_down, dp)
    )
    wqkv = qkv_f[:, :, :qr].reshape(width, 4 * qw)
    wo = wo_f[:, :, :, :, :orow].reshape(n_dev * orow, width)
    wg = wg_f[:, :, :qr].reshape(width, fs)
    wu = wu_f[:, :, :qr].reshape(width, fs)
    wd = wd_f.reshape(fs, width)
    gain_rows = gain_f.reshape(n_dev, 16 * 128)
    full_gains, o = [], 0
    for w in wide:
        full_gains.append(gain_rows[:, o : o + w].reshape(n_dev * w).astype(F32))
        o += w
    gain_in, gain_query, gain_key, gain_attn, gain_pre, gain_post = full_gains

    lengths = doc_lengths[0]
    seg_all, pos_all = segments(lengths, jnp.arange(nb * tok, dtype=jnp.int32))
    seg_me, pos = segments(lengths, me * tok + jnp.arange(tok, dtype=jnp.int32))
    segq = jnp.tile(seg_me, (1, H))[:, :, None]
    segk = seg_all.reshape(micro, nb * tok // 256, 1, 256)
    freq = 1000000.0 ** (-(jnp.arange(HD // 2, dtype=F32) * 2.0 / HD))
    angle = pos.reshape(micro * tok).astype(F32)[:, None] * freq[None, :]
    cosine, sine = jnp.cos(angle), jnp.sin(angle)

    rows = micro * tok
    x = tokens[0].reshape(rows, width).astype(F32)
    dy = cotangent[0].reshape(rows, width)
    normed, pre_pull = jax.vjp(scaled_norm, x, gain_in)
    a = normed.astype(BF16)
    qkv = jnp.dot(a, wqkv, preferred_element_type=F32)
    n_q = H * HD
    q_raw = qkv[:, :n_q].reshape(rows, H, HD)
    k_raw = qkv[:, n_q : n_q + HD]
    v = qkv[:, n_q + HD :].astype(BF16)
    queries, query_pull = jax.vjp(
        lambda r, g: rotate(scaled_norm(r, g), cosine[:, None], sine[:, None]), q_raw, gain_query
    )
    keys, key_pull = jax.vjp(lambda r, g: rotate(scaled_norm(r, g), cosine, sine), k_raw, gain_key)

    def by_head(z):
        return z.reshape(micro, tok, H, HD).transpose(0, 2, 1, 3).reshape(micro, H * tok, HD)

    def by_row(z):
        return z.reshape(micro, H, tok, HD).transpose(0, 2, 1, 3).reshape(rows, H * HD)

    qh = by_head(queries.astype(BF16))
    kv = jnp.concatenate([keys.astype(BF16), v], axis=1).reshape(micro, tok, 2 * HD)
    oh, lse, kvall = attn_fwd(nb, qh, kv, segq, segk)
    o_b = by_row(oh.astype(BF16))
    attn = jnp.dot(o_b, wo, preferred_element_type=F32)
    (h1, ffn_in), mid_pull = jax.vjp(middle, attn, x, gain_attn, gain_pre)

    shape = (micro, tok, width)
    out, db, dg_post, gg, gu, gd = ffn(
        ffn_in.astype(BF16).reshape(shape), h1.reshape(shape), dy.reshape(shape), gain_post[None, :], wg, wu, wd
    )
    d_attn, d_x_mid, dg_attn, dg_pre = mid_pull((dy.astype(F32), db.reshape(rows, width)))
    d_attn = d_attn.astype(BF16)
    grad_out = lax.dot_general(o_b, d_attn, (((0,), (0,)), ((), ())), preferred_element_type=F32).astype(BF16)
    do = lax.dot_general(d_attn, wo, (((1,), (1,)), ((), ())), preferred_element_type=F32).astype(BF16)
    doh = by_head(do)
    delta = jnp.sum(doh.astype(F32) * oh, axis=-1, keepdims=True)
    dqh, dkv = attn_bwd(nb, qh, kvall, doh, lse, delta, segq, segk)
    dkv = dkv.reshape(rows, 2 * HD)
    dq_raw, dg_query = query_pull(by_row(dqh).reshape(rows, H, HD))
    dk_raw, dg_key = key_pull(dkv[:, :HD])
    d_qkv = jnp.concatenate([dq_raw.reshape(rows, n_q), dk_raw, dkv[:, HD:]], axis=1).astype(BF16)
    grad_qkv = lax.dot_general(a, d_qkv, (((0,), (0,)), ((), ())), preferred_element_type=F32).astype(BF16)
    da = lax.dot_general(d_qkv, wqkv, (((1,), (1,)), ((), ())), preferred_element_type=F32)
    d_x_pre, dg_in = pre_pull(da)
    d_x = (d_x_mid + d_x_pre).astype(BF16)

    def quads(z, r, p):
        z = z.reshape(2, nz, r, z.shape[-1])
        return z if r == p else jnp.pad(z, ((0, 0), (0, 0), (0, p - r), (0, 0)))

    go = grad_out.reshape(2, nz, 2, 2, orow, width)
    if op != orow:
        go = jnp.pad(go, ((0, 0),) * 4 + ((0, op - orow), (0, 0)))
    dgains = jnp.concatenate(
        [d.reshape(n_dev, w) for d, w in zip((dg_in, dg_query, dg_key, dg_attn, dg_pre, dg_post[0]), wide)], axis=1
    )
    used = dgains.shape[1]
    dgains = jnp.pad(dgains, ((0, 0), (0, 8 * 128 - used))).reshape(2, nz, 2, 2, 8, 128)
    s_qkv, s_wo, s_gain, s_wg, s_wu, s_wd = reduce_all(
        nz, quads(grad_qkv, qr, qp), go, dgains, quads(gg, qr, qp), quads(gu, qr, qp), gd.reshape(2, nz, dp, width)
    )
    back = jnp.concatenate([s_wg, s_wu, s_qkv], axis=1)[:qr].reshape(4, kr, 2 * fs + qw)
    back = lax.all_to_all(back, "blk", split_axis=0, concat_axis=0, axis_index_groups=groups, tiled=True)
    back = back.astype(F32)

    def rows_of(z):
        z = z.reshape(4, kr, nq, dp)[..., :dr]
        return z.transpose(1, 2, 0, 3).reshape(kr, nq * 4 * dr)

    s_qkv = back[:, :, 2 * fs :].transpose(1, 0, 2).reshape(kr, 4 * qw)
    flat = s_gain.reshape(-1)
    gain_grads, o = [], 0
    for w in wide:
        gain_grads.append(flat[o : o + w])
        o += w
    return (
        out[None],
        d_x.reshape(shape)[None],
        s_qkv[:, :n_q],
        s_qkv[:, n_q : n_q + HD],
        s_qkv[:, n_q + HD :],
        s_wo[:orow],
        rows_of(back[:, :, :fs]),
        rows_of(back[:, :, fs : 2 * fs]),
        s_wd[:dr],
        *gain_grads,
    )


def layer_fused(tokens, cotangent, doc_lengths, w_query, w_key, w_value, w_out, w_gate, w_up, w_down, *gains):
    nb = lax.axis_size("blk")
    nz = nb // 4
    me = lax.axis_index("blk")
    _, micro, tok, width = tokens.shape
    rows = micro * tok
    nq = 2 * nz
    kr, dr = w_gate.shape[0], w_down.shape[0]
    kp, dp = up16(kr), up16(dr)
    shape = (micro, tok, width)

    flat = jnp.stack([jnp.pad(gain, (0, 128 - gain.shape[0])) for gain in gains] + [jnp.zeros((128,), BF16)] * 10)
    lengths = doc_lengths[0]
    _, pos = segments(lengths, me * tok + jnp.arange(tok, dtype=jnp.int32))
    freq = 1000000.0 ** (-(jnp.arange(HD // 2, dtype=F32) * 2.0 / HD))
    angle = pos.reshape(rows).astype(F32)[:, None] * freq[None, :]
    cosine, sine = jnp.cos(angle), jnp.sin(angle)
    x = tokens[0].reshape(rows, width)
    dy = cotangent[0]
    f = front(nz, x, cosine, sine, lengths, w_query, w_key, w_value, w_out, flat, w_gate, w_up, w_down, dp, micro)
    wg, wu, wd = (f[n].reshape(-1, f[n].shape[-1]) for n in ("wg", "wu", "wd"))
    fine = (2 * micro, tok // 2, width)
    out, db, dg_post, gg, gu, gd = mlp(f["ball"], f["h1"].reshape(fine), dy.reshape(fine), f["gd"], wg, wu, wd)
    out, db = out.reshape(shape), db.reshape(shape)
    d_x, s_q, s_k, s_v, s_wo, s_gain, s_wg, s_wu, s_wd = back(
        nz, db, f["h1"], dy.reshape(rows, width), x, cosine, sine, lengths, dg_post, f, gg, gu, gd, kp, dr
    )

    def rows_of(z):
        z = z[:, :kr].reshape(4, kr, nq, dp)[..., :dr].astype(F32)
        return z.transpose(1, 2, 0, 3).reshape(kr, nq * 4 * dr)

    return (
        out[None],
        d_x[None],
        s_q,
        s_k,
        s_v,
        s_wo,
        rows_of(s_wg),
        rows_of(s_wu),
        s_wd,
        *(s_gain[i, : gain.shape[0]] for i, gain in enumerate(gains)),
    )


def shards(tokens, cotangent, doc_lengths, *params):
    nb = lax.axis_size("blk")
    w_out, w_gate = params[3], params[4]
    fits = nb * tokens.shape[2] <= 2048 and (4 * w_gate.shape[0]) % 16 == 0 and w_out.shape[0] % 16 == 0
    layer = layer_fused if fits else layer_apart
    return layer(tokens, cotangent, doc_lengths, *params)


def solution(mesh):
    sequence = P("bucket", None, "blk", None)
    split = ("bucket", "blk")
    return jax.shard_map(
        shards,
        mesh=mesh,
        in_specs=(sequence, sequence, P("bucket", None, None)) + (P(split, None),) * 7 + (P(split),) * 6,
        out_specs=(sequence, sequence) + (P(split, None),) * 7 + (P(split),) * 6,
        check_vma=False,
    )
```

```python
import functools
import math

import jax
import jax.numpy as jnp
from jax import lax
from jax.experimental import pallas as pl
from jax.experimental.pallas import tpu as pltpu
from jax.sharding import PartitionSpec as P

H = 4
HD = 256
F32 = jnp.float32
BF16 = jnp.bfloat16
MESH = pl.DeviceIdType.MESH
ANY = pl.BlockSpec(memory_space=pl.ANY)
VMEM = pl.BlockSpec(memory_space=pltpu.VMEM)
epsilon = 1e-06


def up16(n):
    return -(-n // 16) * 16


def place():
    b = lax.axis_index("bucket")
    k = lax.axis_index("blk")
    return b, k // 4, (k // 2) % 2, k % 2


def at(b, q, y, c):
    return (b, q * 4 + y * 2 + c)


def greet(targets):
    bar = pltpu.get_barrier_semaphore()
    for t in targets:
        pl.semaphore_signal(bar, inc=1, device_id=t, device_id_type=MESH)
    return bar


def remote(src, dst, send, recv, target):
    return pltpu.make_async_remote_copy(src, dst, send, recv, device_id=target, device_id_type=MESH)


def gather_kernel(nz, qkv, wo, gain, wg, wu, wd, qkv_f, wo_f, gain_f, wg_f, wu_f, wd_f, lsem, ssem, rsem, wls, wss, wrs):
    b, q, y, c = place()
    g, e = q // 2, q % 2
    ng = nz // 2
    qw = qkv.shape[1]
    self_in = e == c
    bar = greet(
        [at(b, lax.rem(q + r, nz), y, c) for r in range(1, nz)]
        + [at(1 - b, q, y, c), at(b, q, 1 - y, c), at(b, q, y, 1 - c)]
        + [at(b, lax.rem(g + r, ng) * 2 + c, y, e) for r in range(1, ng)]
    )
    first = at(b, g * 2 + c, y, e)

    @pl.when(jnp.logical_not(self_in))
    def _():
        pl.semaphore_signal(bar, inc=1, device_id=first, device_id_type=MESH)

    pl.semaphore_wait(bar, nz + 1 + ng - jnp.where(self_in, 1, 0) + 1)

    everything = pl.ds(0, nz)

    def view_qkv(ref, yy, cc, xx, qq):
        return ref.at[xx, qq, :, pl.ds(pl.multiple_of((yy * 2 + cc) * qw, 128), qw)]

    def view_lead(ref, yy, cc, xx, qq):
        return ref.at[xx, qq, yy, cc]

    items = [(qkv, qkv_f, view_qkv), (wo, wo_f, view_lead), (gain, gain_f, view_lead)]
    sent = []
    local = []
    for i, (src, dst, view) in enumerate(items):
        cp = pltpu.make_async_copy(src, view(dst, y, c, b, q), lsem.at[i])
        cp.start()
        local.append(cp)
    z_in = []
    for i, (src, dst, view) in enumerate(items):
        row = []
        for r in range(1, nz):
            cp = remote(src, view(dst, y, c, b, q), ssem.at[i, r], rsem.at[i, r], at(b, lax.rem(q + r, nz), y, c))
            cp.start()
            sent.append(cp)
            row.append(
                remote(src, view(dst, y, c, b, lax.rem(q - r + nz, nz)), ssem.at[i, r], rsem.at[i, r], at(b, lax.rem(q + r, nz), y, c))
            )
        z_in.append(row)
    x_in = [[] for _ in items]
    for i, (src, dst, view) in enumerate(items):
        cp = remote(src, view(dst, y, c, b, q), ssem.at[i, nz], rsem.at[i, nz], at(1 - b, q, y, c))
        cp.start()
        sent.append(cp)
        x_in[i].append(remote(src, view(dst, y, c, 1 - b, q), ssem.at[i, nz], rsem.at[i, nz], at(1 - b, q, y, c)))

    units = [(wg, wg_f), (wu, wu_f), (wd, wd_f)]
    u_in = []
    for j, (src, dst) in enumerate(units):
        row = []
        for r in range(ng):
            target = at(b, lax.rem(g + r, ng) * 2 + c, y, e)
            cp = remote(src, dst.at[b, q], wss.at[j, r], wrs.at[j, r], target)
            qs = lax.rem(g - r + ng, ng) * 2 + c
            inc = remote(src, dst.at[b, qs], wss.at[j, r], wrs.at[j, r], target)
            if r == 0:
                lc = pltpu.make_async_copy(src, dst.at[b, q], wls.at[j])

                @pl.when(self_in)
                def _():
                    lc.start()

                @pl.when(jnp.logical_not(self_in))
                def _():
                    cp.start()
            else:
                cp.start()
            row.append((cp, inc, qs, lc if r == 0 else None))
        u_in.append(row)

    for r in range(1, nz):
        qs = lax.rem(q - r + nz, nz)
        for i, (src, dst, view) in enumerate(items):
            z_in[i][r - 1].wait_recv()
            cp = remote(view(dst, y, c, b, qs), view(dst, y, c, b, qs), ssem.at[i, nz + r], rsem.at[i, nz + r], at(1 - b, q, y, c))
            cp.start()
            sent.append(cp)
            x_in[i].append(
                remote(view(dst, y, c, b, qs), view(dst, y, c, 1 - b, qs), ssem.at[i, nz + r], rsem.at[i, nz + r], at(1 - b, q, y, c))
            )
    for cp in local:
        cp.wait()
    y_in = [[] for _ in items]
    for half in range(2):
        for i, (src, dst, view) in enumerate(items):
            xx = b if half == 0 else 1 - b
            if half == 1:
                for cp in x_in[i]:
                    cp.wait_recv()
            s = 2 * nz + half
            cp = remote(view(dst, y, c, xx, everything), view(dst, y, c, xx, everything), ssem.at[i, s], rsem.at[i, s], at(b, q, 1 - y, c))
            cp.start()
            sent.append(cp)
            y_in[i].append(
                remote(view(dst, y, c, xx, everything), view(dst, 1 - y, c, xx, everything), ssem.at[i, s], rsem.at[i, s], at(b, q, 1 - y, c))
            )
    c_in = []

    def to_core(i, yy, s):
        _, dst, view = items[i]
        both = pl.ds(0, 2)
        cp = remote(view(dst, yy, c, both, everything), view(dst, yy, c, both, everything), ssem.at[i, s], rsem.at[i, s], at(b, q, y, 1 - c))
        cp.start()
        sent.append(cp)
        c_in.append(
            remote(view(dst, yy, c, both, everything), view(dst, yy, 1 - c, both, everything), ssem.at[i, s], rsem.at[i, s], at(b, q, y, 1 - c))
        )

    for i in range(len(items)):
        to_core(i, y, 2 * nz + 2)
    for i in range(len(items)):
        for cp in y_in[i]:
            cp.wait_recv()
        to_core(i, 1 - y, 2 * nz + 3)

    d_in = []

    def unit_on(j, xx, qs, s, target, yours):
        _, dst = units[j]
        cp = remote(dst.at[xx, qs], dst.at[xx, qs], wss.at[j, s], wrs.at[j, s], target)
        cp.start()
        sent.append(cp)
        return remote(dst.at[xx, qs], dst.at[yours[0], yours[1]], wss.at[j, s], wrs.at[j, s], target)

    xw = [[] for _ in units]

    def x_round(j):
        for r in range(ng):
            cp, inc, qs, lc = u_in[j][r]
            if r == 0:

                @pl.when(self_in)
                def _():
                    lc.wait()

                @pl.when(jnp.logical_not(self_in))
                def _():
                    inc.wait_recv()
            else:
                inc.wait_recv()
            xw[j].append(unit_on(j, b, qs, ng + r, at(1 - b, q, y, c), (1 - b, qs)))
        for r in range(ng):
            qs = u_in[j][r][2]
            qo = lax.rem(g - r + ng, ng) * 2 + 1 - c
            d_in.append(unit_on(j, b, qs, 2 * ng + r, at(b, q, y, 1 - c), (b, qo)))

    def c_round(j):
        for r in range(ng):
            qs = u_in[j][r][2]
            qo = lax.rem(g - r + ng, ng) * 2 + 1 - c
            xw[j][r].wait_recv()
            d_in.append(unit_on(j, 1 - b, qs, 3 * ng + r, at(b, q, y, 1 - c), (1 - b, qo)))

    x_round(0)
    x_round(1)
    c_round(0)
    x_round(2)
    c_round(1)
    c_round(2)
    for cp in c_in + d_in:
        cp.wait_recv()
    for cp in sent:
        cp.wait_send()
    for j in range(len(units)):
        for r in range(ng):
            cp = u_in[j][r][0]
            if r == 0:

                @pl.when(jnp.logical_not(self_in))
                def _():
                    cp.wait_send()
            else:
                cp.wait_send()


def gather_all(nz, qkv, wo, gain, wg, wu, wd):
    ng = nz // 2
    out = [
        jax.ShapeDtypeStruct((2, nz, qkv.shape[0], 4 * qkv.shape[1]), BF16),
        jax.ShapeDtypeStruct((2, nz, 2, 2) + wo.shape, BF16),
        jax.ShapeDtypeStruct((2, nz, 2, 2) + gain.shape, BF16),
        jax.ShapeDtypeStruct((2, nz) + wg.shape, BF16),
        jax.ShapeDtypeStruct((2, nz) + wu.shape, BF16),
        jax.ShapeDtypeStruct((2, nz) + wd.shape, BF16),
    ]
    ns = 2 * nz + 4
    return pl.pallas_call(
        functools.partial(gather_kernel, nz),
        out_shape=out,
        in_specs=[ANY] * 6,
        out_specs=[ANY] * 6,
        scratch_shapes=[
            pltpu.SemaphoreType.DMA((3,)),
            pltpu.SemaphoreType.DMA((3, ns)),
            pltpu.SemaphoreType.DMA((3, ns)),
            pltpu.SemaphoreType.DMA((3,)),
            pltpu.SemaphoreType.DMA((3, 4 * ng)),
            pltpu.SemaphoreType.DMA((3, 4 * ng)),
        ],
        compiler_params=pltpu.CompilerParams(collective_id=0, has_side_effects=True),
    )(qkv, wo, gain, wg, wu, wd)


def reduce_kernel(nz, qkv, wo, gain, wg, wu, wd, qkv_o, wo_o, gain_o, wg_o, wu_o, wd_o, *scratch):
    b, q, y, c = place()
    g, e = q // 2, q % 2
    ng = nz // 2
    qw = qkv_o.shape[1]
    self_in = e == c
    n_items, n_units = 3, 3
    own = scratch[0:3]
    r1 = scratch[3:6]
    r2 = scratch[6:9]
    r3 = scratch[9:12]
    r4 = scratch[12:15]
    uown = scratch[15:18]
    u1 = scratch[18:21]
    u2 = scratch[21:24]
    u3 = scratch[24:27]
    lsem, ssem, rsem, wls, wss, wrs = scratch[27:]
    bar = greet(
        [at(b, lax.rem(q + r, nz), y, c) for r in range(1, nz)]
        + [at(1 - b, q, y, c), at(b, q, 1 - y, c), at(b, q, y, 1 - c)]
        + [at(b, lax.rem(g + r, ng) * 2 + c, y, e) for r in range(1, ng)]
    )
    first = at(b, g * 2 + c, y, e)

    @pl.when(jnp.logical_not(self_in))
    def _():
        pl.semaphore_signal(bar, inc=1, device_id=first, device_id_type=MESH)

    pl.semaphore_wait(bar, nz + 1 + ng - jnp.where(self_in, 1, 0) + 1)

    other_core = at(b, q, y, 1 - c)
    other_y = at(b, q, 1 - y, c)
    other_x = at(1 - b, q, y, c)
    full = (pl.ds(0, 2), pl.ds(0, nz))

    def view_qkv(ref, yy, cc):
        return ref.at[full[0], full[1], :, pl.ds(pl.multiple_of((yy * 2 + cc) * qw, 128), qw)]

    def view_lead(ref, yy, cc):
        return ref.at[full[0], full[1], yy, cc]

    items = [(qkv, qkv_o, view_qkv), (wo, wo_o, view_lead), (gain, gain_o, view_lead)]
    units = [(wd, wd_o), (wg, wg_o), (wu, wu_o)]
    sent = []
    item_local, item_in = [[] for _ in items], [[] for _ in items]
    unit_local, unit_in = [[] for _ in units], [[] for _ in units]

    def start(cp):
        cp.start()
        sent.append(cp)
        return cp

    def item_core(i):
        src, _, view = items[i]
        for yy in range(2):
            item_in[i].append(start(remote(view(src, yy, 1 - c), r1[i].at[yy], ssem.at[i, yy], rsem.at[i, yy], other_core)))
            cp = pltpu.make_async_copy(view(src, yy, c), own[i].at[yy], lsem.at[i, yy])
            cp.start()
            item_local[i].append(cp)

    def unit_core(j):
        src, _ = units[j]
        for xx in range(2):
            for r in range(ng):
                s = xx * ng + r
                mine, yours = r * 2 + c, r * 2 + 1 - c
                unit_in[j].append(start(remote(src.at[xx, yours], u1[j].at[xx, r], wss.at[j, s], wrs.at[j, s], other_core)))
                cp = pltpu.make_async_copy(src.at[xx, mine], uown[j].at[xx, r], wls.at[j, s])
                cp.start()
                unit_local[j].append(cp)

    def add(dst, src, lead):
        def one(n, _):
            dst[n] = (dst[n].astype(F32) + src[n].astype(F32)).astype(dst.dtype)
            return 0

        lax.fori_loop(0, lead, one, 0)

    def unit_x(j):
        for cp in unit_local[j]:
            cp.wait()
        for cp in unit_in[j]:
            cp.wait_recv()
        add(uown[j].at[1 - b], u1[j].at[1 - b], ng)
        cp = start(remote(uown[j].at[1 - b], u2[j], wss.at[j, 2 * ng], wrs.at[j, 2 * ng], other_x))
        add(uown[j].at[b], u1[j].at[b], ng)
        unit_in[j] = [cp]

    def unit_z(j):
        unit_in[j][0].wait_recv()
        add(uown[j].at[b], u2[j], ng)
        waits = []
        for r in range(ng):
            gs = lax.rem(g + r, ng)
            cp = remote(uown[j].at[b, gs], u3[j].at[r], wss.at[j, 2 * ng + 1 + r], wrs.at[j, 2 * ng + 1 + r], at(b, gs * 2 + c, y, e))
            if r == 0:
                lc = pltpu.make_async_copy(uown[j].at[b, gs], u3[j].at[0], wls.at[j, 2 * ng])

                @pl.when(self_in)
                def _():
                    lc.start()

                @pl.when(jnp.logical_not(self_in))
                def _():
                    cp.start()

                waits.append((cp, lc))
            else:
                start(cp)
                waits.append((cp, None))
        unit_in[j] = waits

    def unit_end(j):
        for cp, lc in unit_in[j]:
            if lc is not None:

                @pl.when(self_in)
                def _():
                    lc.wait()

                @pl.when(jnp.logical_not(self_in))
                def _():
                    cp.wait()
            else:
                cp.wait_recv()
        rows = u3[j].shape[1]
        step = 16

        def one(n, _):
            sl = pl.ds(pl.multiple_of(n * step, step), step)
            total = u3[j][0, sl].astype(F32)
            for r in range(1, ng):
                total = total + u3[j][r, sl].astype(F32)
            units[j][1][sl] = total.astype(units[j][1].dtype)
            return 0

        lax.fori_loop(0, rows // step, one, 0)

    def item_y(i):
        for cp in item_local[i]:
            cp.wait()
        for cp in item_in[i]:
            cp.wait_recv()
        for xx in range(2):
            add(own[i].at[1 - y, xx], r1[i].at[1 - y, xx], nz)
        cp = start(remote(own[i].at[1 - y], r2[i], ssem.at[i, 2], rsem.at[i, 2], other_y))
        for xx in range(2):
            add(own[i].at[y, xx], r1[i].at[y, xx], nz)
        item_in[i] = [cp]

    def item_x(i):
        item_in[i][0].wait_recv()
        add(own[i].at[y, 1 - b], r2[i].at[1 - b], nz)
        cp = start(remote(own[i].at[y, 1 - b], r3[i], ssem.at[i, 3], rsem.at[i, 3], other_x))
        add(own[i].at[y, b], r2[i].at[b], nz)
        item_in[i] = [cp]

    def item_z(i):
        item_in[i][0].wait_recv()
        add(own[i].at[y, b], r3[i], nz)
        waits = []
        for r in range(1, nz):
            qt = lax.rem(q + r, nz)
            waits.append(start(remote(own[i].at[y, b, qt], r4[i].at[r - 1], ssem.at[i, 3 + r], rsem.at[i, 3 + r], at(b, qt, y, c))))
        item_in[i] = waits

    def item_end(i):
        for cp in item_in[i]:
            cp.wait_recv()
        total = own[i][y, b, q].astype(F32)
        for r in range(1, nz):
            total = total + r4[i][r - 1].astype(F32)
        items[i][1][...] = total.astype(items[i][1].dtype)

    for j in range(n_units):
        unit_core(j)
    for i in range(n_items):
        item_core(i)
    for j in range(n_units):
        unit_x(j)
    for i in range(n_items):
        item_y(i)
    unit_z(0)
    for i in range(n_items):
        item_x(i)
    unit_z(1)
    for i in range(n_items):
        item_z(i)
    unit_z(2)
    for i in range(n_items):
        item_end(i)
    for j in range(n_units):
        unit_end(j)
    for cp in sent:
        cp.wait_send()


def reduce_all(nz, qkv, wo, gain, wg, wu, wd):
    ng = nz // 2
    qw = qkv.shape[3] // 4
    blocks = [((qkv.shape[2], qw), BF16), (wo.shape[4:], BF16), (gain.shape[4:], F32)]
    ublocks = [(wd.shape[2:], BF16), (wg.shape[2:], BF16), (wu.shape[2:], BF16)]
    scratch = (
        [pltpu.VMEM((2, 2, nz) + s, t) for s, t in blocks]
        + [pltpu.VMEM((2, 2, nz) + s, t) for s, t in blocks]
        + [pltpu.VMEM((2, nz) + s, t) for s, t in blocks]
        + [pltpu.VMEM((nz,) + s, t) for s, t in blocks]
        + [pltpu.VMEM((nz - 1,) + s, t) for s, t in blocks]
        + [pltpu.VMEM((2, ng) + s, t) for s, t in ublocks]
        + [pltpu.VMEM((2, ng) + s, t) for s, t in ublocks]
        + [pltpu.VMEM((ng,) + s, t) for s, t in ublocks]
        + [pltpu.VMEM((ng,) + s, t) for s, t in ublocks]
        + [
            pltpu.SemaphoreType.DMA((3, 2)),
            pltpu.SemaphoreType.DMA((3, nz + 3)),
            pltpu.SemaphoreType.DMA((3, nz + 3)),
            pltpu.SemaphoreType.DMA((3, 2 * ng + 1)),
            pltpu.SemaphoreType.DMA((3, 3 * ng + 1)),
            pltpu.SemaphoreType.DMA((3, 3 * ng + 1)),
        ]
    )
    out = [
        jax.ShapeDtypeStruct(blocks[0][0], BF16),
        jax.ShapeDtypeStruct(blocks[1][0], F32),
        jax.ShapeDtypeStruct(blocks[2][0], F32),
        jax.ShapeDtypeStruct(ublocks[1][0], BF16),
        jax.ShapeDtypeStruct(ublocks[2][0], BF16),
        jax.ShapeDtypeStruct(ublocks[0][0], F32),
    ]
    return pl.pallas_call(
        functools.partial(reduce_kernel, nz),
        out_shape=out,
        in_specs=[ANY] * 6,
        out_specs=[VMEM] * 6,
        scratch_shapes=scratch,
        compiler_params=pltpu.CompilerParams(collective_id=1, has_side_effects=True, vmem_limit_bytes=60 * 2**20),
    )(qkv, wo, gain, wg, wu, wd)


def chunk_scores(q, kk, segq, segk, qidx, j, scale):
    s = lax.dot_general(q, kk, (((1,), (1,)), ((), ())), preferred_element_type=F32) * scale
    kidx = j * 256 + lax.broadcasted_iota(jnp.int32, (1, 256), 1)
    return s, (segq == segk) & (kidx <= qidx)


def attn_fwd_kernel(nb, q_ref, kv_ref, segq_ref, segk_ref, o_ref, lse_ref, kvall, lsem, ssem, rsem):
    b, q, y, c = place()
    k = lax.axis_index("blk")
    nz = nb // 4
    hz = nz // 2
    half = q // hz
    ql = q - half * hz
    low = k < nb // 2
    is_mid = k == nb // 2
    mid = (b, nb // 2)
    bar = greet(
        [at(b, half * hz + lax.rem(ql + r, hz), y, c) for r in range(1, hz)] + [at(b, q, 1 - y, c), at(b, q, y, 1 - c)]
    )

    @pl.when(low)
    def _():
        pl.semaphore_signal(bar, inc=1, device_id=mid, device_id_type=MESH)

    @pl.when(is_mid)
    def _():
        for j in range(nb // 2):
            pl.semaphore_signal(bar, inc=1, device_id=(b, j), device_id_type=MESH)

    pl.semaphore_wait(bar, hz + 1 + jnp.where(low, 1, 0) + jnp.where(is_mid, nb // 2, 0))

    def view(qq, yy, cc):
        return kvall.at[qq, yy, cc]

    sent = []

    def start(cp):
        cp.start()
        sent.append(cp)
        return cp

    mine = pltpu.make_async_copy(kv_ref, view(q, y, c), lsem)
    mine.start()
    other_y = at(b, q, 1 - y, c)
    other_c = at(b, q, y, 1 - c)
    z_in = []
    for r in range(1, hz):
        target = at(b, half * hz + lax.rem(ql + r, hz), y, c)
        start(remote(kv_ref, view(q, y, c), ssem.at[r], rsem.at[r], target))
        src = half * hz + lax.rem(ql - r + hz, hz)
        z_in.append((remote(kv_ref, view(src, y, c), ssem.at[r], rsem.at[r], target), src))
    start(remote(kv_ref, view(q, y, c), ssem.at[hz], rsem.at[hz], other_y))
    y_in = [(remote(kv_ref, view(q, 1 - y, c), ssem.at[hz], rsem.at[hz], other_y), q)]
    ns = 2 * hz + hz * 2
    to_mid = remote(kv_ref, view(q, y, c), ssem.at[ns], rsem.at[ns + k % (nb // 2)], mid)

    @pl.when(low)
    def _():
        to_mid.start()

    mine.wait()
    c_in = []
    s = 2 * hz

    def to_core(qq, yy, s):
        start(remote(view(qq, yy, c), view(qq, yy, c), ssem.at[s], rsem.at[s], other_c))
        c_in.append(remote(view(qq, yy, c), view(qq, yy, 1 - c), ssem.at[s], rsem.at[s], other_c))

    to_core(q, y, s)
    s += 1
    for r, (cp, src) in enumerate(z_in):
        cp.wait_recv()
        n = hz + 1 + r
        start(remote(view(src, y, c), view(src, y, c), ssem.at[n], rsem.at[n], other_y))
        y_in.append((remote(view(src, y, c), view(src, 1 - y, c), ssem.at[n], rsem.at[n], other_y), src))
        to_core(src, y, s)
        s += 1
    for cp, src in y_in:
        cp.wait_recv()
        to_core(src, 1 - y, s)
        s += 1
    for cp in c_in:
        cp.wait_recv()

    @pl.when(is_mid)
    def _():
        for j in range(nb // 2):
            remote(kv_ref, view(j // 4, (j // 2) % 2, j % 2), ssem.at[ns], rsem.at[ns + j], mid).wait_recv()

    scale = HD ** (-0.5)
    lo = jnp.where(k <= nb // 2, 0, nb // 4)
    hi = k // 2 + 1
    rows = q_ref.shape[1]
    tok = rows // H
    qidx = k * tok + lax.broadcasted_iota(jnp.int32, (rows, 1), 0) % tok
    for m in range(q_ref.shape[0]):
        qm = q_ref[m]
        segq = segq_ref[m]

        def body(j, carry):
            mx, sm, acc = carry
            blk = kvall[j // 2, j % 2, :, m].reshape(256, 2 * HD)
            s, ok = chunk_scores(qm, blk[:, :HD], segq, segk_ref[m, j], qidx, j, scale)
            s = jnp.where(ok, s, -1e30)
            new = jnp.maximum(mx, jnp.max(s, axis=-1, keepdims=True))
            p = jnp.where(ok, jnp.exp(s - new), 0.0)
            alpha = jnp.exp(mx - new)
            sm = sm * alpha + jnp.sum(p, axis=-1, keepdims=True)
            acc = acc * alpha + jnp.dot(p.astype(BF16), blk[:, HD:], preferred_element_type=F32)
            return new, sm, acc

        mx, sm, acc = lax.fori_loop(
            lo, hi, body, (jnp.full((rows, 1), -1e30, F32), jnp.zeros((rows, 1), F32), jnp.zeros((rows, HD), F32))
        )
        o_ref[m] = acc / sm
        lse_ref[m] = mx + jnp.log(sm)
    for cp in sent:
        cp.wait_send()

    @pl.when(low)
    def _():
        to_mid.wait_send()


def attn_fwd(nb, q, kv, segq, segk):
    nz = nb // 4
    ns = 4 * (nz // 2)
    return pl.pallas_call(
        functools.partial(attn_fwd_kernel, nb),
        out_shape=[
            jax.ShapeDtypeStruct(q.shape, F32),
            jax.ShapeDtypeStruct(q.shape[:2] + (1,), F32),
            jax.ShapeDtypeStruct((nz, 2, 2) + kv.shape, BF16),
        ],
        in_specs=[VMEM] * 4,
        out_specs=[VMEM] * 3,
        scratch_shapes=[
            pltpu.SemaphoreType.DMA,
            pltpu.SemaphoreType.DMA((ns + 1,)),
            pltpu.SemaphoreType.DMA((ns + nb // 2,)),
        ],
        compiler_params=pltpu.CompilerParams(collective_id=2, has_side_effects=True, vmem_limit_bytes=60 * 2**20),
    )(q, kv, segq, segk)


def attn_bwd_kernel(
    nb, q_ref, kvall, do_ref, lse_ref, delta_ref, segq_ref, segk_ref, dq_ref, dkv_ref, part, r1, r2, r3, r4, ssem, rsem, msem, nsem
):
    b, q, y, c = place()
    k = lax.axis_index("blk")
    nz = nb // 4
    hz = nz // 2
    half = q // hz
    ql = q - half * hz
    low = k < nb // 2
    is_mid = k == nb // 2
    mid = (b, nb // 2)
    bar = greet(
        [at(b, half * hz + lax.rem(ql + r, hz), y, c) for r in range(1, hz)] + [at(b, q, 1 - y, c), at(b, q, y, 1 - c)]
    )

    @pl.when(low)
    def _():
        pl.semaphore_signal(bar, inc=1, device_id=mid, device_id_type=MESH)

    @pl.when(is_mid)
    def _():
        for j in range(nb // 2):
            pl.semaphore_signal(bar, inc=1, device_id=(b, j), device_id_type=MESH)

    pl.semaphore_wait(bar, hz + 1 + jnp.where(low, 1, 0) + jnp.where(is_mid, nb // 2, 0))
    other_y = at(b, q, 1 - y, c)
    other_c = at(b, q, y, 1 - c)
    sent = []

    def start(cp):
        cp.start()
        sent.append(cp)
        return cp

    def clear(n, _):
        part[half * hz + n // 4, (n // 2) % 2, n % 2] = jnp.zeros(part.shape[3:], BF16)
        return 0

    lax.fori_loop(0, 4 * hz, clear, 0)
    scale = HD ** (-0.5)
    lo = jnp.where(k <= nb // 2, 0, nb // 4)
    hi = k // 2 + 1
    rows = q_ref.shape[1]
    tok = rows // H
    qidx = k * tok + lax.broadcasted_iota(jnp.int32, (rows, 1), 0) % tok
    tn = (((0,), (0,)), ((), ()))
    nt = (((1,), (1,)), ((), ()))
    for m in range(q_ref.shape[0]):
        dq_ref[m] = jnp.zeros(dq_ref.shape[1:], F32)

        def body(j, _):
            qm, dom = q_ref[m], do_ref[m]
            blk = kvall[j // 2, j % 2, :, m].reshape(256, 2 * HD)
            s, ok = chunk_scores(qm, blk[:, :HD], segq_ref[m], segk_ref[m, j], qidx, j, scale)
            p = jnp.where(ok, jnp.exp(jnp.where(ok, s, -1e30) - lse_ref[m]), 0.0)
            dp = lax.dot_general(dom, blk[:, HD:], nt, preferred_element_type=F32)
            ds = (p * (dp - delta_ref[m])).astype(BF16)
            dq_ref[m] += jnp.dot(ds, blk[:, :HD], preferred_element_type=F32) * scale
            dk = lax.dot_general(ds, qm, tn, preferred_element_type=F32) * scale
            dv = lax.dot_general(p.astype(BF16), dom, tn, preferred_element_type=F32)
            part[j // 2, j % 2, :, m] = jnp.concatenate([dk, dv], axis=1).astype(BF16).reshape(2, tok, 2 * HD)
            return 0

        lax.fori_loop(lo, hi, body, 0)

    @pl.when(is_mid)
    def _():
        for j in range(nb // 2):
            remote(part.at[j // 4, (j // 2) % 2, j % 2], r4, msem.at[j], nsem, (b, j)).start()

    hs = pl.ds(half * hz, hz)
    cp = start(remote(part.at[hs, :, 1 - c], r1, ssem.at[0], rsem.at[0], other_c))
    cp.wait_recv()

    def add1(n, _):
        i = half * hz + n // 2
        part[i, n % 2, c] = (part[i, n % 2, c].astype(F32) + r1[n // 2, n % 2].astype(F32)).astype(BF16)
        return 0

    lax.fori_loop(0, 2 * hz, add1, 0)
    cp = start(remote(part.at[hs, 1 - y, c], r2, ssem.at[1], rsem.at[1], other_y))
    cp.wait_recv()

    def add2(n, _):
        i = half * hz + n
        part[i, y, c] = (part[i, y, c].astype(F32) + r2[n].astype(F32)).astype(BF16)
        return 0

    lax.fori_loop(0, hz, add2, 0)
    last = []
    for r in range(1, hz):
        qt = half * hz + lax.rem(ql + r, hz)
        last.append(start(remote(part.at[qt, y, c], r3.at[r - 1], ssem.at[1 + r], rsem.at[1 + r], at(b, qt, y, c))))
    total = part[q, y, c].astype(F32)
    for r, cp in enumerate(last):
        cp.wait_recv()
        total = total + r3[r].astype(F32)
    dkv_ref[...] = total

    @pl.when(low)
    def _():
        remote(part.at[0, 0, 0], r4, msem.at[0], nsem, mid).wait_recv()
        dkv_ref[...] += r4[...].astype(F32)

    for cp in sent:
        cp.wait_send()

    @pl.when(is_mid)
    def _():
        for j in range(nb // 2):
            remote(part.at[j // 4, (j // 2) % 2, j % 2], r4, msem.at[j], nsem, (b, j)).wait_send()


def attn_bwd(nb, q, kvall, do, lse, delta, segq, segk):
    nz = nb // 4
    hz = nz // 2
    blk = kvall.shape[3:]
    return pl.pallas_call(
        functools.partial(attn_bwd_kernel, nb),
        out_shape=[jax.ShapeDtypeStruct(q.shape, F32), jax.ShapeDtypeStruct(blk, F32)],
        in_specs=[VMEM] * 7,
        out_specs=[VMEM] * 2,
        scratch_shapes=[
            pltpu.VMEM(kvall.shape, BF16),
            pltpu.VMEM((hz, 2) + blk, BF16),
            pltpu.VMEM((hz,) + blk, BF16),
            pltpu.VMEM((hz - 1,) + blk, BF16),
            pltpu.VMEM(blk, BF16),
            pltpu.SemaphoreType.DMA((hz + 1,)),
            pltpu.SemaphoreType.DMA((hz + 1,)),
            pltpu.SemaphoreType.DMA((nb // 2,)),
            pltpu.SemaphoreType.DMA,
        ],
        compiler_params=pltpu.CompilerParams(collective_id=3, has_side_effects=True, vmem_limit_bytes=60 * 2**20),
    )(q, kvall, do, lse, delta, segq, segk)


def tiles(n, w):
    return [(i, min(w, n - i)) for i in range(0, n, w)]


def gelu_parts(z):
    k0 = math.sqrt(2.0 / math.pi)
    z2 = z * z
    h = 0.5 + 0.5 * jnp.tanh(z * (k0 + (k0 * 0.044715) * z2))
    value = z * h
    slope = h + 2.0 * value * (1.0 - h) * (k0 + (3.0 * k0 * 0.044715) * z2)
    return value, slope


def ffn_kernel(
    b_ref, h1_ref, dy_ref, gp_ref, wg, wu, wd, out_ref, db_ref, dgp_ref, gg_o, gu_o, gd_o,
    ball, ballt, gate, up, mm, fsend, frecv, dfall, dsend, drecv, sg, su, sd, ssem, rsem, osem,
):
    b, q, y, c = place()
    g = q // 2
    t = lax.rem(q, 2) * 2 + y
    micro, tok, width = b_ref.shape
    hidden = wd.shape[0]
    peers = []
    for p in range(1, 4):
        tt = lax.rem(t + p, 4)
        peers.append((p, tt, at(b, g * 2 + tt // 2, lax.rem(tt, 2), c)))
    bar = greet([p[2] for p in peers])
    pl.semaphore_wait(bar, 3)
    sent = []
    nt = (((1,), (1,)), ((), ()))

    def spread(phase, m, src, dst_of, recv_of):
        waits = []
        for p, tt, target in peers:
            cp = remote(src(tt), dst_of(p, tt), ssem.at[phase, m, p - 1], rsem.at[phase, m, p - 1], target)
            cp.start()
            sent.append(cp)
            ts = lax.rem(t + 4 - p, 4)
            waits.append(remote(src(tt), recv_of(p, ts), ssem.at[phase, m, p - 1], rsem.at[phase, m, p - 1], target))
        return waits

    a_in, f_in, df_in, db_in = [], [], [], []
    for m in range(micro):
        a_in.append(
            spread(0, m, lambda tt, m=m: b_ref.at[m], lambda p, tt, m=m: ball.at[m, t], lambda p, ts, m=m: ball.at[m, ts])
        )
        ball[m, t] = b_ref[m]

    def forward(m):
        for cp in a_in[m]:
            cp.wait_recv()

        def body(n, _):
            cols = pl.ds(pl.multiple_of(n * 256, 256), 256)
            x = ball[m].reshape(4 * tok, width)
            gv = jnp.dot(x, wg[:, cols], preferred_element_type=F32)
            uv = jnp.dot(x, wu[:, cols], preferred_element_type=F32)
            gate[m, :, cols] = gv.astype(BF16)
            up[m, :, cols] = uv.astype(BF16)
            mm[m, :, cols] = (gelu_parts(gv)[0] * uv).astype(BF16)
            return 0

        lax.fori_loop(0, hidden // 256, body, 0)
        for o, w in tiles(width, 256):
            f = jnp.dot(mm[m], wd[:, o : o + w], preferred_element_type=F32)
            fsend[m, :, :, o : o + w] = f.astype(BF16).reshape(4, tok, w)
        f_in.append(
            spread(1, m, lambda tt: fsend.at[m, tt], lambda p, tt: frecv.at[m, p - 1], lambda p, ts: frecv.at[m, p - 1])
        )

    def middle(m):
        for cp in f_in[m]:
            cp.wait_recv()
        f = fsend[m, t].astype(F32)
        for p in range(3):
            f = f + frecv[m, p].astype(F32)
        gp = 1.0 + gp_ref[...]
        r = lax.rsqrt(jnp.mean(f * f, axis=-1, keepdims=True) + epsilon)
        n = f * r
        dy = dy_ref[m].astype(F32)
        out_ref[m] = (h1_ref[m] + n * gp).astype(BF16)
        dg = dy * gp
        df = r * (dg - n * jnp.mean(dg * n, axis=-1, keepdims=True))
        part = jnp.sum(dy * n, axis=0, keepdims=True)
        if m == 0:
            dgp_ref[...] = part
        else:
            dgp_ref[...] += part
        dfall[m, t] = df.astype(BF16)
        df_in.append(
            spread(2, m, lambda tt: dfall.at[m, t], lambda p, tt: dfall.at[m, t], lambda p, ts: dfall.at[m, ts])
        )

    def backward(m):
        for cp in df_in[m]:
            cp.wait_recv()

        def body(n, _):
            cols = pl.ds(pl.multiple_of(n * 256, 256), 256)
            x = dfall[m].reshape(4 * tok, width)
            dm = lax.dot_general(x, wd[cols, :], nt, preferred_element_type=F32)
            value, slope = gelu_parts(gate[m, :, cols].astype(F32))
            uv = up[m, :, cols].astype(F32)
            gate[m, :, cols] = (dm * uv * slope).astype(BF16)
            up[m, :, cols] = (dm * value).astype(BF16)
            return 0

        lax.fori_loop(0, hidden // 256, body, 0)
        for o, w in tiles(width, 256):
            d = lax.dot_general(gate[m], wg[o : o + w, :], nt, preferred_element_type=F32)
            d = d + lax.dot_general(up[m], wu[o : o + w, :], nt, preferred_element_type=F32)
            dsend[m, :, :, o : o + w] = d.astype(BF16).reshape(4, tok, w)
        db_in.append(
            spread(3, m, lambda tt: dsend.at[m, tt], lambda p, tt: drecv.at[m, p - 1], lambda p, ts: drecv.at[m, p - 1])
        )

    for m in range(micro):
        forward(m)
    for m in range(micro):
        for i in range(4):
            ballt[:, (m * 4 + i) * tok : (m * 4 + i + 1) * tok] = ball[m, i].T
    for m in range(micro):
        middle(m)
    for m in range(micro):
        backward(m)

    def grads(n, _):
        cols = pl.ds(pl.multiple_of(n * 256, 256), 256)
        slot = lax.rem(n, 2)

        def out(m, o):
            cc = pl.ds(pl.multiple_of(m * 256, 256), 256)
            return [
                pltpu.make_async_copy(sg.at[o], gg_o.at[:, cc], osem.at[0, o]),
                pltpu.make_async_copy(su.at[o], gu_o.at[:, cc], osem.at[1, o]),
                pltpu.make_async_copy(sd.at[o], gd_o.at[cc, :], osem.at[2, o]),
            ]

        @pl.when(n >= 2)
        def _():
            for cp in out(n, slot):
                cp.wait()

        x = ballt[...]
        sg[slot] = jnp.dot(x, gate[:, :, cols].reshape(-1, 256), preferred_element_type=F32).astype(BF16)
        su[slot] = jnp.dot(x, up[:, :, cols].reshape(-1, 256), preferred_element_type=F32).astype(BF16)
        sd[slot] = jnp.dot(
            mm[:, :, cols].reshape(-1, 256).T, dfall[...].reshape(-1, width), preferred_element_type=F32
        ).astype(BF16)
        for cp in out(n, slot):
            cp.start()
        return 0

    steps = hidden // 256
    lax.fori_loop(0, steps, grads, 0)
    for n in range(max(steps - 2, 0), steps):
        o = n % 2
        pltpu.make_async_copy(sg.at[o], gg_o.at[:, n * 256 : n * 256 + 256], osem.at[0, o]).wait()
        pltpu.make_async_copy(su.at[o], gu_o.at[:, n * 256 : n * 256 + 256], osem.at[1, o]).wait()
        pltpu.make_async_copy(sd.at[o], gd_o.at[n * 256 : n * 256 + 256, :], osem.at[2, o]).wait()
    for m in range(micro):
        for cp in db_in[m]:
            cp.wait_recv()
        d = dsend[m, t].astype(F32)
        for p in range(3):
            d = d + drecv[m, p].astype(F32)
        db_ref[m] = d
    for cp in sent:
        cp.wait_send()


def ffn(b, h1, dy, gp, wg, wu, wd):
    micro, tok, width = b.shape
    hidden = wd.shape[0]
    wide = (micro, 4 * tok, hidden)
    return pl.pallas_call(
        ffn_kernel,
        out_shape=[
            jax.ShapeDtypeStruct(b.shape, BF16),
            jax.ShapeDtypeStruct(b.shape, F32),
            jax.ShapeDtypeStruct((1, width), F32),
            jax.ShapeDtypeStruct(wg.shape, BF16),
            jax.ShapeDtypeStruct(wu.shape, BF16),
            jax.ShapeDtypeStruct(wd.shape, BF16),
        ],
        in_specs=[VMEM] * 7,
        out_specs=[VMEM] * 3 + [ANY] * 3,
        scratch_shapes=[
            pltpu.VMEM((micro, 4, tok, width), BF16),
            pltpu.VMEM((width, micro * 4 * tok), BF16),
            pltpu.VMEM(wide, BF16),
            pltpu.VMEM(wide, BF16),
            pltpu.VMEM(wide, BF16),
            pltpu.VMEM((micro, 4, tok, width), BF16),
            pltpu.VMEM((micro, 3, tok, width), BF16),
            pltpu.VMEM((micro, 4, tok, width), BF16),
            pltpu.VMEM((micro, 4, tok, width), BF16),
            pltpu.VMEM((micro, 3, tok, width), BF16),
            pltpu.VMEM((2, width, 256), BF16),
            pltpu.VMEM((2, width, 256), BF16),
            pltpu.VMEM((2, 256, width), BF16),
            pltpu.SemaphoreType.DMA((4, micro, 3)),
            pltpu.SemaphoreType.DMA((4, micro, 3)),
            pltpu.SemaphoreType.DMA((3, 2)),
        ],
        compiler_params=pltpu.CompilerParams(collective_id=4, has_side_effects=True, vmem_limit_bytes=62 * 2**20),
    )(b, h1, dy, gp, wg, wu, wd)


class Team:
    def __init__(self, place_of, c, ssem, rsem, sent):
        b, g, e, y = place_of
        self.t, self.ty, self.tz, self.td = e * 2 + y, e * 2 + 1 - y, (1 - e) * 2 + y, (1 - e) * 2 + 1 - y
        self.dev_y, self.dev_z = at(b, g * 2 + e, 1 - y, c), at(b, g * 2 + 1 - e, y, c)
        self.ssem, self.rsem, self.sent = ssem, rsem, sent

    def hop(self, src, dst, here, s, target):
        cp = remote(src, dst, self.ssem.at[s], self.rsem.at[s], target)
        cp.start()
        self.sent.append(cp)
        return remote(src, here, self.ssem.at[s], self.rsem.at[s], target)


class Gather(Team):
    def begin(self, slots):
        h = slots.shape[1] // 2
        self.a, self.b = pl.ds(0, h), pl.ds(h, h)
        self.slots = slots
        own = slots.at[self.t]
        y, z = slots.at[self.ty], slots.at[self.tz]
        self.ya = self.hop(own.at[self.a], own.at[self.a], y.at[self.a], 0, self.dev_y)
        self.zb = self.hop(own.at[self.b], own.at[self.b], z.at[self.b], 1, self.dev_z)
        self.yb = self.hop(own.at[self.b], own.at[self.b], y.at[self.b], 2, self.dev_y)
        self.za = self.hop(own.at[self.a], own.at[self.a], z.at[self.a], 3, self.dev_z)

    def forward(self):
        y, z, d = (self.slots.at[i] for i in (self.ty, self.tz, self.td))
        self.ya.wait_recv()
        self.da = self.hop(y.at[self.a], y.at[self.a], d.at[self.a], 4, self.dev_z)
        self.zb.wait_recv()
        self.db = self.hop(z.at[self.b], z.at[self.b], d.at[self.b], 5, self.dev_y)

    def end(self):
        for cp in (self.yb, self.za, self.da, self.db):
            cp.wait_recv()


class Sum(Team):
    def begin(self, parts, got, mid):
        h = parts.shape[1] // 2
        self.a, self.b = pl.ds(0, h), pl.ds(h, h)
        self.parts, self.got, self.mid = parts, got, mid
        y, z, d = (parts.at[i] for i in (self.ty, self.tz, self.td))
        self.ma = self.hop(d.at[self.a], mid.at[0], mid.at[0], 0, self.dev_y)
        self.mb = self.hop(d.at[self.b], mid.at[1], mid.at[1], 1, self.dev_z)
        self.ya = self.hop(y.at[self.a], got.at[0, self.a], got.at[0, self.a], 2, self.dev_y)
        self.zb = self.hop(z.at[self.b], got.at[1, self.b], got.at[1, self.b], 3, self.dev_z)

    def forward(self):
        z, y = self.parts.at[self.tz], self.parts.at[self.ty]
        self.ma.wait_recv()
        z[self.a] = z[self.a] + self.mid[0]
        self.za = self.hop(z.at[self.a], self.got.at[1, self.a], self.got.at[1, self.a], 4, self.dev_z)
        self.mb.wait_recv()
        y[self.b] = y[self.b] + self.mid[1]
        self.yb = self.hop(y.at[self.b], self.got.at[0, self.b], self.got.at[0, self.b], 5, self.dev_y)

    def end(self):
        for cp in (self.ya, self.zb, self.za, self.yb):
            cp.wait_recv()
        own, got = self.parts.at[self.t], self.got
        return own[...].astype(F32) + got[0].astype(F32) + got[1].astype(F32)


def mlp_kernel(
    ball_h, h1_ref, dy_ref, gd_ref, wg_h, wu_h, wd_h, out_ref, db_ref, dgp_ref, gg_o, gu_o, gd_o,
    wg, wu, wd, ball, ballt, gate, up, mm, fsend, frecv, fmid, dfall, dsend, drecv, dmid, sg, su, sd, ssem, rsem, osem, wsem, bsem,
):
    b, q, y, c = place()
    g, e = q // 2, q % 2
    t = e * 2 + y
    micro, tok, width = h1_ref.shape
    hidden = wd.shape[0]

    def load(n):
        cols = pl.ds(pl.multiple_of(n * 256, 256), 256)
        return [
            pltpu.make_async_copy(wg_h.at[:, cols], wg.at[:, cols], wsem.at[0, n]),
            pltpu.make_async_copy(wu_h.at[:, cols], wu.at[:, cols], wsem.at[1, n]),
        ]

    cut = ball_h.shape[2] // tok
    loads = [
        pltpu.make_async_copy(ball_h.at[m // cut, :, pl.ds(m % cut * tok, tok)], ball.at[m], bsem.at[m]) for m in range(micro)
    ]
    loads.append(pltpu.make_async_copy(wd_h, wd, bsem.at[micro]))
    loads[0].start()
    for n in range(hidden // 256):
        for cp in load(n):
            cp.start()
    for cp in loads[1:]:
        cp.start()
    bar = greet([at(b, q, 1 - y, c), at(b, g * 2 + 1 - e, y, c)])
    pl.semaphore_wait(bar, 2)
    sent = []
    nt = (((1,), (1,)), ((), ()))

    def team(kind, phase, m):
        return kind((b, g, e, y), c, ssem.at[phase, m], rsem.at[phase, m], sent)

    f_sum = [team(Sum, 0, m) for m in range(micro)]
    df_all = [team(Gather, 1, m) for m in range(micro)]
    db_sum = [team(Sum, 2, m) for m in range(micro)]

    def rise(m):
        loads[m].wait()

        def body(n, _):
            if m == 0:
                for cp in load(n):
                    cp.wait()
            cols = pl.ds(pl.multiple_of(n * 256, 256), 256)
            x = ball[m].reshape(4 * tok, width)
            gv = jnp.dot(x, wg[:, cols], preferred_element_type=F32)
            uv = jnp.dot(x, wu[:, cols], preferred_element_type=F32)
            value, slope = gelu_parts(gv)
            gate[m, :, cols] = (uv * slope).astype(BF16)
            up[m, :, cols] = value.astype(BF16)
            mm[m, :, cols] = (value * uv).astype(BF16)
            return 0

        lax.fori_loop(0, hidden // 256, body, 0)

    def fall(m):
        if m == 0:
            loads[micro].wait()
        for o, w in tiles(width, 256):
            f = jnp.dot(mm[m], wd[:, o : o + w], preferred_element_type=F32)
            fsend[m, :, :, o : o + w] = f.astype(BF16).reshape(4, tok, w)
        f_sum[m].begin(fsend.at[m], frecv.at[m], fmid.at[m])

    def middle(m):
        f = f_sum[m].end()
        gp = 1.0 + gd_ref[5:6]
        r = lax.rsqrt(jnp.mean(f * f, axis=-1, keepdims=True) + epsilon)
        n = f * r
        dy = dy_ref[m].astype(F32)
        out_ref[m] = (h1_ref[m] + n * gp).astype(BF16)
        dg = dy * gp
        df = r * (dg - n * jnp.mean(dg * n, axis=-1, keepdims=True))
        part = jnp.sum(dy * n, axis=0, keepdims=True)
        if m == 0:
            dgp_ref[...] = part
        else:
            dgp_ref[...] += part
        dfall[m, t] = df.astype(BF16)
        df_all[m].begin(dfall.at[m])

    def back_rise(m):
        df_all[m].end()

        def body(n, _):
            cols = pl.ds(pl.multiple_of(n * 256, 256), 256)
            x = dfall[m].reshape(4 * tok, width)
            dm = lax.dot_general(x, wd[cols, :], nt, preferred_element_type=F32)
            gate[m, :, cols] = (dm * gate[m, :, cols].astype(F32)).astype(BF16)
            up[m, :, cols] = (dm * up[m, :, cols].astype(F32)).astype(BF16)
            return 0

        lax.fori_loop(0, hidden // 256, body, 0)

    def back_fall(m):
        for o, w in tiles(width, 256):
            d = lax.dot_general(gate[m], wg[o : o + w, :], nt, preferred_element_type=F32)
            d = d + lax.dot_general(up[m], wu[o : o + w, :], nt, preferred_element_type=F32)
            dsend[m, :, :, o : o + w] = d.astype(BF16).reshape(4, tok, w)
        db_sum[m].begin(dsend.at[m], drecv.at[m], dmid.at[m])

    for m in range(micro):
        rise(m)
        if m >= 1:
            f_sum[m - 1].forward()
        if m >= 2:
            middle(m - 2)
        if m >= 3:
            df_all[m - 3].forward()
        fall(m)
    for m in range(micro):
        for i in range(4):
            o = (m * 4 + i) * tok
            ballt[:, o : o + tok] = ball[m, i].T
    middle(micro - 2)
    if micro >= 3:
        df_all[micro - 3].forward()
    for m in range(micro):
        back_rise(m)
        if m == 0:
            f_sum[micro - 1].forward()
            df_all[micro - 2].forward()
        else:
            db_sum[m - 1].forward()
        if m == 1:
            df_all[micro - 1].forward()
        back_fall(m)
        if m == 0:
            middle(micro - 1)

    def grads(n, _):
        cols = pl.ds(pl.multiple_of(n * 256, 256), 256)
        slot = lax.rem(n, 2)

        def out(m, o):
            cc = pl.ds(pl.multiple_of(m * 256, 256), 256)
            return [
                pltpu.make_async_copy(sg.at[o], gg_o.at[:, cc], osem.at[0, o]),
                pltpu.make_async_copy(su.at[o], gu_o.at[:, cc], osem.at[1, o]),
                pltpu.make_async_copy(sd.at[o], gd_o.at[cc, :], osem.at[2, o]),
            ]

        @pl.when(n >= 2)
        def _():
            for cp in out(n, slot):
                cp.wait()

        x = ballt[...]
        sg[slot] = jnp.dot(x, gate[:, :, cols].reshape(-1, 256), preferred_element_type=F32).astype(BF16)
        su[slot] = jnp.dot(x, up[:, :, cols].reshape(-1, 256), preferred_element_type=F32).astype(BF16)
        sd[slot] = jnp.dot(
            mm[:, :, cols].reshape(-1, 256).T, dfall[...].reshape(-1, width), preferred_element_type=F32
        ).astype(BF16)
        for cp in out(n, slot):
            cp.start()
        return 0

    steps = hidden // 256
    lax.fori_loop(0, min(2, steps), grads, 0)
    db_sum[micro - 1].forward()
    lax.fori_loop(min(2, steps), steps, grads, 0)
    for n in range(max(steps - 2, 0), steps):
        o = n % 2
        pltpu.make_async_copy(sg.at[o], gg_o.at[:, n * 256 : n * 256 + 256], osem.at[0, o]).wait()
        pltpu.make_async_copy(su.at[o], gu_o.at[:, n * 256 : n * 256 + 256], osem.at[1, o]).wait()
        pltpu.make_async_copy(sd.at[o], gd_o.at[n * 256 : n * 256 + 256, :], osem.at[2, o]).wait()
    for m in range(micro):
        db_ref[m] = db_sum[m].end()
    for cp in sent:
        cp.wait_send()


def mlp(ball, h1, dy, gp, wg, wu, wd):
    micro, tok, width = h1.shape
    hidden = wd.shape[0]
    wide = (micro, 4 * tok, hidden)
    return pl.pallas_call(
        mlp_kernel,
        out_shape=[
            jax.ShapeDtypeStruct(h1.shape, BF16),
            jax.ShapeDtypeStruct(h1.shape, F32),
            jax.ShapeDtypeStruct((1, width), F32),
            jax.ShapeDtypeStruct(wg.shape, BF16),
            jax.ShapeDtypeStruct(wu.shape, BF16),
            jax.ShapeDtypeStruct(wd.shape, BF16),
        ],
        in_specs=[ANY] + [VMEM] * 3 + [ANY] * 3,
        out_specs=[VMEM] * 3 + [ANY] * 3,
        scratch_shapes=[
            pltpu.VMEM(wg.shape, BF16),
            pltpu.VMEM(wu.shape, BF16),
            pltpu.VMEM(wd.shape, BF16),
            pltpu.VMEM((micro, 4, tok, width), BF16),
            pltpu.VMEM((width, micro * 4 * tok), BF16),
            pltpu.VMEM(wide, BF16),
            pltpu.VMEM(wide, BF16),
            pltpu.VMEM(wide, BF16),
            pltpu.VMEM((micro, 4, tok, width), BF16),
            pltpu.VMEM((micro, 2, tok, width), BF16),
            pltpu.VMEM((micro, 2, tok // 2, width), BF16),
            pltpu.VMEM((micro, 4, tok, width), BF16),
            pltpu.VMEM((micro, 4, tok, width), BF16),
            pltpu.VMEM((micro, 2, tok, width), BF16),
            pltpu.VMEM((micro, 2, tok // 2, width), BF16),
            pltpu.VMEM((2, width, 256), BF16),
            pltpu.VMEM((2, width, 256), BF16),
            pltpu.VMEM((2, 256, width), BF16),
            pltpu.SemaphoreType.DMA((3, micro, 6)),
            pltpu.SemaphoreType.DMA((3, micro, 6)),
            pltpu.SemaphoreType.DMA((3, 2)),
            pltpu.SemaphoreType.DMA((2, hidden // 256)),
            pltpu.SemaphoreType.DMA((micro + 1,)),
        ],
        compiler_params=pltpu.CompilerParams(collective_id=7, has_side_effects=True, vmem_limit_bytes=62 * 2**20),
    )(ball, h1, dy, gp, wg, wu, wd)


def halves(n):
    first = up16(n // 2)
    return [(0, first), (first, n - first)] if first < n else [(0, n)]


def norm_of(v):
    r = lax.rsqrt(jnp.mean(v * v, axis=-1, keepdims=True) + epsilon)
    return v * r, r


def norm_back(grad, n, r, scale):
    gs = grad * scale
    return r * (gs - n * jnp.mean(gs * n, axis=-1, keepdims=True)), jnp.sum(grad * n, axis=0, keepdims=True)


def spread_gains(block, width, n_dev):
    w = width // n_dev
    lane = lax.broadcasted_iota(jnp.int32, (128, width), 0)
    col = lax.broadcasted_iota(jnp.int32, (128, width), 1)
    pick = jnp.where(lax.rem(col, w) == lane, 1.0, 0.0).astype(BF16)
    wide = jnp.dot(block, pick, preferred_element_type=F32)
    row = lax.broadcasted_iota(jnp.int32, (n_dev * 16, width), 0) // 16
    mine = lax.broadcasted_iota(jnp.int32, (n_dev * 16, width), 1) // w
    return jnp.sum(jnp.where(row == mine, wide, 0.0).reshape(n_dev, 16, width), axis=0)


def collect_gains(rows, n_dev):
    width = rows.shape[1]
    w = width // n_dev
    row = lax.broadcasted_iota(jnp.int32, (n_dev, 8, width), 0)
    mine = lax.broadcasted_iota(jnp.int32, (n_dev, 8, width), 2) // w
    wide = jnp.where(row == mine, rows[None], 0.0).reshape(n_dev * 8, width)
    col = lax.broadcasted_iota(jnp.int32, (width, 128), 0)
    lane = lax.broadcasted_iota(jnp.int32, (width, 128), 1)
    pick = jnp.where(lax.rem(col, w) == lane, 1.0, 0.0)
    out = jnp.dot(wide, pick, preferred_element_type=F32, precision=lax.Precision.HIGHEST)
    return out.reshape(n_dev, 8, 128)


def pack_rows(kr, kp):
    row = lax.broadcasted_iota(jnp.int32, (4 * kr, 4 * kp), 0)
    col = lax.broadcasted_iota(jnp.int32, (4 * kr, 4 * kp), 1)
    return jnp.where(lax.div(row, kr) * kp + lax.rem(row, kr) == col, 1.0, 0.0).astype(BF16)


def kv_columns(which, qw):
    return 2 * which * qw + HD, (2 * which + 1) * qw + HD


def half_mask(n, tok):
    row = lax.rem(lax.broadcasted_iota(jnp.int32, (n, tok), 0), tok)
    return lax.broadcasted_iota(jnp.int32, (n, tok), 1) <= row


def segment_of(len_ref, m, index):
    end = jnp.int32(0)
    seg = jnp.zeros(index.shape, jnp.int32)
    for i in range(len_ref.shape[1]):
        end = end + len_ref[m, i]
        seg = seg + jnp.where(index >= end, 1, 0)
    return seg


def front_barrier(nz):
    b, q, y, c = place()
    k = lax.axis_index("blk")
    nb = 4 * nz
    g, e = q // 2, q % 2
    ng = nz // 2
    bar = greet(
        [at(b, lax.rem(q + r, nz), y, c) for r in range(1, nz)]
        + [at(1 - b, q, y, c), at(b, q, 1 - y, c), at(b, q, y, 1 - c), at(b, q, 1 - y, 1 - c)]
        + [at(b, lax.rem(g + r, ng) * 2 + c, y, e) for r in range(1, ng)]
    )

    @pl.when(e != c)
    def _():
        pl.semaphore_signal(bar, inc=1, device_id=at(b, g * 2 + c, y, e), device_id_type=MESH)

    is_first, is_mid = k == 0, k == nb // 2

    @pl.when(is_first)
    def _():
        pl.semaphore_signal(bar, inc=1, device_id=(b, nb // 2), device_id_type=MESH)

    @pl.when(is_mid)
    def _():
        pl.semaphore_signal(bar, inc=1, device_id=(b, 0), device_id_type=MESH)

    pl.semaphore_wait(
        bar, nz + 2 + ng + 1 - jnp.where(e == c, 1, 0) + jnp.where(is_first, 1, 0) + jnp.where(is_mid, 1, 0)
    )


def front_kernel(
    nz, x_ref, cos_ref, sin_ref, len_ref, wq_ref, wk_ref, wv_ref, wo_u, gain_u, wg_ref, wu_ref, wd_x,
    ball, h1_o, attn_h, raw_h, q_h, o_h, ob_h, lse_h, kv_h, wqkv_h, wo_h, xq_h, xkv_h, xo_h, xlse_h, gd_o, gh_o, wg_f, wu_f, wd_f,
    attn_s, raw_s, q_s, o_s, ob_s, lse_s, kvall, kv_own, wqkv, wo, gain_f, qkv_u, wg, wu, wd, qkv_x, wg_x, wu_x, qkv_r, wg_r, wu_r,
    xq, xkv, xo_s, xlse_s, xob, xin, xss, xrs,
    lsem, ssem, rsem, wls, wss, wrs, kls, kss, krs, osem, qss, qrs, tss, trs,
):
    b, q, y, c = place()
    k = lax.axis_index("blk")
    nb = 4 * nz
    n_dev = 2 * nb
    g, e = q // 2, q % 2
    ng = nz // 2
    hz = nz // 2
    qw = qkv_u.shape[1]
    self_in = e == c
    front_barrier(nz)
    other_x, other_y, other_c = at(1 - b, q, y, c), at(b, q, 1 - y, c), at(b, q, y, 1 - c)
    everything, both = pl.ds(0, nz), pl.ds(0, 2)
    kr = qkv_u.shape[0] // 4
    dr, dp = wd_x.shape[0], wd.shape[0]

    def split_rows(ref, out):
        out[...] = jnp.zeros(out.shape, BF16)
        for n in range(2 * nz):
            for j in range(4):
                o = (4 * n + j) * dr
                out[j, :kr, n * dp : n * dp + dr] = ref[:, o : o + dr]

    sent = []

    def start(cp):
        cp.start()
        sent.append(cp)
        return cp

    quad = [(y, 1 - c), (1 - y, c), (1 - y, 1 - c)]
    trades = [(qkv_x, qkv_r, qkv_u), (wg_x, wg_r, wg), (wu_x, wu_r, wu)]
    t_in = [[] for _ in trades]

    def trade(i):
        src, dst, _ = trades[i]
        for p, (yy, cc) in enumerate(quad):
            t = at(b, q, yy, cc)
            start(remote(src.at[yy * 2 + cc], dst.at[y * 2 + c], qss.at[i, p], qrs.at[i, p], t))
            t_in[i].append(remote(src.at[yy * 2 + cc], dst.at[yy * 2 + cc], qss.at[i, p], qrs.at[i, p], t))
        t_in[i].append(pltpu.make_async_copy(src.at[y * 2 + c], dst.at[y * 2 + c], qrs.at[i, 3]))
        t_in[i][3].start()

    def traded(i):
        _, src, dst = trades[i]
        for p in range(3):
            t_in[i][p].wait_recv()
        t_in[i][3].wait()
        pick = pack_rows(kr, src.shape[1])
        for o, n in tiles(src.shape[2], 256):
            v = jnp.dot(pick, src[:, :, o : o + n].reshape(4 * src.shape[1], n), preferred_element_type=F32)
            dst[:, o : o + n] = v.astype(BF16)

    def view_q(ref, yy, cc, xx, qq):
        return ref.at[xx, qq, :, pl.ds(pl.multiple_of((yy * 2 + cc) * qw, 128), HD)]

    def view_kv(ref, yy, cc, xx, qq):
        return ref.at[xx, qq, :, pl.ds(pl.multiple_of((yy * 2 + cc) * qw + HD, 128), qw - HD)]

    def view_lead(ref, yy, cc, xx, qq):
        return ref.at[xx, qq, yy, cc]

    GAIN, KV, Q, WO = range(4)
    items = [
        (gain_u, gain_f, view_lead, True),
        (qkv_u.at[:, HD:], wqkv, view_kv, True),
        (qkv_u.at[:, :HD], wqkv, view_q, True),
        (wo_u, wo, view_lead, True),
    ]
    local = [None] * 4
    z_in, a_in, b_in, c_in = ([[] for _ in items] for _ in range(4))

    def hop(i, v, w, s, t):
        start(remote(v, v, ssem.at[i, s], rsem.at[i, s], t))
        return remote(v, w, ssem.at[i, s], rsem.at[i, s], t)

    def second(i):
        return (other_x, 1 - b, y) if items[i][3] else (other_y, b, 1 - y)

    def send_z(i):
        src, dst, view, _ = items[i]
        local[i] = pltpu.make_async_copy(src, view(dst, y, c, b, q), lsem.at[i])
        local[i].start()
        for r in range(1, nz):
            t = at(b, lax.rem(q + r, nz), y, c)
            start(remote(src, view(dst, y, c, b, q), ssem.at[i, r], rsem.at[i, r], t))
            z_in[i].append(
                remote(src, view(dst, y, c, b, lax.rem(q - r + nz, nz)), ssem.at[i, r], rsem.at[i, r], t)
            )
        t, xx, yy = second(i)
        start(remote(src, view(dst, y, c, b, q), ssem.at[i, nz], rsem.at[i, nz], t))
        a_in[i].append(remote(src, view(dst, yy, c, xx, q), ssem.at[i, nz], rsem.at[i, nz], t))

    def send_a(i):
        _, dst, view, _ = items[i]
        t, xx, yy = second(i)
        for r in range(1, nz):
            qs = lax.rem(q - r + nz, nz)
            z_in[i][r - 1].wait_recv()
            a_in[i].append(hop(i, view(dst, y, c, b, qs), view(dst, yy, c, xx, qs), nz + r, t))

    def send_b(i, half):
        _, dst, view, x_first = items[i]
        if half == 0:
            local[i].wait()
            xx, yy = b, y
        else:
            for cp in a_in[i]:
                cp.wait_recv()
            _, xx, yy = second(i)
        t, xi, yi = (other_y, xx, 1 - yy) if x_first else (other_x, 1 - xx, yy)
        b_in[i].append(
            (hop(i, view(dst, yy, c, xx, everything), view(dst, yi, c, xi, everything), 2 * nz + half, t), xi, yi)
        )
        to_core(i, xx, yy, 2 * nz + 2 + half)

    def to_core(i, xx, yy, s):
        _, dst, view, _ = items[i]
        c_in[i].append(hop(i, view(dst, yy, c, xx, everything), view(dst, yy, 1 - c, xx, everything), s, other_c))

    def send_c(i):
        for half, (cp, xx, yy) in enumerate(b_in[i]):
            cp.wait_recv()
            to_core(i, xx, yy, 2 * nz + 4 + half)

    def done(i):
        for cp in c_in[i]:
            cp.wait_recv()

    pieces = [
        (src, dst, o, n) for src, dst in ((wd, wd_f), (wg, wg_f), (wu, wu_f)) for o, n in halves(src.shape[0])
    ]
    w_in, w_x, w_c, w_out = ([[] for _ in pieces] for _ in range(4))

    def w_send(j):
        src, dst, o, n = pieces[j]
        sl = pl.ds(o, n)
        for r in range(ng):
            t = at(b, lax.rem(g + r, ng) * 2 + c, y, e)
            qs = lax.rem(g - r + ng, ng) * 2 + c
            cp = remote(src.at[sl], dst.at[b, q, sl], wss.at[j, r], wrs.at[j, r], t)
            inc = remote(src.at[sl], dst.at[b, qs, sl], wss.at[j, r], wrs.at[j, r], t)
            if r == 0:
                lc = pltpu.make_async_copy(src.at[sl], dst.at[b, q, sl], wls.at[j])

                @pl.when(self_in)
                def _():
                    lc.start()

                @pl.when(jnp.logical_not(self_in))
                def _():
                    cp.start()

                w_in[j].append((inc, qs, lc))
                w_out[j].append(cp)
            else:
                start(cp)
                w_in[j].append((inc, qs, None))

    def w_on(j, xx, qs, s, target, yx, yq):
        _, dst, o, n = pieces[j]
        sl = pl.ds(o, n)
        start(remote(dst.at[xx, qs, sl], dst.at[xx, qs, sl], wss.at[j, s], wrs.at[j, s], target))
        return remote(dst.at[xx, qs, sl], dst.at[yx, yq, sl], wss.at[j, s], wrs.at[j, s], target)

    def w_across(j):
        for r, (inc, qs, lc) in enumerate(w_in[j]):
            if lc is not None:

                @pl.when(self_in)
                def _():
                    lc.wait()

                @pl.when(jnp.logical_not(self_in))
                def _():
                    inc.wait_recv()
            else:
                inc.wait_recv()
            w_x[j].append(w_on(j, b, qs, ng + r, other_x, 1 - b, qs))
        for r, (_, qs, _) in enumerate(w_in[j]):
            w_c[j].append(w_on(j, b, qs, 2 * ng + r, other_c, b, lax.rem(g - r + ng, ng) * 2 + 1 - c))

    def w_core(j):
        for r, (_, qs, _) in enumerate(w_in[j]):
            w_x[j][r].wait_recv()
            w_c[j].append(w_on(j, 1 - b, qs, 3 * ng + r, other_c, 1 - b, lax.rem(g - r + ng, ng) * 2 + 1 - c))

    last = len(pieces)

    kept = []

    def keep(src, dst):
        cp = pltpu.make_async_copy(src, dst, osem.at[len(kept)])
        cp.start()
        kept.append(cp)

    qkv_x[...] = jnp.zeros(qkv_x.shape, BF16)
    per = qw - HD
    for j in range(4):
        qkv_x[j, :kr, :HD] = wq_ref[:, j * HD : (j + 1) * HD]
        o = j * per % HD
        qkv_x[j, :kr, HD:] = (wk_ref if j * per < HD else wv_ref)[:, o : o + per]
    trade(0)
    send_z(GAIN)
    if wd.shape[0] == dr:
        wd[...] = wd_x[...]
    else:
        whole = dr // 16 * 16
        wd[:whole] = wd_x[:whole]
        rest = jnp.zeros((wd.shape[0] - dr, wd.shape[1]), BF16)
        wd[whole:] = jnp.concatenate([wd_x[whole:], rest], axis=0)
    w_send(0)
    traded(0)
    send_z(KV)
    send_z(Q)
    split_rows(wg_ref, wg_x)
    trade(1)
    split_rows(wu_ref, wu_x)
    micro, _, tok, _ = q_s.shape
    rows = micro * tok
    x = x_ref[...].astype(F32)
    n_x = norm_of(x)[0]
    send_a(GAIN)
    send_a(KV)
    send_b(GAIN, 0)
    send_b(KV, 0)
    traded(1)
    w_send(1)
    send_b(GAIN, 1)
    send_b(KV, 1)
    send_a(Q)
    send_b(Q, 0)
    trade(2)
    w_across(0)
    w_send(2)
    send_z(WO)
    send_c(GAIN)
    send_c(KV)
    done(GAIN)
    done(KV)
    width = x_ref.shape[1]
    gains_d = spread_gains(gain_f[...].reshape(n_dev * 16, 128), width, n_dev)
    gains_h = spread_gains(gain_f[...].reshape(n_dev * 16, 128), HD, n_dev)
    gd_o[...] = gains_d
    gh_o[...] = gains_h
    a = (n_x * (1.0 + gains_d[0:1])).astype(BF16)
    cosine, sine = cos_ref[...], sin_ref[...]
    half = HD // 2

    def project(h):
        if h < H:
            w = wqkv[:, :, :, h * qw : h * qw + HD]
        else:
            o1, o2 = kv_columns(h - H, qw)
            w = jnp.concatenate([wqkv[:, :, :, o1 : o1 + half], wqkv[:, :, :, o2 : o2 + half]], axis=3)
        raw = jnp.dot(a, w.reshape(width, HD), preferred_element_type=F32)
        if h == H + 1:
            kv_own[:, :, HD:] = raw.astype(BF16).reshape(micro, tok, HD)
            return
        raw_s[:, h * HD : (h + 1) * HD] = raw
        z = norm_of(raw)[0] * (1.0 + (gains_h[1:2] if h < H else gains_h[2:3]))
        z1, z2 = z[:, :half], z[:, half:]
        z = jnp.concatenate([z1 * cosine - z2 * sine, z2 * cosine + z1 * sine], axis=1).astype(BF16)
        if h < H:
            q_s[:, h] = z.reshape(micro, tok, HD)
        else:
            kv_own[:, :, :HD] = z.reshape(micro, tok, HD)

    project(H)
    project(H + 1)
    ht = tok // 2
    is_first, is_mid = k == 0, k == nb // 2
    first, mid = (b, 0), (b, nb // 2)
    x_kv = remote(kv_own.at[:, :ht], xkv, xss.at[0], xrs.at[0], first)
    x_q = remote(q_s.at[:, :, :ht], xq, xss.at[1], xrs.at[1], first)
    x_o = remote(xob, xin, xss.at[2], xrs.at[2], mid)

    @pl.when(is_mid)
    def _():
        x_kv.start()

    side = q // hz
    ql = q - side * hz

    def kview(qq, yy, cc):
        return kvall.at[qq - side * hz, yy, cc]

    mine = pltpu.make_async_copy(kv_own, kview(q, y, c), kls)
    mine.start()
    kz_in, ky_in, kc_in = [], [], []
    for r in range(1, hz):
        t = at(b, side * hz + lax.rem(ql + r, hz), y, c)
        start(remote(kv_own, kview(q, y, c), kss.at[r], krs.at[r], t))
        src = side * hz + lax.rem(ql - r + hz, hz)
        kz_in.append((remote(kv_own, kview(src, y, c), kss.at[r], krs.at[r], t), src))
    start(remote(kv_own, kview(q, y, c), kss.at[hz], krs.at[hz], other_y))
    ky_in.append((remote(kv_own, kview(q, 1 - y, c), kss.at[hz], krs.at[hz], other_y), q))
    slot = [2 * hz]

    def k_core(qq, yy):
        s = slot[0]
        slot[0] += 1
        start(remote(kview(qq, yy, c), kview(qq, yy, c), kss.at[s], krs.at[s], other_c))
        kc_in.append(remote(kview(qq, yy, c), kview(qq, yy, 1 - c), kss.at[s], krs.at[s], other_c))

    mine.wait()
    k_core(q, y)
    traded(2)
    send_b(Q, 1)
    w_across(1)
    w_send(3)
    w_core(0)
    send_a(WO)
    send_b(WO, 0)
    for r, (cp, src) in enumerate(kz_in):
        cp.wait_recv()
        s = hz + 1 + r
        start(remote(kview(src, y, c), kview(src, y, c), kss.at[s], krs.at[s], other_y))
        ky_in.append((remote(kview(src, y, c), kview(src, 1 - y, c), kss.at[s], krs.at[s], other_y), src))
        k_core(src, y)
    send_c(Q)
    w_across(2)
    w_send(4)
    w_core(1)
    done(Q)
    for h in range(H):
        project(h)

    @pl.when(is_mid)
    def _():
        x_q.start()

    keep(wqkv, wqkv_h)
    keep(raw_s, raw_h)
    keep(q_s, q_h)
    send_b(WO, 1)
    for cp, src in ky_in:
        cp.wait_recv()
        k_core(src, 1 - y)
    w_across(3)
    w_send(5)
    w_core(2)
    for cp in kc_in:
        cp.wait_recv()

    scale = HD ** (-0.5)
    lo = side * (nb // 4)
    hi = k // 2 + 1
    qrows = H * tok
    qidx = k * tok + lax.rem(lax.broadcasted_iota(jnp.int32, (qrows, 1), 0), tok)

    def online(carry, s, ok, values):
        mx, sm, acc = carry
        if ok is not None:
            s = jnp.where(ok, s, -1e30)
        new = jnp.maximum(mx, jnp.max(s, axis=-1, keepdims=True))
        p = jnp.exp(s - new)
        if ok is not None:
            p = jnp.where(ok, p, 0.0)
        alpha = jnp.exp(mx - new)
        sm = sm * alpha + jnp.sum(p, axis=-1, keepdims=True)
        return new, sm, acc * alpha + jnp.dot(p.astype(BF16), values, preferred_element_type=F32)

    def empty(n):
        return jnp.full((n, 1), -1e30, F32), jnp.zeros((n, 1), F32), jnp.zeros((n, HD), F32)

    @pl.when(is_first)
    def _():
        x_kv.wait_recv()
        x_q.wait_recv()
        for m in range(micro):
            qm = xq[m].reshape(H * ht, HD)

            def body(j, carry):
                blk = kvall[j // 2, j % 2, :, m].reshape(256, 2 * HD)
                s = lax.dot_general(qm, blk[:, :HD], (((1,), (1,)), ((), ())), preferred_element_type=F32) * scale
                return online(carry, s, None, blk[:, HD:])

            carry = lax.fori_loop(0, nb // 4, body, empty(H * ht))
            blk = xkv[m]
            s = lax.dot_general(qm, blk[:, :HD], (((1,), (1,)), ((), ())), preferred_element_type=F32) * scale
            mx, sm, acc = online(carry, s, half_mask(H * ht, ht), blk[:, HD:])
            xo_s[m] = acc / sm
            xlse_s[m] = mx + jnp.log(sm)
            xob[m] = xo_s[m].astype(BF16).reshape(H, ht, HD)
        x_o.start()

    b_all = [Gather((b, g, e, y), c, tss.at[m], trs.at[m], sent) for m in range(micro)]
    for m in range(micro):
        qm = q_s[m].reshape(qrows, HD)
        segq = segment_of(len_ref, m, qidx)

        def body(j, carry):
            blk = kvall[j // 2 - side * hz, j % 2, :, m].reshape(256, 2 * HD)
            kidx = j * 256 + lax.broadcasted_iota(jnp.int32, (1, 256), 1)
            s, ok = chunk_scores(qm, blk[:, :HD], segq, segment_of(len_ref, m, kidx), qidx, j, scale)
            return online(carry, s, ok, blk[:, HD:])

        mx, sm, acc = lax.fori_loop(lo, hi, body, empty(qrows))
        o = acc / sm
        o_s[m] = o
        lse_s[m] = mx + jnp.log(sm)
        rs = slice(m * tok, (m + 1) * tok)
        for h in range(H):
            ob_s[rs, h * HD : (h + 1) * HD] = o[h * tok : (h + 1) * tok].astype(BF16)
        if m == 0:
            w_across(4)
            w_core(3)
            send_c(WO)
            done(WO)

            @pl.when(is_mid)
            def _():
                x_o.wait_recv()

        @pl.when(is_mid)
        def _():
            for h in range(H):
                ob_s[m * tok : m * tok + ht, h * HD : (h + 1) * HD] = xin[m, h]

        for o, n in tiles(width, 256):
            w = wo[:, :, :, :, :, o : o + n].reshape(H * HD, n)
            attn_s[rs, o : o + n] = jnp.dot(ob_s[rs], w, preferred_element_type=F32)
        h1 = x_ref[rs].astype(F32) + norm_of(attn_s[rs])[0] * (1.0 + gains_d[3:4])
        h1_o[m] = h1
        ball[m, e * 2 + y] = (norm_of(h1)[0] * (1.0 + gains_d[4:5])).astype(BF16)
        b_all[m].begin(ball.at[m])
        if m > 0:
            b_all[m - 1].forward()
    for src, dst in ((xq, xq_h), (xkv, xkv_h), (xo_s, xo_h), (xlse_s, xlse_h)):
        keep(src, dst)
    keep(o_s, o_h)
    keep(lse_s, lse_h)
    keep(ob_s, ob_h)
    keep(kvall, kv_h)
    keep(attn_s, attn_h)
    keep(wo, wo_h)
    w_across(5)
    w_core(4)
    b_all[micro - 1].forward()
    w_core(5)
    for m in range(micro):
        b_all[m].end()
    for j in range(last):
        for cp in w_c[j]:
            cp.wait_recv()
    for cp in sent:
        cp.wait_send()
    for j in range(last):

        @pl.when(jnp.logical_not(self_in))
        def _():
            w_out[j][0].wait_send()

    @pl.when(is_mid)
    def _():
        x_kv.wait_send()
        x_q.wait_send()

    @pl.when(is_first)
    def _():
        x_o.wait_send()

    for cp in kept:
        cp.wait()


def front(nz, x, cosine, sine, lengths, wq, wk, wv, wo, gain, wg, wu, wd, dp, micro):
    kr, kp = wg.shape[0], up16(wg.shape[0])
    fs = 2 * nz * dp
    qw = (wq.shape[1] + wk.shape[1] + wv.shape[1]) // 4
    ng = nz // 2
    hz = nz // 2
    rows, width = x.shape
    tok = rows // micro
    nb = 4 * nz
    out = {
        "ball": ((micro, 4, tok, width), BF16),
        "h1": ((micro, tok, width), F32),
        "attn": ((rows, width), F32),
        "raw": ((rows, (H + 1) * HD), F32),
        "q": ((micro, H, tok, HD), BF16),
        "o": ((micro, H * tok, HD), F32),
        "ob": ((rows, H * HD), BF16),
        "lse": ((micro, H * tok, 1), F32),
        "kv": ((hz, 2, 2, micro, tok, 2 * HD), BF16),
        "wqkv": ((2, nz, 4 * kr, 4 * qw), BF16),
        "wo": ((2, nz, 2, 2) + wo.shape, BF16),
        "xq": ((micro, H, tok // 2, HD), BF16),
        "xkv": ((micro, tok // 2, 2 * HD), BF16),
        "xo": ((micro, H * tok // 2, HD), F32),
        "xlse": ((micro, H * tok // 2, 1), F32),
        "gd": ((16, width), F32),
        "gh": ((16, HD), F32),
        "wg": ((2, nz, 4 * kr, fs), BF16),
        "wu": ((2, nz, 4 * kr, fs), BF16),
        "wd": ((2, nz, dp, width), BF16),
    }
    shapes = [jax.ShapeDtypeStruct(*v) for v in out.values()]
    scratch = [pltpu.VMEM(*out[n]) for n in ("attn", "raw", "q", "o", "ob", "lse", "kv")]
    ns = 2 * nz + 6
    n_pieces = 2 * len(halves(4 * kr)) + len(halves(dp))
    scratch += [pltpu.VMEM((micro, tok, 2 * HD), BF16), pltpu.VMEM(*out["wqkv"]), pltpu.VMEM(*out["wo"])]
    scratch += [pltpu.VMEM((2, nz, 2, 2) + gain.shape, BF16)]
    scratch += [pltpu.VMEM((4 * kr, n), BF16) for n in (qw, fs, fs)] + [pltpu.VMEM((dp, width), BF16)]
    scratch += [pltpu.VMEM((4, kp, n), BF16) for n in (qw, fs, fs) * 2]
    scratch += [pltpu.VMEM(*out[n]) for n in ("xq", "xkv", "xo", "xlse", "xq", "xq")]
    scratch += [pltpu.SemaphoreType.DMA((3,)), pltpu.SemaphoreType.DMA((3,))]
    scratch += [
        pltpu.SemaphoreType.DMA((4,)),
        pltpu.SemaphoreType.DMA((4, ns)),
        pltpu.SemaphoreType.DMA((4, ns)),
        pltpu.SemaphoreType.DMA((n_pieces,)),
        pltpu.SemaphoreType.DMA((n_pieces, 4 * ng)),
        pltpu.SemaphoreType.DMA((n_pieces, 4 * ng)),
        pltpu.SemaphoreType.DMA,
        pltpu.SemaphoreType.DMA((4 * hz,)),
        pltpu.SemaphoreType.DMA((4 * hz,)),
        pltpu.SemaphoreType.DMA((13,)),
        pltpu.SemaphoreType.DMA((3, 3)),
        pltpu.SemaphoreType.DMA((3, 4)),
        pltpu.SemaphoreType.DMA((micro, 6)),
        pltpu.SemaphoreType.DMA((micro, 6)),
    ]
    specs = [VMEM, VMEM] + [ANY] * 13 + [VMEM, VMEM] + [ANY] * 3
    got = pl.pallas_call(
        functools.partial(front_kernel, nz),
        out_shape=shapes,
        in_specs=[VMEM] * 3 + [pl.BlockSpec(memory_space=pltpu.SMEM)] + [VMEM] * 3 + [ANY] * 2 + [VMEM] * 3,
        out_specs=specs,
        scratch_shapes=scratch,
        compiler_params=pltpu.CompilerParams(collective_id=5, has_side_effects=True, vmem_limit_bytes=60 * 2**20),
    )(x, cosine, sine, lengths, wq, wk, wv, wo, gain, wg, wu, wd)
    return dict(zip(out, got))


def back_kernel(
    nz, db_ref, h1_ref, dy_ref, x_ref, cos_ref, sin_ref, len_ref, gd_ref, gh_ref, dgp_ref,
    attn_h, raw_h, q_h, o_h, ob_h, lse_h, kv_h, wqkv_h, wo_h, xq_h, xkv_h, xo_h, xlse_h, gg, gu, gdn,
    dx_o, q_o, k_o, v_o, wo_o, gain_o, wg_o, wu_o, wd_o,
    attn, raw, q_s, o_s, ob, lse, kvall, wqkv, wo, xq, xkv, xo, xlse,
    xdo, xdq, xdkv, xpart, qin, kvin, dh1, datt, do_s, delta, dqkv, da, gqkv, gwo, ggain,
    k1, k2, k3, *rest,
):
    hops = [rest[4 * i : 4 * i + 4] for i in range(4)]
    rest = rest[16:]
    wown, w1, w2, w3 = (rest[3 * i : 3 * i + 3] for i in range(4))
    q_r, kv_r, q_t, kv_t, wg_t, wu_t = rest[12:18]
    lsem, ssem, rsem, wls, wss, wrs, kss, krs, xss, xrs, qss, qrs = rest[18:]
    b, q, y, c = place()
    k = lax.axis_index("blk")
    nb = 4 * nz
    n_dev = 2 * nb
    g, e = q // 2, q % 2
    ng = nz // 2
    hz = nz // 2
    qw = gqkv.shape[3] // 4
    kr = gqkv.shape[2] // 4
    self_in = e == c
    other_x, other_y, other_c = at(1 - b, q, y, c), at(b, q, 1 - y, c), at(b, q, y, 1 - c)
    both, everything = pl.ds(0, 2), pl.ds(0, nz)
    micro, _, tok, _ = q_s.shape
    rows, width = x_ref.shape
    nt = (((1,), (1,)), ((), ()))
    tn = (((0,), (0,)), ((), ()))
    loads = []
    for i, (src, dst) in enumerate(
        ((attn_h, attn), (wo_h, wo), (o_h, o_s), (q_h, q_s), (kv_h, kvall), (lse_h, lse), (ob_h, ob), (raw_h, raw), (wqkv_h, wqkv),
         (xq_h, xq), (xkv_h, xkv), (xo_h, xo), (xlse_h, xlse))
    ):
        cp = pltpu.make_async_copy(src, dst, lsem.at[i])
        cp.start()
        loads.append(cp)
    front_barrier(nz)
    sent = []

    def start(cp):
        cp.start()
        sent.append(cp)
        return cp

    def add(dst, src, n, step):
        def one(i, _):
            sl = pl.ds(pl.multiple_of(i * step, step), step)
            dst[sl] = dst[sl] + src[sl]
            return 0

        lax.fori_loop(0, n // step, one, 0)

    quad = [(y, 1 - c), (1 - y, c), (1 - y, 1 - c)]
    t_in = []

    def trade(src, dst, s, cols):
        for p, (yy, cc) in enumerate(quad):
            there = remote(src.at[yy * 2 + cc, :, cols], dst.at[y * 2 + c, :, cols], qss.at[s, p], qrs.at[s, p], at(b, q, yy, cc))
            here = remote(src.at[yy * 2 + cc, :, cols], dst.at[yy * 2 + cc, :, cols], qss.at[s, p], qrs.at[s, p], at(b, q, yy, cc))
            start(there)
            t_in.append(here)
        dst[y * 2 + c, :, cols] = src[y * 2 + c, :, cols]

    def unpack_rows(total, kp):
        v = lax.dot_general(pack_rows(kr, kp), total, tn, preferred_element_type=F32)
        return v.astype(BF16).reshape(4, kp, total.shape[1])

    units = [(gg, wg_o, wg_t), (gu, wu_o, wu_t), (gdn, wd_o, None)]
    fs = gg.shape[4]
    near = fs // 256 * 128
    pieces = [(u, (0, gg.shape[3]), cols) for u in range(2) for cols in ((0, near), (near, fs - near))]
    pieces += [(2, r, (0, width)) for r in halves(gdn.shape[3])]
    dr = wd_o.shape[0]
    w_local, w_in = [None] * len(pieces), [None] * len(pieces)

    def part_of(j):
        u, (ro, rn), (co, cn) = pieces[j]
        return u, pl.ds(ro, rn), pl.ds(co, cn), rn

    def w_core(j):
        u, sl, cl, _ = part_of(j)
        src = units[u][0]
        w_in[j] = start(remote(src.at[:, :, 1 - c, sl, cl], w1[u].at[:, :, sl, cl], wss.at[j, 0], wrs.at[j, 0], other_c))
        w_local[j] = pltpu.make_async_copy(src.at[:, :, c, sl, cl], wown[u].at[:, :, sl, cl], wls.at[j, 0])
        w_local[j].start()

    def w_x(j):
        u, sl, cl, n = part_of(j)
        w_local[j].wait()
        w_in[j].wait_recv()
        for r in range(ng):
            add(wown[u].at[1 - b, r, sl, cl], w1[u].at[1 - b, r, sl, cl], n, 16)
        w_in[j] = start(remote(wown[u].at[1 - b, :, sl, cl], w2[u].at[:, sl, cl], wss.at[j, 1], wrs.at[j, 1], other_x))
        for r in range(ng):
            add(wown[u].at[b, r, sl, cl], w1[u].at[b, r, sl, cl], n, 16)

    def w_z(j):
        u, sl, cl, n = part_of(j)
        w_in[j].wait_recv()
        for r in range(ng):
            add(wown[u].at[b, r, sl, cl], w2[u].at[r, sl, cl], n, 16)
        waits = []
        for r in range(ng):
            gs = lax.rem(g + r, ng)
            src, dst = wown[u].at[b, gs, sl, cl], w3[u].at[r, sl, cl]
            cp = remote(src, dst, wss.at[j, 2 + r], wrs.at[j, 2 + r], at(b, gs * 2 + c, y, e))
            lc = None
            if r == 0:
                lc = pltpu.make_async_copy(src, dst, wls.at[j, 1])

                @pl.when(self_in)
                def _():
                    lc.start()

                @pl.when(jnp.logical_not(self_in))
                def _():
                    cp.start()
            else:
                start(cp)
            waits.append((cp, lc))
        w_in[j] = waits

    def w_end(j):
        u, (ro, rn), (co, cn) = pieces[j]
        for cp, lc in w_in[j]:
            if lc is not None:

                @pl.when(self_in)
                def _():
                    lc.wait()

                @pl.when(jnp.logical_not(self_in))
                def _():
                    cp.wait()
            else:
                cp.wait_recv()
        _, out, send = units[u]
        if send is None:

            def total_of(sl):
                total = w3[u][0, sl].astype(F32)
                for r in range(1, ng):
                    total = total + w3[u][r, sl].astype(F32)
                return total

            def one(i, _):
                sl = pl.ds(pl.multiple_of(ro + i * 16, 16), 16)
                out[sl] = total_of(sl)
                return 0

            end = min(ro + rn, dr)
            full = (end - ro) // 16
            lax.fori_loop(0, full, one, 0)
            if ro + full * 16 < end:
                out[ro + full * 16 : end] = total_of(pl.ds(ro + full * 16, 16))[: end - ro - full * 16]
        else:

            def one(i, _):
                cols = pl.ds(pl.multiple_of(co + i * 128, 128), 128)
                total = w3[u][0, :, cols].astype(F32)
                for r in range(1, ng):
                    total = total + w3[u][r, :, cols].astype(F32)
                send[:, :, cols] = unpack_rows(total.astype(BF16), send.shape[1])
                return 0

            lax.fori_loop(0, cn // 128, one, 0)
            trade(send, out, j, pl.ds(co, cn))

    w_core(0)
    w_core(1)

    def view_q(ref, yy, cc):
        return ref.at[:, :, :, pl.ds(pl.multiple_of((yy * 2 + cc) * qw, 128), HD)]

    def view_kv(ref, yy, cc):
        return ref.at[:, :, :, pl.ds(pl.multiple_of((yy * 2 + cc) * qw + HD, 128), qw - HD)]

    def view_lead(ref, yy, cc):
        return ref.at[:, :, yy, cc]

    items = [
        (gqkv, view_q, hops[0], None),
        (gwo, view_lead, hops[1], wo_o),
        (ggain, view_lead, hops[2], gain_o),
        (gqkv, view_kv, hops[3], None),
    ]
    item_in = [[] for _ in items]

    def join(dst, src, lead):
        for idx in lead:
            dst[idx] = dst[idx] + src[idx]

    def grid2(v):
        return [(xx, qq) for xx in range(2) for qq in range(nz)]

    def item_core(i):
        src, view, (r1, _, _, _), _ = items[i]
        for yy in range(2):
            item_in[i].append(start(remote(view(src, yy, 1 - c), r1.at[yy], ssem.at[i, yy], rsem.at[i, yy], other_c)))

    def loop2(fn):
        def one(n, _):
            fn(lax.div(n, nz), lax.rem(n, nz))
            return 0

        lax.fori_loop(0, 2 * nz, one, 0)

    def item_y(i):
        src, view, (r1, r2, _, _), _ = items[i]
        for cp in item_in[i]:
            cp.wait_recv()
        for yy in (1 - y, y):
            v = view(src, yy, c)

            def fn(xx, qq):
                v[xx, qq] = v[xx, qq] + r1[yy, xx, qq]

            loop2(fn)
            if yy is not y:
                item_in[i] = [start(remote(v, r2, ssem.at[i, 2], rsem.at[i, 2], other_y))]

    def item_x(i):
        src, view, (_, r2, r3, _), _ = items[i]
        item_in[i][0].wait_recv()
        v = view(src, y, c)

        def fn(xx, qq):
            v[xx, qq] = v[xx, qq] + r2[xx, qq]

        loop2(fn)
        item_in[i] = [start(remote(v.at[1 - b], r3, ssem.at[i, 3], rsem.at[i, 3], other_x))]

    def item_z(i):
        src, view, (_, _, r3, r4), _ = items[i]
        item_in[i][0].wait_recv()
        v = view(src, y, c)
        for qq in range(nz):
            v[b, qq] = v[b, qq] + r3[qq]
        waits = []
        for r in range(1, nz):
            qt = lax.rem(q + r, nz)
            waits.append(start(remote(v.at[b, qt], r4.at[r - 1], ssem.at[i, 3 + r], rsem.at[i, 3 + r], at(b, qt, y, c))))
        item_in[i] = waits

    def item_end(i):
        src, view, (_, _, _, r4), out = items[i]
        for cp in item_in[i]:
            cp.wait_recv()
        v = view(src, y, c)
        total = v[b, q].astype(F32)
        for r in range(1, nz):
            total = total + r4[r - 1].astype(F32)
        if i in (0, 3):
            send, dst = (q_t, q_r) if i == 0 else (kv_t, kv_r)
            send[...] = unpack_rows(total.astype(BF16), send.shape[1])
            trade(send, dst, len(pieces) + i // 3, pl.ds(0, send.shape[2]))
        else:
            out[...] = total

    gains = gd_ref[...]
    loads[0].wait()
    dy = dy_ref[...].astype(F32)
    n1, r1 = norm_of(h1_ref[...].reshape(rows, width))
    d, dg_pf = norm_back(db_ref[...].reshape(rows, width), n1, r1, 1.0 + gains[4:5])
    dh1[...] = dy + d
    n2, r2 = norm_of(attn[...])
    d, dg_pa = norm_back(dh1[...], n2, r2, 1.0 + gains[3:4])
    datt[...] = d.astype(BF16)
    w_x(0)
    w_core(2)
    w_core(3)
    loads[1].wait()
    loads[2].wait()
    for h in range(H):
        w = wo[...].reshape(H * HD, width)[h * HD : (h + 1) * HD]
        d = lax.dot_general(datt[...], w, nt, preferred_element_type=F32).astype(BF16)
        do_s[:, h] = d.reshape(micro, tok, HD)
        for m in range(micro):
            hs = slice(h * tok, (h + 1) * tok)
            delta[m, hs] = jnp.sum(d[m * tok : (m + 1) * tok].astype(F32) * o_s[m, hs], axis=-1, keepdims=True)
    ht = tok // 2
    is_first, is_mid = k == 0, k == nb // 2
    first, mid = (b, 0), (b, nb // 2)
    x_do = remote(do_s.at[:, :, :ht], xdo, xss.at[0], xrs.at[0], first)
    x_dq = remote(xdq, qin, xss.at[1], xrs.at[1], mid)
    x_dkv = remote(xdkv, kvin, xss.at[2], xrs.at[2], mid)

    @pl.when(is_mid)
    def _():
        x_do.start()

    w_x(1)
    w_core(4)
    w_core(5)
    for i in (3, 4, 5, 9, 10, 11, 12):
        loads[i].wait()

    @pl.when(is_mid)
    def _():
        x_do.wait_send()
        do_s[:, :, :ht] = jnp.zeros((micro, H, ht, HD), BF16)
        for m in range(micro):
            for h in range(H):
                delta[m, h * tok : h * tok + ht] = jnp.zeros((ht, 1), F32)


    side = q // hz
    ql = q - side * hz
    scale = HD ** (-0.5)
    lo = side * (nb // 4)
    hi = k // 2 + 1
    part = kvall

    def clear(j, _):
        part[j // 2 - side * hz, j % 2] = jnp.zeros(part.shape[2:], BF16)
        return 0

    @pl.when(jnp.logical_not(is_first))
    def _():
        lax.fori_loop(hi, (side + 1) * 2 * hz, clear, 0)

    def grads_of(qm, dom, blk, p, dl):
        dp = lax.dot_general(dom, blk[:, HD:], nt, preferred_element_type=F32)
        ds = (p * (dp - dl)).astype(BF16)
        dq = jnp.dot(ds, blk[:, :HD], preferred_element_type=F32) * scale
        dk = lax.dot_general(ds, qm, tn, preferred_element_type=F32) * scale
        dv = lax.dot_general(p.astype(BF16), dom, tn, preferred_element_type=F32)
        return dq, jnp.concatenate([dk, dv], axis=1)

    @pl.when(is_first)
    def _():
        x_do.wait_recv()
        for m in range(micro):
            qm, dom = xq[m].reshape(H * ht, HD), xdo[m].reshape(H * ht, HD)
            dl = jnp.sum(dom.astype(F32) * xo[m], axis=-1, keepdims=True)

            def one(blk, ok):
                s = lax.dot_general(qm, blk[:, :HD], nt, preferred_element_type=F32) * scale
                p = jnp.exp(s - xlse[m]) if ok is None else jnp.where(ok, jnp.exp(jnp.where(ok, s, -1e30) - xlse[m]), 0.0)
                return grads_of(qm, dom, blk, p, dl)

            dq, g0 = one(kvall[0, 0, :, m].reshape(256, 2 * HD), None)
            xpart[m] = g0.astype(BF16)

            def body(j, dq):
                d, g = one(kvall[j // 2, j % 2, :, m].reshape(256, 2 * HD), None)
                part[j // 2, j % 2, :, m] = g.astype(BF16).reshape(2, tok, 2 * HD)
                return dq + d

            dq = lax.fori_loop(1, nb // 4, body, dq)
            d, g = one(xkv[m], half_mask(H * ht, ht))
            xdq[m] = (dq + d).astype(BF16).reshape(H, ht, HD)
            xdkv[m] = g.astype(BF16)
        x_dq.start()
        x_dkv.start()

    qrows = H * tok
    qidx = k * tok + lax.rem(lax.broadcasted_iota(jnp.int32, (qrows, 1), 0), tok)
    dq_s = o_s
    for m in range(micro):
        dq_s[m] = jnp.zeros(dq_s.shape[1:], F32)
        segq = segment_of(len_ref, m, qidx)

        def body(j, _):
            qm, dom = q_s[m].reshape(qrows, HD), do_s[m].reshape(qrows, HD)
            blk = kvall[j // 2 - side * hz, j % 2, :, m].reshape(256, 2 * HD)
            kidx = j * 256 + lax.broadcasted_iota(jnp.int32, (1, 256), 1)
            s, ok = chunk_scores(qm, blk[:, :HD], segq, segment_of(len_ref, m, kidx), qidx, j, scale)
            p = jnp.where(ok, jnp.exp(jnp.where(ok, s, -1e30) - lse[m]), 0.0)
            dq, g = grads_of(qm, dom, blk, p, delta[m])
            dq_s[m] += dq
            part[j // 2 - side * hz, j % 2, :, m] = g.astype(BF16).reshape(2, tok, 2 * HD)
            return 0

        lax.fori_loop(lo, hi, body, 0)

        @pl.when(is_first)
        def _():
            g = part[0, 0, :, m].reshape(256, 2 * HD).astype(F32) + xpart[m].astype(F32)
            part[0, 0, :, m] = g.astype(BF16).reshape(2, tok, 2 * HD)

        w_z(m)
        w_x(m + 2)

    k_in = start(remote(part.at[:, :, 1 - c], k1, kss.at[0], krs.at[0], other_c))
    loads[6].wait()
    obt = [ob[:, h * HD : (h + 1) * HD].T for h in range(H)]
    per = gwo.shape[0] * gwo.shape[1] * 4 // H
    for h in range(H):
        for o, n in tiles(width, 384):
            v = jnp.dot(obt[h], datt[:, o : o + n], preferred_element_type=F32).astype(BF16)
            n_lead = (2 * nz) // H
            xx, qq = (h * n_lead) // nz, (h * n_lead) % nz
            gwo[xx, qq : qq + n_lead, :, :, :, o : o + n] = v.reshape(n_lead, 2, 2, gwo.shape[4], n)
    item_core(1)
    k_in.wait_recv()

    def add1(n, _):
        part[n // 2, n % 2, c] = part[n // 2, n % 2, c] + k1[n // 2, n % 2]
        return 0

    lax.fori_loop(0, 2 * hz, add1, 0)
    k_in = start(remote(part.at[:, 1 - y, c], k2, kss.at[1], krs.at[1], other_y))
    loads[7].wait()
    cosine, sine = cos_ref[...], sin_ref[...]
    half = HD // 2
    gh = gh_ref[...]

    def unrotate(z):
        z1, z2 = z[:, :half], z[:, half:]
        return jnp.concatenate([z1 * cosine + z2 * sine, z2 * cosine - z1 * sine], axis=1)

    @pl.when(is_mid)
    def _():
        x_dq.wait_recv()
        for h in range(H):
            dq_s[:, h * tok : h * tok + ht] = qin[:, h].astype(F32)

    dg_q = jnp.zeros((1, HD), F32)
    for h in range(H):
        z = unrotate(dq_s[:, h * tok : (h + 1) * tok].reshape(rows, HD))
        n3, r3 = norm_of(raw[:, h * HD : (h + 1) * HD])
        d, dg = norm_back(z, n3, r3, 1.0 + gh[1:2])
        dqkv[:, h * qw : h * qw + HD] = d.astype(BF16)
        dg_q = dg_q + dg
    w_z(2)
    w_x(4)
    k_in.wait_recv()

    def add2(n, _):
        part[n, y, c] = part[n, y, c] + k2[n]
        return 0

    lax.fori_loop(0, hz, add2, 0)
    k_last = []
    for r in range(1, hz):
        qt = lax.rem(ql + r, hz)
        t = at(b, side * hz + qt, y, c)
        k_last.append(start(remote(part.at[qt, y, c], k3.at[r - 1], kss.at[1 + r], krs.at[1 + r], t)))
    item_y(1)
    n_x, r_x = norm_of(x_ref[...].astype(F32))
    at_ = (n_x * (1.0 + gains[0:1])).astype(BF16).T

    def weight_grad(o, n):
        v = jnp.dot(at_, dqkv[:, o : o + n], preferred_element_type=F32).astype(BF16)
        gqkv[:, :, :, o : o + n] = v.reshape(gqkv.shape[:3] + (n,))

    for h in range(H):
        weight_grad(h * qw, HD)
    item_core(0)
    w_z(3)
    w_x(5)
    w_end(0)
    total = part[ql, y, c].astype(F32)
    for r, cp in enumerate(k_last):
        cp.wait_recv()
        total = total + k3[r].astype(F32)

    dq_s[:, :tok] = total[:, :, :HD]
    dq_s[:, tok : 2 * tok] = total[:, :, HD:]

    @pl.when(is_mid)
    def _():
        x_dkv.wait_recv()
        dq_s[:, :ht] += kvin[:, :, :HD].astype(F32)
        dq_s[:, tok : tok + ht] += kvin[:, :, HD:].astype(F32)

    d_key, d_value = dq_s[:, :tok].reshape(rows, HD), dq_s[:, tok : 2 * tok].reshape(rows, HD)
    n3, r3 = norm_of(raw[:, H * HD :])
    d, dg_k = norm_back(unrotate(d_key), n3, r3, 1.0 + gh[2:3])
    for i, z in enumerate((d, d_value)):
        for o, v in zip(kv_columns(i, qw), (z[:, :half], z[:, half:])):
            dqkv[:, o : o + half] = v.astype(BF16)
            weight_grad(o, half)
    item_core(3)
    loads[8].wait()
    quads_at_once = max(1, 256 // wqkv.shape[2])
    for xx in range(2):
        for qq in range(0, nz, quads_at_once):
            n = min(quads_at_once, nz - qq)
            w = wqkv[xx, qq : qq + n].reshape(n * wqkv.shape[2], wqkv.shape[3])
            o = (xx * nz + qq) * wqkv.shape[2]
            da[o : o + n * wqkv.shape[2], :] = lax.dot_general(w, dqkv[...], nt, preferred_element_type=F32)
    d, dg_in = norm_back(da[...].T, n_x, r_x, 1.0 + gains[0:1])
    dx_o[...] = (dh1[...] + d).astype(BF16).reshape(dx_o.shape)
    none = jnp.zeros((1, width), F32)
    nohd = jnp.zeros((1, HD), F32)
    wide = jnp.concatenate([dg_in, none, none, dg_pa, dg_pf, dgp_ref[...], none, none], axis=0)
    slim = jnp.concatenate([nohd, dg_q, dg_k] + [nohd] * 5, axis=0)
    ggain[...] = (collect_gains(wide, n_dev) + collect_gains(slim, n_dev)).reshape(ggain.shape)
    item_core(2)
    w_z(4)
    item_x(1)
    item_y(0)
    item_y(3)
    item_y(2)
    w_end(1)
    w_z(5)
    item_z(1)
    w_end(2)
    item_x(0)
    item_x(3)
    item_x(2)
    w_end(3)
    item_z(0)
    item_z(3)
    item_z(2)
    item_end(1)
    w_end(4)
    w_end(5)
    item_end(0)
    item_end(3)
    item_end(2)
    for cp in t_in:
        cp.wait_recv()
    for j in range(4):
        q_o[:, j * HD : (j + 1) * HD] = q_r[j, :kr].astype(F32)
        half_o = k_o if j < 2 else v_o
        half_o[:, j % 2 * half : (j % 2 + 1) * half] = kv_r[j, :kr].astype(F32)
    for cp in sent:
        cp.wait_send()

    @pl.when(is_first)
    def _():
        x_dq.wait_send()
        x_dkv.wait_send()


def back(nz, db, h1, dy, x, cosine, sine, lengths, dgp, f, gg, gu, gd, kp, dr):
    ng = nz // 2
    hz = nz // 2
    nb = 4 * nz
    micro, tok, width = db.shape
    rows = micro * tok
    qr = f["wqkv"].shape[2]
    qw = f["wqkv"].shape[3] // 4
    orow = f["wo"].shape[4]
    kv = f["kv"].shape

    def like(n):
        return pltpu.VMEM(f[n].shape, f[n].dtype)

    gsplit = [z.reshape(2, ng, 2, -1, z.shape[-1]) for z in (gg, gu, gd)]
    ublock = [gsplit[i].shape[3:] for i in (2, 0, 1)]
    iblock = [((qr, HD), BF16), ((orow, width), BF16), ((8, 128), F32), ((qr, qw - HD), BF16)]
    scratch = [like(n) for n in ("attn", "raw", "q", "o", "ob", "lse", "kv", "wqkv", "wo", "xq", "xkv", "xo", "xlse")]
    scratch += [like("xq"), like("xq"), like("xkv"), pltpu.VMEM((micro, 256, 2 * HD), BF16), like("xq"), like("xkv")]
    scratch += [
        pltpu.VMEM((rows, width), F32),
        pltpu.VMEM((rows, width), BF16),
        pltpu.VMEM((micro, H, tok, HD), BF16),
        pltpu.VMEM((micro, H * tok, 1), F32),
        pltpu.VMEM((rows, (H + 2) * HD), BF16),
        pltpu.VMEM((width, rows), F32),
        pltpu.VMEM((2, nz, qr, 4 * qw), BF16),
        pltpu.VMEM((2, nz, 2, 2, orow, width), BF16),
        pltpu.VMEM((2, nz, 2, 2, 8, 128), F32),
        pltpu.VMEM((hz, 2) + kv[3:], BF16),
        pltpu.VMEM((hz,) + kv[3:], BF16),
        pltpu.VMEM((hz - 1,) + kv[3:], BF16),
    ]
    for s, t in iblock:
        scratch += [pltpu.VMEM(lead + s, t) for lead in ((2, 2, nz), (2, nz), (nz,), (nz - 1,))]
    for lead in ((2, ng), (2, ng), (ng,), (ng,)):
        scratch += [pltpu.VMEM(lead + ublock[i], BF16) for i in (1, 2, 0)]
    fs = ublock[1][1]
    scratch += [pltpu.VMEM((4, kp, n), BF16) for n in (HD, qw - HD)]
    scratch += [pltpu.VMEM((4, kp, n), BF16) for n in (HD, qw - HD, fs, fs)]
    n_pieces = 4 + len(halves(ublock[0][0]))
    scratch += [
        pltpu.SemaphoreType.DMA((13,)),
        pltpu.SemaphoreType.DMA((4, nz + 3)),
        pltpu.SemaphoreType.DMA((4, nz + 3)),
        pltpu.SemaphoreType.DMA((n_pieces, 2)),
        pltpu.SemaphoreType.DMA((n_pieces, 2 + ng)),
        pltpu.SemaphoreType.DMA((n_pieces, 2 + ng)),
        pltpu.SemaphoreType.DMA((hz + 1,)),
        pltpu.SemaphoreType.DMA((hz + 1,)),
        pltpu.SemaphoreType.DMA((3,)),
        pltpu.SemaphoreType.DMA((3,)),
        pltpu.SemaphoreType.DMA((n_pieces + 2, 3)),
        pltpu.SemaphoreType.DMA((n_pieces + 2, 3)),
    ]
    out = [
        jax.ShapeDtypeStruct((micro, tok, width), BF16),
        jax.ShapeDtypeStruct((qr // 4, H * HD), F32),
        jax.ShapeDtypeStruct((qr // 4, HD), F32),
        jax.ShapeDtypeStruct((qr // 4, HD), F32),
        jax.ShapeDtypeStruct((orow, width), F32),
        jax.ShapeDtypeStruct((8, 128), F32),
        jax.ShapeDtypeStruct((4, kp, fs), BF16),
        jax.ShapeDtypeStruct((4, kp, fs), BF16),
        jax.ShapeDtypeStruct((dr, width), F32),
    ]
    return pl.pallas_call(
        functools.partial(back_kernel, nz),
        out_shape=out,
        in_specs=[VMEM] * 6 + [pl.BlockSpec(memory_space=pltpu.SMEM)] + [VMEM] * 3 + [ANY] * 16,
        out_specs=[VMEM] * 9,
        scratch_shapes=scratch,
        compiler_params=pltpu.CompilerParams(collective_id=6, has_side_effects=True, vmem_limit_bytes=63 * 2**20),
    )(
        db, h1, dy, x, cosine, sine, lengths, f["gd"], f["gh"], dgp,
        f["attn"], f["raw"], f["q"], f["o"], f["ob"], f["lse"], f["kv"], f["wqkv"], f["wo"],
        f["xq"], f["xkv"], f["xo"], f["xlse"], *gsplit,
    )


def scaled_norm(values, gain):
    return values * lax.rsqrt(jnp.mean(values * values, axis=-1, keepdims=True) + epsilon) * (1.0 + gain)


def segments(lengths, index):
    docs = lengths.shape[1]
    ends = [sum(lengths[:, j] for j in range(i + 1)) for i in range(docs)]
    seg = jnp.zeros((lengths.shape[0], index.shape[0]), jnp.int32)
    first = jnp.zeros_like(seg)
    for i in range(docs):
        past = index[None, :] >= ends[i][:, None]
        seg = seg + past.astype(jnp.int32)
        first = first + jnp.where(past, lengths[:, i][:, None], 0)
    return seg, index[None, :] - first


def rotate(values, cosine, sine):
    half = values.shape[-1] // 2
    a, b = values[..., :half], values[..., half:]
    return jnp.concatenate([a * cosine - b * sine, b * cosine + a * sine], axis=-1)


def middle(attn_value, x_value, gain_attn, gain_pre):
    hidden = x_value + scaled_norm(attn_value, gain_attn)
    return (hidden, scaled_norm(hidden, gain_pre))


def layer_apart(tokens, cotangent, doc_lengths, w_query, w_key, w_value, w_out, w_gate, w_up, w_down, *gains):
    nb = lax.axis_size("blk")
    nz = nb // 4
    me = lax.axis_index("blk")
    _, micro, tok, width = tokens.shape
    n_dev = 2 * nb
    nq = 2 * nz
    kr = w_gate.shape[0]
    qr, qp = 4 * kr, up16(4 * kr)
    dr = w_down.shape[0]
    dp = up16(dr)
    orow = w_out.shape[0]
    op = up16(orow)
    groups = [[4 * i + j for j in range(4)] for i in range(nz)]

    def fit(x, rows):
        return x if x.shape[0] == rows else jnp.pad(x, ((0, rows - x.shape[0]), (0, 0)))

    def slices(w):
        w = jnp.pad(w.reshape(kr, nq, 4, dr), ((0, 0), (0, 0), (0, 0), (0, dp - dr)))
        return w.transpose(2, 0, 1, 3).reshape(4, kr, nq * dp)

    fs = nq * dp
    w_qkv = jnp.concatenate([w_query, w_key, w_value], axis=1)
    qw = w_qkv.shape[1] // 4
    pack = jnp.concatenate([slices(w_gate), slices(w_up), w_qkv.reshape(kr, 4, qw).transpose(1, 0, 2)], axis=2)
    pack = lax.all_to_all(pack, "blk", split_axis=0, concat_axis=0, axis_index_groups=groups, tiled=True)
    pack = fit(pack.reshape(qr, 2 * fs + qw), qp)
    wide = [gain.shape[0] for gain in gains]
    flat = jnp.concatenate(gains)
    flat = jnp.pad(flat, (0, 16 * 128 - flat.shape[0])).reshape(16, 128)

    qkv_f, wo_f, gain_f, wg_f, wu_f, wd_f = gather_all(
        nz, pack[:, 2 * fs :], fit(w_out, op), flat, pack[:, :fs], pack[:, fs : 2 * fs], fit(w_down, dp)
    )
    wqkv = qkv_f[:, :, :qr].reshape(width, 4 * qw)
    wo = wo_f[:, :, :, :, :orow].reshape(n_dev * orow, width)
    wg = wg_f[:, :, :qr].reshape(width, fs)
    wu = wu_f[:, :, :qr].reshape(width, fs)
    wd = wd_f.reshape(fs, width)
    gain_rows = gain_f.reshape(n_dev, 16 * 128)
    full_gains, o = [], 0
    for w in wide:
        full_gains.append(gain_rows[:, o : o + w].reshape(n_dev * w).astype(F32))
        o += w
    gain_in, gain_query, gain_key, gain_attn, gain_pre, gain_post = full_gains

    lengths = doc_lengths[0]
    seg_all, pos_all = segments(lengths, jnp.arange(nb * tok, dtype=jnp.int32))
    seg_me, pos = segments(lengths, me * tok + jnp.arange(tok, dtype=jnp.int32))
    segq = jnp.tile(seg_me, (1, H))[:, :, None]
    segk = seg_all.reshape(micro, nb * tok // 256, 1, 256)
    freq = 1000000.0 ** (-(jnp.arange(HD // 2, dtype=F32) * 2.0 / HD))
    angle = pos.reshape(micro * tok).astype(F32)[:, None] * freq[None, :]
    cosine, sine = jnp.cos(angle), jnp.sin(angle)

    rows = micro * tok
    x = tokens[0].reshape(rows, width).astype(F32)
    dy = cotangent[0].reshape(rows, width)
    normed, pre_pull = jax.vjp(scaled_norm, x, gain_in)
    a = normed.astype(BF16)
    qkv = jnp.dot(a, wqkv, preferred_element_type=F32)
    n_q = H * HD
    q_raw = qkv[:, :n_q].reshape(rows, H, HD)
    k_raw = qkv[:, n_q : n_q + HD]
    v = qkv[:, n_q + HD :].astype(BF16)
    queries, query_pull = jax.vjp(
        lambda r, g: rotate(scaled_norm(r, g), cosine[:, None], sine[:, None]), q_raw, gain_query
    )
    keys, key_pull = jax.vjp(lambda r, g: rotate(scaled_norm(r, g), cosine, sine), k_raw, gain_key)

    def by_head(z):
        return z.reshape(micro, tok, H, HD).transpose(0, 2, 1, 3).reshape(micro, H * tok, HD)

    def by_row(z):
        return z.reshape(micro, H, tok, HD).transpose(0, 2, 1, 3).reshape(rows, H * HD)

    qh = by_head(queries.astype(BF16))
    kv = jnp.concatenate([keys.astype(BF16), v], axis=1).reshape(micro, tok, 2 * HD)
    oh, lse, kvall = attn_fwd(nb, qh, kv, segq, segk)
    o_b = by_row(oh.astype(BF16))
    attn = jnp.dot(o_b, wo, preferred_element_type=F32)
    (h1, ffn_in), mid_pull = jax.vjp(middle, attn, x, gain_attn, gain_pre)

    shape = (micro, tok, width)
    out, db, dg_post, gg, gu, gd = ffn(
        ffn_in.astype(BF16).reshape(shape), h1.reshape(shape), dy.reshape(shape), gain_post[None, :], wg, wu, wd
    )
    d_attn, d_x_mid, dg_attn, dg_pre = mid_pull((dy.astype(F32), db.reshape(rows, width)))
    d_attn = d_attn.astype(BF16)
    grad_out = lax.dot_general(o_b, d_attn, (((0,), (0,)), ((), ())), preferred_element_type=F32).astype(BF16)
    do = lax.dot_general(d_attn, wo, (((1,), (1,)), ((), ())), preferred_element_type=F32).astype(BF16)
    doh = by_head(do)
    delta = jnp.sum(doh.astype(F32) * oh, axis=-1, keepdims=True)
    dqh, dkv = attn_bwd(nb, qh, kvall, doh, lse, delta, segq, segk)
    dkv = dkv.reshape(rows, 2 * HD)
    dq_raw, dg_query = query_pull(by_row(dqh).reshape(rows, H, HD))
    dk_raw, dg_key = key_pull(dkv[:, :HD])
    d_qkv = jnp.concatenate([dq_raw.reshape(rows, n_q), dk_raw, dkv[:, HD:]], axis=1).astype(BF16)
    grad_qkv = lax.dot_general(a, d_qkv, (((0,), (0,)), ((), ())), preferred_element_type=F32).astype(BF16)
    da = lax.dot_general(d_qkv, wqkv, (((1,), (1,)), ((), ())), preferred_element_type=F32)
    d_x_pre, dg_in = pre_pull(da)
    d_x = (d_x_mid + d_x_pre).astype(BF16)

    def quads(z, r, p):
        z = z.reshape(2, nz, r, z.shape[-1])
        return z if r == p else jnp.pad(z, ((0, 0), (0, 0), (0, p - r), (0, 0)))

    go = grad_out.reshape(2, nz, 2, 2, orow, width)
    if op != orow:
        go = jnp.pad(go, ((0, 0),) * 4 + ((0, op - orow), (0, 0)))
    dgains = jnp.concatenate(
        [d.reshape(n_dev, w) for d, w in zip((dg_in, dg_query, dg_key, dg_attn, dg_pre, dg_post[0]), wide)], axis=1
    )
    used = dgains.shape[1]
    dgains = jnp.pad(dgains, ((0, 0), (0, 8 * 128 - used))).reshape(2, nz, 2, 2, 8, 128)
    s_qkv, s_wo, s_gain, s_wg, s_wu, s_wd = reduce_all(
        nz, quads(grad_qkv, qr, qp), go, dgains, quads(gg, qr, qp), quads(gu, qr, qp), gd.reshape(2, nz, dp, width)
    )
    back = jnp.concatenate([s_wg, s_wu, s_qkv], axis=1)[:qr].reshape(4, kr, 2 * fs + qw)
    back = lax.all_to_all(back, "blk", split_axis=0, concat_axis=0, axis_index_groups=groups, tiled=True)
    back = back.astype(F32)

    def rows_of(z):
        z = z.reshape(4, kr, nq, dp)[..., :dr]
        return z.transpose(1, 2, 0, 3).reshape(kr, nq * 4 * dr)

    s_qkv = back[:, :, 2 * fs :].transpose(1, 0, 2).reshape(kr, 4 * qw)
    flat = s_gain.reshape(-1)
    gain_grads, o = [], 0
    for w in wide:
        gain_grads.append(flat[o : o + w])
        o += w
    return (
        out[None],
        d_x.reshape(shape)[None],
        s_qkv[:, :n_q],
        s_qkv[:, n_q : n_q + HD],
        s_qkv[:, n_q + HD :],
        s_wo[:orow],
        rows_of(back[:, :, :fs]),
        rows_of(back[:, :, fs : 2 * fs]),
        s_wd[:dr],
        *gain_grads,
    )


def layer_fused(tokens, cotangent, doc_lengths, w_query, w_key, w_value, w_out, w_gate, w_up, w_down, *gains):
    nb = lax.axis_size("blk")
    nz = nb // 4
    me = lax.axis_index("blk")
    _, micro, tok, width = tokens.shape
    rows = micro * tok
    nq = 2 * nz
    kr, dr = w_gate.shape[0], w_down.shape[0]
    kp, dp = up16(kr), up16(dr)
    shape = (micro, tok, width)

    flat = jnp.stack([jnp.pad(gain, (0, 128 - gain.shape[0])) for gain in gains] + [jnp.zeros((128,), BF16)] * 10)
    lengths = doc_lengths[0]
    _, pos = segments(lengths, me * tok + jnp.arange(tok, dtype=jnp.int32))
    freq = 1000000.0 ** (-(jnp.arange(HD // 2, dtype=F32) * 2.0 / HD))
    angle = pos.reshape(rows).astype(F32)[:, None] * freq[None, :]
    cosine, sine = jnp.cos(angle), jnp.sin(angle)
    x = tokens[0].reshape(rows, width)
    dy = cotangent[0]
    f = front(nz, x, cosine, sine, lengths, w_query, w_key, w_value, w_out, flat, w_gate, w_up, w_down, dp, micro)
    wg, wu, wd = (f[n].reshape(-1, f[n].shape[-1]) for n in ("wg", "wu", "wd"))
    fine = (2 * micro, tok // 2, width)
    out, db, dg_post, gg, gu, gd = mlp(f["ball"], f["h1"].reshape(fine), dy.reshape(fine), f["gd"], wg, wu, wd)
    out, db = out.reshape(shape), db.reshape(shape)
    d_x, s_q, s_k, s_v, s_wo, s_gain, s_wg, s_wu, s_wd = back(
        nz, db, f["h1"], dy.reshape(rows, width), x, cosine, sine, lengths, dg_post, f, gg, gu, gd, kp, dr
    )

    def rows_of(z):
        z = z[:, :kr].reshape(4, kr, nq, dp)[..., :dr].astype(F32)
        return z.transpose(1, 2, 0, 3).reshape(kr, nq * 4 * dr)

    return (
        out[None],
        d_x[None],
        s_q,
        s_k,
        s_v,
        s_wo,
        rows_of(s_wg),
        rows_of(s_wu),
        s_wd,
        *(s_gain[i, : gain.shape[0]] for i, gain in enumerate(gains)),
    )


def shards(tokens, cotangent, doc_lengths, *params):
    nb = lax.axis_size("blk")
    w_out, w_gate = params[3], params[4]
    fits = nb * tokens.shape[2] <= 2048 and (4 * w_gate.shape[0]) % 16 == 0 and w_out.shape[0] % 16 == 0
    layer = layer_fused if fits else layer_apart
    return layer(tokens, cotangent, doc_lengths, *params)


def solution(mesh):
    sequence = P("bucket", None, "blk", None)
    split = ("bucket", "blk")
    return jax.shard_map(
        shards,
        mesh=mesh,
        in_specs=(sequence, sequence, P("bucket", None, None)) + (P(split, None),) * 7 + (P(split),) * 6,
        out_specs=(sequence, sequence) + (P(split, None),) * 7 + (P(split),) * 6,
        check_vma=False,
    )
```

```python
import functools
import math

import jax
import jax.numpy as jnp
from jax import lax
from jax.experimental import pallas as pl
from jax.experimental.pallas import tpu as pltpu
from jax.sharding import PartitionSpec as P

H = 4
HD = 256
F32 = jnp.float32
BF16 = jnp.bfloat16
MESH = pl.DeviceIdType.MESH
ANY = pl.BlockSpec(memory_space=pl.ANY)
VMEM = pl.BlockSpec(memory_space=pltpu.VMEM)
epsilon = 1e-06


def up16(n):
    return -(-n // 16) * 16


def place():
    b = lax.axis_index("bucket")
    k = lax.axis_index("blk")
    return b, k // 4, (k // 2) % 2, k % 2


def at(b, q, y, c):
    return (b, q * 4 + y * 2 + c)


def greet(targets):
    bar = pltpu.get_barrier_semaphore()
    for t in targets:
        pl.semaphore_signal(bar, inc=1, device_id=t, device_id_type=MESH)
    return bar


def remote(src, dst, send, recv, target):
    return pltpu.make_async_remote_copy(src, dst, send, recv, device_id=target, device_id_type=MESH)


def gather_kernel(nz, qkv, wo, gain, wg, wu, wd, qkv_f, wo_f, gain_f, wg_f, wu_f, wd_f, lsem, ssem, rsem, wls, wss, wrs):
    b, q, y, c = place()
    g, e = q // 2, q % 2
    ng = nz // 2
    qw = qkv.shape[1]
    self_in = e == c
    bar = greet(
        [at(b, lax.rem(q + r, nz), y, c) for r in range(1, nz)]
        + [at(1 - b, q, y, c), at(b, q, 1 - y, c), at(b, q, y, 1 - c)]
        + [at(b, lax.rem(g + r, ng) * 2 + c, y, e) for r in range(1, ng)]
    )
    first = at(b, g * 2 + c, y, e)

    @pl.when(jnp.logical_not(self_in))
    def _():
        pl.semaphore_signal(bar, inc=1, device_id=first, device_id_type=MESH)

    pl.semaphore_wait(bar, nz + 1 + ng - jnp.where(self_in, 1, 0) + 1)

    everything = pl.ds(0, nz)

    def view_qkv(ref, yy, cc, xx, qq):
        return ref.at[xx, qq, :, pl.ds(pl.multiple_of((yy * 2 + cc) * qw, 128), qw)]

    def view_lead(ref, yy, cc, xx, qq):
        return ref.at[xx, qq, yy, cc]

    items = [(qkv, qkv_f, view_qkv), (wo, wo_f, view_lead), (gain, gain_f, view_lead)]
    sent = []
    local = []
    for i, (src, dst, view) in enumerate(items):
        cp = pltpu.make_async_copy(src, view(dst, y, c, b, q), lsem.at[i])
        cp.start()
        local.append(cp)
    z_in = []
    for i, (src, dst, view) in enumerate(items):
        row = []
        for r in range(1, nz):
            cp = remote(src, view(dst, y, c, b, q), ssem.at[i, r], rsem.at[i, r], at(b, lax.rem(q + r, nz), y, c))
            cp.start()
            sent.append(cp)
            row.append(
                remote(src, view(dst, y, c, b, lax.rem(q - r + nz, nz)), ssem.at[i, r], rsem.at[i, r], at(b, lax.rem(q + r, nz), y, c))
            )
        z_in.append(row)
    x_in = [[] for _ in items]
    for i, (src, dst, view) in enumerate(items):
        cp = remote(src, view(dst, y, c, b, q), ssem.at[i, nz], rsem.at[i, nz], at(1 - b, q, y, c))
        cp.start()
        sent.append(cp)
        x_in[i].append(remote(src, view(dst, y, c, 1 - b, q), ssem.at[i, nz], rsem.at[i, nz], at(1 - b, q, y, c)))

    units = [(wg, wg_f), (wu, wu_f), (wd, wd_f)]
    u_in = []
    for j, (src, dst) in enumerate(units):
        row = []
        for r in range(ng):
            target = at(b, lax.rem(g + r, ng) * 2 + c, y, e)
            cp = remote(src, dst.at[b, q], wss.at[j, r], wrs.at[j, r], target)
            qs = lax.rem(g - r + ng, ng) * 2 + c
            inc = remote(src, dst.at[b, qs], wss.at[j, r], wrs.at[j, r], target)
            if r == 0:
                lc = pltpu.make_async_copy(src, dst.at[b, q], wls.at[j])

                @pl.when(self_in)
                def _():
                    lc.start()

                @pl.when(jnp.logical_not(self_in))
                def _():
                    cp.start()
            else:
                cp.start()
            row.append((cp, inc, qs, lc if r == 0 else None))
        u_in.append(row)

    for r in range(1, nz):
        qs = lax.rem(q - r + nz, nz)
        for i, (src, dst, view) in enumerate(items):
            z_in[i][r - 1].wait_recv()
            cp = remote(view(dst, y, c, b, qs), view(dst, y, c, b, qs), ssem.at[i, nz + r], rsem.at[i, nz + r], at(1 - b, q, y, c))
            cp.start()
            sent.append(cp)
            x_in[i].append(
                remote(view(dst, y, c, b, qs), view(dst, y, c, 1 - b, qs), ssem.at[i, nz + r], rsem.at[i, nz + r], at(1 - b, q, y, c))
            )
    for cp in local:
        cp.wait()
    y_in = [[] for _ in items]
    for half in range(2):
        for i, (src, dst, view) in enumerate(items):
            xx = b if half == 0 else 1 - b
            if half == 1:
                for cp in x_in[i]:
                    cp.wait_recv()
            s = 2 * nz + half
            cp = remote(view(dst, y, c, xx, everything), view(dst, y, c, xx, everything), ssem.at[i, s], rsem.at[i, s], at(b, q, 1 - y, c))
            cp.start()
            sent.append(cp)
            y_in[i].append(
                remote(view(dst, y, c, xx, everything), view(dst, 1 - y, c, xx, everything), ssem.at[i, s], rsem.at[i, s], at(b, q, 1 - y, c))
            )
    c_in = []

    def to_core(i, yy, s):
        _, dst, view = items[i]
        both = pl.ds(0, 2)
        cp = remote(view(dst, yy, c, both, everything), view(dst, yy, c, both, everything), ssem.at[i, s], rsem.at[i, s], at(b, q, y, 1 - c))
        cp.start()
        sent.append(cp)
        c_in.append(
            remote(view(dst, yy, c, both, everything), view(dst, yy, 1 - c, both, everything), ssem.at[i, s], rsem.at[i, s], at(b, q, y, 1 - c))
        )

    for i in range(len(items)):
        to_core(i, y, 2 * nz + 2)
    for i in range(len(items)):
        for cp in y_in[i]:
            cp.wait_recv()
        to_core(i, 1 - y, 2 * nz + 3)

    d_in = []

    def unit_on(j, xx, qs, s, target, yours):
        _, dst = units[j]
        cp = remote(dst.at[xx, qs], dst.at[xx, qs], wss.at[j, s], wrs.at[j, s], target)
        cp.start()
        sent.append(cp)
        return remote(dst.at[xx, qs], dst.at[yours[0], yours[1]], wss.at[j, s], wrs.at[j, s], target)

    xw = [[] for _ in units]

    def x_round(j):
        for r in range(ng):
            cp, inc, qs, lc = u_in[j][r]
            if r == 0:

                @pl.when(self_in)
                def _():
                    lc.wait()

                @pl.when(jnp.logical_not(self_in))
                def _():
                    inc.wait_recv()
            else:
                inc.wait_recv()
            xw[j].append(unit_on(j, b, qs, ng + r, at(1 - b, q, y, c), (1 - b, qs)))
        for r in range(ng):
            qs = u_in[j][r][2]
            qo = lax.rem(g - r + ng, ng) * 2 + 1 - c
            d_in.append(unit_on(j, b, qs, 2 * ng + r, at(b, q, y, 1 - c), (b, qo)))

    def c_round(j):
        for r in range(ng):
            qs = u_in[j][r][2]
            qo = lax.rem(g - r + ng, ng) * 2 + 1 - c
            xw[j][r].wait_recv()
            d_in.append(unit_on(j, 1 - b, qs, 3 * ng + r, at(b, q, y, 1 - c), (1 - b, qo)))

    x_round(0)
    x_round(1)
    c_round(0)
    x_round(2)
    c_round(1)
    c_round(2)
    for cp in c_in + d_in:
        cp.wait_recv()
    for cp in sent:
        cp.wait_send()
    for j in range(len(units)):
        for r in range(ng):
            cp = u_in[j][r][0]
            if r == 0:

                @pl.when(jnp.logical_not(self_in))
                def _():
                    cp.wait_send()
            else:
                cp.wait_send()


def gather_all(nz, qkv, wo, gain, wg, wu, wd):
    ng = nz // 2
    out = [
        jax.ShapeDtypeStruct((2, nz, qkv.shape[0], 4 * qkv.shape[1]), BF16),
        jax.ShapeDtypeStruct((2, nz, 2, 2) + wo.shape, BF16),
        jax.ShapeDtypeStruct((2, nz, 2, 2) + gain.shape, BF16),
        jax.ShapeDtypeStruct((2, nz) + wg.shape, BF16),
        jax.ShapeDtypeStruct((2, nz) + wu.shape, BF16),
        jax.ShapeDtypeStruct((2, nz) + wd.shape, BF16),
    ]
    ns = 2 * nz + 4
    return pl.pallas_call(
        functools.partial(gather_kernel, nz),
        out_shape=out,
        in_specs=[ANY] * 6,
        out_specs=[ANY] * 6,
        scratch_shapes=[
            pltpu.SemaphoreType.DMA((3,)),
            pltpu.SemaphoreType.DMA((3, ns)),
            pltpu.SemaphoreType.DMA((3, ns)),
            pltpu.SemaphoreType.DMA((3,)),
            pltpu.SemaphoreType.DMA((3, 4 * ng)),
            pltpu.SemaphoreType.DMA((3, 4 * ng)),
        ],
        compiler_params=pltpu.CompilerParams(collective_id=0, has_side_effects=True),
    )(qkv, wo, gain, wg, wu, wd)


def reduce_kernel(nz, qkv, wo, gain, wg, wu, wd, qkv_o, wo_o, gain_o, wg_o, wu_o, wd_o, *scratch):
    b, q, y, c = place()
    g, e = q // 2, q % 2
    ng = nz // 2
    qw = qkv_o.shape[1]
    self_in = e == c
    n_items, n_units = 3, 3
    own = scratch[0:3]
    r1 = scratch[3:6]
    r2 = scratch[6:9]
    r3 = scratch[9:12]
    r4 = scratch[12:15]
    uown = scratch[15:18]
    u1 = scratch[18:21]
    u2 = scratch[21:24]
    u3 = scratch[24:27]
    lsem, ssem, rsem, wls, wss, wrs = scratch[27:]
    bar = greet(
        [at(b, lax.rem(q + r, nz), y, c) for r in range(1, nz)]
        + [at(1 - b, q, y, c), at(b, q, 1 - y, c), at(b, q, y, 1 - c)]
        + [at(b, lax.rem(g + r, ng) * 2 + c, y, e) for r in range(1, ng)]
    )
    first = at(b, g * 2 + c, y, e)

    @pl.when(jnp.logical_not(self_in))
    def _():
        pl.semaphore_signal(bar, inc=1, device_id=first, device_id_type=MESH)

    pl.semaphore_wait(bar, nz + 1 + ng - jnp.where(self_in, 1, 0) + 1)

    other_core = at(b, q, y, 1 - c)
    other_y = at(b, q, 1 - y, c)
    other_x = at(1 - b, q, y, c)
    full = (pl.ds(0, 2), pl.ds(0, nz))

    def view_qkv(ref, yy, cc):
        return ref.at[full[0], full[1], :, pl.ds(pl.multiple_of((yy * 2 + cc) * qw, 128), qw)]

    def view_lead(ref, yy, cc):
        return ref.at[full[0], full[1], yy, cc]

    items = [(qkv, qkv_o, view_qkv), (wo, wo_o, view_lead), (gain, gain_o, view_lead)]
    units = [(wd, wd_o), (wg, wg_o), (wu, wu_o)]
    sent = []
    item_local, item_in = [[] for _ in items], [[] for _ in items]
    unit_local, unit_in = [[] for _ in units], [[] for _ in units]

    def start(cp):
        cp.start()
        sent.append(cp)
        return cp

    def item_core(i):
        src, _, view = items[i]
        for yy in range(2):
            item_in[i].append(start(remote(view(src, yy, 1 - c), r1[i].at[yy], ssem.at[i, yy], rsem.at[i, yy], other_core)))
            cp = pltpu.make_async_copy(view(src, yy, c), own[i].at[yy], lsem.at[i, yy])
            cp.start()
            item_local[i].append(cp)

    def unit_core(j):
        src, _ = units[j]
        for xx in range(2):
            for r in range(ng):
                s = xx * ng + r
                mine, yours = r * 2 + c, r * 2 + 1 - c
                unit_in[j].append(start(remote(src.at[xx, yours], u1[j].at[xx, r], wss.at[j, s], wrs.at[j, s], other_core)))
                cp = pltpu.make_async_copy(src.at[xx, mine], uown[j].at[xx, r], wls.at[j, s])
                cp.start()
                unit_local[j].append(cp)

    def add(dst, src, lead):
        def one(n, _):
            dst[n] = (dst[n].astype(F32) + src[n].astype(F32)).astype(dst.dtype)
            return 0

        lax.fori_loop(0, lead, one, 0)

    def unit_x(j):
        for cp in unit_local[j]:
            cp.wait()
        for cp in unit_in[j]:
            cp.wait_recv()
        add(uown[j].at[1 - b], u1[j].at[1 - b], ng)
        cp = start(remote(uown[j].at[1 - b], u2[j], wss.at[j, 2 * ng], wrs.at[j, 2 * ng], other_x))
        add(uown[j].at[b], u1[j].at[b], ng)
        unit_in[j] = [cp]

    def unit_z(j):
        unit_in[j][0].wait_recv()
        add(uown[j].at[b], u2[j], ng)
        waits = []
        for r in range(ng):
            gs = lax.rem(g + r, ng)
            cp = remote(uown[j].at[b, gs], u3[j].at[r], wss.at[j, 2 * ng + 1 + r], wrs.at[j, 2 * ng + 1 + r], at(b, gs * 2 + c, y, e))
            if r == 0:
                lc = pltpu.make_async_copy(uown[j].at[b, gs], u3[j].at[0], wls.at[j, 2 * ng])

                @pl.when(self_in)
                def _():
                    lc.start()

                @pl.when(jnp.logical_not(self_in))
                def _():
                    cp.start()

                waits.append((cp, lc))
            else:
                start(cp)
                waits.append((cp, None))
        unit_in[j] = waits

    def unit_end(j):
        for cp, lc in unit_in[j]:
            if lc is not None:

                @pl.when(self_in)
                def _():
                    lc.wait()

                @pl.when(jnp.logical_not(self_in))
                def _():
                    cp.wait()
            else:
                cp.wait_recv()
        rows = u3[j].shape[1]
        step = 16

        def one(n, _):
            sl = pl.ds(pl.multiple_of(n * step, step), step)
            total = u3[j][0, sl].astype(F32)
            for r in range(1, ng):
                total = total + u3[j][r, sl].astype(F32)
            units[j][1][sl] = total.astype(units[j][1].dtype)
            return 0

        lax.fori_loop(0, rows // step, one, 0)

    def item_y(i):
        for cp in item_local[i]:
            cp.wait()
        for cp in item_in[i]:
            cp.wait_recv()
        for xx in range(2):
            add(own[i].at[1 - y, xx], r1[i].at[1 - y, xx], nz)
        cp = start(remote(own[i].at[1 - y], r2[i], ssem.at[i, 2], rsem.at[i, 2], other_y))
        for xx in range(2):
            add(own[i].at[y, xx], r1[i].at[y, xx], nz)
        item_in[i] = [cp]

    def item_x(i):
        item_in[i][0].wait_recv()
        add(own[i].at[y, 1 - b], r2[i].at[1 - b], nz)
        cp = start(remote(own[i].at[y, 1 - b], r3[i], ssem.at[i, 3], rsem.at[i, 3], other_x))
        add(own[i].at[y, b], r2[i].at[b], nz)
        item_in[i] = [cp]

    def item_z(i):
        item_in[i][0].wait_recv()
        add(own[i].at[y, b], r3[i], nz)
        waits = []
        for r in range(1, nz):
            qt = lax.rem(q + r, nz)
            waits.append(start(remote(own[i].at[y, b, qt], r4[i].at[r - 1], ssem.at[i, 3 + r], rsem.at[i, 3 + r], at(b, qt, y, c))))
        item_in[i] = waits

    def item_end(i):
        for cp in item_in[i]:
            cp.wait_recv()
        total = own[i][y, b, q].astype(F32)
        for r in range(1, nz):
            total = total + r4[i][r - 1].astype(F32)
        items[i][1][...] = total.astype(items[i][1].dtype)

    for j in range(n_units):
        unit_core(j)
    for i in range(n_items):
        item_core(i)
    for j in range(n_units):
        unit_x(j)
    for i in range(n_items):
        item_y(i)
    unit_z(0)
    for i in range(n_items):
        item_x(i)
    unit_z(1)
    for i in range(n_items):
        item_z(i)
    unit_z(2)
    for i in range(n_items):
        item_end(i)
    for j in range(n_units):
        unit_end(j)
    for cp in sent:
        cp.wait_send()


def reduce_all(nz, qkv, wo, gain, wg, wu, wd):
    ng = nz // 2
    qw = qkv.shape[3] // 4
    blocks = [((qkv.shape[2], qw), BF16), (wo.shape[4:], BF16), (gain.shape[4:], F32)]
    ublocks = [(wd.shape[2:], BF16), (wg.shape[2:], BF16), (wu.shape[2:], BF16)]
    scratch = (
        [pltpu.VMEM((2, 2, nz) + s, t) for s, t in blocks]
        + [pltpu.VMEM((2, 2, nz) + s, t) for s, t in blocks]
        + [pltpu.VMEM((2, nz) + s, t) for s, t in blocks]
        + [pltpu.VMEM((nz,) + s, t) for s, t in blocks]
        + [pltpu.VMEM((nz - 1,) + s, t) for s, t in blocks]
        + [pltpu.VMEM((2, ng) + s, t) for s, t in ublocks]
        + [pltpu.VMEM((2, ng) + s, t) for s, t in ublocks]
        + [pltpu.VMEM((ng,) + s, t) for s, t in ublocks]
        + [pltpu.VMEM((ng,) + s, t) for s, t in ublocks]
        + [
            pltpu.SemaphoreType.DMA((3, 2)),
            pltpu.SemaphoreType.DMA((3, nz + 3)),
            pltpu.SemaphoreType.DMA((3, nz + 3)),
            pltpu.SemaphoreType.DMA((3, 2 * ng + 1)),
            pltpu.SemaphoreType.DMA((3, 3 * ng + 1)),
            pltpu.SemaphoreType.DMA((3, 3 * ng + 1)),
        ]
    )
    out = [
        jax.ShapeDtypeStruct(blocks[0][0], BF16),
        jax.ShapeDtypeStruct(blocks[1][0], F32),
        jax.ShapeDtypeStruct(blocks[2][0], F32),
        jax.ShapeDtypeStruct(ublocks[1][0], BF16),
        jax.ShapeDtypeStruct(ublocks[2][0], BF16),
        jax.ShapeDtypeStruct(ublocks[0][0], F32),
    ]
    return pl.pallas_call(
        functools.partial(reduce_kernel, nz),
        out_shape=out,
        in_specs=[ANY] * 6,
        out_specs=[VMEM] * 6,
        scratch_shapes=scratch,
        compiler_params=pltpu.CompilerParams(collective_id=1, has_side_effects=True, vmem_limit_bytes=60 * 2**20),
    )(qkv, wo, gain, wg, wu, wd)


def chunk_scores(q, kk, segq, segk, qidx, j, scale):
    s = lax.dot_general(q, kk, (((1,), (1,)), ((), ())), preferred_element_type=F32) * scale
    kidx = j * 256 + lax.broadcasted_iota(jnp.int32, (1, 256), 1)
    return s, (segq == segk) & (kidx <= qidx)


def attn_fwd_kernel(nb, q_ref, kv_ref, segq_ref, segk_ref, o_ref, lse_ref, kvall, lsem, ssem, rsem):
    b, q, y, c = place()
    k = lax.axis_index("blk")
    nz = nb // 4
    hz = nz // 2
    half = q // hz
    ql = q - half * hz
    low = k < nb // 2
    is_mid = k == nb // 2
    mid = (b, nb // 2)
    bar = greet(
        [at(b, half * hz + lax.rem(ql + r, hz), y, c) for r in range(1, hz)] + [at(b, q, 1 - y, c), at(b, q, y, 1 - c)]
    )

    @pl.when(low)
    def _():
        pl.semaphore_signal(bar, inc=1, device_id=mid, device_id_type=MESH)

    @pl.when(is_mid)
    def _():
        for j in range(nb // 2):
            pl.semaphore_signal(bar, inc=1, device_id=(b, j), device_id_type=MESH)

    pl.semaphore_wait(bar, hz + 1 + jnp.where(low, 1, 0) + jnp.where(is_mid, nb // 2, 0))

    def view(qq, yy, cc):
        return kvall.at[qq, yy, cc]

    sent = []

    def start(cp):
        cp.start()
        sent.append(cp)
        return cp

    mine = pltpu.make_async_copy(kv_ref, view(q, y, c), lsem)
    mine.start()
    other_y = at(b, q, 1 - y, c)
    other_c = at(b, q, y, 1 - c)
    z_in = []
    for r in range(1, hz):
        target = at(b, half * hz + lax.rem(ql + r, hz), y, c)
        start(remote(kv_ref, view(q, y, c), ssem.at[r], rsem.at[r], target))
        src = half * hz + lax.rem(ql - r + hz, hz)
        z_in.append((remote(kv_ref, view(src, y, c), ssem.at[r], rsem.at[r], target), src))
    start(remote(kv_ref, view(q, y, c), ssem.at[hz], rsem.at[hz], other_y))
    y_in = [(remote(kv_ref, view(q, 1 - y, c), ssem.at[hz], rsem.at[hz], other_y), q)]
    ns = 2 * hz + hz * 2
    to_mid = remote(kv_ref, view(q, y, c), ssem.at[ns], rsem.at[ns + k % (nb // 2)], mid)

    @pl.when(low)
    def _():
        to_mid.start()

    mine.wait()
    c_in = []
    s = 2 * hz

    def to_core(qq, yy, s):
        start(remote(view(qq, yy, c), view(qq, yy, c), ssem.at[s], rsem.at[s], other_c))
        c_in.append(remote(view(qq, yy, c), view(qq, yy, 1 - c), ssem.at[s], rsem.at[s], other_c))

    to_core(q, y, s)
    s += 1
    for r, (cp, src) in enumerate(z_in):
        cp.wait_recv()
        n = hz + 1 + r
        start(remote(view(src, y, c), view(src, y, c), ssem.at[n], rsem.at[n], other_y))
        y_in.append((remote(view(src, y, c), view(src, 1 - y, c), ssem.at[n], rsem.at[n], other_y), src))
        to_core(src, y, s)
        s += 1
    for cp, src in y_in:
        cp.wait_recv()
        to_core(src, 1 - y, s)
        s += 1
    for cp in c_in:
        cp.wait_recv()

    @pl.when(is_mid)
    def _():
        for j in range(nb // 2):
            remote(kv_ref, view(j // 4, (j // 2) % 2, j % 2), ssem.at[ns], rsem.at[ns + j], mid).wait_recv()

    scale = HD ** (-0.5)
    lo = jnp.where(k <= nb // 2, 0, nb // 4)
    hi = k // 2 + 1
    rows = q_ref.shape[1]
    tok = rows // H
    qidx = k * tok + lax.broadcasted_iota(jnp.int32, (rows, 1), 0) % tok
    for m in range(q_ref.shape[0]):
        qm = q_ref[m]
        segq = segq_ref[m]

        def body(j, carry):
            mx, sm, acc = carry
            blk = kvall[j // 2, j % 2, :, m].reshape(256, 2 * HD)
            s, ok = chunk_scores(qm, blk[:, :HD], segq, segk_ref[m, j], qidx, j, scale)
            s = jnp.where(ok, s, -1e30)
            new = jnp.maximum(mx, jnp.max(s, axis=-1, keepdims=True))
            p = jnp.where(ok, jnp.exp(s - new), 0.0)
            alpha = jnp.exp(mx - new)
            sm = sm * alpha + jnp.sum(p, axis=-1, keepdims=True)
            acc = acc * alpha + jnp.dot(p.astype(BF16), blk[:, HD:], preferred_element_type=F32)
            return new, sm, acc

        mx, sm, acc = lax.fori_loop(
            lo, hi, body, (jnp.full((rows, 1), -1e30, F32), jnp.zeros((rows, 1), F32), jnp.zeros((rows, HD), F32))
        )
        o_ref[m] = acc / sm
        lse_ref[m] = mx + jnp.log(sm)
    for cp in sent:
        cp.wait_send()

    @pl.when(low)
    def _():
        to_mid.wait_send()


def attn_fwd(nb, q, kv, segq, segk):
    nz = nb // 4
    ns = 4 * (nz // 2)
    return pl.pallas_call(
        functools.partial(attn_fwd_kernel, nb),
        out_shape=[
            jax.ShapeDtypeStruct(q.shape, F32),
            jax.ShapeDtypeStruct(q.shape[:2] + (1,), F32),
            jax.ShapeDtypeStruct((nz, 2, 2) + kv.shape, BF16),
        ],
        in_specs=[VMEM] * 4,
        out_specs=[VMEM] * 3,
        scratch_shapes=[
            pltpu.SemaphoreType.DMA,
            pltpu.SemaphoreType.DMA((ns + 1,)),
            pltpu.SemaphoreType.DMA((ns + nb // 2,)),
        ],
        compiler_params=pltpu.CompilerParams(collective_id=2, has_side_effects=True, vmem_limit_bytes=60 * 2**20),
    )(q, kv, segq, segk)


def attn_bwd_kernel(
    nb, q_ref, kvall, do_ref, lse_ref, delta_ref, segq_ref, segk_ref, dq_ref, dkv_ref, part, r1, r2, r3, r4, ssem, rsem, msem, nsem
):
    b, q, y, c = place()
    k = lax.axis_index("blk")
    nz = nb // 4
    hz = nz // 2
    half = q // hz
    ql = q - half * hz
    low = k < nb // 2
    is_mid = k == nb // 2
    mid = (b, nb // 2)
    bar = greet(
        [at(b, half * hz + lax.rem(ql + r, hz), y, c) for r in range(1, hz)] + [at(b, q, 1 - y, c), at(b, q, y, 1 - c)]
    )

    @pl.when(low)
    def _():
        pl.semaphore_signal(bar, inc=1, device_id=mid, device_id_type=MESH)

    @pl.when(is_mid)
    def _():
        for j in range(nb // 2):
            pl.semaphore_signal(bar, inc=1, device_id=(b, j), device_id_type=MESH)

    pl.semaphore_wait(bar, hz + 1 + jnp.where(low, 1, 0) + jnp.where(is_mid, nb // 2, 0))
    other_y = at(b, q, 1 - y, c)
    other_c = at(b, q, y, 1 - c)
    sent = []

    def start(cp):
        cp.start()
        sent.append(cp)
        return cp

    def clear(n, _):
        part[half * hz + n // 4, (n // 2) % 2, n % 2] = jnp.zeros(part.shape[3:], BF16)
        return 0

    lax.fori_loop(0, 4 * hz, clear, 0)
    scale = HD ** (-0.5)
    lo = jnp.where(k <= nb // 2, 0, nb // 4)
    hi = k // 2 + 1
    rows = q_ref.shape[1]
    tok = rows // H
    qidx = k * tok + lax.broadcasted_iota(jnp.int32, (rows, 1), 0) % tok
    tn = (((0,), (0,)), ((), ()))
    nt = (((1,), (1,)), ((), ()))
    for m in range(q_ref.shape[0]):
        dq_ref[m] = jnp.zeros(dq_ref.shape[1:], F32)

        def body(j, _):
            qm, dom = q_ref[m], do_ref[m]
            blk = kvall[j // 2, j % 2, :, m].reshape(256, 2 * HD)
            s, ok = chunk_scores(qm, blk[:, :HD], segq_ref[m], segk_ref[m, j], qidx, j, scale)
            p = jnp.where(ok, jnp.exp(jnp.where(ok, s, -1e30) - lse_ref[m]), 0.0)
            dp = lax.dot_general(dom, blk[:, HD:], nt, preferred_element_type=F32)
            ds = (p * (dp - delta_ref[m])).astype(BF16)
            dq_ref[m] += jnp.dot(ds, blk[:, :HD], preferred_element_type=F32) * scale
            dk = lax.dot_general(ds, qm, tn, preferred_element_type=F32) * scale
            dv = lax.dot_general(p.astype(BF16), dom, tn, preferred_element_type=F32)
            part[j // 2, j % 2, :, m] = jnp.concatenate([dk, dv], axis=1).astype(BF16).reshape(2, tok, 2 * HD)
            return 0

        lax.fori_loop(lo, hi, body, 0)

    @pl.when(is_mid)
    def _():
        for j in range(nb // 2):
            remote(part.at[j // 4, (j // 2) % 2, j % 2], r4, msem.at[j], nsem, (b, j)).start()

    hs = pl.ds(half * hz, hz)
    cp = start(remote(part.at[hs, :, 1 - c], r1, ssem.at[0], rsem.at[0], other_c))
    cp.wait_recv()

    def add1(n, _):
        i = half * hz + n // 2
        part[i, n % 2, c] = (part[i, n % 2, c].astype(F32) + r1[n // 2, n % 2].astype(F32)).astype(BF16)
        return 0

    lax.fori_loop(0, 2 * hz, add1, 0)
    cp = start(remote(part.at[hs, 1 - y, c], r2, ssem.at[1], rsem.at[1], other_y))
    cp.wait_recv()

    def add2(n, _):
        i = half * hz + n
        part[i, y, c] = (part[i, y, c].astype(F32) + r2[n].astype(F32)).astype(BF16)
        return 0

    lax.fori_loop(0, hz, add2, 0)
    last = []
    for r in range(1, hz):
        qt = half * hz + lax.rem(ql + r, hz)
        last.append(start(remote(part.at[qt, y, c], r3.at[r - 1], ssem.at[1 + r], rsem.at[1 + r], at(b, qt, y, c))))
    total = part[q, y, c].astype(F32)
    for r, cp in enumerate(last):
        cp.wait_recv()
        total = total + r3[r].astype(F32)
    dkv_ref[...] = total

    @pl.when(low)
    def _():
        remote(part.at[0, 0, 0], r4, msem.at[0], nsem, mid).wait_recv()
        dkv_ref[...] += r4[...].astype(F32)

    for cp in sent:
        cp.wait_send()

    @pl.when(is_mid)
    def _():
        for j in range(nb // 2):
            remote(part.at[j // 4, (j // 2) % 2, j % 2], r4, msem.at[j], nsem, (b, j)).wait_send()


def attn_bwd(nb, q, kvall, do, lse, delta, segq, segk):
    nz = nb // 4
    hz = nz // 2
    blk = kvall.shape[3:]
    return pl.pallas_call(
        functools.partial(attn_bwd_kernel, nb),
        out_shape=[jax.ShapeDtypeStruct(q.shape, F32), jax.ShapeDtypeStruct(blk, F32)],
        in_specs=[VMEM] * 7,
        out_specs=[VMEM] * 2,
        scratch_shapes=[
            pltpu.VMEM(kvall.shape, BF16),
            pltpu.VMEM((hz, 2) + blk, BF16),
            pltpu.VMEM((hz,) + blk, BF16),
            pltpu.VMEM((hz - 1,) + blk, BF16),
            pltpu.VMEM(blk, BF16),
            pltpu.SemaphoreType.DMA((hz + 1,)),
            pltpu.SemaphoreType.DMA((hz + 1,)),
            pltpu.SemaphoreType.DMA((nb // 2,)),
            pltpu.SemaphoreType.DMA,
        ],
        compiler_params=pltpu.CompilerParams(collective_id=3, has_side_effects=True, vmem_limit_bytes=60 * 2**20),
    )(q, kvall, do, lse, delta, segq, segk)


def tiles(n, w):
    return [(i, min(w, n - i)) for i in range(0, n, w)]


def gelu_parts(z):
    k0 = math.sqrt(2.0 / math.pi)
    z2 = z * z
    h = 0.5 + 0.5 * jnp.tanh(z * (k0 + (k0 * 0.044715) * z2))
    value = z * h
    slope = h + 2.0 * value * (1.0 - h) * (k0 + (3.0 * k0 * 0.044715) * z2)
    return value, slope


def ffn_kernel(
    b_ref, h1_ref, dy_ref, gp_ref, wg, wu, wd, out_ref, db_ref, dgp_ref, gg_o, gu_o, gd_o,
    ball, ballt, gate, up, mm, fsend, frecv, dfall, dsend, drecv, sg, su, sd, ssem, rsem, osem,
):
    b, q, y, c = place()
    g = q // 2
    t = lax.rem(q, 2) * 2 + y
    micro, tok, width = b_ref.shape
    hidden = wd.shape[0]
    peers = []
    for p in range(1, 4):
        tt = lax.rem(t + p, 4)
        peers.append((p, tt, at(b, g * 2 + tt // 2, lax.rem(tt, 2), c)))
    bar = greet([p[2] for p in peers])
    pl.semaphore_wait(bar, 3)
    sent = []
    nt = (((1,), (1,)), ((), ()))

    def spread(phase, m, src, dst_of, recv_of):
        waits = []
        for p, tt, target in peers:
            cp = remote(src(tt), dst_of(p, tt), ssem.at[phase, m, p - 1], rsem.at[phase, m, p - 1], target)
            cp.start()
            sent.append(cp)
            ts = lax.rem(t + 4 - p, 4)
            waits.append(remote(src(tt), recv_of(p, ts), ssem.at[phase, m, p - 1], rsem.at[phase, m, p - 1], target))
        return waits

    a_in, f_in, df_in, db_in = [], [], [], []
    for m in range(micro):
        a_in.append(
            spread(0, m, lambda tt, m=m: b_ref.at[m], lambda p, tt, m=m: ball.at[m, t], lambda p, ts, m=m: ball.at[m, ts])
        )
        ball[m, t] = b_ref[m]

    def forward(m):
        for cp in a_in[m]:
            cp.wait_recv()

        def body(n, _):
            cols = pl.ds(pl.multiple_of(n * 256, 256), 256)
            x = ball[m].reshape(4 * tok, width)
            gv = jnp.dot(x, wg[:, cols], preferred_element_type=F32)
            uv = jnp.dot(x, wu[:, cols], preferred_element_type=F32)
            gate[m, :, cols] = gv.astype(BF16)
            up[m, :, cols] = uv.astype(BF16)
            mm[m, :, cols] = (gelu_parts(gv)[0] * uv).astype(BF16)
            return 0

        lax.fori_loop(0, hidden // 256, body, 0)
        for o, w in tiles(width, 256):
            f = jnp.dot(mm[m], wd[:, o : o + w], preferred_element_type=F32)
            fsend[m, :, :, o : o + w] = f.astype(BF16).reshape(4, tok, w)
        f_in.append(
            spread(1, m, lambda tt: fsend.at[m, tt], lambda p, tt: frecv.at[m, p - 1], lambda p, ts: frecv.at[m, p - 1])
        )

    def middle(m):
        for cp in f_in[m]:
            cp.wait_recv()
        f = fsend[m, t].astype(F32)
        for p in range(3):
            f = f + frecv[m, p].astype(F32)
        gp = 1.0 + gp_ref[...]
        r = lax.rsqrt(jnp.mean(f * f, axis=-1, keepdims=True) + epsilon)
        n = f * r
        dy = dy_ref[m].astype(F32)
        out_ref[m] = (h1_ref[m] + n * gp).astype(BF16)
        dg = dy * gp
        df = r * (dg - n * jnp.mean(dg * n, axis=-1, keepdims=True))
        part = jnp.sum(dy * n, axis=0, keepdims=True)
        if m == 0:
            dgp_ref[...] = part
        else:
            dgp_ref[...] += part
        dfall[m, t] = df.astype(BF16)
        df_in.append(
            spread(2, m, lambda tt: dfall.at[m, t], lambda p, tt: dfall.at[m, t], lambda p, ts: dfall.at[m, ts])
        )

    def backward(m):
        for cp in df_in[m]:
            cp.wait_recv()

        def body(n, _):
            cols = pl.ds(pl.multiple_of(n * 256, 256), 256)
            x = dfall[m].reshape(4 * tok, width)
            dm = lax.dot_general(x, wd[cols, :], nt, preferred_element_type=F32)
            value, slope = gelu_parts(gate[m, :, cols].astype(F32))
            uv = up[m, :, cols].astype(F32)
            gate[m, :, cols] = (dm * uv * slope).astype(BF16)
            up[m, :, cols] = (dm * value).astype(BF16)
            return 0

        lax.fori_loop(0, hidden // 256, body, 0)
        for o, w in tiles(width, 256):
            d = lax.dot_general(gate[m], wg[o : o + w, :], nt, preferred_element_type=F32)
            d = d + lax.dot_general(up[m], wu[o : o + w, :], nt, preferred_element_type=F32)
            dsend[m, :, :, o : o + w] = d.astype(BF16).reshape(4, tok, w)
        db_in.append(
            spread(3, m, lambda tt: dsend.at[m, tt], lambda p, tt: drecv.at[m, p - 1], lambda p, ts: drecv.at[m, p - 1])
        )

    for m in range(micro):
        forward(m)
    for m in range(micro):
        for i in range(4):
            ballt[:, (m * 4 + i) * tok : (m * 4 + i + 1) * tok] = ball[m, i].T
    for m in range(micro):
        middle(m)
    for m in range(micro):
        backward(m)

    def grads(n, _):
        cols = pl.ds(pl.multiple_of(n * 256, 256), 256)
        slot = lax.rem(n, 2)

        def out(m, o):
            cc = pl.ds(pl.multiple_of(m * 256, 256), 256)
            return [
                pltpu.make_async_copy(sg.at[o], gg_o.at[:, cc], osem.at[0, o]),
                pltpu.make_async_copy(su.at[o], gu_o.at[:, cc], osem.at[1, o]),
                pltpu.make_async_copy(sd.at[o], gd_o.at[cc, :], osem.at[2, o]),
            ]

        @pl.when(n >= 2)
        def _():
            for cp in out(n, slot):
                cp.wait()

        x = ballt[...]
        sg[slot] = jnp.dot(x, gate[:, :, cols].reshape(-1, 256), preferred_element_type=F32).astype(BF16)
        su[slot] = jnp.dot(x, up[:, :, cols].reshape(-1, 256), preferred_element_type=F32).astype(BF16)
        sd[slot] = jnp.dot(
            mm[:, :, cols].reshape(-1, 256).T, dfall[...].reshape(-1, width), preferred_element_type=F32
        ).astype(BF16)
        for cp in out(n, slot):
            cp.start()
        return 0

    steps = hidden // 256
    lax.fori_loop(0, steps, grads, 0)
    for n in range(max(steps - 2, 0), steps):
        o = n % 2
        pltpu.make_async_copy(sg.at[o], gg_o.at[:, n * 256 : n * 256 + 256], osem.at[0, o]).wait()
        pltpu.make_async_copy(su.at[o], gu_o.at[:, n * 256 : n * 256 + 256], osem.at[1, o]).wait()
        pltpu.make_async_copy(sd.at[o], gd_o.at[n * 256 : n * 256 + 256, :], osem.at[2, o]).wait()
    for m in range(micro):
        for cp in db_in[m]:
            cp.wait_recv()
        d = dsend[m, t].astype(F32)
        for p in range(3):
            d = d + drecv[m, p].astype(F32)
        db_ref[m] = d
    for cp in sent:
        cp.wait_send()


def ffn(b, h1, dy, gp, wg, wu, wd):
    micro, tok, width = b.shape
    hidden = wd.shape[0]
    wide = (micro, 4 * tok, hidden)
    return pl.pallas_call(
        ffn_kernel,
        out_shape=[
            jax.ShapeDtypeStruct(b.shape, BF16),
            jax.ShapeDtypeStruct(b.shape, F32),
            jax.ShapeDtypeStruct((1, width), F32),
            jax.ShapeDtypeStruct(wg.shape, BF16),
            jax.ShapeDtypeStruct(wu.shape, BF16),
            jax.ShapeDtypeStruct(wd.shape, BF16),
        ],
        in_specs=[VMEM] * 7,
        out_specs=[VMEM] * 3 + [ANY] * 3,
        scratch_shapes=[
            pltpu.VMEM((micro, 4, tok, width), BF16),
            pltpu.VMEM((width, micro * 4 * tok), BF16),
            pltpu.VMEM(wide, BF16),
            pltpu.VMEM(wide, BF16),
            pltpu.VMEM(wide, BF16),
            pltpu.VMEM((micro, 4, tok, width), BF16),
            pltpu.VMEM((micro, 3, tok, width), BF16),
            pltpu.VMEM((micro, 4, tok, width), BF16),
            pltpu.VMEM((micro, 4, tok, width), BF16),
            pltpu.VMEM((micro, 3, tok, width), BF16),
            pltpu.VMEM((2, width, 256), BF16),
            pltpu.VMEM((2, width, 256), BF16),
            pltpu.VMEM((2, 256, width), BF16),
            pltpu.SemaphoreType.DMA((4, micro, 3)),
            pltpu.SemaphoreType.DMA((4, micro, 3)),
            pltpu.SemaphoreType.DMA((3, 2)),
        ],
        compiler_params=pltpu.CompilerParams(collective_id=4, has_side_effects=True, vmem_limit_bytes=62 * 2**20),
    )(b, h1, dy, gp, wg, wu, wd)


class Team:
    def __init__(self, place_of, c, ssem, rsem, sent):
        b, g, e, y = place_of
        self.t, self.ty, self.tz, self.td = e * 2 + y, e * 2 + 1 - y, (1 - e) * 2 + y, (1 - e) * 2 + 1 - y
        self.dev_y, self.dev_z = at(b, g * 2 + e, 1 - y, c), at(b, g * 2 + 1 - e, y, c)
        self.ssem, self.rsem, self.sent = ssem, rsem, sent

    def hop(self, src, dst, here, s, target):
        cp = remote(src, dst, self.ssem.at[s], self.rsem.at[s], target)
        cp.start()
        self.sent.append(cp)
        return remote(src, here, self.ssem.at[s], self.rsem.at[s], target)


class Gather(Team):
    def begin(self, slots):
        h = slots.shape[1] // 2
        self.a, self.b = pl.ds(0, h), pl.ds(h, h)
        self.slots = slots
        own = slots.at[self.t]
        y, z = slots.at[self.ty], slots.at[self.tz]
        self.ya = self.hop(own.at[self.a], own.at[self.a], y.at[self.a], 0, self.dev_y)
        self.zb = self.hop(own.at[self.b], own.at[self.b], z.at[self.b], 1, self.dev_z)
        self.yb = self.hop(own.at[self.b], own.at[self.b], y.at[self.b], 2, self.dev_y)
        self.za = self.hop(own.at[self.a], own.at[self.a], z.at[self.a], 3, self.dev_z)

    def forward(self):
        y, z, d = (self.slots.at[i] for i in (self.ty, self.tz, self.td))
        self.ya.wait_recv()
        self.da = self.hop(y.at[self.a], y.at[self.a], d.at[self.a], 4, self.dev_z)
        self.zb.wait_recv()
        self.db = self.hop(z.at[self.b], z.at[self.b], d.at[self.b], 5, self.dev_y)

    def end(self):
        for cp in (self.yb, self.za, self.da, self.db):
            cp.wait_recv()


class Sum(Team):
    def begin(self, parts, got, mid):
        h = parts.shape[1] // 2
        self.a, self.b = pl.ds(0, h), pl.ds(h, h)
        self.parts, self.got, self.mid = parts, got, mid
        y, z, d = (parts.at[i] for i in (self.ty, self.tz, self.td))
        self.ma = self.hop(d.at[self.a], mid.at[0], mid.at[0], 0, self.dev_y)
        self.mb = self.hop(d.at[self.b], mid.at[1], mid.at[1], 1, self.dev_z)
        self.ya = self.hop(y.at[self.a], got.at[0, self.a], got.at[0, self.a], 2, self.dev_y)
        self.zb = self.hop(z.at[self.b], got.at[1, self.b], got.at[1, self.b], 3, self.dev_z)

    def forward(self):
        z, y = self.parts.at[self.tz], self.parts.at[self.ty]
        self.ma.wait_recv()
        z[self.a] = z[self.a] + self.mid[0]
        self.za = self.hop(z.at[self.a], self.got.at[1, self.a], self.got.at[1, self.a], 4, self.dev_z)
        self.mb.wait_recv()
        y[self.b] = y[self.b] + self.mid[1]
        self.yb = self.hop(y.at[self.b], self.got.at[0, self.b], self.got.at[0, self.b], 5, self.dev_y)

    def end(self):
        for cp in (self.ya, self.zb, self.za, self.yb):
            cp.wait_recv()
        own, got = self.parts.at[self.t], self.got
        return own[...].astype(F32) + got[0].astype(F32) + got[1].astype(F32)


def mlp_kernel(
    ball_h, h1_ref, dy_ref, gd_ref, wg_h, wu_h, wd_h, out_ref, db_ref, dgp_ref, gg_o, gu_o, gd_o,
    wg, wu, wd, ball, ballt, gate, up, mm, fsend, frecv, fmid, dfall, dsend, drecv, dmid, sg, su, sd, ssem, rsem, osem, wsem, bsem,
):
    b, q, y, c = place()
    g, e = q // 2, q % 2
    t = e * 2 + y
    micro, tok, width = h1_ref.shape
    hidden = wd.shape[0]

    def load(n):
        cols = pl.ds(pl.multiple_of(n * 256, 256), 256)
        return [
            pltpu.make_async_copy(wg_h.at[:, cols], wg.at[:, cols], wsem.at[0, n]),
            pltpu.make_async_copy(wu_h.at[:, cols], wu.at[:, cols], wsem.at[1, n]),
        ]

    cut = ball_h.shape[2] // tok
    loads = [
        pltpu.make_async_copy(ball_h.at[m // cut, :, pl.ds(m % cut * tok, tok)], ball.at[m], bsem.at[m]) for m in range(micro)
    ]
    loads.append(pltpu.make_async_copy(wd_h, wd, bsem.at[micro]))
    loads[0].start()
    for n in range(hidden // 256):
        for cp in load(n):
            cp.start()
    for cp in loads[1:]:
        cp.start()
    bar = greet([at(b, q, 1 - y, c), at(b, g * 2 + 1 - e, y, c)])
    pl.semaphore_wait(bar, 2)
    sent = []
    nt = (((1,), (1,)), ((), ()))

    def team(kind, phase, m):
        return kind((b, g, e, y), c, ssem.at[phase, m], rsem.at[phase, m], sent)

    f_sum = [team(Sum, 0, m) for m in range(micro)]
    df_all = [team(Gather, 1, m) for m in range(micro)]
    db_sum = [team(Sum, 2, m) for m in range(micro)]

    def rise(m):
        loads[m].wait()

        def body(n, _):
            if m == 0:
                for cp in load(n):
                    cp.wait()
            cols = pl.ds(pl.multiple_of(n * 256, 256), 256)
            x = ball[m].reshape(4 * tok, width)
            gv = jnp.dot(x, wg[:, cols], preferred_element_type=F32)
            uv = jnp.dot(x, wu[:, cols], preferred_element_type=F32)
            value, slope = gelu_parts(gv)
            gate[m, :, cols] = (uv * slope).astype(BF16)
            up[m, :, cols] = value.astype(BF16)
            mm[m, :, cols] = (value * uv).astype(BF16)
            return 0

        lax.fori_loop(0, hidden // 256, body, 0)

    def fall(m):
        if m == 0:
            loads[micro].wait()
        for o, w in tiles(width, 256):
            f = jnp.dot(mm[m], wd[:, o : o + w], preferred_element_type=F32)
            fsend[m, :, :, o : o + w] = f.astype(BF16).reshape(4, tok, w)
        f_sum[m].begin(fsend.at[m], frecv.at[m], fmid.at[m])

    def middle(m):
        f = f_sum[m].end()
        gp = 1.0 + gd_ref[5:6]
        r = lax.rsqrt(jnp.mean(f * f, axis=-1, keepdims=True) + epsilon)
        n = f * r
        dy = dy_ref[m].astype(F32)
        out_ref[m] = (h1_ref[m] + n * gp).astype(BF16)
        dg = dy * gp
        df = r * (dg - n * jnp.mean(dg * n, axis=-1, keepdims=True))
        part = jnp.sum(dy * n, axis=0, keepdims=True)
        if m == 0:
            dgp_ref[...] = part
        else:
            dgp_ref[...] += part
        dfall[m, t] = df.astype(BF16)
        df_all[m].begin(dfall.at[m])

    def back_rise(m):
        df_all[m].end()

        def body(n, _):
            cols = pl.ds(pl.multiple_of(n * 256, 256), 256)
            x = dfall[m].reshape(4 * tok, width)
            dm = lax.dot_general(x, wd[cols, :], nt, preferred_element_type=F32)
            gate[m, :, cols] = (dm * gate[m, :, cols].astype(F32)).astype(BF16)
            up[m, :, cols] = (dm * up[m, :, cols].astype(F32)).astype(BF16)
            return 0

        lax.fori_loop(0, hidden // 256, body, 0)

    def back_fall(m):
        for o, w in tiles(width, 256):
            d = lax.dot_general(gate[m], wg[o : o + w, :], nt, preferred_element_type=F32)
            d = d + lax.dot_general(up[m], wu[o : o + w, :], nt, preferred_element_type=F32)
            dsend[m, :, :, o : o + w] = d.astype(BF16).reshape(4, tok, w)
        db_sum[m].begin(dsend.at[m], drecv.at[m], dmid.at[m])

    for m in range(micro):
        rise(m)
        if m >= 1:
            f_sum[m - 1].forward()
        if m >= 2:
            middle(m - 2)
        if m >= 3:
            df_all[m - 3].forward()
        fall(m)
    for m in range(micro):
        for i in range(4):
            o = (m * 4 + i) * tok
            ballt[:, o : o + tok] = ball[m, i].T
    middle(micro - 2)
    if micro >= 3:
        df_all[micro - 3].forward()
    for m in range(micro):
        back_rise(m)
        if m == 0:
            f_sum[micro - 1].forward()
            df_all[micro - 2].forward()
            middle(micro - 1)
        else:
            db_sum[m - 1].forward()
        if m == 1:
            df_all[micro - 1].forward()
        back_fall(m)

    def grads(n, _):
        cols = pl.ds(pl.multiple_of(n * 256, 256), 256)
        slot = lax.rem(n, 2)

        def out(m, o):
            cc = pl.ds(pl.multiple_of(m * 256, 256), 256)
            return [
                pltpu.make_async_copy(sg.at[o], gg_o.at[:, cc], osem.at[0, o]),
                pltpu.make_async_copy(su.at[o], gu_o.at[:, cc], osem.at[1, o]),
                pltpu.make_async_copy(sd.at[o], gd_o.at[cc, :], osem.at[2, o]),
            ]

        @pl.when(n >= 2)
        def _():
            for cp in out(n, slot):
                cp.wait()

        x = ballt[...]
        sg[slot] = jnp.dot(x, gate[:, :, cols].reshape(-1, 256), preferred_element_type=F32).astype(BF16)
        su[slot] = jnp.dot(x, up[:, :, cols].reshape(-1, 256), preferred_element_type=F32).astype(BF16)
        sd[slot] = jnp.dot(
            mm[:, :, cols].reshape(-1, 256).T, dfall[...].reshape(-1, width), preferred_element_type=F32
        ).astype(BF16)
        for cp in out(n, slot):
            cp.start()
        return 0

    steps = hidden // 256
    lax.fori_loop(0, min(2, steps), grads, 0)
    db_sum[micro - 1].forward()
    lax.fori_loop(min(2, steps), steps, grads, 0)
    for n in range(max(steps - 2, 0), steps):
        o = n % 2
        pltpu.make_async_copy(sg.at[o], gg_o.at[:, n * 256 : n * 256 + 256], osem.at[0, o]).wait()
        pltpu.make_async_copy(su.at[o], gu_o.at[:, n * 256 : n * 256 + 256], osem.at[1, o]).wait()
        pltpu.make_async_copy(sd.at[o], gd_o.at[n * 256 : n * 256 + 256, :], osem.at[2, o]).wait()
    for m in range(micro):
        db_ref[m] = db_sum[m].end()
    for cp in sent:
        cp.wait_send()


def mlp(ball, h1, dy, gp, wg, wu, wd):
    micro, tok, width = h1.shape
    hidden = wd.shape[0]
    wide = (micro, 4 * tok, hidden)
    return pl.pallas_call(
        mlp_kernel,
        out_shape=[
            jax.ShapeDtypeStruct(h1.shape, BF16),
            jax.ShapeDtypeStruct(h1.shape, F32),
            jax.ShapeDtypeStruct((1, width), F32),
            jax.ShapeDtypeStruct(wg.shape, BF16),
            jax.ShapeDtypeStruct(wu.shape, BF16),
            jax.ShapeDtypeStruct(wd.shape, BF16),
        ],
        in_specs=[ANY] + [VMEM] * 3 + [ANY] * 3,
        out_specs=[VMEM] * 3 + [ANY] * 3,
        scratch_shapes=[
            pltpu.VMEM(wg.shape, BF16),
            pltpu.VMEM(wu.shape, BF16),
            pltpu.VMEM(wd.shape, BF16),
            pltpu.VMEM((micro, 4, tok, width), BF16),
            pltpu.VMEM((width, micro * 4 * tok), BF16),
            pltpu.VMEM(wide, BF16),
            pltpu.VMEM(wide, BF16),
            pltpu.VMEM(wide, BF16),
            pltpu.VMEM((micro, 4, tok, width), BF16),
            pltpu.VMEM((micro, 2, tok, width), BF16),
            pltpu.VMEM((micro, 2, tok // 2, width), BF16),
            pltpu.VMEM((micro, 4, tok, width), BF16),
            pltpu.VMEM((micro, 4, tok, width), BF16),
            pltpu.VMEM((micro, 2, tok, width), BF16),
            pltpu.VMEM((micro, 2, tok // 2, width), BF16),
            pltpu.VMEM((2, width, 256), BF16),
            pltpu.VMEM((2, width, 256), BF16),
            pltpu.VMEM((2, 256, width), BF16),
            pltpu.SemaphoreType.DMA((3, micro, 6)),
            pltpu.SemaphoreType.DMA((3, micro, 6)),
            pltpu.SemaphoreType.DMA((3, 2)),
            pltpu.SemaphoreType.DMA((2, hidden // 256)),
            pltpu.SemaphoreType.DMA((micro + 1,)),
        ],
        compiler_params=pltpu.CompilerParams(collective_id=7, has_side_effects=True, vmem_limit_bytes=62 * 2**20),
    )(ball, h1, dy, gp, wg, wu, wd)


def halves(n):
    first = up16(n // 2)
    return [(0, first), (first, n - first)] if first < n else [(0, n)]


def norm_of(v):
    r = lax.rsqrt(jnp.mean(v * v, axis=-1, keepdims=True) + epsilon)
    return v * r, r


def norm_back(grad, n, r, scale):
    gs = grad * scale
    return r * (gs - n * jnp.mean(gs * n, axis=-1, keepdims=True)), jnp.sum(grad * n, axis=0, keepdims=True)


def spread_gains(block, width, n_dev):
    w = width // n_dev
    lane = lax.broadcasted_iota(jnp.int32, (128, width), 0)
    col = lax.broadcasted_iota(jnp.int32, (128, width), 1)
    pick = jnp.where(lax.rem(col, w) == lane, 1.0, 0.0).astype(BF16)
    wide = jnp.dot(block, pick, preferred_element_type=F32)
    row = lax.broadcasted_iota(jnp.int32, (n_dev * 16, width), 0) // 16
    mine = lax.broadcasted_iota(jnp.int32, (n_dev * 16, width), 1) // w
    return jnp.sum(jnp.where(row == mine, wide, 0.0).reshape(n_dev, 16, width), axis=0)


def collect_gains(rows, n_dev):
    width = rows.shape[1]
    w = width // n_dev
    row = lax.broadcasted_iota(jnp.int32, (n_dev, 8, width), 0)
    mine = lax.broadcasted_iota(jnp.int32, (n_dev, 8, width), 2) // w
    wide = jnp.where(row == mine, rows[None], 0.0).reshape(n_dev * 8, width)
    col = lax.broadcasted_iota(jnp.int32, (width, 128), 0)
    lane = lax.broadcasted_iota(jnp.int32, (width, 128), 1)
    pick = jnp.where(lax.rem(col, w) == lane, 1.0, 0.0)
    out = jnp.dot(wide, pick, preferred_element_type=F32, precision=lax.Precision.HIGHEST)
    return out.reshape(n_dev, 8, 128)


def pack_rows(kr, kp):
    row = lax.broadcasted_iota(jnp.int32, (4 * kr, 4 * kp), 0)
    col = lax.broadcasted_iota(jnp.int32, (4 * kr, 4 * kp), 1)
    return jnp.where(lax.div(row, kr) * kp + lax.rem(row, kr) == col, 1.0, 0.0).astype(BF16)


def kv_columns(which, qw):
    return 2 * which * qw + HD, (2 * which + 1) * qw + HD


def half_mask(n, tok):
    row = lax.rem(lax.broadcasted_iota(jnp.int32, (n, tok), 0), tok)
    return lax.broadcasted_iota(jnp.int32, (n, tok), 1) <= row


def segment_of(len_ref, m, index):
    end = jnp.int32(0)
    seg = jnp.zeros(index.shape, jnp.int32)
    for i in range(len_ref.shape[1]):
        end = end + len_ref[m, i]
        seg = seg + jnp.where(index >= end, 1, 0)
    return seg


def front_barrier(nz):
    b, q, y, c = place()
    k = lax.axis_index("blk")
    nb = 4 * nz
    g, e = q // 2, q % 2
    ng = nz // 2
    bar = greet(
        [at(b, lax.rem(q + r, nz), y, c) for r in range(1, nz)]
        + [at(1 - b, q, y, c), at(b, q, 1 - y, c), at(b, q, y, 1 - c), at(b, q, 1 - y, 1 - c)]
        + [at(b, lax.rem(g + r, ng) * 2 + c, y, e) for r in range(1, ng)]
    )

    @pl.when(e != c)
    def _():
        pl.semaphore_signal(bar, inc=1, device_id=at(b, g * 2 + c, y, e), device_id_type=MESH)

    is_first, is_mid = k == 0, k == nb // 2

    @pl.when(is_first)
    def _():
        pl.semaphore_signal(bar, inc=1, device_id=(b, nb // 2), device_id_type=MESH)

    @pl.when(is_mid)
    def _():
        pl.semaphore_signal(bar, inc=1, device_id=(b, 0), device_id_type=MESH)

    pl.semaphore_wait(
        bar, nz + 2 + ng + 1 - jnp.where(e == c, 1, 0) + jnp.where(is_first, 1, 0) + jnp.where(is_mid, 1, 0)
    )


def front_kernel(
    nz, x_ref, cos_ref, sin_ref, len_ref, wq_ref, wk_ref, wv_ref, wo_u, gain_u, wg_ref, wu_ref, wd_x,
    ball, h1_o, attn_h, raw_h, q_h, o_h, ob_h, lse_h, kv_h, wqkv_h, wo_h, xq_h, xkv_h, xo_h, xlse_h, gd_o, gh_o, wg_f, wu_f, wd_f,
    attn_s, raw_s, q_s, o_s, ob_s, lse_s, kvall, kv_own, wqkv, wo, gain_f, qkv_u, wg, wu, wd, qkv_x, wg_x, wu_x, qkv_r, wg_r, wu_r,
    xq, xkv, xo_s, xlse_s, xob, xin, xss, xrs,
    lsem, ssem, rsem, wls, wss, wrs, kls, kss, krs, osem, qss, qrs, tss, trs,
):
    b, q, y, c = place()
    k = lax.axis_index("blk")
    nb = 4 * nz
    n_dev = 2 * nb
    g, e = q // 2, q % 2
    ng = nz // 2
    hz = nz // 2
    qw = qkv_u.shape[1]
    self_in = e == c
    front_barrier(nz)
    other_x, other_y, other_c = at(1 - b, q, y, c), at(b, q, 1 - y, c), at(b, q, y, 1 - c)
    everything, both = pl.ds(0, nz), pl.ds(0, 2)
    kr = qkv_u.shape[0] // 4
    dr, dp = wd_x.shape[0], wd.shape[0]

    def split_rows(ref, out):
        out[...] = jnp.zeros(out.shape, BF16)
        for n in range(2 * nz):
            for j in range(4):
                o = (4 * n + j) * dr
                out[j, :kr, n * dp : n * dp + dr] = ref[:, o : o + dr]

    sent = []

    def start(cp):
        cp.start()
        sent.append(cp)
        return cp

    quad = [(y, 1 - c), (1 - y, c), (1 - y, 1 - c)]
    trades = [(qkv_x, qkv_r, qkv_u), (wg_x, wg_r, wg), (wu_x, wu_r, wu)]
    t_in = [[] for _ in trades]

    def trade(i):
        src, dst, _ = trades[i]
        for p, (yy, cc) in enumerate(quad):
            t = at(b, q, yy, cc)
            start(remote(src.at[yy * 2 + cc], dst.at[y * 2 + c], qss.at[i, p], qrs.at[i, p], t))
            t_in[i].append(remote(src.at[yy * 2 + cc], dst.at[yy * 2 + cc], qss.at[i, p], qrs.at[i, p], t))
        t_in[i].append(pltpu.make_async_copy(src.at[y * 2 + c], dst.at[y * 2 + c], qrs.at[i, 3]))
        t_in[i][3].start()

    def traded(i):
        _, src, dst = trades[i]
        for p in range(3):
            t_in[i][p].wait_recv()
        t_in[i][3].wait()
        pick = pack_rows(kr, src.shape[1])
        for o, n in tiles(src.shape[2], 256):
            v = jnp.dot(pick, src[:, :, o : o + n].reshape(4 * src.shape[1], n), preferred_element_type=F32)
            dst[:, o : o + n] = v.astype(BF16)

    def view_q(ref, yy, cc, xx, qq):
        return ref.at[xx, qq, :, pl.ds(pl.multiple_of((yy * 2 + cc) * qw, 128), HD)]

    def view_kv(ref, yy, cc, xx, qq):
        return ref.at[xx, qq, :, pl.ds(pl.multiple_of((yy * 2 + cc) * qw + HD, 128), qw - HD)]

    def view_lead(ref, yy, cc, xx, qq):
        return ref.at[xx, qq, yy, cc]

    GAIN, KV, Q, WO = range(4)
    items = [
        (gain_u, gain_f, view_lead, True),
        (qkv_u.at[:, HD:], wqkv, view_kv, True),
        (qkv_u.at[:, :HD], wqkv, view_q, True),
        (wo_u, wo, view_lead, True),
    ]
    local = [None] * 4
    z_in, a_in, b_in, c_in = ([[] for _ in items] for _ in range(4))

    def hop(i, v, w, s, t):
        start(remote(v, v, ssem.at[i, s], rsem.at[i, s], t))
        return remote(v, w, ssem.at[i, s], rsem.at[i, s], t)

    def second(i):
        return (other_x, 1 - b, y) if items[i][3] else (other_y, b, 1 - y)

    def send_z(i):
        src, dst, view, _ = items[i]
        local[i] = pltpu.make_async_copy(src, view(dst, y, c, b, q), lsem.at[i])
        local[i].start()
        for r in range(1, nz):
            t = at(b, lax.rem(q + r, nz), y, c)
            start(remote(src, view(dst, y, c, b, q), ssem.at[i, r], rsem.at[i, r], t))
            z_in[i].append(
                remote(src, view(dst, y, c, b, lax.rem(q - r + nz, nz)), ssem.at[i, r], rsem.at[i, r], t)
            )
        t, xx, yy = second(i)
        start(remote(src, view(dst, y, c, b, q), ssem.at[i, nz], rsem.at[i, nz], t))
        a_in[i].append(remote(src, view(dst, yy, c, xx, q), ssem.at[i, nz], rsem.at[i, nz], t))

    def send_a(i):
        _, dst, view, _ = items[i]
        t, xx, yy = second(i)
        for r in range(1, nz):
            qs = lax.rem(q - r + nz, nz)
            z_in[i][r - 1].wait_recv()
            a_in[i].append(hop(i, view(dst, y, c, b, qs), view(dst, yy, c, xx, qs), nz + r, t))

    def send_b(i, half):
        _, dst, view, x_first = items[i]
        if half == 0:
            local[i].wait()
            xx, yy = b, y
        else:
            for cp in a_in[i]:
                cp.wait_recv()
            _, xx, yy = second(i)
        t, xi, yi = (other_y, xx, 1 - yy) if x_first else (other_x, 1 - xx, yy)
        b_in[i].append(
            (hop(i, view(dst, yy, c, xx, everything), view(dst, yi, c, xi, everything), 2 * nz + half, t), xi, yi)
        )
        to_core(i, xx, yy, 2 * nz + 2 + half)

    def to_core(i, xx, yy, s):
        _, dst, view, _ = items[i]
        c_in[i].append(hop(i, view(dst, yy, c, xx, everything), view(dst, yy, 1 - c, xx, everything), s, other_c))

    def send_c(i):
        for half, (cp, xx, yy) in enumerate(b_in[i]):
            cp.wait_recv()
            to_core(i, xx, yy, 2 * nz + 4 + half)

    def done(i):
        for cp in c_in[i]:
            cp.wait_recv()

    pieces = [
        (src, dst, o, n) for src, dst in ((wd, wd_f), (wg, wg_f), (wu, wu_f)) for o, n in halves(src.shape[0])
    ]
    w_in, w_x, w_c, w_out = ([[] for _ in pieces] for _ in range(4))

    def w_send(j):
        src, dst, o, n = pieces[j]
        sl = pl.ds(o, n)
        for r in range(ng):
            t = at(b, lax.rem(g + r, ng) * 2 + c, y, e)
            qs = lax.rem(g - r + ng, ng) * 2 + c
            cp = remote(src.at[sl], dst.at[b, q, sl], wss.at[j, r], wrs.at[j, r], t)
            inc = remote(src.at[sl], dst.at[b, qs, sl], wss.at[j, r], wrs.at[j, r], t)
            if r == 0:
                lc = pltpu.make_async_copy(src.at[sl], dst.at[b, q, sl], wls.at[j])

                @pl.when(self_in)
                def _():
                    lc.start()

                @pl.when(jnp.logical_not(self_in))
                def _():
                    cp.start()

                w_in[j].append((inc, qs, lc))
                w_out[j].append(cp)
            else:
                start(cp)
                w_in[j].append((inc, qs, None))

    def w_on(j, xx, qs, s, target, yx, yq):
        _, dst, o, n = pieces[j]
        sl = pl.ds(o, n)
        start(remote(dst.at[xx, qs, sl], dst.at[xx, qs, sl], wss.at[j, s], wrs.at[j, s], target))
        return remote(dst.at[xx, qs, sl], dst.at[yx, yq, sl], wss.at[j, s], wrs.at[j, s], target)

    def w_across(j):
        for r, (inc, qs, lc) in enumerate(w_in[j]):
            if lc is not None:

                @pl.when(self_in)
                def _():
                    lc.wait()

                @pl.when(jnp.logical_not(self_in))
                def _():
                    inc.wait_recv()
            else:
                inc.wait_recv()
            w_x[j].append(w_on(j, b, qs, ng + r, other_x, 1 - b, qs))
        for r, (_, qs, _) in enumerate(w_in[j]):
            w_c[j].append(w_on(j, b, qs, 2 * ng + r, other_c, b, lax.rem(g - r + ng, ng) * 2 + 1 - c))

    def w_core(j):
        for r, (_, qs, _) in enumerate(w_in[j]):
            w_x[j][r].wait_recv()
            w_c[j].append(w_on(j, 1 - b, qs, 3 * ng + r, other_c, 1 - b, lax.rem(g - r + ng, ng) * 2 + 1 - c))

    last = len(pieces)

    kept = []

    def keep(src, dst):
        cp = pltpu.make_async_copy(src, dst, osem.at[len(kept)])
        cp.start()
        kept.append(cp)

    qkv_x[...] = jnp.zeros(qkv_x.shape, BF16)
    per = qw - HD
    for j in range(4):
        qkv_x[j, :kr, :HD] = wq_ref[:, j * HD : (j + 1) * HD]
        o = j * per % HD
        qkv_x[j, :kr, HD:] = (wk_ref if j * per < HD else wv_ref)[:, o : o + per]
    trade(0)
    send_z(GAIN)
    if wd.shape[0] == dr:
        wd[...] = wd_x[...]
    else:
        whole = dr // 16 * 16
        wd[:whole] = wd_x[:whole]
        rest = jnp.zeros((wd.shape[0] - dr, wd.shape[1]), BF16)
        wd[whole:] = jnp.concatenate([wd_x[whole:], rest], axis=0)
    w_send(0)
    traded(0)
    send_z(KV)
    send_z(Q)
    split_rows(wg_ref, wg_x)
    trade(1)
    split_rows(wu_ref, wu_x)
    micro, _, tok, _ = q_s.shape
    rows = micro * tok
    x = x_ref[...].astype(F32)
    n_x = norm_of(x)[0]
    send_a(GAIN)
    send_a(KV)
    send_b(GAIN, 0)
    send_b(KV, 0)
    traded(1)
    w_send(1)
    send_b(GAIN, 1)
    send_b(KV, 1)
    send_a(Q)
    send_b(Q, 0)
    trade(2)
    w_across(0)
    w_send(2)
    send_z(WO)
    send_c(GAIN)
    send_c(KV)
    done(GAIN)
    done(KV)
    width = x_ref.shape[1]
    gains_d = spread_gains(gain_f[...].reshape(n_dev * 16, 128), width, n_dev)
    gains_h = spread_gains(gain_f[...].reshape(n_dev * 16, 128), HD, n_dev)
    gd_o[...] = gains_d
    gh_o[...] = gains_h
    a = (n_x * (1.0 + gains_d[0:1])).astype(BF16)
    cosine, sine = cos_ref[...], sin_ref[...]
    half = HD // 2

    def project(h):
        if h < H:
            w = wqkv[:, :, :, h * qw : h * qw + HD]
        else:
            o1, o2 = kv_columns(h - H, qw)
            w = jnp.concatenate([wqkv[:, :, :, o1 : o1 + half], wqkv[:, :, :, o2 : o2 + half]], axis=3)
        raw = jnp.dot(a, w.reshape(width, HD), preferred_element_type=F32)
        if h == H + 1:
            kv_own[:, :, HD:] = raw.astype(BF16).reshape(micro, tok, HD)
            return
        raw_s[:, h * HD : (h + 1) * HD] = raw
        z = norm_of(raw)[0] * (1.0 + (gains_h[1:2] if h < H else gains_h[2:3]))
        z1, z2 = z[:, :half], z[:, half:]
        z = jnp.concatenate([z1 * cosine - z2 * sine, z2 * cosine + z1 * sine], axis=1).astype(BF16)
        if h < H:
            q_s[:, h] = z.reshape(micro, tok, HD)
        else:
            kv_own[:, :, :HD] = z.reshape(micro, tok, HD)

    project(H)
    project(H + 1)
    ht = tok // 2
    is_first, is_mid = k == 0, k == nb // 2
    first, mid = (b, 0), (b, nb // 2)
    x_kv = remote(kv_own.at[:, :ht], xkv, xss.at[0], xrs.at[0], first)
    x_q = remote(q_s.at[:, :, :ht], xq, xss.at[1], xrs.at[1], first)
    x_o = remote(xob, xin, xss.at[2], xrs.at[2], mid)

    @pl.when(is_mid)
    def _():
        x_kv.start()

    side = q // hz
    ql = q - side * hz

    def kview(qq, yy, cc):
        return kvall.at[qq - side * hz, yy, cc]

    mine = pltpu.make_async_copy(kv_own, kview(q, y, c), kls)
    mine.start()
    kz_in, ky_in, kc_in = [], [], []
    for r in range(1, hz):
        t = at(b, side * hz + lax.rem(ql + r, hz), y, c)
        start(remote(kv_own, kview(q, y, c), kss.at[r], krs.at[r], t))
        src = side * hz + lax.rem(ql - r + hz, hz)
        kz_in.append((remote(kv_own, kview(src, y, c), kss.at[r], krs.at[r], t), src))
    start(remote(kv_own, kview(q, y, c), kss.at[hz], krs.at[hz], other_y))
    ky_in.append((remote(kv_own, kview(q, 1 - y, c), kss.at[hz], krs.at[hz], other_y), q))
    slot = [2 * hz]

    def k_core(qq, yy):
        s = slot[0]
        slot[0] += 1
        start(remote(kview(qq, yy, c), kview(qq, yy, c), kss.at[s], krs.at[s], other_c))
        kc_in.append(remote(kview(qq, yy, c), kview(qq, yy, 1 - c), kss.at[s], krs.at[s], other_c))

    mine.wait()
    k_core(q, y)
    traded(2)
    send_b(Q, 1)
    w_across(1)
    w_send(3)
    w_core(0)
    send_a(WO)
    send_b(WO, 0)
    for r, (cp, src) in enumerate(kz_in):
        cp.wait_recv()
        s = hz + 1 + r
        start(remote(kview(src, y, c), kview(src, y, c), kss.at[s], krs.at[s], other_y))
        ky_in.append((remote(kview(src, y, c), kview(src, 1 - y, c), kss.at[s], krs.at[s], other_y), src))
        k_core(src, y)
    send_c(Q)
    w_across(2)
    w_send(4)
    w_core(1)
    done(Q)
    for h in range(H):
        project(h)

    @pl.when(is_mid)
    def _():
        x_q.start()

    keep(wqkv, wqkv_h)
    keep(raw_s, raw_h)
    keep(q_s, q_h)
    send_b(WO, 1)
    for cp, src in ky_in:
        cp.wait_recv()
        k_core(src, 1 - y)
    w_across(3)
    w_send(5)
    w_core(2)
    for cp in kc_in:
        cp.wait_recv()

    scale = HD ** (-0.5)
    lo = side * (nb // 4)
    hi = k // 2 + 1
    qrows = H * tok
    qidx = k * tok + lax.rem(lax.broadcasted_iota(jnp.int32, (qrows, 1), 0), tok)

    def online(carry, s, ok, values):
        mx, sm, acc = carry
        if ok is not None:
            s = jnp.where(ok, s, -1e30)
        new = jnp.maximum(mx, jnp.max(s, axis=-1, keepdims=True))
        p = jnp.exp(s - new)
        if ok is not None:
            p = jnp.where(ok, p, 0.0)
        alpha = jnp.exp(mx - new)
        sm = sm * alpha + jnp.sum(p, axis=-1, keepdims=True)
        return new, sm, acc * alpha + jnp.dot(p.astype(BF16), values, preferred_element_type=F32)

    def empty(n):
        return jnp.full((n, 1), -1e30, F32), jnp.zeros((n, 1), F32), jnp.zeros((n, HD), F32)

    @pl.when(is_first)
    def _():
        x_kv.wait_recv()
        x_q.wait_recv()
        for m in range(micro):
            qm = xq[m].reshape(H * ht, HD)

            def body(j, carry):
                blk = kvall[j // 2, j % 2, :, m].reshape(256, 2 * HD)
                s = lax.dot_general(qm, blk[:, :HD], (((1,), (1,)), ((), ())), preferred_element_type=F32) * scale
                return online(carry, s, None, blk[:, HD:])

            carry = lax.fori_loop(0, nb // 4, body, empty(H * ht))
            blk = xkv[m]
            s = lax.dot_general(qm, blk[:, :HD], (((1,), (1,)), ((), ())), preferred_element_type=F32) * scale
            mx, sm, acc = online(carry, s, half_mask(H * ht, ht), blk[:, HD:])
            xo_s[m] = acc / sm
            xlse_s[m] = mx + jnp.log(sm)
            xob[m] = xo_s[m].astype(BF16).reshape(H, ht, HD)
        x_o.start()

    b_all = [Gather((b, g, e, y), c, tss.at[m], trs.at[m], sent) for m in range(micro)]
    for m in range(micro):
        qm = q_s[m].reshape(qrows, HD)
        segq = segment_of(len_ref, m, qidx)

        def body(j, carry):
            blk = kvall[j // 2 - side * hz, j % 2, :, m].reshape(256, 2 * HD)
            kidx = j * 256 + lax.broadcasted_iota(jnp.int32, (1, 256), 1)
            s, ok = chunk_scores(qm, blk[:, :HD], segq, segment_of(len_ref, m, kidx), qidx, j, scale)
            return online(carry, s, ok, blk[:, HD:])

        mx, sm, acc = lax.fori_loop(lo, hi, body, empty(qrows))
        o = acc / sm
        o_s[m] = o
        lse_s[m] = mx + jnp.log(sm)
        rs = slice(m * tok, (m + 1) * tok)
        for h in range(H):
            ob_s[rs, h * HD : (h + 1) * HD] = o[h * tok : (h + 1) * tok].astype(BF16)
        if m == 0:
            w_across(4)
            w_core(3)
            send_c(WO)
            done(WO)

            @pl.when(is_mid)
            def _():
                x_o.wait_recv()

        @pl.when(is_mid)
        def _():
            for h in range(H):
                ob_s[m * tok : m * tok + ht, h * HD : (h + 1) * HD] = xin[m, h]

        for o, n in tiles(width, 256):
            w = wo[:, :, :, :, :, o : o + n].reshape(H * HD, n)
            attn_s[rs, o : o + n] = jnp.dot(ob_s[rs], w, preferred_element_type=F32)
        h1 = x_ref[rs].astype(F32) + norm_of(attn_s[rs])[0] * (1.0 + gains_d[3:4])
        h1_o[m] = h1
        ball[m, e * 2 + y] = (norm_of(h1)[0] * (1.0 + gains_d[4:5])).astype(BF16)
        b_all[m].begin(ball.at[m])
        if m > 0:
            b_all[m - 1].forward()
    for src, dst in ((xq, xq_h), (xkv, xkv_h), (xo_s, xo_h), (xlse_s, xlse_h)):
        keep(src, dst)
    keep(o_s, o_h)
    keep(lse_s, lse_h)
    keep(ob_s, ob_h)
    keep(kvall, kv_h)
    keep(attn_s, attn_h)
    keep(wo, wo_h)
    w_across(5)
    w_core(4)
    b_all[micro - 1].forward()
    w_core(5)
    for m in range(micro):
        b_all[m].end()
    for j in range(last):
        for cp in w_c[j]:
            cp.wait_recv()
    for cp in sent:
        cp.wait_send()
    for j in range(last):

        @pl.when(jnp.logical_not(self_in))
        def _():
            w_out[j][0].wait_send()

    @pl.when(is_mid)
    def _():
        x_kv.wait_send()
        x_q.wait_send()

    @pl.when(is_first)
    def _():
        x_o.wait_send()

    for cp in kept:
        cp.wait()


def front(nz, x, cosine, sine, lengths, wq, wk, wv, wo, gain, wg, wu, wd, dp, micro):
    kr, kp = wg.shape[0], up16(wg.shape[0])
    fs = 2 * nz * dp
    qw = (wq.shape[1] + wk.shape[1] + wv.shape[1]) // 4
    ng = nz // 2
    hz = nz // 2
    rows, width = x.shape
    tok = rows // micro
    nb = 4 * nz
    out = {
        "ball": ((micro, 4, tok, width), BF16),
        "h1": ((micro, tok, width), F32),
        "attn": ((rows, width), F32),
        "raw": ((rows, (H + 1) * HD), F32),
        "q": ((micro, H, tok, HD), BF16),
        "o": ((micro, H * tok, HD), F32),
        "ob": ((rows, H * HD), BF16),
        "lse": ((micro, H * tok, 1), F32),
        "kv": ((hz, 2, 2, micro, tok, 2 * HD), BF16),
        "wqkv": ((2, nz, 4 * kr, 4 * qw), BF16),
        "wo": ((2, nz, 2, 2) + wo.shape, BF16),
        "xq": ((micro, H, tok // 2, HD), BF16),
        "xkv": ((micro, tok // 2, 2 * HD), BF16),
        "xo": ((micro, H * tok // 2, HD), F32),
        "xlse": ((micro, H * tok // 2, 1), F32),
        "gd": ((16, width), F32),
        "gh": ((16, HD), F32),
        "wg": ((2, nz, 4 * kr, fs), BF16),
        "wu": ((2, nz, 4 * kr, fs), BF16),
        "wd": ((2, nz, dp, width), BF16),
    }
    shapes = [jax.ShapeDtypeStruct(*v) for v in out.values()]
    scratch = [pltpu.VMEM(*out[n]) for n in ("attn", "raw", "q", "o", "ob", "lse", "kv")]
    ns = 2 * nz + 6
    n_pieces = 2 * len(halves(4 * kr)) + len(halves(dp))
    scratch += [pltpu.VMEM((micro, tok, 2 * HD), BF16), pltpu.VMEM(*out["wqkv"]), pltpu.VMEM(*out["wo"])]
    scratch += [pltpu.VMEM((2, nz, 2, 2) + gain.shape, BF16)]
    scratch += [pltpu.VMEM((4 * kr, n), BF16) for n in (qw, fs, fs)] + [pltpu.VMEM((dp, width), BF16)]
    scratch += [pltpu.VMEM((4, kp, n), BF16) for n in (qw, fs, fs) * 2]
    scratch += [pltpu.VMEM(*out[n]) for n in ("xq", "xkv", "xo", "xlse", "xq", "xq")]
    scratch += [pltpu.SemaphoreType.DMA((3,)), pltpu.SemaphoreType.DMA((3,))]
    scratch += [
        pltpu.SemaphoreType.DMA((4,)),
        pltpu.SemaphoreType.DMA((4, ns)),
        pltpu.SemaphoreType.DMA((4, ns)),
        pltpu.SemaphoreType.DMA((n_pieces,)),
        pltpu.SemaphoreType.DMA((n_pieces, 4 * ng)),
        pltpu.SemaphoreType.DMA((n_pieces, 4 * ng)),
        pltpu.SemaphoreType.DMA,
        pltpu.SemaphoreType.DMA((4 * hz,)),
        pltpu.SemaphoreType.DMA((4 * hz,)),
        pltpu.SemaphoreType.DMA((13,)),
        pltpu.SemaphoreType.DMA((3, 3)),
        pltpu.SemaphoreType.DMA((3, 4)),
        pltpu.SemaphoreType.DMA((micro, 6)),
        pltpu.SemaphoreType.DMA((micro, 6)),
    ]
    specs = [VMEM, VMEM] + [ANY] * 13 + [VMEM, VMEM] + [ANY] * 3
    got = pl.pallas_call(
        functools.partial(front_kernel, nz),
        out_shape=shapes,
        in_specs=[VMEM] * 3 + [pl.BlockSpec(memory_space=pltpu.SMEM)] + [VMEM] * 3 + [ANY] * 2 + [VMEM] * 3,
        out_specs=specs,
        scratch_shapes=scratch,
        compiler_params=pltpu.CompilerParams(collective_id=5, has_side_effects=True, vmem_limit_bytes=60 * 2**20),
    )(x, cosine, sine, lengths, wq, wk, wv, wo, gain, wg, wu, wd)
    return dict(zip(out, got))


def back_kernel(
    nz, db_ref, h1_ref, dy_ref, x_ref, cos_ref, sin_ref, len_ref, gd_ref, gh_ref, dgp_ref,
    attn_h, raw_h, q_h, o_h, ob_h, lse_h, kv_h, wqkv_h, wo_h, xq_h, xkv_h, xo_h, xlse_h, gg, gu, gdn,
    dx_o, q_o, k_o, v_o, wo_o, gain_o, wg_o, wu_o, wd_o,
    attn, raw, q_s, o_s, ob, lse, kvall, wqkv, wo, xq, xkv, xo, xlse,
    xdo, xdq, xdkv, xpart, qin, kvin, dh1, datt, do_s, delta, dqkv, da, gqkv, gwo, ggain,
    k1, k2, k3, *rest,
):
    hops = [rest[4 * i : 4 * i + 4] for i in range(4)]
    rest = rest[16:]
    wown, w1, w2, w3 = (rest[3 * i : 3 * i + 3] for i in range(4))
    q_r, kv_r, q_t, kv_t, wg_t, wu_t = rest[12:18]
    lsem, ssem, rsem, wls, wss, wrs, kss, krs, xss, xrs, qss, qrs = rest[18:]
    b, q, y, c = place()
    k = lax.axis_index("blk")
    nb = 4 * nz
    n_dev = 2 * nb
    g, e = q // 2, q % 2
    ng = nz // 2
    hz = nz // 2
    qw = gqkv.shape[3] // 4
    kr = gqkv.shape[2] // 4
    self_in = e == c
    other_x, other_y, other_c = at(1 - b, q, y, c), at(b, q, 1 - y, c), at(b, q, y, 1 - c)
    both, everything = pl.ds(0, 2), pl.ds(0, nz)
    micro, _, tok, _ = q_s.shape
    rows, width = x_ref.shape
    nt = (((1,), (1,)), ((), ()))
    tn = (((0,), (0,)), ((), ()))
    loads = []
    for i, (src, dst) in enumerate(
        ((attn_h, attn), (wo_h, wo), (o_h, o_s), (q_h, q_s), (kv_h, kvall), (lse_h, lse), (ob_h, ob), (raw_h, raw), (wqkv_h, wqkv),
         (xq_h, xq), (xkv_h, xkv), (xo_h, xo), (xlse_h, xlse))
    ):
        cp = pltpu.make_async_copy(src, dst, lsem.at[i])
        cp.start()
        loads.append(cp)
    front_barrier(nz)
    sent = []

    def start(cp):
        cp.start()
        sent.append(cp)
        return cp

    def add(dst, src, n, step):
        def one(i, _):
            sl = pl.ds(pl.multiple_of(i * step, step), step)
            dst[sl] = dst[sl] + src[sl]
            return 0

        lax.fori_loop(0, n // step, one, 0)

    quad = [(y, 1 - c), (1 - y, c), (1 - y, 1 - c)]
    t_in = []

    def trade(src, dst, s, cols):
        for p, (yy, cc) in enumerate(quad):
            there = remote(src.at[yy * 2 + cc, :, cols], dst.at[y * 2 + c, :, cols], qss.at[s, p], qrs.at[s, p], at(b, q, yy, cc))
            here = remote(src.at[yy * 2 + cc, :, cols], dst.at[yy * 2 + cc, :, cols], qss.at[s, p], qrs.at[s, p], at(b, q, yy, cc))
            start(there)
            t_in.append(here)
        dst[y * 2 + c, :, cols] = src[y * 2 + c, :, cols]

    def unpack_rows(total, kp):
        v = lax.dot_general(pack_rows(kr, kp), total, tn, preferred_element_type=F32)
        return v.astype(BF16).reshape(4, kp, total.shape[1])

    units = [(gg, wg_o, wg_t), (gu, wu_o, wu_t), (gdn, wd_o, None)]
    fs = gg.shape[4]
    near = fs // 256 * 128
    pieces = [(u, (0, gg.shape[3]), cols) for u in range(2) for cols in ((0, near), (near, fs - near))]
    pieces += [(2, r, (0, width)) for r in halves(gdn.shape[3])]
    dr = wd_o.shape[0]
    w_local, w_in = [None] * len(pieces), [None] * len(pieces)

    def part_of(j):
        u, (ro, rn), (co, cn) = pieces[j]
        return u, pl.ds(ro, rn), pl.ds(co, cn), rn

    def w_core(j):
        u, sl, cl, _ = part_of(j)
        src = units[u][0]
        w_in[j] = start(remote(src.at[:, :, 1 - c, sl, cl], w1[u].at[:, :, sl, cl], wss.at[j, 0], wrs.at[j, 0], other_c))
        w_local[j] = pltpu.make_async_copy(src.at[:, :, c, sl, cl], wown[u].at[:, :, sl, cl], wls.at[j, 0])
        w_local[j].start()

    def w_x(j):
        u, sl, cl, n = part_of(j)
        w_local[j].wait()
        w_in[j].wait_recv()
        for r in range(ng):
            add(wown[u].at[1 - b, r, sl, cl], w1[u].at[1 - b, r, sl, cl], n, 16)
        w_in[j] = start(remote(wown[u].at[1 - b, :, sl, cl], w2[u].at[:, sl, cl], wss.at[j, 1], wrs.at[j, 1], other_x))
        for r in range(ng):
            add(wown[u].at[b, r, sl, cl], w1[u].at[b, r, sl, cl], n, 16)

    def w_z(j):
        u, sl, cl, n = part_of(j)
        w_in[j].wait_recv()
        for r in range(ng):
            add(wown[u].at[b, r, sl, cl], w2[u].at[r, sl, cl], n, 16)
        waits = []
        for r in range(ng):
            gs = lax.rem(g + r, ng)
            src, dst = wown[u].at[b, gs, sl, cl], w3[u].at[r, sl, cl]
            cp = remote(src, dst, wss.at[j, 2 + r], wrs.at[j, 2 + r], at(b, gs * 2 + c, y, e))
            lc = None
            if r == 0:
                lc = pltpu.make_async_copy(src, dst, wls.at[j, 1])

                @pl.when(self_in)
                def _():
                    lc.start()

                @pl.when(jnp.logical_not(self_in))
                def _():
                    cp.start()
            else:
                start(cp)
            waits.append((cp, lc))
        w_in[j] = waits

    def w_end(j):
        u, (ro, rn), (co, cn) = pieces[j]
        for cp, lc in w_in[j]:
            if lc is not None:

                @pl.when(self_in)
                def _():
                    lc.wait()

                @pl.when(jnp.logical_not(self_in))
                def _():
                    cp.wait()
            else:
                cp.wait_recv()
        _, out, send = units[u]
        if send is None:

            def total_of(sl):
                total = w3[u][0, sl].astype(F32)
                for r in range(1, ng):
                    total = total + w3[u][r, sl].astype(F32)
                return total

            def one(i, _):
                sl = pl.ds(pl.multiple_of(ro + i * 16, 16), 16)
                out[sl] = total_of(sl)
                return 0

            end = min(ro + rn, dr)
            full = (end - ro) // 16
            lax.fori_loop(0, full, one, 0)
            if ro + full * 16 < end:
                out[ro + full * 16 : end] = total_of(pl.ds(ro + full * 16, 16))[: end - ro - full * 16]
        else:

            def one(i, _):
                cols = pl.ds(pl.multiple_of(co + i * 128, 128), 128)
                total = w3[u][0, :, cols].astype(F32)
                for r in range(1, ng):
                    total = total + w3[u][r, :, cols].astype(F32)
                send[:, :, cols] = unpack_rows(total.astype(BF16), send.shape[1])
                return 0

            lax.fori_loop(0, cn // 128, one, 0)
            trade(send, out, j, pl.ds(co, cn))

    w_core(0)
    w_core(1)

    def view_q(ref, yy, cc):
        return ref.at[:, :, :, pl.ds(pl.multiple_of((yy * 2 + cc) * qw, 128), HD)]

    def view_kv(ref, yy, cc):
        return ref.at[:, :, :, pl.ds(pl.multiple_of((yy * 2 + cc) * qw + HD, 128), qw - HD)]

    def view_lead(ref, yy, cc):
        return ref.at[:, :, yy, cc]

    items = [
        (gqkv, view_q, hops[0], None),
        (gwo, view_lead, hops[1], wo_o),
        (ggain, view_lead, hops[2], gain_o),
        (gqkv, view_kv, hops[3], None),
    ]
    item_in = [[] for _ in items]

    def join(dst, src, lead):
        for idx in lead:
            dst[idx] = dst[idx] + src[idx]

    def grid2(v):
        return [(xx, qq) for xx in range(2) for qq in range(nz)]

    def item_core(i):
        src, view, (r1, _, _, _), _ = items[i]
        for yy in range(2):
            item_in[i].append(start(remote(view(src, yy, 1 - c), r1.at[yy], ssem.at[i, yy], rsem.at[i, yy], other_c)))

    def loop2(fn):
        def one(n, _):
            fn(lax.div(n, nz), lax.rem(n, nz))
            return 0

        lax.fori_loop(0, 2 * nz, one, 0)

    def item_y(i):
        src, view, (r1, r2, _, _), _ = items[i]
        for cp in item_in[i]:
            cp.wait_recv()
        for yy in (1 - y, y):
            v = view(src, yy, c)

            def fn(xx, qq):
                v[xx, qq] = v[xx, qq] + r1[yy, xx, qq]

            loop2(fn)
            if yy is not y:
                item_in[i] = [start(remote(v, r2, ssem.at[i, 2], rsem.at[i, 2], other_y))]

    def item_x(i):
        src, view, (_, r2, r3, _), _ = items[i]
        item_in[i][0].wait_recv()
        v = view(src, y, c)

        def fn(xx, qq):
            v[xx, qq] = v[xx, qq] + r2[xx, qq]

        loop2(fn)
        item_in[i] = [start(remote(v.at[1 - b], r3, ssem.at[i, 3], rsem.at[i, 3], other_x))]

    def item_z(i):
        src, view, (_, _, r3, r4), _ = items[i]
        item_in[i][0].wait_recv()
        v = view(src, y, c)
        for qq in range(nz):
            v[b, qq] = v[b, qq] + r3[qq]
        waits = []
        for r in range(1, nz):
            qt = lax.rem(q + r, nz)
            waits.append(start(remote(v.at[b, qt], r4.at[r - 1], ssem.at[i, 3 + r], rsem.at[i, 3 + r], at(b, qt, y, c))))
        item_in[i] = waits

    def item_end(i):
        src, view, (_, _, _, r4), out = items[i]
        for cp in item_in[i]:
            cp.wait_recv()
        v = view(src, y, c)
        total = v[b, q].astype(F32)
        for r in range(1, nz):
            total = total + r4[r - 1].astype(F32)
        if i in (0, 3):
            send, dst = (q_t, q_r) if i == 0 else (kv_t, kv_r)
            send[...] = unpack_rows(total.astype(BF16), send.shape[1])
            trade(send, dst, len(pieces) + i // 3, pl.ds(0, send.shape[2]))
        else:
            out[...] = total

    gains = gd_ref[...]
    loads[0].wait()
    dy = dy_ref[...].astype(F32)
    n1, r1 = norm_of(h1_ref[...].reshape(rows, width))
    d, dg_pf = norm_back(db_ref[...].reshape(rows, width), n1, r1, 1.0 + gains[4:5])
    dh1[...] = dy + d
    n2, r2 = norm_of(attn[...])
    d, dg_pa = norm_back(dh1[...], n2, r2, 1.0 + gains[3:4])
    datt[...] = d.astype(BF16)
    w_x(0)
    w_core(2)
    w_core(3)
    loads[1].wait()
    loads[2].wait()
    for h in range(H):
        w = wo[...].reshape(H * HD, width)[h * HD : (h + 1) * HD]
        d = lax.dot_general(datt[...], w, nt, preferred_element_type=F32).astype(BF16)
        do_s[:, h] = d.reshape(micro, tok, HD)
        for m in range(micro):
            hs = slice(h * tok, (h + 1) * tok)
            delta[m, hs] = jnp.sum(d[m * tok : (m + 1) * tok].astype(F32) * o_s[m, hs], axis=-1, keepdims=True)
    ht = tok // 2
    is_first, is_mid = k == 0, k == nb // 2
    first, mid = (b, 0), (b, nb // 2)
    x_do = remote(do_s.at[:, :, :ht], xdo, xss.at[0], xrs.at[0], first)
    x_dq = remote(xdq, qin, xss.at[1], xrs.at[1], mid)
    x_dkv = remote(xdkv, kvin, xss.at[2], xrs.at[2], mid)

    @pl.when(is_mid)
    def _():
        x_do.start()

    w_x(1)
    w_core(4)
    w_core(5)
    for i in (3, 4, 5, 9, 10, 11, 12):
        loads[i].wait()

    @pl.when(is_mid)
    def _():
        x_do.wait_send()
        do_s[:, :, :ht] = jnp.zeros((micro, H, ht, HD), BF16)
        for m in range(micro):
            for h in range(H):
                delta[m, h * tok : h * tok + ht] = jnp.zeros((ht, 1), F32)


    side = q // hz
    ql = q - side * hz
    scale = HD ** (-0.5)
    lo = side * (nb // 4)
    hi = k // 2 + 1
    part = kvall

    def clear(j, _):
        part[j // 2 - side * hz, j % 2] = jnp.zeros(part.shape[2:], BF16)
        return 0

    @pl.when(jnp.logical_not(is_first))
    def _():
        lax.fori_loop(hi, (side + 1) * 2 * hz, clear, 0)

    def grads_of(qm, dom, blk, p, dl):
        dp = lax.dot_general(dom, blk[:, HD:], nt, preferred_element_type=F32)
        ds = (p * (dp - dl)).astype(BF16)
        dq = jnp.dot(ds, blk[:, :HD], preferred_element_type=F32) * scale
        dk = lax.dot_general(ds, qm, tn, preferred_element_type=F32) * scale
        dv = lax.dot_general(p.astype(BF16), dom, tn, preferred_element_type=F32)
        return dq, jnp.concatenate([dk, dv], axis=1)

    @pl.when(is_first)
    def _():
        x_do.wait_recv()
        for m in range(micro):
            qm, dom = xq[m].reshape(H * ht, HD), xdo[m].reshape(H * ht, HD)
            dl = jnp.sum(dom.astype(F32) * xo[m], axis=-1, keepdims=True)

            def one(blk, ok):
                s = lax.dot_general(qm, blk[:, :HD], nt, preferred_element_type=F32) * scale
                p = jnp.exp(s - xlse[m]) if ok is None else jnp.where(ok, jnp.exp(jnp.where(ok, s, -1e30) - xlse[m]), 0.0)
                return grads_of(qm, dom, blk, p, dl)

            dq, g0 = one(kvall[0, 0, :, m].reshape(256, 2 * HD), None)
            xpart[m] = g0.astype(BF16)

            def body(j, dq):
                d, g = one(kvall[j // 2, j % 2, :, m].reshape(256, 2 * HD), None)
                part[j // 2, j % 2, :, m] = g.astype(BF16).reshape(2, tok, 2 * HD)
                return dq + d

            dq = lax.fori_loop(1, nb // 4, body, dq)
            d, g = one(xkv[m], half_mask(H * ht, ht))
            xdq[m] = (dq + d).astype(BF16).reshape(H, ht, HD)
            xdkv[m] = g.astype(BF16)
        x_dq.start()
        x_dkv.start()

    qrows = H * tok
    qidx = k * tok + lax.rem(lax.broadcasted_iota(jnp.int32, (qrows, 1), 0), tok)
    dq_s = o_s
    for m in range(micro):
        dq_s[m] = jnp.zeros(dq_s.shape[1:], F32)
        segq = segment_of(len_ref, m, qidx)

        def body(j, _):
            qm, dom = q_s[m].reshape(qrows, HD), do_s[m].reshape(qrows, HD)
            blk = kvall[j // 2 - side * hz, j % 2, :, m].reshape(256, 2 * HD)
            kidx = j * 256 + lax.broadcasted_iota(jnp.int32, (1, 256), 1)
            s, ok = chunk_scores(qm, blk[:, :HD], segq, segment_of(len_ref, m, kidx), qidx, j, scale)
            p = jnp.where(ok, jnp.exp(jnp.where(ok, s, -1e30) - lse[m]), 0.0)
            dq, g = grads_of(qm, dom, blk, p, delta[m])
            dq_s[m] += dq
            part[j // 2 - side * hz, j % 2, :, m] = g.astype(BF16).reshape(2, tok, 2 * HD)
            return 0

        lax.fori_loop(lo, hi, body, 0)

        @pl.when(is_first)
        def _():
            g = part[0, 0, :, m].reshape(256, 2 * HD).astype(F32) + xpart[m].astype(F32)
            part[0, 0, :, m] = g.astype(BF16).reshape(2, tok, 2 * HD)

        w_z(m)
        w_x(m + 2)

    k_in = start(remote(part.at[:, :, 1 - c], k1, kss.at[0], krs.at[0], other_c))
    loads[6].wait()
    obt = [ob[:, h * HD : (h + 1) * HD].T for h in range(H)]
    per = gwo.shape[0] * gwo.shape[1] * 4 // H
    for h in range(H):
        for o, n in tiles(width, 384):
            v = jnp.dot(obt[h], datt[:, o : o + n], preferred_element_type=F32).astype(BF16)
            n_lead = (2 * nz) // H
            xx, qq = (h * n_lead) // nz, (h * n_lead) % nz
            gwo[xx, qq : qq + n_lead, :, :, :, o : o + n] = v.reshape(n_lead, 2, 2, gwo.shape[4], n)
    item_core(1)
    k_in.wait_recv()

    def add1(n, _):
        part[n // 2, n % 2, c] = part[n // 2, n % 2, c] + k1[n // 2, n % 2]
        return 0

    lax.fori_loop(0, 2 * hz, add1, 0)
    k_in = start(remote(part.at[:, 1 - y, c], k2, kss.at[1], krs.at[1], other_y))
    loads[7].wait()
    cosine, sine = cos_ref[...], sin_ref[...]
    half = HD // 2
    gh = gh_ref[...]

    def unrotate(z):
        z1, z2 = z[:, :half], z[:, half:]
        return jnp.concatenate([z1 * cosine + z2 * sine, z2 * cosine - z1 * sine], axis=1)

    @pl.when(is_mid)
    def _():
        x_dq.wait_recv()
        for h in range(H):
            dq_s[:, h * tok : h * tok + ht] = qin[:, h].astype(F32)

    dg_q = jnp.zeros((1, HD), F32)
    for h in range(H):
        z = unrotate(dq_s[:, h * tok : (h + 1) * tok].reshape(rows, HD))
        n3, r3 = norm_of(raw[:, h * HD : (h + 1) * HD])
        d, dg = norm_back(z, n3, r3, 1.0 + gh[1:2])
        dqkv[:, h * qw : h * qw + HD] = d.astype(BF16)
        dg_q = dg_q + dg
    w_z(2)
    w_x(4)
    k_in.wait_recv()

    def add2(n, _):
        part[n, y, c] = part[n, y, c] + k2[n]
        return 0

    lax.fori_loop(0, hz, add2, 0)
    k_last = []
    for r in range(1, hz):
        qt = lax.rem(ql + r, hz)
        t = at(b, side * hz + qt, y, c)
        k_last.append(start(remote(part.at[qt, y, c], k3.at[r - 1], kss.at[1 + r], krs.at[1 + r], t)))
    item_y(1)
    n_x, r_x = norm_of(x_ref[...].astype(F32))
    at_ = (n_x * (1.0 + gains[0:1])).astype(BF16).T

    def weight_grad(o, n):
        v = jnp.dot(at_, dqkv[:, o : o + n], preferred_element_type=F32).astype(BF16)
        gqkv[:, :, :, o : o + n] = v.reshape(gqkv.shape[:3] + (n,))

    for h in range(H):
        weight_grad(h * qw, HD)
    item_core(0)
    w_z(3)
    w_x(5)
    w_end(0)
    total = part[ql, y, c].astype(F32)
    for r, cp in enumerate(k_last):
        cp.wait_recv()
        total = total + k3[r].astype(F32)

    dq_s[:, :tok] = total[:, :, :HD]
    dq_s[:, tok : 2 * tok] = total[:, :, HD:]

    @pl.when(is_mid)
    def _():
        x_dkv.wait_recv()
        dq_s[:, :ht] += kvin[:, :, :HD].astype(F32)
        dq_s[:, tok : tok + ht] += kvin[:, :, HD:].astype(F32)

    d_key, d_value = dq_s[:, :tok].reshape(rows, HD), dq_s[:, tok : 2 * tok].reshape(rows, HD)
    n3, r3 = norm_of(raw[:, H * HD :])
    d, dg_k = norm_back(unrotate(d_key), n3, r3, 1.0 + gh[2:3])
    for i, z in enumerate((d, d_value)):
        for o, v in zip(kv_columns(i, qw), (z[:, :half], z[:, half:])):
            dqkv[:, o : o + half] = v.astype(BF16)
            weight_grad(o, half)
    item_core(3)
    loads[8].wait()
    quads_at_once = max(1, 256 // wqkv.shape[2])
    for xx in range(2):
        for qq in range(0, nz, quads_at_once):
            n = min(quads_at_once, nz - qq)
            w = wqkv[xx, qq : qq + n].reshape(n * wqkv.shape[2], wqkv.shape[3])
            o = (xx * nz + qq) * wqkv.shape[2]
            da[o : o + n * wqkv.shape[2], :] = lax.dot_general(w, dqkv[...], nt, preferred_element_type=F32)
    d, dg_in = norm_back(da[...].T, n_x, r_x, 1.0 + gains[0:1])
    dx_o[...] = (dh1[...] + d).astype(BF16).reshape(dx_o.shape)
    none = jnp.zeros((1, width), F32)
    nohd = jnp.zeros((1, HD), F32)
    wide = jnp.concatenate([dg_in, none, none, dg_pa, dg_pf, dgp_ref[...], none, none], axis=0)
    slim = jnp.concatenate([nohd, dg_q, dg_k] + [nohd] * 5, axis=0)
    ggain[...] = (collect_gains(wide, n_dev) + collect_gains(slim, n_dev)).reshape(ggain.shape)
    item_core(2)
    w_z(4)
    item_x(1)
    item_y(0)
    item_y(3)
    item_y(2)
    w_end(1)
    w_z(5)
    item_z(1)
    w_end(2)
    item_x(0)
    item_x(3)
    item_x(2)
    w_end(3)
    item_z(0)
    item_z(3)
    item_z(2)
    item_end(1)
    w_end(4)
    w_end(5)
    item_end(0)
    item_end(3)
    item_end(2)
    for cp in t_in:
        cp.wait_recv()
    for j in range(4):
        q_o[:, j * HD : (j + 1) * HD] = q_r[j, :kr].astype(F32)
        half_o = k_o if j < 2 else v_o
        half_o[:, j % 2 * half : (j % 2 + 1) * half] = kv_r[j, :kr].astype(F32)
    for cp in sent:
        cp.wait_send()

    @pl.when(is_first)
    def _():
        x_dq.wait_send()
        x_dkv.wait_send()


def back(nz, db, h1, dy, x, cosine, sine, lengths, dgp, f, gg, gu, gd, kp, dr):
    ng = nz // 2
    hz = nz // 2
    nb = 4 * nz
    micro, tok, width = db.shape
    rows = micro * tok
    qr = f["wqkv"].shape[2]
    qw = f["wqkv"].shape[3] // 4
    orow = f["wo"].shape[4]
    kv = f["kv"].shape

    def like(n):
        return pltpu.VMEM(f[n].shape, f[n].dtype)

    gsplit = [z.reshape(2, ng, 2, -1, z.shape[-1]) for z in (gg, gu, gd)]
    ublock = [gsplit[i].shape[3:] for i in (2, 0, 1)]
    iblock = [((qr, HD), BF16), ((orow, width), BF16), ((8, 128), F32), ((qr, qw - HD), BF16)]
    scratch = [like(n) for n in ("attn", "raw", "q", "o", "ob", "lse", "kv", "wqkv", "wo", "xq", "xkv", "xo", "xlse")]
    scratch += [like("xq"), like("xq"), like("xkv"), pltpu.VMEM((micro, 256, 2 * HD), BF16), like("xq"), like("xkv")]
    scratch += [
        pltpu.VMEM((rows, width), F32),
        pltpu.VMEM((rows, width), BF16),
        pltpu.VMEM((micro, H, tok, HD), BF16),
        pltpu.VMEM((micro, H * tok, 1), F32),
        pltpu.VMEM((rows, (H + 2) * HD), BF16),
        pltpu.VMEM((width, rows), F32),
        pltpu.VMEM((2, nz, qr, 4 * qw), BF16),
        pltpu.VMEM((2, nz, 2, 2, orow, width), BF16),
        pltpu.VMEM((2, nz, 2, 2, 8, 128), F32),
        pltpu.VMEM((hz, 2) + kv[3:], BF16),
        pltpu.VMEM((hz,) + kv[3:], BF16),
        pltpu.VMEM((hz - 1,) + kv[3:], BF16),
    ]
    for s, t in iblock:
        scratch += [pltpu.VMEM(lead + s, t) for lead in ((2, 2, nz), (2, nz), (nz,), (nz - 1,))]
    for lead in ((2, ng), (2, ng), (ng,), (ng,)):
        scratch += [pltpu.VMEM(lead + ublock[i], BF16) for i in (1, 2, 0)]
    fs = ublock[1][1]
    scratch += [pltpu.VMEM((4, kp, n), BF16) for n in (HD, qw - HD)]
    scratch += [pltpu.VMEM((4, kp, n), BF16) for n in (HD, qw - HD, fs, fs)]
    n_pieces = 4 + len(halves(ublock[0][0]))
    scratch += [
        pltpu.SemaphoreType.DMA((13,)),
        pltpu.SemaphoreType.DMA((4, nz + 3)),
        pltpu.SemaphoreType.DMA((4, nz + 3)),
        pltpu.SemaphoreType.DMA((n_pieces, 2)),
        pltpu.SemaphoreType.DMA((n_pieces, 2 + ng)),
        pltpu.SemaphoreType.DMA((n_pieces, 2 + ng)),
        pltpu.SemaphoreType.DMA((hz + 1,)),
        pltpu.SemaphoreType.DMA((hz + 1,)),
        pltpu.SemaphoreType.DMA((3,)),
        pltpu.SemaphoreType.DMA((3,)),
        pltpu.SemaphoreType.DMA((n_pieces + 2, 3)),
        pltpu.SemaphoreType.DMA((n_pieces + 2, 3)),
    ]
    out = [
        jax.ShapeDtypeStruct((micro, tok, width), BF16),
        jax.ShapeDtypeStruct((qr // 4, H * HD), F32),
        jax.ShapeDtypeStruct((qr // 4, HD), F32),
        jax.ShapeDtypeStruct((qr // 4, HD), F32),
        jax.ShapeDtypeStruct((orow, width), F32),
        jax.ShapeDtypeStruct((8, 128), F32),
        jax.ShapeDtypeStruct((4, kp, fs), BF16),
        jax.ShapeDtypeStruct((4, kp, fs), BF16),
        jax.ShapeDtypeStruct((dr, width), F32),
    ]
    return pl.pallas_call(
        functools.partial(back_kernel, nz),
        out_shape=out,
        in_specs=[VMEM] * 6 + [pl.BlockSpec(memory_space=pltpu.SMEM)] + [VMEM] * 3 + [ANY] * 16,
        out_specs=[VMEM] * 9,
        scratch_shapes=scratch,
        compiler_params=pltpu.CompilerParams(collective_id=6, has_side_effects=True, vmem_limit_bytes=63 * 2**20),
    )(
        db, h1, dy, x, cosine, sine, lengths, f["gd"], f["gh"], dgp,
        f["attn"], f["raw"], f["q"], f["o"], f["ob"], f["lse"], f["kv"], f["wqkv"], f["wo"],
        f["xq"], f["xkv"], f["xo"], f["xlse"], *gsplit,
    )


def scaled_norm(values, gain):
    return values * lax.rsqrt(jnp.mean(values * values, axis=-1, keepdims=True) + epsilon) * (1.0 + gain)


def segments(lengths, index):
    docs = lengths.shape[1]
    ends = [sum(lengths[:, j] for j in range(i + 1)) for i in range(docs)]
    seg = jnp.zeros((lengths.shape[0], index.shape[0]), jnp.int32)
    first = jnp.zeros_like(seg)
    for i in range(docs):
        past = index[None, :] >= ends[i][:, None]
        seg = seg + past.astype(jnp.int32)
        first = first + jnp.where(past, lengths[:, i][:, None], 0)
    return seg, index[None, :] - first


def rotate(values, cosine, sine):
    half = values.shape[-1] // 2
    a, b = values[..., :half], values[..., half:]
    return jnp.concatenate([a * cosine - b * sine, b * cosine + a * sine], axis=-1)


def middle(attn_value, x_value, gain_attn, gain_pre):
    hidden = x_value + scaled_norm(attn_value, gain_attn)
    return (hidden, scaled_norm(hidden, gain_pre))


def layer_apart(tokens, cotangent, doc_lengths, w_query, w_key, w_value, w_out, w_gate, w_up, w_down, *gains):
    nb = lax.axis_size("blk")
    nz = nb // 4
    me = lax.axis_index("blk")
    _, micro, tok, width = tokens.shape
    n_dev = 2 * nb
    nq = 2 * nz
    kr = w_gate.shape[0]
    qr, qp = 4 * kr, up16(4 * kr)
    dr = w_down.shape[0]
    dp = up16(dr)
    orow = w_out.shape[0]
    op = up16(orow)
    groups = [[4 * i + j for j in range(4)] for i in range(nz)]

    def fit(x, rows):
        return x if x.shape[0] == rows else jnp.pad(x, ((0, rows - x.shape[0]), (0, 0)))

    def slices(w):
        w = jnp.pad(w.reshape(kr, nq, 4, dr), ((0, 0), (0, 0), (0, 0), (0, dp - dr)))
        return w.transpose(2, 0, 1, 3).reshape(4, kr, nq * dp)

    fs = nq * dp
    w_qkv = jnp.concatenate([w_query, w_key, w_value], axis=1)
    qw = w_qkv.shape[1] // 4
    pack = jnp.concatenate([slices(w_gate), slices(w_up), w_qkv.reshape(kr, 4, qw).transpose(1, 0, 2)], axis=2)
    pack = lax.all_to_all(pack, "blk", split_axis=0, concat_axis=0, axis_index_groups=groups, tiled=True)
    pack = fit(pack.reshape(qr, 2 * fs + qw), qp)
    wide = [gain.shape[0] for gain in gains]
    flat = jnp.concatenate(gains)
    flat = jnp.pad(flat, (0, 16 * 128 - flat.shape[0])).reshape(16, 128)

    qkv_f, wo_f, gain_f, wg_f, wu_f, wd_f = gather_all(
        nz, pack[:, 2 * fs :], fit(w_out, op), flat, pack[:, :fs], pack[:, fs : 2 * fs], fit(w_down, dp)
    )
    wqkv = qkv_f[:, :, :qr].reshape(width, 4 * qw)
    wo = wo_f[:, :, :, :, :orow].reshape(n_dev * orow, width)
    wg = wg_f[:, :, :qr].reshape(width, fs)
    wu = wu_f[:, :, :qr].reshape(width, fs)
    wd = wd_f.reshape(fs, width)
    gain_rows = gain_f.reshape(n_dev, 16 * 128)
    full_gains, o = [], 0
    for w in wide:
        full_gains.append(gain_rows[:, o : o + w].reshape(n_dev * w).astype(F32))
        o += w
    gain_in, gain_query, gain_key, gain_attn, gain_pre, gain_post = full_gains

    lengths = doc_lengths[0]
    seg_all, pos_all = segments(lengths, jnp.arange(nb * tok, dtype=jnp.int32))
    seg_me, pos = segments(lengths, me * tok + jnp.arange(tok, dtype=jnp.int32))
    segq = jnp.tile(seg_me, (1, H))[:, :, None]
    segk = seg_all.reshape(micro, nb * tok // 256, 1, 256)
    freq = 1000000.0 ** (-(jnp.arange(HD // 2, dtype=F32) * 2.0 / HD))
    angle = pos.reshape(micro * tok).astype(F32)[:, None] * freq[None, :]
    cosine, sine = jnp.cos(angle), jnp.sin(angle)

    rows = micro * tok
    x = tokens[0].reshape(rows, width).astype(F32)
    dy = cotangent[0].reshape(rows, width)
    normed, pre_pull = jax.vjp(scaled_norm, x, gain_in)
    a = normed.astype(BF16)
    qkv = jnp.dot(a, wqkv, preferred_element_type=F32)
    n_q = H * HD
    q_raw = qkv[:, :n_q].reshape(rows, H, HD)
    k_raw = qkv[:, n_q : n_q + HD]
    v = qkv[:, n_q + HD :].astype(BF16)
    queries, query_pull = jax.vjp(
        lambda r, g: rotate(scaled_norm(r, g), cosine[:, None], sine[:, None]), q_raw, gain_query
    )
    keys, key_pull = jax.vjp(lambda r, g: rotate(scaled_norm(r, g), cosine, sine), k_raw, gain_key)

    def by_head(z):
        return z.reshape(micro, tok, H, HD).transpose(0, 2, 1, 3).reshape(micro, H * tok, HD)

    def by_row(z):
        return z.reshape(micro, H, tok, HD).transpose(0, 2, 1, 3).reshape(rows, H * HD)

    qh = by_head(queries.astype(BF16))
    kv = jnp.concatenate([keys.astype(BF16), v], axis=1).reshape(micro, tok, 2 * HD)
    oh, lse, kvall = attn_fwd(nb, qh, kv, segq, segk)
    o_b = by_row(oh.astype(BF16))
    attn = jnp.dot(o_b, wo, preferred_element_type=F32)
    (h1, ffn_in), mid_pull = jax.vjp(middle, attn, x, gain_attn, gain_pre)

    shape = (micro, tok, width)
    out, db, dg_post, gg, gu, gd = ffn(
        ffn_in.astype(BF16).reshape(shape), h1.reshape(shape), dy.reshape(shape), gain_post[None, :], wg, wu, wd
    )
    d_attn, d_x_mid, dg_attn, dg_pre = mid_pull((dy.astype(F32), db.reshape(rows, width)))
    d_attn = d_attn.astype(BF16)
    grad_out = lax.dot_general(o_b, d_attn, (((0,), (0,)), ((), ())), preferred_element_type=F32).astype(BF16)
    do = lax.dot_general(d_attn, wo, (((1,), (1,)), ((), ())), preferred_element_type=F32).astype(BF16)
    doh = by_head(do)
    delta = jnp.sum(doh.astype(F32) * oh, axis=-1, keepdims=True)
    dqh, dkv = attn_bwd(nb, qh, kvall, doh, lse, delta, segq, segk)
    dkv = dkv.reshape(rows, 2 * HD)
    dq_raw, dg_query = query_pull(by_row(dqh).reshape(rows, H, HD))
    dk_raw, dg_key = key_pull(dkv[:, :HD])
    d_qkv = jnp.concatenate([dq_raw.reshape(rows, n_q), dk_raw, dkv[:, HD:]], axis=1).astype(BF16)
    grad_qkv = lax.dot_general(a, d_qkv, (((0,), (0,)), ((), ())), preferred_element_type=F32).astype(BF16)
    da = lax.dot_general(d_qkv, wqkv, (((1,), (1,)), ((), ())), preferred_element_type=F32)
    d_x_pre, dg_in = pre_pull(da)
    d_x = (d_x_mid + d_x_pre).astype(BF16)

    def quads(z, r, p):
        z = z.reshape(2, nz, r, z.shape[-1])
        return z if r == p else jnp.pad(z, ((0, 0), (0, 0), (0, p - r), (0, 0)))

    go = grad_out.reshape(2, nz, 2, 2, orow, width)
    if op != orow:
        go = jnp.pad(go, ((0, 0),) * 4 + ((0, op - orow), (0, 0)))
    dgains = jnp.concatenate(
        [d.reshape(n_dev, w) for d, w in zip((dg_in, dg_query, dg_key, dg_attn, dg_pre, dg_post[0]), wide)], axis=1
    )
    used = dgains.shape[1]
    dgains = jnp.pad(dgains, ((0, 0), (0, 8 * 128 - used))).reshape(2, nz, 2, 2, 8, 128)
    s_qkv, s_wo, s_gain, s_wg, s_wu, s_wd = reduce_all(
        nz, quads(grad_qkv, qr, qp), go, dgains, quads(gg, qr, qp), quads(gu, qr, qp), gd.reshape(2, nz, dp, width)
    )
    back = jnp.concatenate([s_wg, s_wu, s_qkv], axis=1)[:qr].reshape(4, kr, 2 * fs + qw)
    back = lax.all_to_all(back, "blk", split_axis=0, concat_axis=0, axis_index_groups=groups, tiled=True)
    back = back.astype(F32)

    def rows_of(z):
        z = z.reshape(4, kr, nq, dp)[..., :dr]
        return z.transpose(1, 2, 0, 3).reshape(kr, nq * 4 * dr)

    s_qkv = back[:, :, 2 * fs :].transpose(1, 0, 2).reshape(kr, 4 * qw)
    flat = s_gain.reshape(-1)
    gain_grads, o = [], 0
    for w in wide:
        gain_grads.append(flat[o : o + w])
        o += w
    return (
        out[None],
        d_x.reshape(shape)[None],
        s_qkv[:, :n_q],
        s_qkv[:, n_q : n_q + HD],
        s_qkv[:, n_q + HD :],
        s_wo[:orow],
        rows_of(back[:, :, :fs]),
        rows_of(back[:, :, fs : 2 * fs]),
        s_wd[:dr],
        *gain_grads,
    )


def layer_fused(tokens, cotangent, doc_lengths, w_query, w_key, w_value, w_out, w_gate, w_up, w_down, *gains):
    nb = lax.axis_size("blk")
    nz = nb // 4
    me = lax.axis_index("blk")
    _, micro, tok, width = tokens.shape
    rows = micro * tok
    nq = 2 * nz
    kr, dr = w_gate.shape[0], w_down.shape[0]
    kp, dp = up16(kr), up16(dr)
    shape = (micro, tok, width)

    flat = jnp.stack([jnp.pad(gain, (0, 128 - gain.shape[0])) for gain in gains] + [jnp.zeros((128,), BF16)] * 10)
    lengths = doc_lengths[0]
    _, pos = segments(lengths, me * tok + jnp.arange(tok, dtype=jnp.int32))
    freq = 1000000.0 ** (-(jnp.arange(HD // 2, dtype=F32) * 2.0 / HD))
    angle = pos.reshape(rows).astype(F32)[:, None] * freq[None, :]
    cosine, sine = jnp.cos(angle), jnp.sin(angle)
    x = tokens[0].reshape(rows, width)
    dy = cotangent[0]
    f = front(nz, x, cosine, sine, lengths, w_query, w_key, w_value, w_out, flat, w_gate, w_up, w_down, dp, micro)
    wg, wu, wd = (f[n].reshape(-1, f[n].shape[-1]) for n in ("wg", "wu", "wd"))
    fine = (2 * micro, tok // 2, width)
    out, db, dg_post, gg, gu, gd = mlp(f["ball"], f["h1"].reshape(fine), dy.reshape(fine), f["gd"], wg, wu, wd)
    out, db = out.reshape(shape), db.reshape(shape)
    d_x, s_q, s_k, s_v, s_wo, s_gain, s_wg, s_wu, s_wd = back(
        nz, db, f["h1"], dy.reshape(rows, width), x, cosine, sine, lengths, dg_post, f, gg, gu, gd, kp, dr
    )

    def rows_of(z):
        z = z[:, :kr].reshape(4, kr, nq, dp)[..., :dr].astype(F32)
        return z.transpose(1, 2, 0, 3).reshape(kr, nq * 4 * dr)

    return (
        out[None],
        d_x[None],
        s_q,
        s_k,
        s_v,
        s_wo,
        rows_of(s_wg),
        rows_of(s_wu),
        s_wd,
        *(s_gain[i, : gain.shape[0]] for i, gain in enumerate(gains)),
    )


def shards(tokens, cotangent, doc_lengths, *params):
    nb = lax.axis_size("blk")
    w_out, w_gate = params[3], params[4]
    fits = nb * tokens.shape[2] <= 2048 and (4 * w_gate.shape[0]) % 16 == 0 and w_out.shape[0] % 16 == 0
    layer = layer_fused if fits else layer_apart
    return layer(tokens, cotangent, doc_lengths, *params)


def solution(mesh):
    sequence = P("bucket", None, "blk", None)
    split = ("bucket", "blk")
    return jax.shard_map(
        shards,
        mesh=mesh,
        in_specs=(sequence, sequence, P("bucket", None, None)) + (P(split, None),) * 7 + (P(split),) * 6,
        out_specs=(sequence, sequence) + (P(split, None),) * 7 + (P(split),) * 6,
        check_vma=False,
    )
```
